32 devices in a mesh: dp: 8 (over z, x), mp: 4 (over y, core).
Axes of the slice: x: 2, y: 2, z: 4, core: 2. Of those that a mesh axis runs over, the one named last changes fastest.
Arguments:
- tokens: bfloat16 [16384, 768], P('dp'), may hold values from -6 to 6
- cotangent: bfloat16 [16384, 768], P('dp'), may hold values from -1.796875 to 1.796875
- lengths: int32 [8, 8], P('dp'), may hold values from 1 to 400, 2048 in all within a row
- gold: int32 [64], replicated, may hold values from 0 to 8191
- passages: bfloat16 [8192, 768], P('dp'), may hold values from -2 to 2
- w_query: bfloat16 [768, 768], P('dp', 'mp'), may hold values from -0.21875 to 0.21875
- w_key: bfloat16 [768, 768], P('dp', 'mp'), may hold values from -0.21875 to 0.21875
- w_value: bfloat16 [768, 768], P('dp', 'mp'), may hold values from -0.21875 to 0.21875
- b_query: float32 [768], P('mp'), may hold values from -1.2 to 1.2
- b_value: float32 [768], P('mp'), may hold values from -1.2 to 1.2
- w_out: bfloat16 [768, 768], P('mp', 'dp'), may hold values from -0.875 to 0.875
- b_out: float32 [768], replicated, may hold values from -1.2 to 1.2
- gain_attn: float32 [768], replicated, may hold values from 0.5 to 1.5
- shift_attn: float32 [768], replicated, may hold values from -1.2 to 1.2
- w_up: bfloat16 [768, 3072], P('dp', 'mp'), may hold values from -0.21875 to 0.21875
- b_up: float32 [3072], P('mp'), may hold values from -1.2 to 1.2
- w_down: bfloat16 [3072, 768], P('mp', 'dp'), may hold values from -0.109375 to 0.109375
- b_down: float32 [768], replicated, may hold values from -1.2 to 1.2
- gain_ffn: float32 [768], replicated, may hold values from 0.5 to 1.5
- shift_ffn: float32 [768], replicated, may hold values from -1.2 to 1.2
Outputs:
- scores: float32 [64, 8192], P(None, 'dp')
- query_lse: float32 [64], P('dp')
- encoded: bfloat16 [16384, 768], P('dp')
- token_grad: float32 [16384, 768], P('dp')
- grad_w_query: float32 [768, 768], P('dp', 'mp')
- grad_w_key: float32 [768, 768], P('dp', 'mp')
- grad_w_value: float32 [768, 768], P('dp', 'mp')
- grad_b_query: float32 [768], P('mp')
- grad_b_value: float32 [768], P('mp')
- grad_w_out: float32 [768, 768], P('mp', 'dp')
- grad_b_out: float32 [768], replicated
- grad_gain_attn: float32 [768], replicated
- grad_shift_attn: float32 [768], replicated
- grad_w_up: float32 [768, 3072], P('dp', 'mp')
- grad_b_up: float32 [3072], P('mp')
- grad_w_down: float32 [3072, 768], P('mp', 'dp')
- grad_b_down: float32 [768], replicated
- grad_gain_ffn: float32 [768], replicated
- grad_shift_ffn: float32 [768], replicated
The draws below stay inside these ranges and needn't reach their ends.
Inputs may be any that keep to these rules, and one draw needn't show every extreme that they name: Each row holds, in order, the lengths of the 8 documents packed into one sequence; every row sums to 2048 and its largest entry is 400. `gold`: the index of each query's correct passage among all 8192.
All inputs are finite; a program needn't handle non-finite values.
Results may differ from the reference program's by a relative error of at most 0.025.
Values may be sent and summed in bfloat16 or wider, within the bound.
A program may use at most 192 MiB of HBM per device.

```python
import math
import jax
import jax.numpy as jnp
import numpy as np
from jax import lax

D = 768
HEADS = 12
HEAD = 64
FF = 3072
TOK_DEV = 2048
MOST = 400
DOCS = 8
SEQS = 8
TOKENS = 16384
QUERIES = 64
PASSAGES = 8192
N_MP = 4


def draw_passages(key, part):
    key = jax.random.fold_in(key, 7)
    place = jnp.arange(PASSAGES, dtype=jnp.float32) / (PASSAGES - 1)
    top_scale = 5.5 / D ** 0.5
    entries = jnp.clip(jax.random.normal(key, (PASSAGES, D), jnp.float32), -4.0, 4.0)
    row_scale = top_scale * jnp.exp((place - 1.0) * 2.3025851)
    return (entries * row_scale[:, None]).astype(jnp.bfloat16)


def touch_ends(values, key, smallest, top_value):
    longest = values.shape.index(max(values.shape))
    spots = []
    for shift in (0, 1):
        where = [jax.random.randint(jax.random.fold_in(key, axis), (), 0, length) for axis, length in enumerate(values.shape)]
        where[longest] = (where[longest] + shift) % values.shape[longest]
        spots.append(tuple(where))
    return values.at[spots[0]].set(smallest).at[spots[1]].set(top_value)


def level_of(rng, extent, split, least, largest):
    level, own = 1.0, jax.random.fold_in(rng, 6)
    for dim, parts in split:
        heights = jnp.exp(jax.random.uniform(jax.random.fold_in(own, dim), (parts,), jnp.float32, least / len(split), largest / len(split)))
        level = level * jnp.repeat(heights, extent[dim] // parts).reshape([-1 if axis == dim else 1 for axis in range(len(extent))])
    return level


def profile(number_of, total, most, skew):
    portions = [(1 << 20) // math.isqrt(standing ** skew) + 1 for standing in range(2, number_of + 1)]
    spare, given = total - most - (number_of - 1), [1] * (number_of - 1)
    while spare > 0:
        movable = [i for i in range(number_of - 1) if given[i] < most]
        whole, left = sum([portions[i] for i in movable]), spare
        for i in movable:
            extra = min(most - given[i], max(1, left * portions[i] // whole), spare)
            given[i] = given[i] + extra
            spare = spare - extra
    return np.array([most] + given)


def ragged_sizes(stream_key, number_of, total, reach, slope):
    if number_of == 2:
        one = jax.random.randint(stream_key, (), max(1, total - reach), min(reach, total - 1) + 1)
        return jnp.stack([one, total - one])
    sizes = jnp.asarray(profile(number_of, total, reach, slope), jnp.int32)
    couples = (number_of - 1) // 2
    giver, receiver = sizes[1:1 + 2 * couples:2], sizes[2:2 + 2 * couples:2]
    room = jnp.minimum(giver - 1, reach - receiver)
    moved = jax.random.randint(jax.random.fold_in(stream_key, 1), (couples,), 0, 1 << 20) % (room + 1)
    sizes = sizes.at[1:1 + 2 * couples:2].set(giver - moved).at[2:2 + 2 * couples:2].set(receiver + moved)
    return sizes[jax.random.permutation(jax.random.fold_in(stream_key, 2), number_of)]


def gaussian(key, extent, width, bound, pieces=(), kind=jnp.bfloat16):
    array = width * jax.random.normal(key, extent, jnp.float32)
    if pieces:
        array = array * level_of(key, extent, pieces, -0.22, 0.18)
    return jnp.clip(array, -bound, bound).astype(kind)


def setup_inputs(seed: int = 0) -> dict:
    key_of = jax.random.split(jax.random.key(seed), 21)
    return {
        "tokens": gaussian(key_of[0], (TOKENS, D), 1.0, 6.0, ((0, 8),)),
        "cotangent": gaussian(key_of[1], (TOKENS, D), 0.3, 1.796875, ((0, 8),)),
        "lengths": jax.vmap(lambda own: ragged_sizes(own, DOCS, TOK_DEV, MOST, 2))(jax.random.split(key_of[2], SEQS)).reshape((SEQS, DOCS)).astype(jnp.int32),
        "gold": touch_ends(jax.random.randint(key_of[3], (QUERIES,), 0, PASSAGES), jax.random.fold_in(key_of[3], 1), 0, PASSAGES - 1).astype(jnp.int32),
        "passages": draw_passages(jax.random.fold_in(key_of[20], 71), 0),
        "w_query": gaussian(key_of[5], (D, D), D ** -0.5, 0.21875, ((0, 8), (1, 4))),
        "w_key": gaussian(key_of[6], (D, D), D ** -0.5, 0.21875, ((0, 8), (1, 4))),
        "w_value": gaussian(key_of[7], (D, D), D ** -0.5, 0.21875, ((0, 8), (1, 4))),
        "b_query": gaussian(key_of[8], (D,), 0.2, 1.2, ((0, 4),), jnp.float32),
        "b_value": gaussian(key_of[9], (D,), 0.2, 1.2, ((0, 4),), jnp.float32),
        "w_out": gaussian(key_of[10], (D, D), (D // 16) ** -0.5, 0.875, ((0, 4), (1, 8))),
        "b_out": gaussian(key_of[11], (D,), 0.2, 1.2, (), jnp.float32),
        "gain_attn": jnp.clip(1.0 + 0.1 * jax.random.normal(key_of[12], (D,), jnp.float32), 0.5, 1.5),
        "shift_attn": gaussian(key_of[13], (D,), 0.2, 1.2, (), jnp.float32),
        "w_up": gaussian(key_of[14], (D, FF), D ** -0.5, 0.21875, ((0, 8), (1, 4))),
        "b_up": gaussian(key_of[15], (FF,), 0.2, 1.2, ((0, 4),), jnp.float32),
        "w_down": gaussian(key_of[16], (FF, D), FF ** -0.5, 0.109375, ((0, 4), (1, 8))),
        "b_down": gaussian(key_of[17], (D,), 0.2, 1.2, (), jnp.float32),
        "gain_ffn": jnp.clip(1.0 + 0.1 * jax.random.normal(key_of[18], (D,), jnp.float32), 0.5, 1.5),
        "shift_ffn": gaussian(key_of[19], (D,), 0.2, 1.2, (), jnp.float32),
    }


EPSILON = 1e-05
NEGATIVE = -1e+30

@jax.custom_vjp
def low(v):
    return lax.optimization_barrier(v.astype(jnp.bfloat16)).astype(jnp.float32)

@jax.custom_vjp
def low_back(v):
    return v

def low_keep(v):
    return (low(v), None)

def low_pass(kept, grad):
    return (grad,)

def back_keep(v):
    return (v, None)

def back_low(kept, grad):
    return (low(grad),)
low.defvjp(low_keep, low_pass)
low_back.defvjp(back_keep, back_low)

def product(form, left, right):
    return jnp.einsum(form, left, right, precision=lax.Precision.HIGHEST)

def normalize(hidden, gain, shift):
    average = lax.optimization_barrier(jnp.mean(hidden, axis=-1, keepdims=True))
    centred = hidden - average
    spread = lax.optimization_barrier(jnp.mean(centred * centred, axis=-1, keepdims=True))
    return centred * lax.rsqrt(spread + EPSILON) * gain + shift

def document_marks(lengths, span):
    ends = jnp.cumsum(lengths, axis=-1).astype(jnp.int32)
    places = jnp.arange(span, dtype=jnp.int32)
    segments = lax.optimization_barrier(jnp.sum((places[None, None, :] >= ends[:, :, None]).astype(jnp.int32), axis=1)).astype(jnp.int32)
    return (segments, (ends - lengths).astype(jnp.int32))

def grouped(weight, inner_width):
    return weight.reshape(D, N_MP, inner_width).transpose(1, 0, 2)

def encode(tokens_in, segments, params):
    w_query, w_key, w_value, b_query, b_value, w_out, b_out, gain_attn, shift_attn, w_up, b_up, w_down, b_down, gain_ffn, shift_ffn = params
    span = tokens_in.shape[0]
    head_cols = D // N_MP
    head_count = HEADS // N_MP
    ffn_cols = FF // N_MP
    score_scale = HEAD ** (-0.5)
    copies = low(low_back(jnp.broadcast_to(tokens_in, (N_MP, span, D))))
    query_rows = low(low_back(product('gld,gde->gle', copies, grouped(w_query, head_cols))) + b_query.reshape(N_MP, 1, head_cols))
    key_rows = low(low_back(product('gld,gde->gle', copies, grouped(w_key, head_cols))))
    value_rows = low(low_back(product('gld,gde->gle', copies, grouped(w_value, head_cols))) + b_value.reshape(N_MP, 1, head_cols))
    query_rows = query_rows.reshape(N_MP, span, head_count, HEAD)
    key_rows = key_rows.reshape(N_MP, span, head_count, HEAD)
    value_rows = value_rows.reshape(N_MP, span, head_count, HEAD)
    raw_scores = low_back(product('glhe,gmhe->ghlm', query_rows, key_rows) * score_scale)
    same_doc = segments[:, None] == segments[None, :]
    soft_weights = jax.nn.softmax(jnp.where(same_doc, raw_scores, NEGATIVE), axis=-1)
    context = product('ghlm,gmhe->glhe', low(soft_weights), value_rows).reshape(N_MP, span, head_cols)
    context = low(low_back(context))
    partial_attn = low(product('gle,ged->gld', context, w_out.reshape(N_MP, head_cols, D)))
    hidden_one = tokens_in + low_back(lax.optimization_barrier(jnp.sum(partial_attn, axis=0))) + b_out
    normed_one = normalize(hidden_one, gain_attn, shift_attn)
    copies_ffn = low(low_back(jnp.broadcast_to(normed_one, (N_MP, span, D))))
    activation = low_back(product('gld,gdf->glf', copies_ffn, grouped(w_up, ffn_cols))) + b_up.reshape(N_MP, 1, ffn_cols)
    gelu_out = low(jax.nn.gelu(activation, approximate=False))
    partial_ffn = low(product('glf,gfd->gld', gelu_out, w_down.reshape(N_MP, ffn_cols, D)))
    hidden_two = normed_one + low_back(lax.optimization_barrier(jnp.sum(partial_ffn, axis=0))) + b_down
    return normalize(hidden_two, gain_ffn, shift_ffn)

def reference(tokens, cotangent, lengths, gold, passages, w_query, w_key, w_value, b_query, b_value, w_out, b_out, gain_attn, shift_attn, w_up, b_up, w_down, b_down, gain_ffn, shift_ffn):
    segments, starts = document_marks(lengths, TOK_DEV)
    params = tuple((weight.astype(jnp.float32) for weight in (w_query, w_key, w_value, b_query, b_value, w_out, b_out, gain_attn, shift_attn, w_up, b_up, w_down, b_down, gain_ffn, shift_ffn)))
    inputs_f = tokens.astype(jnp.float32).reshape(SEQS, TOK_DEV, D)
    cot_f = cotangent.astype(jnp.float32).reshape(SEQS, TOK_DEV, D)
    table = passages.astype(jnp.float32)
    encode_saved = jax.checkpoint(encode)

    def objective(inputs_all, weights_all):
        encoded_all = lax.map(lambda packed: encode_saved(packed[0], packed[1], weights_all), (inputs_all, segments))
        first_rows = jnp.take_along_axis(encoded_all, starts[:, :, None], axis=1).reshape(QUERIES, D)
        score_table = low_back(product('qd,pd->qp', low(first_rows), table))
        picked = jnp.take_along_axis(score_table, gold[:, None], axis=1)[:, 0]
        row_lse = jax.nn.logsumexp(score_table, axis=-1)
        loss = jnp.sum(row_lse - picked)
        return (jnp.sum(cot_f * encoded_all) + loss, (score_table, row_lse, encoded_all))
    objective_value, pullback, (score_table, row_lse, encoded_all) = jax.vjp(objective, inputs_f, params, has_aux=True)
    grad_inputs, grads = pullback(jnp.ones_like(objective_value))
    return (score_table, row_lse, encoded_all.reshape(TOKENS, D).astype(jnp.bfloat16), grad_inputs.reshape(TOKENS, D), grads[0], grads[1], grads[2], grads[3], grads[4], grads[5], grads[6], grads[7], grads[8], grads[9], grads[10], grads[11], grads[12], grads[13], grads[14])
```

```python
import functools

import jax
import jax.numpy as jnp
from jax import lax
from jax.experimental import pallas as pl
from jax.experimental.pallas import tpu as pltpu
from jax.sharding import PartitionSpec as P

HEAD = 64
LONGEST = 400
QUERY_BLOCK = 256
EPSILON = 1e-05
NEGATIVE = -1e30
LANES = 128
KEY_AT = ((0, 0), (0, 1), (1, 0))
VALUE_AT = ((1, 1), (2, 0), (2, 1))
QUERY_AT = ((0, 0), (0, 1), (1, 0))
CONTEXT_AT = ((0, 1), (1, 0), (1, 1))
F32, BF16 = jnp.float32, jnp.bfloat16
VMEM, ANY, SMEM = pltpu.VMEM, pl.ANY, pltpu.SMEM


def dot(left, right, left_dim=1, right_dim=0):
    return lax.dot_general(
        left, right, (((left_dim,), (right_dim,)), ((), ())), preferred_element_type=F32
    )


def tile(index, count=1):
    return slice(index * LANES, (index + count) * LANES)


def half_mask(half, dtype):
    lane = lax.broadcasted_iota(jnp.int32, (1, LANES), 1)
    return jnp.where((lane >= HEAD) == (half == 1), 1.0, 0.0).astype(dtype)


def norm_stats(hidden):
    centred = hidden - jnp.mean(hidden, axis=-1, keepdims=True)
    factor = lax.rsqrt(jnp.mean(centred * centred, axis=-1, keepdims=True) + EPSILON)
    return centred * factor, factor


def norm_back(grad_out, normed, factor, gain):
    scaled = grad_out * gain
    inner = jnp.mean(scaled * normed, axis=-1, keepdims=True)
    return factor * (scaled - jnp.mean(scaled, axis=-1, keepdims=True) - normed * inner)


def gelu_and_slope(a):
    size = jnp.abs(a)
    t = 1.0 / (1.0 + (0.3275911 * 0.7071067811865476) * size)
    bell = jnp.exp(-0.5 * a * a)
    poly = t * (
        0.127414796 + t * (-0.142248368 + t * (0.7107068705 + t * (-0.7265760135 + t * 0.5307027145)))
    )
    tail = poly * bell
    phi = jnp.where(a >= 0.0, 1.0 - tail, tail)
    return a * phi, phi + a * bell * 0.3989422804014327


class Sizes:
    def __init__(self, length, width, groups):
        self.length, self.width, self.groups = length, width, groups
        self.own = length // groups
        self.window = min(length, self.own + 2 * LONGEST)
        self.block = min(QUERY_BLOCK, self.own)
        self.blocks = self.own // self.block
        self.keys = min(length, self.block + 2 * LONGEST)

    def window_start(self, me):
        return jnp.clip(self.own * me - LONGEST, 0, self.length - self.window)

    def own_offset(self, me):
        return pl.multiple_of(self.own * me - self.window_start(me), 16)

    def key_start(self, me, block):
        first = self.own * me + block * self.block
        return jnp.clip(first - LONGEST, 0, self.length - self.keys)

    def key_offset(self, me, block):
        return pl.multiple_of(self.key_start(me, block) - self.window_start(me), 16)


def document_bounds(lens, places):
    start = jnp.zeros_like(places)
    end = jnp.zeros_like(places)
    total = jnp.int32(0)
    for d in range(lens.shape[1]):
        count = lens[0, d]
        end = end + jnp.where(places >= total, count, 0)
        total = total + count
        start = start + jnp.where(places >= total, count, 0)
    return start, end


def fill_mask(sizes, me, lens, bias):
    for b in range(sizes.blocks):
        places = (
            sizes.own * me
            + b * sizes.block
            + lax.broadcasted_iota(jnp.int32, (1, sizes.block), 1)
        )
        start, end = document_bounds(lens, places)
        keys = sizes.key_start(me, b) + lax.broadcasted_iota(
            jnp.int32, (sizes.keys, sizes.block), 0
        )
        bias[b] = jnp.where((keys >= start) & (keys < end), 0.0, NEGATIVE)


def start_rows(sizes, me, lens):
    docs = lens.shape[1]
    row = lax.broadcasted_iota(jnp.int32, (docs, sizes.own), 0)
    place = sizes.own * me + lax.broadcasted_iota(jnp.int32, (docs, sizes.own), 1)
    picked = jnp.zeros((docs, sizes.own), F32)
    total = jnp.int32(0)
    for d in range(docs):
        picked = jnp.where((row == d) & (place == total), 1.0, picked)
        total = total + lens[0, d]
    return picked


def project(sizes, me, tokens, w_attn, biases, kv, q):
    cut = sizes.window // 2
    own = pl.ds(sizes.own_offset(me), sizes.own)

    @pl.loop(0, sizes.groups)
    def _(g):
        for part in range(2):
            rows = pl.ds(part * cut, cut)
            made = dot(tokens[rows, :], w_attn[g, :, tile(0, 3)]) + biases[g, :, tile(0, 3)]
            kv[g, rows, :] = made.astype(BF16)
        made = dot(tokens[own, :], w_attn[g, :, tile(3, 2)]) + biases[g, :, tile(3, 2)]
        q[g] = made.astype(BF16) * jnp.asarray(HEAD**-0.5, BF16)


def attend(sizes, me, kv, q, bias, lse, ctx):
    @pl.loop(0, sizes.groups)
    def _(g):
        @pl.loop(0, sizes.blocks)
        def _(b):
            keys = pl.ds(sizes.key_offset(me, b), sizes.keys)
            rows = pl.ds(pl.multiple_of(b * sizes.block, sizes.block), sizes.block)
            made = [jnp.zeros((HEAD, sizes.block), F32)]
            logs = []
            for j in range(3):
                kt, kh = KEY_AT[j]
                vt, vh = VALUE_AT[j]
                qt, _ = QUERY_AT[j]
                query = q[g, rows, tile(qt)] * half_mask(kh, BF16)
                s = dot(kv[g, keys, tile(kt)], query, 1, 1) + bias[b]
                peak = jnp.max(s, axis=0, keepdims=True)
                e = jnp.exp(s - peak)
                total = jnp.sum(e, axis=0, keepdims=True)
                mixed = dot(kv[g, keys, tile(vt)], e.astype(BF16), 0, 0)
                made.append(mixed[vh * HEAD : (vh + 1) * HEAD] / total)
                logs.append(peak + jnp.log(total))
            ctx[g, rows, :] = jnp.concatenate(made, axis=0).T.astype(BF16)
            for j in range(3):
                lse[g, b, j : j + 1, :] = logs[j]


def attend_back(sizes, me, kv, q, bias, lse, ctx, dctx, delta, dkv, dq):
    lane = lax.broadcasted_iota(jnp.int32, (8, 2 * LANES), 1)
    row = lax.broadcasted_iota(jnp.int32, (8, 2 * LANES), 0)
    pick = jnp.where(lane // HEAD == row + 1, 1.0, 0.0).astype(BF16)

    @pl.loop(0, sizes.groups)
    def _(g):
        product = dctx[g].astype(F32) * ctx[g].astype(F32)
        high = product.astype(BF16)
        low = (product - high.astype(F32)).astype(BF16)
        delta[...] = dot(pick, high, 1, 1) + dot(pick, low, 1, 1)
        dkv[g] = jnp.zeros_like(dkv[g])

        for b in range(sizes.blocks):
            keys = pl.ds(sizes.key_offset(me, b), sizes.keys)
            rows = slice(b * sizes.block, (b + 1) * sizes.block)
            made = []
            for j in range(3):
                kt, kh = KEY_AT[j]
                vt, vh = VALUE_AT[j]
                qt, _ = QUERY_AT[j]
                ct, _ = CONTEXT_AT[j]
                query = q[g, rows, tile(qt)] * half_mask(kh, BF16)
                grad = dctx[g, rows, tile(ct)] * half_mask(vh, BF16)
                s = dot(kv[g, keys, tile(kt)], query, 1, 1) + bias[b]
                p = jnp.exp(s - lse[g, b, j : j + 1, :])
                dp = dot(kv[g, keys, tile(vt)], grad, 1, 1)
                ds = (p * (dp - delta[j : j + 1, rows])).astype(BF16)
                dkv[g, keys, tile(kt)] += dot(ds, query)
                dkv[g, keys, tile(vt)] += dot(p.astype(BF16), grad)
                back = dot(kv[g, keys, tile(kt)], ds, 0, 0)
                made.append(back[kh * HEAD : (kh + 1) * HEAD] * HEAD**-0.5)
            made.append(jnp.zeros((HEAD, sizes.block), F32))
            dq[g, rows, :] = jnp.concatenate(made, axis=0).T


def forward_kernel(
    sizes,
    lens,
    tokens,
    weights,
    biases,
    b_out,
    gain_1,
    shift_1,
    b_down,
    gain_2,
    shift_2,
    encoded,
    cls,
    n_1,
    r_1,
    n_2,
    r_2,
    z,
    slope,
    kv,
    q,
    lse,
    ctx,
    x,
    w,
    bias,
    hidden,
    sems,
):
    me = lax.axis_index("mp")
    first = pl.multiple_of(sizes.window_start(me), 16)
    load = pltpu.make_async_copy(tokens.at[pl.ds(first, sizes.window)], x, sems.at[3])
    load.start()
    loads = []
    for s in range(3):
        loads.append(pltpu.make_async_copy(weights.at[:, s], w.at[s], sems.at[s]))
        loads[-1].start()
    fill_mask(sizes, me, lens, bias)
    load.wait()
    loads[0].wait()
    project(sizes, me, x, w.at[0], biases, kv, q)
    attend(sizes, me, kv, q, bias, lse, ctx)

    own = pl.ds(sizes.own_offset(me), sizes.own)
    hidden[...] = x[own, :].astype(F32) + b_out[...]
    for g in range(sizes.groups):
        hidden[...] += dot(ctx[g], w[0, g, :, tile(4, 2)], 1, 1)
    normed, factor = norm_stats(hidden[...])
    n_1[...] = normed
    r_1[...] = factor
    y_1 = normed * gain_1[...] + shift_1[...]
    hidden[...] = y_1 + b_down[...]
    encoded[...] = y_1.astype(BF16)
    loads[1].wait()
    loads[2].wait()

    @pl.loop(0, sizes.groups)
    def _(g):
        a = dot(encoded[...], w[1, g]) + biases[g, :, 5 * LANES :]
        out, grad = gelu_and_slope(a)
        z[g] = out.astype(BF16)
        slope[g] = grad.astype(BF16)
        hidden[...] += dot(z[g], w[2, g], 1, 1)

    normed, factor = norm_stats(hidden[...])
    n_2[...] = normed
    r_2[...] = factor
    y_2 = (normed * gain_2[...] + shift_2[...]).astype(BF16)
    encoded[...] = y_2
    cls[...] = dot(start_rows(sizes, me, lens).astype(BF16), y_2)


def backward_kernel(
    sizes,
    lens,
    cotangent,
    dcls,
    weights,
    gain_1,
    shift_1,
    gain_2,
    n_1,
    r_1,
    n_2,
    r_2,
    z,
    slope,
    kv,
    q,
    lse,
    ctx,
    dh_1,
    dkv,
    dq,
    grads,
    grads_out,
    small,
    w_attn,
    w_up,
    w_down,
    cot,
    dh,
    low,
    other,
    turned,
    stage,
    dctx,
    delta,
    bias,
    sems,
    out_sems,
):
    me = lax.axis_index("mp")
    load_cot = pltpu.make_async_copy(
        cotangent.at[pl.ds(pl.multiple_of(sizes.own * me, 16), sizes.own)], cot, sems.at[3]
    )
    load_cot.start()
    loads = []
    for s, buffer in ((2, w_down), (1, w_up), (0, w_attn)):
        loads.append(pltpu.make_async_copy(weights.at[:, s], buffer, sems.at[s]))
        loads[-1].start()
    fill_mask(sizes, me, lens, bias)
    picked = start_rows(sizes, me, lens).astype(BF16)
    high = dcls[...].astype(BF16)
    low_part = (dcls[...] - high.astype(F32)).astype(BF16)
    load_cot.wait()
    dy = cot[...].astype(F32) + dot(picked, high, 0, 0) + dot(picked, low_part, 0, 0)
    small[0:1, :] = jnp.sum(dy * n_2[...], axis=0, keepdims=True)
    small[1:2, :] = jnp.sum(dy, axis=0, keepdims=True)
    grad = norm_back(dy, n_2[...], r_2[...], gain_2[...])
    small[2:3, :] = jnp.sum(grad, axis=0, keepdims=True)
    dh[...] = grad
    low[...] = grad.astype(BF16)
    turned[0] = grad.T.astype(BF16)
    y_1 = n_1[...] * gain_1[...] + shift_1[...]
    other[...] = y_1.astype(BF16)
    turned[1] = y_1.T.astype(BF16)
    for load in loads:
        load.wait()

    def out_copy(section, g, slot):
        return pltpu.make_async_copy(
            stage.at[slot], grads.at[section, g], out_sems.at[slot]
        )

    @pl.loop(0, sizes.groups)
    def _(g):
        @pl.when(g > 0)
        def _():
            out_copy(1, 0, 0).wait()
            out_copy(1, 0, 1).wait()

        stage[1] = dot(turned[0], z[g]).astype(BF16)
        out_copy(1, g, 1).start()
        da = dot(low[...], w_down[g]) * slope[g].astype(F32)
        small[pl.ds(8 + g, 1), :] = jnp.sum(da, axis=0, keepdims=True)
        da_low = da.astype(BF16)
        stage[0] = dot(turned[1], da_low).astype(BF16)
        out_copy(0, g, 0).start()
        dh[...] += dot(da_low, w_up[g], 1, 1)

    dy = dh[...]
    small[3:4, :] = jnp.sum(dy * n_1[...], axis=0, keepdims=True)
    small[4:5, :] = jnp.sum(dy, axis=0, keepdims=True)
    grad = norm_back(dy, n_1[...], r_1[...], gain_1[...])
    small[5:6, :] = jnp.sum(grad, axis=0, keepdims=True)
    small[6:8, :] = jnp.zeros_like(small[6:8, :])
    small[12:16, :] = jnp.zeros_like(small[12:16, :])
    dh_1[...] = grad
    low[...] = grad.astype(BF16)
    turned[0] = grad.T.astype(BF16)

    @pl.loop(0, sizes.groups)
    def _(g):
        dctx[g] = dot(low[...], w_attn[g, :, tile(4, 2)]).astype(BF16)
        grads_out[g] = dot(turned[0], ctx[g])

    attend_back(sizes, me, kv, q, bias, lse, ctx, dctx, delta, dkv, dq)
    out_copy(1, 0, 0).wait()
    out_copy(1, 0, 1).wait()


def input_kernel(sizes, tokens, weights, dkv, dq, dh_1, grads_out, token_grad, grads, small, turned, low):
    turned[...] = tokens[...].astype(F32).T.astype(BF16)
    total = dh_1[...]
    for g in range(sizes.groups):
        small[g, :, tile(0, 3)] = jnp.sum(dkv[g], axis=0, keepdims=True)
        small[g, :, tile(3, 2)] = jnp.sum(dq[g], axis=0, keepdims=True)
        low[:, tile(0, 3)] = dkv[g].astype(BF16)
        low[:, tile(3, 2)] = dq[g].astype(BF16)
        total = total + dot(low[...], weights[g, :, tile(0, 5)], 1, 1)
        made = dot(turned[...], low[...])
        grads[g, :, tile(0, 4)] = made[:, tile(0, 4)].astype(BF16)
        grads[g, :, tile(4)] = (made[:, tile(4)] + grads_out[g, :, tile(0)]).astype(BF16)
        grads[g, :, tile(5)] = grads_out[g, :, tile(1)].astype(BF16)
    token_grad[...] = total.astype(BF16)


def specs(*spaces):
    return [pl.BlockSpec(memory_space=s) for s in spaces]


def params(**more):
    return pltpu.CompilerParams(vmem_limit_bytes=62 * 2**20, **more)


def run_forward(sizes, lengths, tokens, weights, biases, rows):
    own, width, groups = sizes.own, sizes.width, sizes.groups
    docs = lengths.shape[1]
    shape = jax.ShapeDtypeStruct
    outs = (
        shape((own, width), BF16),
        shape((docs, width), F32),
        shape((own, width), F32),
        shape((own, 1), F32),
        shape((own, width), F32),
        shape((own, 1), F32),
        shape((groups, own, width), BF16),
        shape((groups, own, width), BF16),
        shape((groups, sizes.window, 3 * LANES), BF16),
        shape((groups, own, 2 * LANES), BF16),
        shape((groups, sizes.blocks, 8, sizes.block), F32),
        shape((groups, own, 2 * LANES), BF16),
    )
    return pl.pallas_call(
        functools.partial(forward_kernel, sizes),
        out_shape=outs,
        in_specs=specs(SMEM, ANY, ANY, *[VMEM] * 7),
        out_specs=specs(*[VMEM] * len(outs)),
        scratch_shapes=[
            pltpu.VMEM((sizes.window, width), BF16),
            pltpu.VMEM((3, groups, width, width), BF16),
            pltpu.VMEM((sizes.blocks, sizes.keys, sizes.block), F32),
            pltpu.VMEM((own, width), F32),
            pltpu.SemaphoreType.DMA((4,)),
        ],
        compiler_params=params(),
        name="forward",
    )(lengths, tokens, weights, biases, *rows)


def run_backward(sizes, lengths, cotangent, dcls, weights, gain_1, shift_1, gain_2, saved):
    own, width, groups = sizes.own, sizes.width, sizes.groups
    shape = jax.ShapeDtypeStruct
    outs = (
        shape((own, width), F32),
        shape((groups, sizes.window, 3 * LANES), F32),
        shape((groups, own, 2 * LANES), F32),
        shape((2, groups, width, width), BF16),
        shape((groups, width, 2 * LANES), F32),
        shape((16, width), F32),
    )
    return pl.pallas_call(
        functools.partial(backward_kernel, sizes),
        out_shape=outs,
        in_specs=specs(SMEM, ANY, VMEM, ANY, *[VMEM] * (3 + len(saved))),
        out_specs=specs(VMEM, VMEM, VMEM, ANY, VMEM, VMEM),
        scratch_shapes=[
            pltpu.VMEM((groups, width, width), BF16),
            pltpu.VMEM((groups, width, width), BF16),
            pltpu.VMEM((groups, width, width), BF16),
            pltpu.VMEM((own, width), BF16),
            pltpu.VMEM((own, width), F32),
            pltpu.VMEM((own, width), BF16),
            pltpu.VMEM((own, width), BF16),
            pltpu.VMEM((2, width, own), BF16),
            pltpu.VMEM((2, width, width), BF16),
            pltpu.VMEM((groups, own, 2 * LANES), BF16),
            pltpu.VMEM((8, own), F32),
            pltpu.VMEM((sizes.blocks, sizes.keys, sizes.block), F32),
            pltpu.SemaphoreType.DMA((4,)),
            pltpu.SemaphoreType.DMA((2,)),
        ],
        compiler_params=params(),
        name="backward",
    )(lengths, cotangent, dcls, weights, gain_1, shift_1, gain_2, *saved)


def run_input(sizes, own_tokens, w_attn, dkv, dq, dh_1, grads_out):
    own, width, groups = sizes.own, sizes.width, sizes.groups
    shape = jax.ShapeDtypeStruct
    outs = (
        shape((own, width), BF16),
        shape((groups, width, width), BF16),
        shape((groups, 1, 5 * LANES), F32),
    )
    return pl.pallas_call(
        functools.partial(input_kernel, sizes),
        out_shape=outs,
        in_specs=specs(*[VMEM] * 6),
        out_specs=specs(*[VMEM] * 3),
        scratch_shapes=[pltpu.VMEM((width, own), BF16), pltpu.VMEM((own, 5 * LANES), BF16)],
        compiler_params=params(),
        name="inputs",
    )(own_tokens, w_attn, dkv, dq, dh_1, grads_out)


def cut_along(array, dim, devices):
    before, after = (array.shape[:dim], array.shape[dim + 1 :])
    return jnp.moveaxis(array.reshape(*before, devices, -1, *after), dim, 0)


def summed_on_arrival(array, axis, dim):
    pieces = cut_along(array, dim, lax.axis_size(axis))
    arrived = lax.all_to_all(pieces, axis, split_axis=0, concat_axis=0, tiled=True)
    return arrived.astype(F32).sum(axis=0)


def score(cls, passages, gold):
    all_first = lax.all_gather(cls, "dp", axis=0, tiled=True)
    table = dot(all_first, passages, 1, 1)
    peak = lax.pmax(jnp.max(table, axis=1), "dp")
    total = lax.psum(jnp.sum(jnp.exp(table - peak[:, None]), axis=1), "dp")
    own = cls.shape[0]
    lse = lax.dynamic_slice_in_dim(peak + jnp.log(total), lax.axis_index("dp") * own, own)
    soft = jnp.exp(table - peak[:, None]) / total[:, None]
    first = lax.axis_index("dp") * table.shape[1]
    columns = first + jnp.arange(table.shape[1], dtype=jnp.int32)
    target = (gold[:, None] == columns[None, :]).astype(F32)
    grad = dot((soft - target).astype(BF16), passages)
    return table, lse, summed_on_arrival(grad.astype(BF16), "dp", 0)


def body(
    tokens,
    cotangent,
    lengths,
    gold,
    passages,
    w_query,
    w_key,
    w_value,
    b_query,
    b_value,
    w_out,
    b_out,
    gain_attn,
    shift_attn,
    w_up,
    b_up,
    w_down,
    b_down,
    gain_ffn,
    shift_ffn,
):
    groups = lax.axis_size("mp")
    sizes = Sizes(tokens.shape[0], tokens.shape[1], groups)
    me = lax.axis_index("mp")
    head_cols = w_query.shape[1]
    packed = jnp.stack(
        [jnp.concatenate([w_key, w_value, w_query, w_out.T], axis=1), w_up, w_down.T]
    )
    whole = lax.all_gather(lax.all_gather(packed, "dp", axis=1, tiled=True), "mp", axis=0)
    zeros = jnp.zeros((head_cols,), F32)
    own_bias = jnp.concatenate([zeros, b_value, b_query, zeros[:HEAD], b_up])
    biases = lax.all_gather(own_bias[None], "mp", axis=0)
    rows = [r[None] for r in (b_out, gain_attn, shift_attn, b_down, gain_ffn, shift_ffn)]
    encoded, cls, *saved = run_forward(sizes, lengths, tokens, whole, biases, rows)
    cls = lax.psum(cls, "mp").astype(BF16)
    table, lse, dcls = score(cls, passages, gold)
    n_1, r_1, n_2, r_2, z, slope, kv, q, logs, ctx = saved
    dh_1, dkv, dq, grads_ffn, grads_out, small = run_backward(
        sizes, lengths, cotangent, dcls, whole, rows[1], rows[2], rows[4], saved
    )
    halo, own = LONGEST, sizes.own
    offset = own * me - sizes.window_start(me)
    to_left = lax.dynamic_slice_in_dim(dkv, offset - halo, halo, axis=1).astype(BF16)
    to_right = lax.dynamic_slice_in_dim(dkv, offset + own, halo, axis=1).astype(BF16)
    from_right = lax.ppermute(to_left, "mp", [(i, i - 1) for i in range(1, groups)])
    from_left = lax.ppermute(to_right, "mp", [(i, i + 1) for i in range(groups - 1)])
    dkv = lax.dynamic_slice_in_dim(dkv, offset, own, axis=1)
    dkv = dkv.at[:, own - halo :].add(from_right.astype(F32))
    dkv = dkv.at[:, :halo].add(from_left.astype(F32))
    own_tokens = lax.dynamic_slice_in_dim(tokens, own * me, own, axis=0)
    token_part, grads_attn, small_attn = run_input(
        sizes, own_tokens, whole[:, 0], dkv, dq, dh_1, grads_out
    )
    token_grad = lax.all_gather(token_part, "mp", axis=0, tiled=True).astype(F32)
    encoded = lax.all_gather(encoded, "mp", axis=0, tiled=True)
    grads = jnp.stack([grads_attn, grads_ffn[0], grads_ffn[1]])
    grads = summed_on_arrival(grads, "mp", 1)[:, 0].astype(BF16)
    grads = summed_on_arrival(grads, "dp", 1)
    small, small_attn = lax.psum((small, small_attn), ("dp", "mp"))
    mine = lax.dynamic_index_in_dim(small_attn[:, 0], me, 0, keepdims=False)
    up_bias = lax.dynamic_index_in_dim(small, 8 + me, 0, keepdims=False)
    c = head_cols
    return (
        table,
        lse,
        encoded,
        token_grad,
        grads[0, :, 2 * c : 3 * c],
        grads[0, :, :c],
        grads[0, :, c : 2 * c],
        mine[2 * c : 3 * c],
        mine[c : 2 * c],
        grads[0, :, 3 * c :].T,
        small[5],
        small[3],
        small[4],
        grads[1],
        up_bias,
        grads[2].T,
        small[2],
        small[0],
        small[1],
    )


def solution(mesh):
    by_dp, shared, cross = P("dp", None), P(), P("dp", "mp")
    return jax.shard_map(
        body,
        mesh=mesh,
        in_specs=(
            by_dp,
            by_dp,
            by_dp,
            shared,
            by_dp,
            cross,
            cross,
            cross,
            P("mp"),
            P("mp"),
            P("mp", "dp"),
            shared,
            shared,
            shared,
            cross,
            P("mp"),
            P("mp", "dp"),
            shared,
            shared,
            shared,
        ),
        out_specs=(
            P(None, "dp"),
            P("dp"),
            by_dp,
            by_dp,
            cross,
            cross,
            cross,
            P("mp"),
            P("mp"),
            P("mp", "dp"),
            shared,
            shared,
            shared,
            cross,
            P("mp"),
            P("mp", "dp"),
            shared,
            shared,
            shared,
        ),
        check_vma=False,
    )
```

```python
import functools

import jax
import jax.numpy as jnp
from jax import lax
from jax.experimental import pallas as pl
from jax.experimental.pallas import tpu as pltpu
from jax.sharding import PartitionSpec as P

HEAD = 64
LONGEST = 400
QUERY_BLOCK = 256
EPSILON = 1e-05
NEGATIVE = -1e30
LANES = 128
KEY_AT = ((0, 0), (0, 1), (1, 0))
VALUE_AT = ((1, 1), (2, 0), (2, 1))
QUERY_AT = ((0, 0), (0, 1), (1, 0))
CONTEXT_AT = ((0, 1), (1, 0), (1, 1))
F32, BF16 = jnp.float32, jnp.bfloat16
VMEM, ANY, SMEM = pltpu.VMEM, pl.ANY, pltpu.SMEM


def dot(left, right, left_dim=1, right_dim=0):
    return lax.dot_general(
        left, right, (((left_dim,), (right_dim,)), ((), ())), preferred_element_type=F32
    )


def tile(index, count=1):
    return slice(index * LANES, (index + count) * LANES)


def half_mask(half, dtype):
    lane = lax.broadcasted_iota(jnp.int32, (1, LANES), 1)
    return jnp.where((lane >= HEAD) == (half == 1), 1.0, 0.0).astype(dtype)


def norm_stats(hidden):
    centred = hidden - jnp.mean(hidden, axis=-1, keepdims=True)
    factor = lax.rsqrt(jnp.mean(centred * centred, axis=-1, keepdims=True) + EPSILON)
    return centred * factor, factor


def norm_back(grad_out, normed, factor, gain):
    scaled = grad_out * gain
    inner = jnp.mean(scaled * normed, axis=-1, keepdims=True)
    return factor * (scaled - jnp.mean(scaled, axis=-1, keepdims=True) - normed * inner)


def gelu_and_slope(a):
    size = jnp.abs(a)
    t = 1.0 / (1.0 + (0.3275911 * 0.7071067811865476) * size)
    bell = jnp.exp(-0.5 * a * a)
    poly = t * (
        0.127414796 + t * (-0.142248368 + t * (0.7107068705 + t * (-0.7265760135 + t * 0.5307027145)))
    )
    tail = poly * bell
    phi = jnp.where(a >= 0.0, 1.0 - tail, tail)
    return a * phi, phi + a * bell * 0.3989422804014327


class Sizes:
    def __init__(self, length, width, groups):
        self.length, self.width, self.groups = length, width, groups
        self.own = length // groups
        self.window = min(length, self.own + 2 * LONGEST)
        self.block = min(QUERY_BLOCK, self.own)
        self.blocks = self.own // self.block
        self.keys = min(length, self.block + 2 * LONGEST)

    def window_start(self, me):
        return jnp.clip(self.own * me - LONGEST, 0, self.length - self.window)

    def own_offset(self, me):
        return pl.multiple_of(self.own * me - self.window_start(me), 16)

    def key_start(self, me, block):
        first = self.own * me + block * self.block
        return jnp.clip(first - LONGEST, 0, self.length - self.keys)

    def key_offset(self, me, block):
        return pl.multiple_of(self.key_start(me, block) - self.window_start(me), 16)


def document_bounds(lens, places):
    start = jnp.zeros_like(places)
    end = jnp.zeros_like(places)
    total = jnp.int32(0)
    for d in range(lens.shape[1]):
        count = lens[0, d]
        end = end + jnp.where(places >= total, count, 0)
        total = total + count
        start = start + jnp.where(places >= total, count, 0)
    return start, end


def fill_mask(sizes, me, lens, bias):
    for b in range(sizes.blocks):
        places = (
            sizes.own * me
            + b * sizes.block
            + lax.broadcasted_iota(jnp.int32, (1, sizes.block), 1)
        )
        start, end = document_bounds(lens, places)
        keys = sizes.key_start(me, b) + lax.broadcasted_iota(
            jnp.int32, (sizes.keys, sizes.block), 0
        )
        bias[b] = jnp.where((keys >= start) & (keys < end), 0.0, NEGATIVE)


def start_rows(sizes, me, lens):
    docs = lens.shape[1]
    row = lax.broadcasted_iota(jnp.int32, (docs, sizes.own), 0)
    place = sizes.own * me + lax.broadcasted_iota(jnp.int32, (docs, sizes.own), 1)
    picked = jnp.zeros((docs, sizes.own), F32)
    total = jnp.int32(0)
    for d in range(docs):
        picked = jnp.where((row == d) & (place == total), 1.0, picked)
        total = total + lens[0, d]
    return picked


def project(sizes, me, tokens, w_attn, biases, kv, q):
    cut = sizes.window // 2
    own = pl.ds(sizes.own_offset(me), sizes.own)

    @pl.loop(0, sizes.groups)
    def _(g):
        for part in range(2):
            rows = pl.ds(part * cut, cut)
            made = dot(tokens[rows, :], w_attn[g, :, tile(0, 3)]) + biases[g, :, tile(0, 3)]
            kv[g, rows, :] = made.astype(BF16)
        made = dot(tokens[own, :], w_attn[g, :, tile(3, 2)]) + biases[g, :, tile(3, 2)]
        q[g] = made.astype(BF16) * jnp.asarray(HEAD**-0.5, BF16)


def attend(sizes, me, kv, q, bias, lse, ctx, tick=None):
    @pl.loop(0, sizes.groups)
    def _(g):
        @pl.loop(0, sizes.blocks)
        def _(b):
            if tick is not None:
                tick(g * sizes.blocks + b)
            keys = pl.ds(sizes.key_offset(me, b), sizes.keys)
            rows = pl.ds(pl.multiple_of(b * sizes.block, sizes.block), sizes.block)
            made = [jnp.zeros((HEAD, sizes.block), F32)]
            logs = []
            for j in range(3):
                kt, kh = KEY_AT[j]
                vt, vh = VALUE_AT[j]
                qt, _ = QUERY_AT[j]
                query = q[g, rows, tile(qt)] * half_mask(kh, BF16)
                s = dot(kv[g, keys, tile(kt)], query, 1, 1) + bias[b]
                peak = jnp.max(s, axis=0, keepdims=True)
                e = jnp.exp(s - peak)
                total = jnp.sum(e, axis=0, keepdims=True)
                mixed = dot(kv[g, keys, tile(vt)], e.astype(BF16), 0, 0)
                made.append(mixed[vh * HEAD : (vh + 1) * HEAD] / total)
                logs.append(peak + jnp.log(total))
            ctx[g, rows, :] = jnp.concatenate(made, axis=0).T.astype(BF16)
            for j in range(3):
                lse[g, b, j : j + 1, :] = logs[j]


def attend_back(sizes, me, kv, q, bias, lse, ctx, dctx, delta, dkv, dq):
    lane = lax.broadcasted_iota(jnp.int32, (8, 2 * LANES), 1)
    row = lax.broadcasted_iota(jnp.int32, (8, 2 * LANES), 0)
    pick = jnp.where(lane // HEAD == row + 1, 1.0, 0.0).astype(BF16)

    @pl.loop(0, sizes.groups)
    def _(g):
        product = dctx[g].astype(F32) * ctx[g].astype(F32)
        high = product.astype(BF16)
        low = (product - high.astype(F32)).astype(BF16)
        delta[...] = dot(pick, high, 1, 1) + dot(pick, low, 1, 1)
        dkv[g] = jnp.zeros_like(dkv[g])

        for b in range(sizes.blocks):
            keys = pl.ds(sizes.key_offset(me, b), sizes.keys)
            rows = slice(b * sizes.block, (b + 1) * sizes.block)
            made = []
            for j in range(3):
                kt, kh = KEY_AT[j]
                vt, vh = VALUE_AT[j]
                qt, _ = QUERY_AT[j]
                ct, _ = CONTEXT_AT[j]
                query = q[g, rows, tile(qt)] * half_mask(kh, BF16)
                grad = dctx[g, rows, tile(ct)] * half_mask(vh, BF16)
                s = dot(kv[g, keys, tile(kt)], query, 1, 1) + bias[b]
                p = jnp.exp(s - lse[g, b, j : j + 1, :])
                dp = dot(kv[g, keys, tile(vt)], grad, 1, 1)
                ds = (p * (dp - delta[j : j + 1, rows])).astype(BF16)
                dkv[g, keys, tile(kt)] += dot(ds, query)
                dkv[g, keys, tile(vt)] += dot(p.astype(BF16), grad)
                back = dot(kv[g, keys, tile(kt)], ds, 0, 0)
                made.append(back[kh * HEAD : (kh + 1) * HEAD] * HEAD**-0.5)
            made.append(jnp.zeros((HEAD, sizes.block), F32))
            dq[g, rows, :] = jnp.concatenate(made, axis=0).T


class Loads:
    def __init__(self, weights, w, sems):
        self.copies = [pltpu.make_async_copy(weights.at[s], w.at[s], sems.at[s]) for s in range(3)]

    def begin(self):
        for copy in self.copies:
            copy.start()

    def ready(self, section):
        self.copies[section].wait()

    def tick(self, step):
        pass

    def end(self):
        pass


MESH = pl.DeviceIdType.MESH


class Place:
    def __init__(self):
        self.dp, self.mp = lax.axis_index("dp"), lax.axis_index("mp")
        self.z, self.x, self.y, self.core = self.dp // 2, self.dp % 2, self.mp // 2, self.mp % 2
        flip = 1 - self.core
        self.across = 2 * (1 - self.y) + self.core
        self.sibling = (self.dp, 2 * self.y + flip)
        x_peer = 2 * self.z + 1 - self.x
        self.first = (self.dp + flip * (x_peer - self.dp), self.mp + self.core * (self.across - self.mp))
        self.second = (self.dp + self.core * (x_peer - self.dp), self.mp + flip * (self.across - self.mp))
        self.zs = [self.z, self.z + 1 - 2 * (self.z % 2), (self.z + 2) % 4, 3 - self.z]
        self.line = [(2 * z + self.x, self.mp) for z in self.zs]
        self.own_column = (self.mp, self.x)
        self.first_column = (
            self.mp + self.core * (self.across - self.mp),
            self.x + flip * (1 - 2 * self.x),
        )
        self.second_columns = (
            (self.mp + flip * (self.across - self.mp), self.x + self.core * (1 - 2 * self.x)),
            (self.across, 1 - self.x),
        )
        self.diagonal = (self.dp, 2 * (1 - self.y) + flip)
        self.peers = [*self.line[1:], self.first, self.second, self.sibling, self.diagonal]


def greet(peers):
    barrier = pltpu.get_barrier_semaphore()
    for peer in peers:
        pl.semaphore_signal(barrier, inc=1, device_id=peer, device_id_type=MESH)
    pl.semaphore_wait(barrier, len(peers))


class Gather:
    def __init__(self, place, packed, own_bias, w, biases, kept, send, recv, local, bias_sems):
        self.at, self.packed, self.w, self.kept = place, packed, w, kept
        self.own_bias, self.biases = own_bias, biases
        self.send_sems, self.recv_sems, self.local, self.bias_sems = send, recv, local, bias_sems
        self.rows = packed.shape[1]
        self.shards = w.shape[2] // self.rows

    def shard(self, s, g, d):
        return self.w.at[s, g, pl.ds(pl.multiple_of(d * self.rows, 16), self.rows)]

    def copy(self, s, g, d, slot, peer, source=None):
        here = self.shard(s, g, d)
        return pltpu.make_async_remote_copy(
            src_ref=here if source is None else source,
            dst_ref=here,
            send_sem=self.send_sems.at[s, slot],
            recv_sem=self.recv_sems.at[s, g * self.shards + d],
            device_id=peer,
            device_id_type=MESH,
        )

    def arrived(self, s, g, d):
        self.copy(s, g, d, 0, self.at.sibling).wait_recv()

    def own_copy(self, s):
        return pltpu.make_async_copy(
            self.packed.at[s], self.shard(s, self.at.mp, self.at.dp), self.local.at[s]
        )

    def along_z(self, s):
        at = self.at
        for k in range(1, 4):
            self.copy(s, at.mp, at.dp, k - 1, at.line[k], self.packed.at[s]).start()

    def own_out(self, s):
        at = self.at
        self.own_copy(s).start()
        source = self.packed.at[s]
        self.copy(s, at.mp, at.dp, 3, at.first, source).start()
        self.copy(s, at.mp, at.dp, 7, at.second, source).start()
        self.copy(s, at.mp, at.dp, 15, at.sibling, source).start()

    def from_z(self, s, k):
        at, (g, x) = self.at, self.at.own_column
        d = 2 * at.zs[k] + x
        self.arrived(s, g, d)
        self.copy(s, g, d, 3 + k, at.first).start()
        self.copy(s, g, d, 7 + k, at.second).start()
        self.copy(s, g, d, 15 + k, at.sibling).start()

    def from_first(self, s, k):
        at, (g, x) = self.at, self.at.first_column
        d = 2 * at.zs[k] + x
        self.arrived(s, g, d)
        self.copy(s, g, d, 11 + k, at.second).start()
        self.copy(s, g, d, 19 + k, at.sibling).start()

    def from_second(self, s, k):
        at, (g, x) = self.at, self.at.second_columns[k // 4]
        d = 2 * at.zs[k % 4] + x
        self.arrived(s, g, d)
        self.copy(s, g, d, 23 + k, at.sibling).start()

    def from_sibling(self, s):
        at = self.at
        for g in (at.sibling[1], at.diagonal[1]):

            @pl.loop(0, self.shards)
            def _(d):
                self.arrived(s, g, d)

    def keep(self, s):
        return pltpu.make_async_copy(self.w.at[s], self.kept.at[s], self.local.at[3 + s])

    def bias_copy(self, k, peer):
        return pltpu.make_async_remote_copy(
            src_ref=self.own_bias,
            dst_ref=self.biases.at[self.at.mp],
            send_sem=self.bias_sems.at[0, k],
            recv_sem=self.bias_sems.at[1, k],
            device_id=peer,
            device_id_type=MESH,
        )

    def bias_copies(self):
        at = self.at
        across = (at.dp, at.across)
        return [self.bias_copy(k, peer) for k, peer in enumerate((at.sibling, across, at.diagonal))]

    def begin(self):
        greet(self.at.peers)
        self.along_z(0)
        self.own_out(0)
        for copy in self.bias_copies():
            copy.start()
        self.biases[self.at.mp] = self.own_bias[...]

    def ready(self, section):
        if section == 0:
            self.from_z(0, 1)
            self.from_z(0, 2)
            self.from_z(0, 3)
            self.along_z(1)
            for k in range(4):
                self.from_first(0, k)
            self.own_out(1)
            for k in range(8):
                self.from_second(0, k)
            for copy in self.bias_copies():
                copy.wait_recv()
            self.steps(0)
            self.from_sibling(0)
        elif section == 1:
            self.steps(9)
            self.from_sibling(1)
        else:
            self.steps(10)
            self.from_sibling(2)
        self.own_copy(section).wait()
        self.keep(section).start()

    def steps(self, step):
        if step == 0:
            for k in range(1, 4):
                self.from_z(1, k)
            self.along_z(2)
        elif step == 2:
            self.from_first(1, 0)
            self.from_first(1, 1)
        elif step == 3:
            self.from_first(1, 2)
            self.from_first(1, 3)
        elif step == 4:
            self.own_out(2)
            for k in range(1, 4):
                self.from_z(2, k)
        elif step == 5:
            for k in range(4):
                self.from_second(1, k)
        elif step == 6:
            for k in range(4, 8):
                self.from_second(1, k)
        elif step == 7:
            self.from_first(2, 0)
            self.from_first(2, 1)
        elif step == 9:
            self.from_first(2, 2)
            self.from_first(2, 3)
        elif step == 10:
            for k in range(8):
                self.from_second(2, k)

    def tick(self, step):
        for k in range(2, 8):
            pl.when(step == k)(functools.partial(self.steps, k))

    def end(self):
        for copy in self.bias_copies():
            copy.wait_send()
        for s in range(3):

            @pl.loop(0, 31)
            def _(slot):
                self.copy(s, 0, 0, slot, self.at.sibling).wait_send()

            self.keep(s).wait()


def forward_math(
    sizes,
    source,
    lens,
    tokens,
    biases,
    b_out,
    gain_1,
    shift_1,
    b_down,
    gain_2,
    shift_2,
    encoded,
    cls,
    n_1,
    r_1,
    n_2,
    r_2,
    z_out,
    slope_out,
    kv_out,
    q,
    lse,
    ctx,
    x,
    w,
    bias,
    hidden,
    kv,
    z,
    slope,
    sems,
):
    me = lax.axis_index("mp")
    first = pl.multiple_of(sizes.window_start(me), 16)
    load = pltpu.make_async_copy(tokens.at[pl.ds(first, sizes.window)], x, sems.at[0])
    load.start()
    source.begin()
    fill_mask(sizes, me, lens, bias)
    load.wait()
    source.ready(0)
    project(sizes, me, x, w.at[0], biases, kv, q)
    save_kv = pltpu.make_async_copy(kv, kv_out, sems.at[1])
    save_kv.start()
    attend(sizes, me, kv, q, bias, lse, ctx, source.tick)

    own = pl.ds(sizes.own_offset(me), sizes.own)
    hidden[...] = x[own, :].astype(F32) + b_out[...]
    for g in range(sizes.groups):
        hidden[...] += dot(ctx[g], w[0, g, :, tile(4, 2)], 1, 1)
    normed, factor = norm_stats(hidden[...])
    n_1[...] = normed
    r_1[...] = factor
    y_1 = normed * gain_1[...] + shift_1[...]
    hidden[...] = y_1 + b_down[...]
    encoded[...] = y_1.astype(BF16)
    source.ready(1)

    @pl.loop(0, sizes.groups)
    def _(g):
        a = dot(encoded[...], w[1, g]) + biases[g, :, 5 * LANES :]
        out, grad = gelu_and_slope(a)
        z[g] = out.astype(BF16)
        slope[g] = grad.astype(BF16)

    save_z = pltpu.make_async_copy(z, z_out, sems.at[2])
    save_slope = pltpu.make_async_copy(slope, slope_out, sems.at[3])
    save_z.start()
    save_slope.start()
    source.ready(2)

    @pl.loop(0, sizes.groups)
    def _(g):
        hidden[...] += dot(z[g], w[2, g], 1, 1)

    normed, factor = norm_stats(hidden[...])
    n_2[...] = normed
    r_2[...] = factor
    y_2 = (normed * gain_2[...] + shift_2[...]).astype(BF16)
    encoded[...] = y_2
    cls[...] = dot(start_rows(sizes, me, lens).astype(BF16), y_2)
    source.end()
    save_kv.wait()
    save_z.wait()
    save_slope.wait()


def forward_kernel(sizes, lens, tokens, weights, biases, *rest):
    *refs, w, bias, hidden, kv, z, slope, sems, loads = rest
    source = Loads(weights, w, loads)
    forward_math(sizes, source, lens, tokens, biases, *refs, w, bias, hidden, kv, z, slope, sems)


def gathering_kernel(sizes, lens, tokens, packed, own_bias, *rest):
    rows, (kept, *outs) = rest[:6], rest[6:]
    *refs, w, bias, hidden, kv, z, slope, sems, biases, send, recv, local, bias_sems = outs
    source = Gather(Place(), packed, own_bias, w, biases, kept, send, recv, local, bias_sems)
    forward_math(
        sizes, source, lens, tokens, biases, *rows, *refs, w, bias, hidden, kv, z, slope, sems
    )


def backward_kernel(
    sizes,
    lens,
    cotangent,
    dcls,
    weights,
    gain_1,
    shift_1,
    gain_2,
    n_1,
    r_1,
    n_2,
    r_2,
    z,
    slope,
    kv,
    q,
    lse,
    ctx,
    dh_1,
    dkv,
    dq,
    grads,
    grads_out,
    small,
    w_attn,
    w_up,
    w_down,
    cot,
    dh,
    low,
    other,
    turned,
    stage,
    dctx,
    delta,
    bias,
    sems,
    out_sems,
):
    me = lax.axis_index("mp")
    load_cot = pltpu.make_async_copy(
        cotangent.at[pl.ds(pl.multiple_of(sizes.own * me, 16), sizes.own)], cot, sems.at[3]
    )
    load_cot.start()
    loads = []
    for s, buffer in ((2, w_down), (1, w_up), (0, w_attn)):
        loads.append(pltpu.make_async_copy(weights.at[s], buffer, sems.at[s]))
        loads[-1].start()
    fill_mask(sizes, me, lens, bias)
    picked = start_rows(sizes, me, lens).astype(BF16)
    high = dcls[...].astype(BF16)
    low_part = (dcls[...] - high.astype(F32)).astype(BF16)
    load_cot.wait()
    dy = cot[...].astype(F32) + dot(picked, high, 0, 0) + dot(picked, low_part, 0, 0)
    small[0:1, :] = jnp.sum(dy * n_2[...], axis=0, keepdims=True)
    small[1:2, :] = jnp.sum(dy, axis=0, keepdims=True)
    grad = norm_back(dy, n_2[...], r_2[...], gain_2[...])
    small[2:3, :] = jnp.sum(grad, axis=0, keepdims=True)
    dh[...] = grad
    low[...] = grad.astype(BF16)
    turned[0] = grad.T.astype(BF16)
    y_1 = n_1[...] * gain_1[...] + shift_1[...]
    other[...] = y_1.astype(BF16)
    turned[1] = y_1.T.astype(BF16)
    for load in loads:
        load.wait()

    def out_copy(section, g, slot):
        return pltpu.make_async_copy(
            stage.at[slot], grads.at[section, g], out_sems.at[slot]
        )

    @pl.loop(0, sizes.groups)
    def _(g):
        @pl.when(g > 0)
        def _():
            out_copy(1, 0, 0).wait()
            out_copy(1, 0, 1).wait()

        stage[1] = dot(turned[0], z[g]).astype(BF16)
        out_copy(1, g, 1).start()
        da = dot(low[...], w_down[g]) * slope[g].astype(F32)
        small[pl.ds(8 + g, 1), :] = jnp.sum(da, axis=0, keepdims=True)
        da_low = da.astype(BF16)
        stage[0] = dot(turned[1], da_low).astype(BF16)
        out_copy(0, g, 0).start()
        dh[...] += dot(da_low, w_up[g], 1, 1)

    dy = dh[...]
    small[3:4, :] = jnp.sum(dy * n_1[...], axis=0, keepdims=True)
    small[4:5, :] = jnp.sum(dy, axis=0, keepdims=True)
    grad = norm_back(dy, n_1[...], r_1[...], gain_1[...])
    small[5:6, :] = jnp.sum(grad, axis=0, keepdims=True)
    small[6:8, :] = jnp.zeros_like(small[6:8, :])
    small[12:16, :] = jnp.zeros_like(small[12:16, :])
    dh_1[...] = grad
    low[...] = grad.astype(BF16)
    turned[0] = grad.T.astype(BF16)

    @pl.loop(0, sizes.groups)
    def _(g):
        dctx[g] = dot(low[...], w_attn[g, :, tile(4, 2)]).astype(BF16)
        grads_out[g] = dot(turned[0], ctx[g])

    attend_back(sizes, me, kv, q, bias, lse, ctx, dctx, delta, dkv, dq)
    out_copy(1, 0, 0).wait()
    out_copy(1, 0, 1).wait()


def input_kernel(sizes, tokens, weights, dkv, dq, dh_1, grads_out, token_grad, grads, small, turned, low):
    turned[...] = tokens[...].astype(F32).T.astype(BF16)
    total = dh_1[...]
    for g in range(sizes.groups):
        small[g, :, tile(0, 3)] = jnp.sum(dkv[g], axis=0, keepdims=True)
        small[g, :, tile(3, 2)] = jnp.sum(dq[g], axis=0, keepdims=True)
        low[:, tile(0, 3)] = dkv[g].astype(BF16)
        low[:, tile(3, 2)] = dq[g].astype(BF16)
        total = total + dot(low[...], weights[g, :, tile(0, 5)], 1, 1)
        made = dot(turned[...], low[...])
        grads[g, :, tile(0, 4)] = made[:, tile(0, 4)].astype(BF16)
        grads[g, :, tile(4)] = (made[:, tile(4)] + grads_out[g, :, tile(0)]).astype(BF16)
        grads[g, :, tile(5)] = grads_out[g, :, tile(1)].astype(BF16)
    token_grad[...] = total.astype(BF16)


def specs(*spaces):
    return [pl.BlockSpec(memory_space=s) for s in spaces]


def params(**more):
    return pltpu.CompilerParams(vmem_limit_bytes=62 * 2**20, **more)


def run_forward(sizes, lengths, tokens, weights, biases, rows, gathers):
    own, width, groups = sizes.own, sizes.width, sizes.groups
    docs = lengths.shape[1]
    shape = jax.ShapeDtypeStruct
    outs = [
        shape((own, width), BF16),
        shape((docs, width), F32),
        shape((own, width), F32),
        shape((own, 1), F32),
        shape((own, width), F32),
        shape((own, 1), F32),
        shape((groups, own, width), BF16),
        shape((groups, own, width), BF16),
        shape((groups, sizes.window, 3 * LANES), BF16),
        shape((groups, own, 2 * LANES), BF16),
        shape((groups, sizes.blocks, 8, sizes.block), F32),
        shape((groups, own, 2 * LANES), BF16),
    ]
    spaces = [*[VMEM] * 6, ANY, ANY, ANY, *[VMEM] * 3]
    scratch = [
        pltpu.VMEM((sizes.window, width), BF16),
        pltpu.VMEM((3, groups, width, width), BF16),
        pltpu.VMEM((sizes.blocks, sizes.keys, sizes.block), F32),
        pltpu.VMEM((own, width), F32),
        pltpu.VMEM((groups, sizes.window, 3 * LANES), BF16),
        pltpu.VMEM((groups, own, width), BF16),
        pltpu.VMEM((groups, own, width), BF16),
        pltpu.SemaphoreType.DMA((4,)),
    ]
    if gathers:
        outs.insert(0, shape((3, groups, width, width), BF16))
        spaces.insert(0, ANY)
        scratch += [
            pltpu.VMEM((groups, 1, biases.shape[1]), F32),
            pltpu.SemaphoreType.DMA((3, 31)),
            pltpu.SemaphoreType.DMA((3, 32)),
            pltpu.SemaphoreType.DMA((6,)),
            pltpu.SemaphoreType.DMA((2, 3)),
        ]
        kernel, more = gathering_kernel, {"collective_id": 0, "has_side_effects": True}
    else:
        scratch.append(pltpu.SemaphoreType.DMA((3,)))
        kernel, more = forward_kernel, {}
    return pl.pallas_call(
        functools.partial(kernel, sizes),
        out_shape=outs,
        in_specs=specs(SMEM, ANY, VMEM if gathers else ANY, *[VMEM] * 7),
        out_specs=specs(*spaces),
        scratch_shapes=scratch,
        compiler_params=params(**more),
        name="forward",
    )(lengths, tokens, weights, biases, *rows)


def run_backward(sizes, lengths, cotangent, dcls, weights, gain_1, shift_1, gain_2, saved):
    own, width, groups = sizes.own, sizes.width, sizes.groups
    shape = jax.ShapeDtypeStruct
    outs = (
        shape((own, width), F32),
        shape((groups, sizes.window, 3 * LANES), F32),
        shape((groups, own, 2 * LANES), F32),
        shape((2, groups, width, width), BF16),
        shape((groups, width, 2 * LANES), F32),
        shape((16, width), F32),
    )
    return pl.pallas_call(
        functools.partial(backward_kernel, sizes),
        out_shape=outs,
        in_specs=specs(SMEM, ANY, VMEM, ANY, *[VMEM] * (3 + len(saved))),
        out_specs=specs(VMEM, VMEM, VMEM, ANY, VMEM, VMEM),
        scratch_shapes=[
            pltpu.VMEM((groups, width, width), BF16),
            pltpu.VMEM((groups, width, width), BF16),
            pltpu.VMEM((groups, width, width), BF16),
            pltpu.VMEM((own, width), BF16),
            pltpu.VMEM((own, width), F32),
            pltpu.VMEM((own, width), BF16),
            pltpu.VMEM((own, width), BF16),
            pltpu.VMEM((2, width, own), BF16),
            pltpu.VMEM((2, width, width), BF16),
            pltpu.VMEM((groups, own, 2 * LANES), BF16),
            pltpu.VMEM((8, own), F32),
            pltpu.VMEM((sizes.blocks, sizes.keys, sizes.block), F32),
            pltpu.SemaphoreType.DMA((4,)),
            pltpu.SemaphoreType.DMA((2,)),
        ],
        compiler_params=params(),
        name="backward",
    )(lengths, cotangent, dcls, weights, gain_1, shift_1, gain_2, *saved)


def run_input(sizes, own_tokens, w_attn, dkv, dq, dh_1, grads_out):
    own, width, groups = sizes.own, sizes.width, sizes.groups
    shape = jax.ShapeDtypeStruct
    outs = (
        shape((own, width), BF16),
        shape((groups, width, width), BF16),
        shape((groups, 1, 5 * LANES), F32),
    )
    return pl.pallas_call(
        functools.partial(input_kernel, sizes),
        out_shape=outs,
        in_specs=specs(*[VMEM] * 6),
        out_specs=specs(*[VMEM] * 3),
        scratch_shapes=[pltpu.VMEM((width, own), BF16), pltpu.VMEM((own, 5 * LANES), BF16)],
        compiler_params=params(),
        name="inputs",
    )(own_tokens, w_attn, dkv, dq, dh_1, grads_out)


def cut_along(array, dim, devices):
    before, after = (array.shape[:dim], array.shape[dim + 1 :])
    return jnp.moveaxis(array.reshape(*before, devices, -1, *after), dim, 0)


def summed_on_arrival(array, axis, dim):
    pieces = cut_along(array, dim, lax.axis_size(axis))
    arrived = lax.all_to_all(pieces, axis, split_axis=0, concat_axis=0, tiled=True)
    return arrived.astype(F32).sum(axis=0)


def score(cls, passages, gold):
    all_first = lax.all_gather(cls, "dp", axis=0, tiled=True)
    table = dot(all_first, passages, 1, 1)
    peak = lax.pmax(jnp.max(table, axis=1), "dp")
    total = lax.psum(jnp.sum(jnp.exp(table - peak[:, None]), axis=1), "dp")
    own = cls.shape[0]
    lse = lax.dynamic_slice_in_dim(peak + jnp.log(total), lax.axis_index("dp") * own, own)
    soft = jnp.exp(table - peak[:, None]) / total[:, None]
    first = lax.axis_index("dp") * table.shape[1]
    columns = first + jnp.arange(table.shape[1], dtype=jnp.int32)
    target = (gold[:, None] == columns[None, :]).astype(F32)
    grad = dot((soft - target).astype(BF16), passages)
    return table, lse, summed_on_arrival(grad.astype(BF16), "dp", 0)


def body(
    tokens,
    cotangent,
    lengths,
    gold,
    passages,
    w_query,
    w_key,
    w_value,
    b_query,
    b_value,
    w_out,
    b_out,
    gain_attn,
    shift_attn,
    w_up,
    b_up,
    w_down,
    b_down,
    gain_ffn,
    shift_ffn,
):
    groups = lax.axis_size("mp")
    sizes = Sizes(tokens.shape[0], tokens.shape[1], groups)
    me = lax.axis_index("mp")
    head_cols = w_query.shape[1]
    packed = jnp.stack(
        [jnp.concatenate([w_key, w_value, w_query, w_out.T], axis=1), w_up, w_down.T]
    )
    zeros = jnp.zeros((head_cols,), F32)
    own_bias = jnp.concatenate([zeros, b_value, b_query, zeros[:HEAD], b_up])[None]
    rows = [r[None] for r in (b_out, gain_attn, shift_attn, b_down, gain_ffn, shift_ffn)]
    if lax.axis_size("dp") == 8 and groups == 4:
        whole, encoded, cls, *saved = run_forward(
            sizes, lengths, tokens, packed, own_bias, rows, True
        )
    else:
        whole = lax.all_gather(lax.all_gather(packed, "dp", axis=1, tiled=True), "mp", axis=1)
        biases = lax.all_gather(own_bias, "mp", axis=0)
        encoded, cls, *saved = run_forward(sizes, lengths, tokens, whole, biases, rows, False)
    cls = lax.psum(cls, "mp").astype(BF16)
    table, lse, dcls = score(cls, passages, gold)
    n_1, r_1, n_2, r_2, z, slope, kv, q, logs, ctx = saved
    dh_1, dkv, dq, grads_ffn, grads_out, small = run_backward(
        sizes, lengths, cotangent, dcls, whole, rows[1], rows[2], rows[4], saved
    )
    halo, own = LONGEST, sizes.own
    offset = own * me - sizes.window_start(me)
    to_left = lax.dynamic_slice_in_dim(dkv, offset - halo, halo, axis=1).astype(BF16)
    to_right = lax.dynamic_slice_in_dim(dkv, offset + own, halo, axis=1).astype(BF16)
    from_right = lax.ppermute(to_left, "mp", [(i, i - 1) for i in range(1, groups)])
    from_left = lax.ppermute(to_right, "mp", [(i, i + 1) for i in range(groups - 1)])
    dkv = lax.dynamic_slice_in_dim(dkv, offset, own, axis=1)
    dkv = dkv.at[:, own - halo :].add(from_right.astype(F32))
    dkv = dkv.at[:, :halo].add(from_left.astype(F32))
    own_tokens = lax.dynamic_slice_in_dim(tokens, own * me, own, axis=0)
    token_part, grads_attn, small_attn = run_input(
        sizes, own_tokens, whole[0], dkv, dq, dh_1, grads_out
    )
    token_grad = lax.all_gather(token_part, "mp", axis=0, tiled=True).astype(F32)
    encoded = lax.all_gather(encoded, "mp", axis=0, tiled=True)
    grads = jnp.stack([grads_attn, grads_ffn[0], grads_ffn[1]])
    grads = summed_on_arrival(grads, "mp", 1)[:, 0].astype(BF16)
    grads = summed_on_arrival(grads, "dp", 1)
    small, small_attn = lax.psum((small, small_attn), ("dp", "mp"))
    mine = lax.dynamic_index_in_dim(small_attn[:, 0], me, 0, keepdims=False)
    up_bias = lax.dynamic_index_in_dim(small, 8 + me, 0, keepdims=False)
    c = head_cols
    return (
        table,
        lse,
        encoded,
        token_grad,
        grads[0, :, 2 * c : 3 * c],
        grads[0, :, :c],
        grads[0, :, c : 2 * c],
        mine[2 * c : 3 * c],
        mine[c : 2 * c],
        grads[0, :, 3 * c :].T,
        small[5],
        small[3],
        small[4],
        grads[1],
        up_bias,
        grads[2].T,
        small[2],
        small[0],
        small[1],
    )


def solution(mesh):
    by_dp, shared, cross = P("dp", None), P(), P("dp", "mp")
    return jax.shard_map(
        body,
        mesh=mesh,
        in_specs=(
            by_dp,
            by_dp,
            by_dp,
            shared,
            by_dp,
            cross,
            cross,
            cross,
            P("mp"),
            P("mp"),
            P("mp", "dp"),
            shared,
            shared,
            shared,
            cross,
            P("mp"),
            P("mp", "dp"),
            shared,
            shared,
            shared,
        ),
        out_specs=(
            P(None, "dp"),
            P("dp"),
            by_dp,
            by_dp,
            cross,
            cross,
            cross,
            P("mp"),
            P("mp"),
            P("mp", "dp"),
            shared,
            shared,
            shared,
            cross,
            P("mp"),
            P("mp", "dp"),
            shared,
            shared,
            shared,
        ),
        check_vma=False,
    )
```

```python
import functools

import jax
import jax.numpy as jnp
from jax import lax
from jax.experimental import pallas as pl
from jax.experimental.pallas import tpu as pltpu
from jax.sharding import PartitionSpec as P

HEAD = 64
LONGEST = 400
QUERY_BLOCK = 256
EPSILON = 1e-05
NEGATIVE = -1e30
LANES = 128
KEY_AT = ((0, 0), (0, 1), (1, 0))
VALUE_AT = ((1, 1), (2, 0), (2, 1))
QUERY_AT = ((0, 0), (0, 1), (1, 0))
CONTEXT_AT = ((0, 1), (1, 0), (1, 1))
F32, BF16 = jnp.float32, jnp.bfloat16
VMEM, ANY, SMEM = pltpu.VMEM, pl.ANY, pltpu.SMEM


def dot(left, right, left_dim=1, right_dim=0):
    return lax.dot_general(
        left, right, (((left_dim,), (right_dim,)), ((), ())), preferred_element_type=F32
    )


def tile(index, count=1):
    return slice(index * LANES, (index + count) * LANES)


def half_mask(half, dtype):
    lane = lax.broadcasted_iota(jnp.int32, (1, LANES), 1)
    return jnp.where((lane >= HEAD) == (half == 1), 1.0, 0.0).astype(dtype)


def norm_stats(hidden):
    centred = hidden - jnp.mean(hidden, axis=-1, keepdims=True)
    factor = lax.rsqrt(jnp.mean(centred * centred, axis=-1, keepdims=True) + EPSILON)
    return centred * factor, factor


def norm_back(grad_out, normed, factor, gain):
    scaled = grad_out * gain
    inner = jnp.mean(scaled * normed, axis=-1, keepdims=True)
    return factor * (scaled - jnp.mean(scaled, axis=-1, keepdims=True) - normed * inner)


def gelu_and_slope(a):
    size = jnp.abs(a)
    t = 1.0 / (1.0 + (0.3275911 * 0.7071067811865476) * size)
    bell = jnp.exp(-0.5 * a * a)
    poly = t * (
        0.127414796 + t * (-0.142248368 + t * (0.7107068705 + t * (-0.7265760135 + t * 0.5307027145)))
    )
    tail = poly * bell
    phi = jnp.where(a >= 0.0, 1.0 - tail, tail)
    return a * phi, phi + a * bell * 0.3989422804014327


class Sizes:
    def __init__(self, length, width, groups):
        self.length, self.width, self.groups = length, width, groups
        self.own = length // groups
        self.window = min(length, self.own + 2 * LONGEST)
        self.block = min(QUERY_BLOCK, self.own)
        self.blocks = self.own // self.block
        self.keys = min(length, self.block + 2 * LONGEST)

    def window_start(self, me):
        return jnp.clip(self.own * me - LONGEST, 0, self.length - self.window)

    def own_offset(self, me):
        return pl.multiple_of(self.own * me - self.window_start(me), 16)

    def key_start(self, me, block):
        first = self.own * me + block * self.block
        return jnp.clip(first - LONGEST, 0, self.length - self.keys)

    def key_offset(self, me, block):
        return pl.multiple_of(self.key_start(me, block) - self.window_start(me), 16)


def document_bounds(lens, places):
    start = jnp.zeros_like(places)
    end = jnp.zeros_like(places)
    total = jnp.int32(0)
    for d in range(lens.shape[1]):
        count = lens[0, d]
        end = end + jnp.where(places >= total, count, 0)
        total = total + count
        start = start + jnp.where(places >= total, count, 0)
    return start, end


def fill_mask(sizes, me, lens, bias):
    for b in range(sizes.blocks):
        places = (
            sizes.own * me
            + b * sizes.block
            + lax.broadcasted_iota(jnp.int32, (1, sizes.block), 1)
        )
        start, end = document_bounds(lens, places)
        keys = sizes.key_start(me, b) + lax.broadcasted_iota(
            jnp.int32, (sizes.keys, sizes.block), 0
        )
        bias[b] = jnp.where((keys >= start) & (keys < end), 0.0, NEGATIVE)


def start_rows(sizes, me, lens):
    docs = lens.shape[1]
    row = lax.broadcasted_iota(jnp.int32, (docs, sizes.own), 0)
    place = sizes.own * me + lax.broadcasted_iota(jnp.int32, (docs, sizes.own), 1)
    picked = jnp.zeros((docs, sizes.own), F32)
    total = jnp.int32(0)
    for d in range(docs):
        picked = jnp.where((row == d) & (place == total), 1.0, picked)
        total = total + lens[0, d]
    return picked


def project(sizes, me, tokens, w_attn, biases, kv, q):
    cut = sizes.window // 2
    own = pl.ds(sizes.own_offset(me), sizes.own)

    @pl.loop(0, sizes.groups)
    def _(g):
        for part in range(2):
            rows = pl.ds(part * cut, cut)
            made = dot(tokens[rows, :], w_attn[g, :, tile(0, 3)]) + biases[g, :, tile(0, 3)]
            kv[g, rows, :] = made.astype(BF16)
        made = dot(tokens[own, :], w_attn[g, :, tile(3, 2)]) + biases[g, :, tile(3, 2)]
        q[g] = made.astype(BF16) * jnp.asarray(HEAD**-0.5, BF16)


def attend(sizes, me, kv, q, bias, lse, ctx, tick=None):
    @pl.loop(0, sizes.groups)
    def _(g):
        @pl.loop(0, sizes.blocks)
        def _(b):
            if tick is not None:
                tick(g * sizes.blocks + b)
            keys = pl.ds(sizes.key_offset(me, b), sizes.keys)
            rows = pl.ds(pl.multiple_of(b * sizes.block, sizes.block), sizes.block)
            made = [jnp.zeros((HEAD, sizes.block), F32)]
            logs = []
            for j in range(3):
                kt, kh = KEY_AT[j]
                vt, vh = VALUE_AT[j]
                qt, _ = QUERY_AT[j]
                query = q[g, rows, tile(qt)] * half_mask(kh, BF16)
                s = dot(kv[g, keys, tile(kt)], query, 1, 1) + bias[b]
                peak = jnp.max(s, axis=0, keepdims=True)
                e = jnp.exp(s - peak)
                total = jnp.sum(e, axis=0, keepdims=True)
                mixed = dot(kv[g, keys, tile(vt)], e.astype(BF16), 0, 0)
                made.append(mixed[vh * HEAD : (vh + 1) * HEAD] / total)
                logs.append(peak + jnp.log(total))
            ctx[g, rows, :] = jnp.concatenate(made, axis=0).T.astype(BF16)
            for j in range(3):
                lse[g, b, j : j + 1, :] = logs[j]


def delta_rows(dctx, ctx):
    lane = lax.broadcasted_iota(jnp.int32, (8, 2 * LANES), 1)
    row = lax.broadcasted_iota(jnp.int32, (8, 2 * LANES), 0)
    pick = jnp.where(lane // HEAD == row + 1, 1.0, 0.0).astype(BF16)
    product = dctx.astype(F32) * ctx.astype(F32)
    high = product.astype(BF16)
    low = (product - high.astype(F32)).astype(BF16)
    return dot(pick, high, 1, 1) + dot(pick, low, 1, 1)


def attend_back_block(sizes, me, g, b, kv, q, bias, lse, dctx, delta, dkv):
    keys = pl.ds(sizes.key_offset(me, b), sizes.keys)
    rows = slice(b * sizes.block, (b + 1) * sizes.block)
    made = []
    for j in range(3):
        kt, kh = KEY_AT[j]
        vt, vh = VALUE_AT[j]
        qt, _ = QUERY_AT[j]
        ct, _ = CONTEXT_AT[j]
        query = q[g, rows, tile(qt)] * half_mask(kh, BF16)
        grad = dctx[g, rows, tile(ct)] * half_mask(vh, BF16)
        s = dot(kv[keys, tile(kt)], query, 1, 1) + bias[b]
        p = jnp.exp(s - lse[g, b, j : j + 1, :])
        dp = dot(kv[keys, tile(vt)], grad, 1, 1)
        ds = (p * (dp - delta[j : j + 1, rows])).astype(BF16)
        dkv[keys, tile(kt)] += dot(ds, query)
        dkv[keys, tile(vt)] += dot(p.astype(BF16), grad)
        back = dot(kv[keys, tile(kt)], ds, 0, 0)
        made.append(back[kh * HEAD : (kh + 1) * HEAD] * HEAD**-0.5)
    made.append(jnp.zeros((HEAD, sizes.block), F32))
    return jnp.concatenate(made, axis=0).T


def attend_back(sizes, me, kv, q, bias, lse, ctx, dctx, delta, dkv, dq):
    @pl.loop(0, sizes.groups)
    def _(g):
        delta[...] = delta_rows(dctx[g], ctx[g])
        dkv[g] = jnp.zeros_like(dkv[g])
        for b in range(sizes.blocks):
            rows = slice(b * sizes.block, (b + 1) * sizes.block)
            dq[g, rows, :] = attend_back_block(
                sizes, me, g, b, kv.at[g], q, bias, lse, dctx, delta, dkv.at[g]
            )


class Loads:
    def __init__(self, weights, w, sems):
        self.copies = [pltpu.make_async_copy(weights.at[s], w.at[s], sems.at[s]) for s in range(3)]

    def begin(self):
        for copy in self.copies:
            copy.start()

    def ready(self, section):
        self.copies[section].wait()

    def tick(self, step):
        pass

    def end(self):
        pass


MESH = pl.DeviceIdType.MESH


class Place:
    def __init__(self):
        self.dp, self.mp = lax.axis_index("dp"), lax.axis_index("mp")
        self.z, self.x, self.y, self.core = self.dp // 2, self.dp % 2, self.mp // 2, self.mp % 2
        flip = 1 - self.core
        self.across = 2 * (1 - self.y) + self.core
        self.sibling = (self.dp, 2 * self.y + flip)
        x_peer = 2 * self.z + 1 - self.x
        self.first = (self.dp + flip * (x_peer - self.dp), self.mp + self.core * (self.across - self.mp))
        self.second = (self.dp + self.core * (x_peer - self.dp), self.mp + flip * (self.across - self.mp))
        self.zs = [self.z, self.z + 1 - 2 * (self.z % 2), (self.z + 2) % 4, 3 - self.z]
        self.line = [(2 * z + self.x, self.mp) for z in self.zs]
        self.own_column = (self.mp, self.x)
        self.first_column = (
            self.mp + self.core * (self.across - self.mp),
            self.x + flip * (1 - 2 * self.x),
        )
        self.second_columns = (
            (self.mp + flip * (self.across - self.mp), self.x + self.core * (1 - 2 * self.x)),
            (self.across, 1 - self.x),
        )
        self.diagonal = (self.dp, 2 * (1 - self.y) + flip)
        self.peers = [*self.line[1:], self.first, self.second, self.sibling, self.diagonal]


def greet(peers):
    barrier = pltpu.get_barrier_semaphore()
    for peer in peers:
        pl.semaphore_signal(barrier, inc=1, device_id=peer, device_id_type=MESH)
    pl.semaphore_wait(barrier, len(peers))


class Gather:
    def __init__(self, place, packed, own_bias, w, biases, kept, send, recv, local, bias_sems):
        self.at, self.packed, self.w, self.kept = place, packed, w, kept
        self.own_bias, self.biases = own_bias, biases
        self.send_sems, self.recv_sems, self.local, self.bias_sems = send, recv, local, bias_sems
        self.rows = packed.shape[1]
        self.shards = w.shape[2] // self.rows

    def shard(self, s, g, d):
        return self.w.at[s, g, pl.ds(pl.multiple_of(d * self.rows, 16), self.rows)]

    def copy(self, s, g, d, slot, peer, source=None):
        here = self.shard(s, g, d)
        return pltpu.make_async_remote_copy(
            src_ref=here if source is None else source,
            dst_ref=here,
            send_sem=self.send_sems.at[s, slot],
            recv_sem=self.recv_sems.at[s, g * self.shards + d],
            device_id=peer,
            device_id_type=MESH,
        )

    def arrived(self, s, g, d):
        self.copy(s, g, d, 0, self.at.sibling).wait_recv()

    def own_copy(self, s):
        return pltpu.make_async_copy(
            self.packed.at[s], self.shard(s, self.at.mp, self.at.dp), self.local.at[s]
        )

    def along_z(self, s):
        at = self.at
        for k in range(1, 4):
            self.copy(s, at.mp, at.dp, k - 1, at.line[k], self.packed.at[s]).start()

    def own_out(self, s):
        at = self.at
        self.own_copy(s).start()
        source = self.packed.at[s]
        self.copy(s, at.mp, at.dp, 3, at.first, source).start()
        self.copy(s, at.mp, at.dp, 7, at.second, source).start()
        self.copy(s, at.mp, at.dp, 15, at.sibling, source).start()

    def from_z(self, s, k):
        at, (g, x) = self.at, self.at.own_column
        d = 2 * at.zs[k] + x
        self.arrived(s, g, d)
        self.copy(s, g, d, 3 + k, at.first).start()
        self.copy(s, g, d, 7 + k, at.second).start()
        self.copy(s, g, d, 15 + k, at.sibling).start()

    def from_first(self, s, k):
        at, (g, x) = self.at, self.at.first_column
        d = 2 * at.zs[k] + x
        self.arrived(s, g, d)
        self.copy(s, g, d, 11 + k, at.second).start()
        self.copy(s, g, d, 19 + k, at.sibling).start()

    def from_second(self, s, k):
        at, (g, x) = self.at, self.at.second_columns[k // 4]
        d = 2 * at.zs[k % 4] + x
        self.arrived(s, g, d)
        self.copy(s, g, d, 23 + k, at.sibling).start()

    def from_sibling(self, s):
        at = self.at
        for g in (at.sibling[1], at.diagonal[1]):

            @pl.loop(0, self.shards)
            def _(d):
                self.arrived(s, g, d)

    def keep(self, s):
        return pltpu.make_async_copy(self.w.at[s], self.kept.at[s], self.local.at[3 + s])

    def bias_copy(self, k, peer):
        return pltpu.make_async_remote_copy(
            src_ref=self.own_bias,
            dst_ref=self.biases.at[self.at.mp],
            send_sem=self.bias_sems.at[0, k],
            recv_sem=self.bias_sems.at[1, k],
            device_id=peer,
            device_id_type=MESH,
        )

    def bias_copies(self):
        at = self.at
        across = (at.dp, at.across)
        return [self.bias_copy(k, peer) for k, peer in enumerate((at.sibling, across, at.diagonal))]

    def begin(self):
        greet(self.at.peers)
        self.along_z(0)
        self.own_out(0)
        for copy in self.bias_copies():
            copy.start()
        self.biases[self.at.mp] = self.own_bias[...]

    def ready(self, section):
        if section == 0:
            self.from_z(0, 1)
            self.from_z(0, 2)
            self.from_z(0, 3)
            self.along_z(1)
            for k in range(4):
                self.from_first(0, k)
            self.own_out(1)
            for k in range(8):
                self.from_second(0, k)
            for copy in self.bias_copies():
                copy.wait_recv()
            self.steps(0)
            self.from_sibling(0)
        elif section == 1:
            self.steps(9)
            self.from_sibling(1)
        else:
            self.steps(10)
            self.from_sibling(2)
        self.own_copy(section).wait()
        self.keep(section).start()

    def steps(self, step):
        if step == 0:
            for k in range(1, 4):
                self.from_z(1, k)
            self.along_z(2)
        elif step == 2:
            self.from_first(1, 0)
            self.from_first(1, 1)
        elif step == 3:
            self.from_first(1, 2)
            self.from_first(1, 3)
        elif step == 4:
            self.own_out(2)
            for k in range(1, 4):
                self.from_z(2, k)
        elif step == 5:
            for k in range(4):
                self.from_second(1, k)
        elif step == 6:
            for k in range(4, 8):
                self.from_second(1, k)
        elif step == 7:
            self.from_first(2, 0)
            self.from_first(2, 1)
        elif step == 9:
            self.from_first(2, 2)
            self.from_first(2, 3)
        elif step == 10:
            for k in range(8):
                self.from_second(2, k)

    def tick(self, step):
        for k in range(2, 8):
            pl.when(step == k)(functools.partial(self.steps, k))

    def end(self):
        for copy in self.bias_copies():
            copy.wait_send()
        for s in range(3):

            @pl.loop(0, 31)
            def _(slot):
                self.copy(s, 0, 0, slot, self.at.sibling).wait_send()

            self.keep(s).wait()


def forward_math(
    sizes,
    source,
    lens,
    tokens,
    biases,
    b_out,
    gain_1,
    shift_1,
    b_down,
    gain_2,
    shift_2,
    encoded,
    cls,
    n_1,
    r_1,
    n_2,
    r_2,
    z_out,
    slope_out,
    kv_out,
    q,
    lse,
    ctx,
    x,
    w,
    bias,
    hidden,
    kv,
    z,
    slope,
    sems,
):
    me = lax.axis_index("mp")
    first = pl.multiple_of(sizes.window_start(me), 16)
    load = pltpu.make_async_copy(tokens.at[pl.ds(first, sizes.window)], x, sems.at[0])
    load.start()
    source.begin()
    fill_mask(sizes, me, lens, bias)
    load.wait()
    source.ready(0)
    project(sizes, me, x, w.at[0], biases, kv, q)
    save_kv = pltpu.make_async_copy(kv, kv_out, sems.at[1])
    save_kv.start()
    attend(sizes, me, kv, q, bias, lse, ctx, source.tick)

    own = pl.ds(sizes.own_offset(me), sizes.own)
    hidden[...] = x[own, :].astype(F32) + b_out[...]
    for g in range(sizes.groups):
        hidden[...] += dot(ctx[g], w[0, g, :, tile(4, 2)], 1, 1)
    normed, factor = norm_stats(hidden[...])
    n_1[...] = normed
    r_1[...] = factor
    y_1 = normed * gain_1[...] + shift_1[...]
    hidden[...] = y_1 + b_down[...]
    encoded[...] = y_1.astype(BF16)
    source.ready(1)

    @pl.loop(0, sizes.groups)
    def _(g):
        a = dot(encoded[...], w[1, g]) + biases[g, :, 5 * LANES :]
        out, grad = gelu_and_slope(a)
        z[g] = out.astype(BF16)
        slope[g] = grad.astype(BF16)

    save_z = pltpu.make_async_copy(z, z_out, sems.at[2])
    save_slope = pltpu.make_async_copy(slope, slope_out, sems.at[3])
    save_z.start()
    save_slope.start()
    source.ready(2)

    @pl.loop(0, sizes.groups)
    def _(g):
        hidden[...] += dot(z[g], w[2, g], 1, 1)

    normed, factor = norm_stats(hidden[...])
    n_2[...] = normed
    r_2[...] = factor
    y_2 = (normed * gain_2[...] + shift_2[...]).astype(BF16)
    encoded[...] = y_2
    cls[...] = dot(start_rows(sizes, me, lens).astype(BF16), y_2)
    source.end()
    save_kv.wait()
    save_z.wait()
    save_slope.wait()


def forward_kernel(sizes, lens, tokens, weights, biases, *rest):
    *refs, w, bias, hidden, kv, z, slope, sems, loads = rest
    source = Loads(weights, w, loads)
    forward_math(sizes, source, lens, tokens, biases, *refs, w, bias, hidden, kv, z, slope, sems)


def gathering_kernel(sizes, lens, tokens, packed, own_bias, *rest):
    rows, (kept, *outs) = rest[:6], rest[6:]
    *refs, w, bias, hidden, kv, z, slope, sems, biases, send, recv, local, bias_sems = outs
    source = Gather(Place(), packed, own_bias, w, biases, kept, send, recv, local, bias_sems)
    forward_math(
        sizes, source, lens, tokens, biases, *rows, *refs, w, bias, hidden, kv, z, slope, sems
    )


def backward_kernel(
    sizes,
    lens,
    cotangent,
    dcls,
    weights,
    gain_1,
    shift_1,
    gain_2,
    n_1,
    r_1,
    n_2,
    r_2,
    z,
    slope,
    kv,
    q,
    lse,
    ctx,
    dh_1,
    dkv,
    dq,
    grads,
    grads_out,
    small,
    w_attn,
    w_up,
    w_down,
    cot,
    dh,
    low,
    other,
    turned,
    stage,
    dctx,
    delta,
    bias,
    sems,
    out_sems,
):
    me = lax.axis_index("mp")
    load_cot = pltpu.make_async_copy(
        cotangent.at[pl.ds(pl.multiple_of(sizes.own * me, 16), sizes.own)], cot, sems.at[3]
    )
    load_cot.start()
    loads = []
    for s, buffer in ((2, w_down), (1, w_up), (0, w_attn)):
        loads.append(pltpu.make_async_copy(weights.at[s], buffer, sems.at[s]))
        loads[-1].start()
    fill_mask(sizes, me, lens, bias)
    picked = start_rows(sizes, me, lens).astype(BF16)
    high = dcls[...].astype(BF16)
    low_part = (dcls[...] - high.astype(F32)).astype(BF16)
    load_cot.wait()
    dy = cot[...].astype(F32) + dot(picked, high, 0, 0) + dot(picked, low_part, 0, 0)
    small[0:1, :] = jnp.sum(dy * n_2[...], axis=0, keepdims=True)
    small[1:2, :] = jnp.sum(dy, axis=0, keepdims=True)
    grad = norm_back(dy, n_2[...], r_2[...], gain_2[...])
    small[2:3, :] = jnp.sum(grad, axis=0, keepdims=True)
    dh[...] = grad
    low[...] = grad.astype(BF16)
    turned[0] = grad.T.astype(BF16)
    y_1 = n_1[...] * gain_1[...] + shift_1[...]
    other[...] = y_1.astype(BF16)
    turned[1] = y_1.T.astype(BF16)
    for load in loads:
        load.wait()

    def out_copy(section, g, slot):
        return pltpu.make_async_copy(
            stage.at[slot], grads.at[section, g], out_sems.at[slot]
        )

    @pl.loop(0, sizes.groups)
    def _(g):
        @pl.when(g > 0)
        def _():
            out_copy(1, 0, 0).wait()
            out_copy(1, 0, 1).wait()

        stage[1] = dot(turned[0], z[g]).astype(BF16)
        out_copy(1, g, 1).start()
        da = dot(low[...], w_down[g]) * slope[g].astype(F32)
        small[pl.ds(8 + g, 1), :] = jnp.sum(da, axis=0, keepdims=True)
        da_low = da.astype(BF16)
        stage[0] = dot(turned[1], da_low).astype(BF16)
        out_copy(0, g, 0).start()
        dh[...] += dot(da_low, w_up[g], 1, 1)

    dy = dh[...]
    small[3:4, :] = jnp.sum(dy * n_1[...], axis=0, keepdims=True)
    small[4:5, :] = jnp.sum(dy, axis=0, keepdims=True)
    grad = norm_back(dy, n_1[...], r_1[...], gain_1[...])
    small[5:6, :] = jnp.sum(grad, axis=0, keepdims=True)
    small[6:8, :] = jnp.zeros_like(small[6:8, :])
    small[12:16, :] = jnp.zeros_like(small[12:16, :])
    dh_1[...] = grad
    low[...] = grad.astype(BF16)
    turned[0] = grad.T.astype(BF16)

    @pl.loop(0, sizes.groups)
    def _(g):
        dctx[g] = dot(low[...], w_attn[g, :, tile(4, 2)]).astype(BF16)
        grads_out[g] = dot(turned[0], ctx[g])

    attend_back(sizes, me, kv, q, bias, lse, ctx, dctx, delta, dkv, dq)
    out_copy(1, 0, 0).wait()
    out_copy(1, 0, 1).wait()


def remote(source, target, send, recv, peer):
    return pltpu.make_async_remote_copy(
        src_ref=source,
        dst_ref=target,
        send_sem=send,
        recv_sem=recv,
        device_id=peer,
        device_id_type=MESH,
    )


def square(parts, index):
    side = parts.shape[1]
    return parts.at[pl.ds(pl.multiple_of(index * side, side), side)]


class Spread:
    def __init__(self, place, source, whole, send, recv, local):
        self.at, self.source, self.whole = place, source, whole
        self.send, self.recv, self.local = send, recv, local
        self.count = source.shape[0]

    def rows(self, mp):
        return self.whole.at[pl.ds(pl.multiple_of(mp * self.count, 16), self.count)]

    def copy(self, k):
        at = self.at
        target = self.rows(at.across if k == 2 else at.mp)
        source = target if k == 2 else self.source
        peer = (at.dp, at.across) if k == 1 else at.sibling
        return remote(source, target, self.send.at[k], self.recv.at[k], peer)

    def own(self):
        return pltpu.make_async_copy(self.source, self.rows(self.at.mp), self.local)

    def begin(self):
        self.copy(1).start()
        self.copy(0).start()
        self.own().start()

    def forward(self):
        self.copy(1).wait_recv()
        self.copy(2).start()

    def end(self):
        self.copy(0).wait()
        self.copy(1).wait_send()
        self.copy(2).wait()
        self.own().wait()


class Scatter:
    STAGE = (0, 2, 0)
    HELD = (8, 6, 4)

    def __init__(self, place, parts, inbox, by_second, by_first, by_line, shards, sems):
        self.at, self.parts, self.inbox, self.shards = place, parts, inbox, shards
        self.by_second, self.by_first, self.by_line = by_second, by_first, by_line
        self.core_sems, self.second_sems, self.first_sems, self.line_sems = sems
        self.rows = shards.shape[1]

    def shard(self, s, g, d):
        first = (self.HELD[s] + g // 2) * self.parts.shape[1] + d * self.rows
        return self.parts.at[pl.ds(pl.multiple_of(first, 16), self.rows)]

    def part(self, index):
        return square(self.parts, index)

    def to_sibling(self, s, k):
        at = self.STAGE[s] + k
        return remote(
            self.part(at),
            self.inbox.at[at],
            self.core_sems.at[0, s, k],
            self.core_sems.at[1, s, k],
            self.at.sibling,
        )

    def to_second(self, s, k):
        g, x = self.at.second_columns[1 - k // 4]
        return remote(
            self.shard(s, g, 2 * (k % 4) + x),
            self.by_second.at[s, k],
            self.second_sems.at[0, s, k],
            self.second_sems.at[1, s, k],
            self.at.second,
        )

    def to_first(self, s, k):
        g, x = self.at.first_column
        return remote(
            self.shard(s, g, 2 * k + x),
            self.by_first.at[s, k],
            self.first_sems.at[0, s, k],
            self.first_sems.at[1, s, k],
            self.at.first,
        )

    def to_line(self, s, j):
        at = self.at
        return remote(
            self.shard(s, at.mp, 2 * at.zs[j] + at.x),
            self.by_line.at[s, j - 1],
            self.line_sems.at[0, s, j - 1],
            self.line_sems.at[1, s, j - 1],
            at.line[j],
        )

    def chip_sum(self, s):
        for k in range(2):
            self.to_sibling(s, k).wait_recv()
            held, more = self.part(self.HELD[s] + k), self.inbox.at[self.STAGE[s] + k]

            @pl.loop(0, held.shape[0] // self.rows)
            def _(d):
                rows = pl.ds(pl.multiple_of(d * self.rows, 16), self.rows)
                held[rows, :] = (held[rows, :].astype(F32) + more[rows, :].astype(F32)).astype(BF16)

        for k in range(8):
            self.to_second(s, k).start()

    def from_second(self, s):
        g, x = self.at.first_column
        for k in range(4):
            self.to_second(s, k).wait_recv()
            mine = self.shard(s, g, 2 * k + x)
            mine[...] = (mine[...].astype(F32) + self.by_second[s, k].astype(F32)).astype(BF16)
            self.to_first(s, k).start()

    def from_first(self, s):
        at = self.at
        for k in range(4):
            self.to_second(s, 4 + k).wait_recv()
            self.to_first(s, k).wait_recv()
        for j in (3, 2, 1, 0):
            z = at.zs[j]
            mine = self.shard(s, at.mp, 2 * z + at.x)
            total = (
                mine[...].astype(F32)
                + self.by_second[s, 4 + z].astype(F32)
                + self.by_first[s, z].astype(F32)
            )
            if j:
                mine[...] = total.astype(BF16)
                self.to_line(s, j).start()
            else:
                self.shards[s] = total

    def from_line(self, s):
        for j in range(1, 4):
            self.to_line(s, j).wait_recv()
            self.shards[s] += self.by_line[s, j - 1].astype(F32)

    def sent_to_sibling(self, s):
        for k in range(2):
            self.to_sibling(s, k).wait_send()

    def end(self):
        for s in range(3):
            for k in range(8):
                self.to_second(s, k).wait_send()
            for k in range(4):
                self.to_first(s, k).wait_send()
            for j in range(1, 4):
                self.to_line(s, j).wait_send()


class SmallSums:
    def __init__(self, place, sums, inbox, sems):
        self.at, self.sums, self.inbox, self.sems = place, sums, inbox, sems
        at = place
        self.peers = [at.sibling, (2 * at.z + 1 - at.x, at.mp), (at.dp, at.across), *at.line[1:]]

    def copy(self, k):
        return remote(
            self.sums.at[min(k, 3)],
            self.inbox.at[k],
            self.sems.at[0, k],
            self.sems.at[1, k],
            self.peers[k],
        )

    def begin(self):
        self.copy(0).start()

    def step(self, k):
        self.copy(k).wait_recv()
        self.sums[k + 1] = self.sums[k] + self.inbox[k]
        for nxt in (k + 1,) if k < 2 else (3, 4, 5):
            self.copy(nxt).start()

    def end(self, out):
        for k in range(3, 6):
            self.copy(k).wait_recv()
        out[...] = (self.sums[3] + self.inbox[3]) + (self.inbox[4] + self.inbox[5])
        for k in range(6):
            self.copy(k).wait_send()


def fold(rows):
    half = rows.shape[1] // 2
    return jnp.concatenate([rows[:, :half], rows[:, half:]], axis=0).astype(BF16)


def unfold(packed):
    wide = packed.astype(F32)
    return jnp.concatenate([wide[:8], wide[8:]], axis=1)


class Scoring:
    def __init__(self, place, ways, cls, gold, passages, scores, lse, buffers, sems):
        self.at, self.ways, self.cls, self.gold = place, ways, cls, gold
        self.passages, self.scores, self.lse = passages, scores, lse
        self.part, self.parts, self.firsts, self.rows = buffers[:4]
        self.sent, self.got, self.stats, self.got_stats = buffers[4:]
        self.mp_sems, self.sems = sems
        at = place
        self.mates = (at.sibling, (at.dp, at.across), at.diagonal)
        self.others = [(lax.rem(at.dp + k, ways), at.mp) for k in range(1, ways)]

    def mate(self, k):
        return remote(
            self.part, self.parts.at[k], self.mp_sems.at[0, k], self.mp_sems.at[1, k], self.mates[k]
        )

    def first_copy(self, k):
        mine = self.firsts.at[self.at.dp]
        return remote(
            mine, mine, self.sems.at[0, 0, k - 1], self.sems.at[0, 1, k - 1], self.others[k - 1]
        )

    def back_copy(self, which, k):
        peer = self.others[k - 1]
        return remote(
            self.sent.at[which, peer[0]],
            self.got.at[which, self.at.dp],
            self.sems.at[1 + which, 0, k - 1],
            self.sems.at[1 + which, 1, k - 1],
            peer,
        )

    def stat_copy(self, k):
        peer = self.others[k - 1]
        return remote(
            self.stats.at[peer[0]],
            self.got_stats.at[self.at.dp],
            self.sems.at[3, 0, k - 1],
            self.sems.at[3, 1, k - 1],
            peer,
        )

    def start_cls(self):
        self.part[...] = fold(self.cls[...])
        for k in range(3):
            self.mate(k).start()

    def start_gold(self):
        columns = self.at.dp * self.passages.shape[0] + lax.broadcasted_iota(
            jnp.int32, (self.gold.shape[0], self.passages.shape[0]), 1
        )
        target = jnp.where(self.gold[...] == columns, 1.0, 0.0).astype(BF16)
        self.put(0, dot(target, self.passages[...]))
        for k in range(1, self.ways):
            self.back_copy(0, k).start()

    def put(self, which, rows):
        for d in range(self.ways):
            self.sent[which, d] = fold(rows[8 * d : 8 * d + 8])
        self.got[which, self.at.dp] = self.sent[which, self.at.dp]

    def start_firsts(self):
        total = self.part[...].astype(F32)
        for k in range(3):
            self.mate(k).wait_recv()
            total = total + self.parts[k].astype(F32)
        self.firsts[self.at.dp] = total.astype(BF16)
        for k in range(1, self.ways):
            self.first_copy(k).start()

    def start_back(self):
        for k in range(1, self.ways):
            self.first_copy(k).wait_recv()
        for d in range(self.ways):
            self.rows[8 * d : 8 * d + 8, :] = unfold(self.firsts[d])
        table = dot(self.rows[...].astype(BF16), self.passages[...], 1, 1)
        self.scores[...] = table
        peak = jnp.max(table, axis=1, keepdims=True)
        e = jnp.exp(table - peak)
        total = jnp.sum(e, axis=1, keepdims=True)
        lane = lax.broadcasted_iota(jnp.int32, (8, LANES), 1)
        for d in range(self.ways):
            rows = slice(8 * d, 8 * d + 8)
            self.stats[d] = jnp.where(lane == 0, peak[rows], total[rows])
        self.got_stats[self.at.dp] = self.stats[self.at.dp]
        for k in range(1, self.ways):
            self.stat_copy(k).start()
        self.put(1, dot(e.astype(BF16), self.passages[...]))
        for k in range(1, self.ways):
            self.back_copy(1, k).start()

    def result(self):
        for k in range(1, self.ways):
            self.back_copy(0, k).wait_recv()
            self.stat_copy(k).wait_recv()
        peaks = [self.got_stats[d][:, 0:1] for d in range(self.ways)]
        top = functools.reduce(jnp.maximum, peaks)
        scales = [jnp.exp(peak - top) for peak in peaks]
        total = sum(scale * self.got_stats[d][:, 1:2] for d, scale in enumerate(scales))
        self.lse[...] = top + jnp.log(total)
        for k in range(1, self.ways):
            self.back_copy(1, k).wait_recv()
        grad = -sum(unfold(self.got[0, d]) for d in range(self.ways))
        for d in range(self.ways):
            grad = grad + (scales[d] / total) * unfold(self.got[1, d])
        return grad

    def end(self):
        for k in range(3):
            self.mate(k).wait_send()
        for k in range(1, self.ways):
            self.first_copy(k).wait_send()
            self.back_copy(0, k).wait_send()
            self.back_copy(1, k).wait_send()
            self.stat_copy(k).wait_send()


class Halo:
    def __init__(self, sizes, place, dkv, sent, got, sems):
        self.sizes, self.at, self.dkv, self.sent, self.got, self.sems = sizes, place, dkv, sent, got, sems
        self.has = (place.mp > 0, place.mp < sizes.groups - 1)
        offset = sizes.own_offset(place.mp)
        self.starts = (offset - LONGEST, offset + sizes.own)
        self.into = (sizes.own - LONGEST, 0)

    def copy(self, g, side):
        slot = g % 2
        return remote(
            self.sent.at[slot, side],
            self.got.at[g, side],
            self.sems.at[0, slot, side],
            self.sems.at[1, g, side],
            (self.at.dp, self.at.mp + 2 * side - 1),
        )

    def start(self, g):
        for side in range(2):

            @pl.when(self.has[side])
            def _():
                pl.when(g > 1)(self.copy(g, side).wait_send)
                rows = pl.ds(pl.multiple_of(self.starts[side], 16), LONGEST)
                self.sent[g % 2, side] = self.dkv[rows, :].astype(BF16)
                self.copy(g, side).start()

    def add(self, g, own):
        for side in range(2):

            @pl.when(self.has[1 - side])
            def _():
                self.copy(g, side).wait_recv()
                rows = pl.ds(self.into[side], LONGEST)
                own[rows, :] += self.got[g, side].astype(F32)

    def end(self):
        for side in range(2):

            @pl.when(self.has[side])
            def _():
                self.copy(2, side).wait_send()
                self.copy(3, side).wait_send()


def finish_kernel(
    sizes,
    lens,
    cls,
    gold,
    gain_1,
    shift_1,
    gain_2,
    r_1,
    r_2,
    lse,
    tokens,
    cotangent,
    passages,
    encoded,
    weights,
    n_1_in,
    n_2_in,
    z_in,
    slope_in,
    kv_in,
    q_in,
    ctx_in,
    scores,
    query_lse,
    small_out,
    shards,
    encoded_whole,
    token_whole,
    w,
    ffn,
    parts,
    inbox,
    by_second,
    by_first,
    by_line,
    kv,
    q,
    ctx,
    dctx,
    dkv,
    own_kv,
    halo_sent,
    halo_got,
    n_1,
    work,
    rows_low,
    row_in,
    turned,
    low,
    bias,
    delta,
    sums,
    sums_in,
    part,
    parts_in,
    firsts,
    first_rows,
    back_sent,
    back_got,
    stats,
    stats_got,
    load_sems,
    kv_sems,
    ffn_sems,
    spread_sems,
    core_sems,
    second_sems,
    first_sems,
    line_sems,
    halo_sems,
    small_sems,
    mp_sems,
    score_sems,
):
    at = Place()
    me = at.mp
    own_rows = pl.ds(pl.multiple_of(sizes.own * me, 16), sizes.own)
    ways = firsts.shape[0]
    table = parts.at[pl.ds(Scatter.HELD[0] * sizes.width, passages.shape[0])]
    scatter = Scatter(
        at, parts, inbox, by_second, by_first, by_line, shards,
        (core_sems, second_sems, first_sems, line_sems),
    )
    halo = Halo(sizes, at, dkv, halo_sent, halo_got, halo_sems)
    spread = Spread(at, encoded, encoded_whole, spread_sems.at[0, 0], spread_sems.at[0, 1], load_sems.at[8])
    token_spread = Spread(
        at, rows_low, token_whole, spread_sems.at[1, 0], spread_sems.at[1, 1], load_sems.at[9]
    )
    small = SmallSums(at, sums, sums_in, small_sems)

    def load(k, source, target):
        return pltpu.make_async_copy(source, target, load_sems.at[k])

    loads = [
        load(0, passages, table),
        load(1, cotangent.at[own_rows], row_in),
        load(2, n_2_in, work.at[1]),
        load(3, n_1_in, n_1),
        load(5, q_in, q),
        load(6, ctx_in, ctx),
    ]

    def kv_load(g):
        return pltpu.make_async_copy(kv_in.at[g], kv.at[g % 2], kv_sems.at[g % 2])

    for copy in loads:
        copy.start()
    kv_load(0).start()

    def group_of(i):
        return jnp.where(i < 2, 1 - at.core + 2 * i, at.core + 2 * (i - 2))

    def ffn_loads(i):
        slot, g = i % 2, group_of(i)
        return [
            pltpu.make_async_copy(weights.at[2, g], w.at[2 * slot], ffn_sems.at[slot, 0]),
            pltpu.make_async_copy(weights.at[1, g], w.at[2 * slot + 1], ffn_sems.at[slot, 1]),
            pltpu.make_async_copy(z_in.at[g], ffn.at[slot, 0], ffn_sems.at[slot, 2]),
            pltpu.make_async_copy(slope_in.at[g], ffn.at[slot, 1], ffn_sems.at[slot, 3]),
        ]

    for copy in ffn_loads(0):
        copy.start()

    scoring = Scoring(
        at,
        ways,
        cls,
        gold,
        table,
        scores,
        query_lse,
        (part, parts_in, firsts, first_rows, back_sent, back_got, stats, stats_got),
        (mp_sems, score_sems),
    )
    greet([*scoring.mates, *scoring.others])
    scoring.start_cls()
    loads[0].wait()
    scoring.start_gold()
    scoring.start_firsts()
    spread.begin()
    fill_mask(sizes, me, lens, bias)
    picked = start_rows(sizes, me, lens).astype(BF16)
    loads[3].wait()
    turned[1] = (n_1[...] * gain_1[...] + shift_1[...]).T.astype(BF16)
    scoring.start_back()
    loads[1].wait()
    loads[2].wait()
    dcls = scoring.result()
    high = dcls.astype(BF16)
    rest = (dcls - high.astype(F32)).astype(BF16)
    dy = row_in[...].astype(F32) + dot(picked, high, 0, 0) + dot(picked, rest, 0, 0)
    mine = sums.at[0]
    mine[0:1, :] = jnp.sum(dy * work[1], axis=0, keepdims=True)
    mine[1:2, :] = jnp.sum(dy, axis=0, keepdims=True)
    grad = norm_back(dy, work[1], r_2[...], gain_2[...])
    mine[2:3, :] = jnp.sum(grad, axis=0, keepdims=True)
    work[0] = grad
    rows_low[...] = grad.astype(BF16)
    turned[0] = grad.T.astype(BF16)

    for half in range(2):

        @pl.loop(2 * half, 2 * half + 2)
        def _(i):
            slot, g = i % 2, group_of(i)
            for copy in ffn_loads(i):
                copy.wait()

            @pl.when(i < 3)
            def _():
                for copy in ffn_loads(i + 1):
                    copy.start()

            k = i - 2 * half
            into = [(Scatter.HELD if half else Scatter.STAGE)[s] + k for s in range(3)]
            square(parts, into[2])[...] = dot(turned[0], ffn[slot, 0]).astype(BF16)
            if not half:
                scatter.to_sibling(2, k).start()
            da = dot(rows_low[...], w[2 * slot]) * ffn[slot, 1].astype(F32)
            mine[pl.ds(8 + g, 1), :] = jnp.sum(da, axis=0, keepdims=True)
            da_low = da.astype(BF16)
            square(parts, into[1])[...] = dot(turned[1], da_low).astype(BF16)
            if not half:
                scatter.to_sibling(1, k).start()
            work[0] += dot(da_low, w[2 * slot + 1], 1, 1)

    load_w = pltpu.make_async_copy(weights.at[0], w, load_sems.at[7])
    load_w.start()
    load_x = load(1, tokens.at[own_rows], row_in)
    load_x.start()
    scatter.chip_sum(2)
    scatter.chip_sum(1)
    scatter.sent_to_sibling(2)

    dy = work[0]
    mine[3:4, :] = jnp.sum(dy * n_1[...], axis=0, keepdims=True)
    mine[4:5, :] = jnp.sum(dy, axis=0, keepdims=True)
    grad = norm_back(dy, n_1[...], r_1[...], gain_1[...])
    mine[5:6, :] = jnp.sum(grad, axis=0, keepdims=True)
    mine[6:8, :] = jnp.zeros((2, sizes.width), F32)
    mine[12:24, :] = jnp.zeros((12, sizes.width), F32)
    work[1] = grad
    rows_low[...] = grad.astype(BF16)
    turned[0] = grad.T.astype(BF16)
    load_x.wait()
    turned[1] = row_in[...].astype(F32).T.astype(BF16)
    spread.forward()
    load_w.wait()
    for copy in loads[4:]:
        copy.wait()

    @pl.loop(0, sizes.groups)
    def _(g):
        dctx[g] = dot(rows_low[...], w[g, :, tile(4, 2)]).astype(BF16)

    def step(k):
        if k == 2:
            scatter.from_second(2)
        elif k == 4:
            scatter.from_first(2)
        elif k == 5:
            scatter.from_second(1)
        elif k == 6:
            scatter.from_line(2)

    def tick(now):
        for k in (2, 4, 5, 6):
            pl.when(now == k)(functools.partial(step, k))

    def finalize(g):
        slot = g % 2
        halo.add(g, own_kv.at[slot])
        dkv_own = own_kv[slot]
        mine[pl.ds(16 + g, 1), tile(0, 3)] = jnp.sum(dkv_own, axis=0, keepdims=True)
        low[slot, :, tile(0, 3)] = dkv_own.astype(BF16)
        work[1] += dot(low[slot], w[g, :, tile(0, 5)], 1, 1)
        into = jnp.where(g % 2 == at.core, Scatter.HELD[0], Scatter.STAGE[0]) + g // 2
        made = dot(turned[1], low[slot])
        more = dot(turned[0], ctx[g])
        target = square(parts, into)
        target[:, tile(0, 4)] = made[:, tile(0, 4)].astype(BF16)
        target[:, tile(4)] = (made[:, tile(4)] + more[:, tile(0)]).astype(BF16)
        target[:, tile(5)] = more[:, tile(1)].astype(BF16)

        @pl.when(g % 2 != at.core)
        def _():
            scatter.to_sibling(0, g // 2).start()

    own = pl.ds(sizes.own_offset(me), sizes.own)

    @pl.loop(0, sizes.groups)
    def _(g):
        slot = g % 2
        kv_load(g).wait()

        @pl.when(g < sizes.groups - 1)
        def _():
            kv_load(g + 1).start()

        delta[...] = delta_rows(dctx[g], ctx[g])
        dkv[...] = jnp.zeros_like(dkv)
        for b in range(sizes.blocks):
            tick(g * sizes.blocks + b)
            rows = slice(b * sizes.block, (b + 1) * sizes.block)
            dq = attend_back_block(
                sizes, me, g, b, kv.at[slot], q, bias, lse, dctx, delta, dkv
            )
            total = jnp.sum(dq, axis=0, keepdims=True)
            mine[pl.ds(16 + g, 1), tile(3, 2)] += total
            low[slot, rows, tile(3, 2)] = dq.astype(BF16)
        halo.start(g)
        own_kv[slot] = dkv[own, :]

        @pl.when(g > 0)
        def _():
            finalize(g - 1)

    scatter.from_first(1)
    finalize(sizes.groups - 1)
    small.begin()
    rows_low[...] = work[1].astype(BF16)
    scatter.chip_sum(0)
    token_spread.begin()
    small.step(0)
    scatter.from_line(1)
    scatter.from_second(0)
    small.step(1)
    scatter.from_first(0)
    small.step(2)
    token_spread.forward()
    scatter.from_line(0)
    small.end(small_out)
    scatter.sent_to_sibling(1)
    scatter.sent_to_sibling(0)
    scatter.end()
    halo.end()
    scoring.end()
    spread.end()
    token_spread.end()


def input_kernel(sizes, tokens, weights, dkv, dq, dh_1, grads_out, token_grad, grads, small, turned, low):
    turned[...] = tokens[...].astype(F32).T.astype(BF16)
    total = dh_1[...]
    for g in range(sizes.groups):
        small[g, :, tile(0, 3)] = jnp.sum(dkv[g], axis=0, keepdims=True)
        small[g, :, tile(3, 2)] = jnp.sum(dq[g], axis=0, keepdims=True)
        low[:, tile(0, 3)] = dkv[g].astype(BF16)
        low[:, tile(3, 2)] = dq[g].astype(BF16)
        total = total + dot(low[...], weights[g, :, tile(0, 5)], 1, 1)
        made = dot(turned[...], low[...])
        grads[g, :, tile(0, 4)] = made[:, tile(0, 4)].astype(BF16)
        grads[g, :, tile(4)] = (made[:, tile(4)] + grads_out[g, :, tile(0)]).astype(BF16)
        grads[g, :, tile(5)] = grads_out[g, :, tile(1)].astype(BF16)
    token_grad[...] = total.astype(BF16)


def specs(*spaces):
    return [pl.BlockSpec(memory_space=s) for s in spaces]


def params(**more):
    return pltpu.CompilerParams(vmem_limit_bytes=63 * 2**20, **more)


def run_forward(sizes, lengths, tokens, weights, biases, rows, gathers):
    own, width, groups = sizes.own, sizes.width, sizes.groups
    docs = lengths.shape[1]
    shape = jax.ShapeDtypeStruct
    outs = [
        shape((own, width), BF16),
        shape((docs, width), F32),
        shape((own, width), F32),
        shape((own, 1), F32),
        shape((own, width), F32),
        shape((own, 1), F32),
        shape((groups, own, width), BF16),
        shape((groups, own, width), BF16),
        shape((groups, sizes.window, 3 * LANES), BF16),
        shape((groups, own, 2 * LANES), BF16),
        shape((groups, sizes.blocks, 8, sizes.block), F32),
        shape((groups, own, 2 * LANES), BF16),
    ]
    spaces = [*[VMEM] * 6, ANY, ANY, ANY, *[VMEM] * 3]
    scratch = [
        pltpu.VMEM((sizes.window, width), BF16),
        pltpu.VMEM((3, groups, width, width), BF16),
        pltpu.VMEM((sizes.blocks, sizes.keys, sizes.block), F32),
        pltpu.VMEM((own, width), F32),
        pltpu.VMEM((groups, sizes.window, 3 * LANES), BF16),
        pltpu.VMEM((groups, own, width), BF16),
        pltpu.VMEM((groups, own, width), BF16),
        pltpu.SemaphoreType.DMA((4,)),
    ]
    if gathers:
        outs.insert(0, shape((3, groups, width, width), BF16))
        spaces.insert(0, ANY)
        scratch += [
            pltpu.VMEM((groups, 1, biases.shape[1]), F32),
            pltpu.SemaphoreType.DMA((3, 31)),
            pltpu.SemaphoreType.DMA((3, 32)),
            pltpu.SemaphoreType.DMA((6,)),
            pltpu.SemaphoreType.DMA((2, 3)),
        ]
        kernel, more = gathering_kernel, {"collective_id": 0, "has_side_effects": True}
    else:
        scratch.append(pltpu.SemaphoreType.DMA((3,)))
        kernel, more = forward_kernel, {}
    return pl.pallas_call(
        functools.partial(kernel, sizes),
        out_shape=outs,
        in_specs=specs(SMEM, ANY, VMEM if gathers else ANY, *[VMEM] * 7),
        out_specs=specs(*spaces),
        scratch_shapes=scratch,
        compiler_params=params(**more),
        name="forward",
    )(lengths, tokens, weights, biases, *rows)


def run_backward(sizes, lengths, cotangent, dcls, weights, gain_1, shift_1, gain_2, saved):
    own, width, groups = sizes.own, sizes.width, sizes.groups
    shape = jax.ShapeDtypeStruct
    outs = (
        shape((own, width), F32),
        shape((groups, sizes.window, 3 * LANES), F32),
        shape((groups, own, 2 * LANES), F32),
        shape((2, groups, width, width), BF16),
        shape((groups, width, 2 * LANES), F32),
        shape((16, width), F32),
    )
    return pl.pallas_call(
        functools.partial(backward_kernel, sizes),
        out_shape=outs,
        in_specs=specs(SMEM, ANY, VMEM, ANY, *[VMEM] * (3 + len(saved))),
        out_specs=specs(VMEM, VMEM, VMEM, ANY, VMEM, VMEM),
        scratch_shapes=[
            pltpu.VMEM((groups, width, width), BF16),
            pltpu.VMEM((groups, width, width), BF16),
            pltpu.VMEM((groups, width, width), BF16),
            pltpu.VMEM((own, width), BF16),
            pltpu.VMEM((own, width), F32),
            pltpu.VMEM((own, width), BF16),
            pltpu.VMEM((own, width), BF16),
            pltpu.VMEM((2, width, own), BF16),
            pltpu.VMEM((2, width, width), BF16),
            pltpu.VMEM((groups, own, 2 * LANES), BF16),
            pltpu.VMEM((8, own), F32),
            pltpu.VMEM((sizes.blocks, sizes.keys, sizes.block), F32),
            pltpu.SemaphoreType.DMA((4,)),
            pltpu.SemaphoreType.DMA((2,)),
        ],
        compiler_params=params(),
        name="backward",
    )(lengths, cotangent, dcls, weights, gain_1, shift_1, gain_2, *saved)


def run_input(sizes, own_tokens, w_attn, dkv, dq, dh_1, grads_out):
    own, width, groups = sizes.own, sizes.width, sizes.groups
    shape = jax.ShapeDtypeStruct
    outs = (
        shape((own, width), BF16),
        shape((groups, width, width), BF16),
        shape((groups, 1, 5 * LANES), F32),
    )
    return pl.pallas_call(
        functools.partial(input_kernel, sizes),
        out_shape=outs,
        in_specs=specs(*[VMEM] * 6),
        out_specs=specs(*[VMEM] * 3),
        scratch_shapes=[pltpu.VMEM((width, own), BF16), pltpu.VMEM((own, 5 * LANES), BF16)],
        compiler_params=params(),
        name="inputs",
    )(own_tokens, w_attn, dkv, dq, dh_1, grads_out)


def run_finish(sizes, small_in, large_in):
    own, width, groups = sizes.own, sizes.width, sizes.groups
    tokens, passages = large_in[0], large_in[2]
    queries = small_in[2].shape[0]
    ways = queries // 8
    shard = width // ways
    shape = jax.ShapeDtypeStruct
    outs = (
        shape((queries, passages.shape[0]), F32),
        shape((8, 1), F32),
        shape((24, width), F32),
        shape((3, shard, width), F32),
        shape(tokens.shape, BF16),
        shape(tokens.shape, BF16),
    )
    dma = pltpu.SemaphoreType.DMA
    scratch = [
        pltpu.VMEM((groups, width, width), BF16),
        pltpu.VMEM((2, 2, own, width), BF16),
        pltpu.VMEM((10 * width, width), BF16),
        pltpu.VMEM((4, width, width), BF16),
        pltpu.VMEM((3, 8, shard, width), BF16),
        pltpu.VMEM((3, 4, shard, width), BF16),
        pltpu.VMEM((3, 3, shard, width), BF16),
        pltpu.VMEM((2, sizes.window, 3 * LANES), BF16),
        pltpu.VMEM((groups, own, 2 * LANES), BF16),
        pltpu.VMEM((groups, own, 2 * LANES), BF16),
        pltpu.VMEM((groups, own, 2 * LANES), BF16),
        pltpu.VMEM((sizes.window, 3 * LANES), F32),
        pltpu.VMEM((2, own, 3 * LANES), F32),
        pltpu.VMEM((2, 2, LONGEST, 3 * LANES), BF16),
        pltpu.VMEM((groups, 2, LONGEST, 3 * LANES), BF16),
        pltpu.VMEM((own, width), F32),
        pltpu.VMEM((2, own, width), F32),
        pltpu.VMEM((own, width), BF16),
        pltpu.VMEM((own, width), BF16),
        pltpu.VMEM((2, width, own), BF16),
        pltpu.VMEM((2, own, 5 * LANES), BF16),
        pltpu.VMEM((sizes.blocks, sizes.keys, sizes.block), F32),
        pltpu.VMEM((8, own), F32),
        pltpu.VMEM((4, 24, width), F32),
        pltpu.VMEM((6, 24, width), F32),
        pltpu.VMEM((16, width // 2), BF16),
        pltpu.VMEM((3, 16, width // 2), BF16),
        pltpu.VMEM((ways, 16, width // 2), BF16),
        pltpu.VMEM((queries, width), F32),
        pltpu.VMEM((2, ways, 16, width // 2), BF16),
        pltpu.VMEM((2, ways, 16, width // 2), BF16),
        pltpu.VMEM((ways, 8, LANES), F32),
        pltpu.VMEM((ways, 8, LANES), F32),
        dma((10,)),
        dma((2,)),
        dma((2, 4)),
        dma((2, 2, 3)),
        dma((2, 3, 2)),
        dma((2, 3, 8)),
        dma((2, 3, 4)),
        dma((2, 3, 3)),
        dma((2, 4, 2)),
        dma((2, 6)),
        dma((2, 3)),
        dma((4, 2, ways - 1)),
    ]
    return pl.pallas_call(
        functools.partial(finish_kernel, sizes),
        out_shape=outs,
        in_specs=specs(SMEM, *[VMEM] * (len(small_in) - 1), *[ANY] * len(large_in)),
        out_specs=specs(*[VMEM] * 4, ANY, ANY),
        scratch_shapes=scratch,
        compiler_params=params(collective_id=1, has_side_effects=True),
        name="finish",
    )(*small_in, *large_in)


def cut_along(array, dim, devices):
    before, after = (array.shape[:dim], array.shape[dim + 1 :])
    return jnp.moveaxis(array.reshape(*before, devices, -1, *after), dim, 0)


def summed_on_arrival(array, axis, dim):
    pieces = cut_along(array, dim, lax.axis_size(axis))
    arrived = lax.all_to_all(pieces, axis, split_axis=0, concat_axis=0, tiled=True)
    return arrived.astype(F32).sum(axis=0)


def score(cls, passages, gold):
    all_first = lax.all_gather(cls, "dp", axis=0, tiled=True)
    table = dot(all_first, passages, 1, 1)
    peak = lax.pmax(jnp.max(table, axis=1), "dp")
    total = lax.psum(jnp.sum(jnp.exp(table - peak[:, None]), axis=1), "dp")
    own = cls.shape[0]
    lse = lax.dynamic_slice_in_dim(peak + jnp.log(total), lax.axis_index("dp") * own, own)
    soft = jnp.exp(table - peak[:, None]) / total[:, None]
    first = lax.axis_index("dp") * table.shape[1]
    columns = first + jnp.arange(table.shape[1], dtype=jnp.int32)
    target = (gold[:, None] == columns[None, :]).astype(F32)
    grad = dot((soft - target).astype(BF16), passages)
    return table, lse, summed_on_arrival(grad.astype(BF16), "dp", 0)


def plain_layer(sizes, tokens, cotangent, lengths, gold, passages, packed, own_bias, rows):
    me, groups = lax.axis_index("mp"), sizes.groups
    whole = lax.all_gather(lax.all_gather(packed, "dp", axis=1, tiled=True), "mp", axis=1)
    biases = lax.all_gather(own_bias, "mp", axis=0)
    encoded, cls, *saved = run_forward(sizes, lengths, tokens, whole, biases, rows, False)
    cls = lax.psum(cls, "mp").astype(BF16)
    table, lse, dcls = score(cls, passages, gold)
    n_1, r_1, n_2, r_2, z, slope, kv, q, logs, ctx = saved
    dh_1, dkv, dq, grads_ffn, grads_out, small = run_backward(
        sizes, lengths, cotangent, dcls, whole, rows[1], rows[2], rows[4], saved
    )
    halo, own = LONGEST, sizes.own
    offset = own * me - sizes.window_start(me)
    to_left = lax.dynamic_slice_in_dim(dkv, offset - halo, halo, axis=1).astype(BF16)
    to_right = lax.dynamic_slice_in_dim(dkv, offset + own, halo, axis=1).astype(BF16)
    from_right = lax.ppermute(to_left, "mp", [(i, i - 1) for i in range(1, groups)])
    from_left = lax.ppermute(to_right, "mp", [(i, i + 1) for i in range(groups - 1)])
    dkv = lax.dynamic_slice_in_dim(dkv, offset, own, axis=1)
    dkv = dkv.at[:, own - halo :].add(from_right.astype(F32))
    dkv = dkv.at[:, :halo].add(from_left.astype(F32))
    own_tokens = lax.dynamic_slice_in_dim(tokens, own * me, own, axis=0)
    token_part, grads_attn, small_attn = run_input(
        sizes, own_tokens, whole[0], dkv, dq, dh_1, grads_out
    )
    token_grad = lax.all_gather(token_part, "mp", axis=0, tiled=True).astype(F32)
    encoded = lax.all_gather(encoded, "mp", axis=0, tiled=True)
    grads = jnp.stack([grads_attn, grads_ffn[0], grads_ffn[1]])
    grads = summed_on_arrival(grads, "mp", 1)[:, 0].astype(BF16)
    grads = summed_on_arrival(grads, "dp", 1)
    small, small_attn = lax.psum((small, small_attn), ("dp", "mp"))
    return table, lse, encoded, token_grad, grads, small, small_attn[:, 0]


def body(
    tokens,
    cotangent,
    lengths,
    gold,
    passages,
    w_query,
    w_key,
    w_value,
    b_query,
    b_value,
    w_out,
    b_out,
    gain_attn,
    shift_attn,
    w_up,
    b_up,
    w_down,
    b_down,
    gain_ffn,
    shift_ffn,
):
    groups = lax.axis_size("mp")
    sizes = Sizes(tokens.shape[0], tokens.shape[1], groups)
    me = lax.axis_index("mp")
    head_cols = w_query.shape[1]
    packed = jnp.stack(
        [jnp.concatenate([w_key, w_value, w_query, w_out.T], axis=1), w_up, w_down.T]
    )
    zeros = jnp.zeros((head_cols,), F32)
    own_bias = jnp.concatenate([zeros, b_value, b_query, zeros[:HEAD], b_up])[None]
    rows = [r[None] for r in (b_out, gain_attn, shift_attn, b_down, gain_ffn, shift_ffn)]
    c = head_cols
    if lax.axis_size("dp") == 8 and groups == 4:
        whole, encoded, cls, n_1, r_1, n_2, r_2, z, slope, kv, q, logs, ctx = run_forward(
            sizes, lengths, tokens, packed, own_bias, rows, True
        )
        table, lse, small, grads, encoded, token_part = run_finish(
            sizes,
            (lengths, cls, gold[:, None], rows[1], rows[2], rows[4], r_1, r_2, logs),
            (tokens, cotangent, passages, encoded, whole, n_1, n_2, z, slope, kv, q, ctx),
        )
        lse, token_grad, small_attn = lse[:, 0], token_part.astype(F32), small[16:20]
    else:
        table, lse, encoded, token_grad, grads, small, small_attn = plain_layer(
            sizes, tokens, cotangent, lengths, gold, passages, packed, own_bias, rows
        )
    mine = lax.dynamic_index_in_dim(small_attn, me, 0, keepdims=False)
    up_bias = lax.dynamic_index_in_dim(small, 8 + me, 0, keepdims=False)
    return (
        table,
        lse,
        encoded,
        token_grad,
        grads[0, :, 2 * c : 3 * c],
        grads[0, :, :c],
        grads[0, :, c : 2 * c],
        mine[2 * c : 3 * c],
        mine[c : 2 * c],
        grads[0, :, 3 * c :].T,
        small[5],
        small[3],
        small[4],
        grads[1],
        up_bias,
        grads[2].T,
        small[2],
        small[0],
        small[1],
    )


def solution(mesh):
    by_dp, shared, cross = P("dp", None), P(), P("dp", "mp")
    return jax.shard_map(
        body,
        mesh=mesh,
        in_specs=(
            by_dp,
            by_dp,
            by_dp,
            shared,
            by_dp,
            cross,
            cross,
            cross,
            P("mp"),
            P("mp"),
            P("mp", "dp"),
            shared,
            shared,
            shared,
            cross,
            P("mp"),
            P("mp", "dp"),
            shared,
            shared,
            shared,
        ),
        out_specs=(
            P(None, "dp"),
            P("dp"),
            by_dp,
            by_dp,
            cross,
            cross,
            cross,
            P("mp"),
            P("mp"),
            P("mp", "dp"),
            shared,
            shared,
            shared,
            cross,
            P("mp"),
            P("mp", "dp"),
            shared,
            shared,
            shared,
        ),
        check_vma=False,
    )
```

```python
import functools

import jax
import jax.numpy as jnp
from jax import lax
from jax.experimental import pallas as pl
from jax.experimental.pallas import tpu as pltpu
from jax.sharding import PartitionSpec as P

HEAD = 64
LONGEST = 400
QUERY_BLOCK = 256
EPSILON = 1e-05
NEGATIVE = -1e30
LANES = 128
KEY_AT = ((0, 0), (0, 1), (1, 0))
VALUE_AT = ((1, 1), (2, 0), (2, 1))
QUERY_AT = ((0, 0), (0, 1), (1, 0))
CONTEXT_AT = ((0, 1), (1, 0), (1, 1))
F32, BF16 = jnp.float32, jnp.bfloat16
VMEM, ANY, SMEM = pltpu.VMEM, pl.ANY, pltpu.SMEM


def dot(left, right, left_dim=1, right_dim=0):
    return lax.dot_general(
        left, right, (((left_dim,), (right_dim,)), ((), ())), preferred_element_type=F32
    )


def tile(index, count=1):
    return slice(index * LANES, (index + count) * LANES)


def half_mask(half, dtype):
    lane = lax.broadcasted_iota(jnp.int32, (1, LANES), 1)
    return jnp.where((lane >= HEAD) == (half == 1), 1.0, 0.0).astype(dtype)


def norm_stats(hidden):
    centred = hidden - jnp.mean(hidden, axis=-1, keepdims=True)
    factor = lax.rsqrt(jnp.mean(centred * centred, axis=-1, keepdims=True) + EPSILON)
    return centred * factor, factor


def norm_back(grad_out, normed, factor, gain):
    scaled = grad_out * gain
    inner = jnp.mean(scaled * normed, axis=-1, keepdims=True)
    return factor * (scaled - jnp.mean(scaled, axis=-1, keepdims=True) - normed * inner)


def gelu_and_slope(a):
    size = jnp.abs(a)
    t = 1.0 / (1.0 + (0.3275911 * 0.7071067811865476) * size)
    bell = jnp.exp(-0.5 * a * a)
    poly = t * (
        0.127414796 + t * (-0.142248368 + t * (0.7107068705 + t * (-0.7265760135 + t * 0.5307027145)))
    )
    tail = poly * bell
    phi = jnp.where(a >= 0.0, 1.0 - tail, tail)
    return a * phi, phi + a * bell * 0.3989422804014327


def as_row(ref):
    return ref[...].reshape(1, ref.shape[0])


class Sizes:
    def __init__(self, length, width, groups):
        self.length, self.width, self.groups = length, width, groups
        self.own = length // groups
        self.window = min(length, self.own + 2 * LONGEST)
        self.block = min(QUERY_BLOCK, self.own)
        self.blocks = self.own // self.block
        self.keys = min(length, self.block + 2 * LONGEST)

    def window_start(self, me):
        return jnp.clip(self.own * me - LONGEST, 0, self.length - self.window)

    def own_offset(self, me):
        return pl.multiple_of(self.own * me - self.window_start(me), 16)

    def key_start(self, me, block):
        first = self.own * me + block * self.block
        return jnp.clip(first - LONGEST, 0, self.length - self.keys)

    def key_offset(self, me, block):
        return pl.multiple_of(self.key_start(me, block) - self.window_start(me), 16)


def document_bounds(lens, places):
    start = jnp.zeros_like(places)
    end = jnp.zeros_like(places)
    total = jnp.int32(0)
    for d in range(lens.shape[1]):
        count = lens[0, d]
        end = end + jnp.where(places >= total, count, 0)
        total = total + count
        start = start + jnp.where(places >= total, count, 0)
    return start, end


def fill_mask(sizes, me, lens, bias):
    for b in range(sizes.blocks):
        places = (
            sizes.own * me
            + b * sizes.block
            + lax.broadcasted_iota(jnp.int32, (1, sizes.block), 1)
        )
        start, end = document_bounds(lens, places)
        keys = sizes.key_start(me, b) + lax.broadcasted_iota(
            jnp.int32, (sizes.keys, sizes.block), 0
        )
        bias[b] = jnp.where((keys >= start) & (keys < end), 0.0, NEGATIVE)


def start_rows(sizes, me, lens):
    docs = lens.shape[1]
    row = lax.broadcasted_iota(jnp.int32, (docs, sizes.own), 0)
    place = sizes.own * me + lax.broadcasted_iota(jnp.int32, (docs, sizes.own), 1)
    picked = jnp.zeros((docs, sizes.own), F32)
    total = jnp.int32(0)
    for d in range(docs):
        picked = jnp.where((row == d) & (place == total), 1.0, picked)
        total = total + lens[0, d]
    return picked


def project(sizes, me, group, span, tokens, w_attn, biases, kv, q):
    cut = sizes.window // 2
    own = pl.ds(sizes.own_offset(me), sizes.own)

    @pl.loop(*span)
    def _(i):
        g = group(i)
        for part in range(2):
            rows = pl.ds(part * cut, cut)
            made = dot(tokens[rows, :], w_attn[g, :, tile(0, 3)]) + biases[g, :, tile(0, 3)]
            kv[g, rows, :] = made.astype(BF16)
        made = dot(tokens[own, :], w_attn[g, :, tile(3, 2)]) + biases[g, :, tile(3, 2)]
        q[g] = made.astype(BF16) * jnp.asarray(HEAD**-0.5, BF16)


def attend(sizes, me, group, span, tick, kv, q, bias, lse, ctx):
    @pl.loop(*span)
    def _(i):
        g = group(i)

        @pl.loop(0, sizes.blocks)
        def _(b):
            tick(i * sizes.blocks + b)
            keys = pl.ds(sizes.key_offset(me, b), sizes.keys)
            rows = pl.ds(pl.multiple_of(b * sizes.block, sizes.block), sizes.block)
            made = [jnp.zeros((HEAD, sizes.block), F32)]
            logs = []
            for j in range(3):
                kt, kh = KEY_AT[j]
                vt, vh = VALUE_AT[j]
                qt, _ = QUERY_AT[j]
                query = q[g, rows, tile(qt)] * half_mask(kh, BF16)
                s = dot(kv[g, keys, tile(kt)], query, 1, 1) + bias[b]
                peak = jnp.max(s, axis=0, keepdims=True)
                e = jnp.exp(s - peak)
                total = jnp.sum(e, axis=0, keepdims=True)
                mixed = dot(kv[g, keys, tile(vt)], e.astype(BF16), 0, 0)
                made.append(mixed[vh * HEAD : (vh + 1) * HEAD] / total)
                logs.append(peak + jnp.log(total))
            ctx[g, rows, :] = jnp.concatenate(made, axis=0).T.astype(BF16)
            for j in range(3):
                lse[g, b, j : j + 1, :] = logs[j]


def delta_rows(dctx, ctx):
    lane = lax.broadcasted_iota(jnp.int32, (8, 2 * LANES), 1)
    row = lax.broadcasted_iota(jnp.int32, (8, 2 * LANES), 0)
    pick = jnp.where(lane // HEAD == row + 1, 1.0, 0.0).astype(BF16)
    product = dctx.astype(F32) * ctx.astype(F32)
    high = product.astype(BF16)
    low = (product - high.astype(F32)).astype(BF16)
    return dot(pick, high, 1, 1) + dot(pick, low, 1, 1)


def attend_back_block(sizes, me, g, b, kv, q, bias, lse, dctx, delta, dkv):
    keys = pl.ds(sizes.key_offset(me, b), sizes.keys)
    rows = slice(b * sizes.block, (b + 1) * sizes.block)
    made = []
    for j in range(3):
        kt, kh = KEY_AT[j]
        vt, vh = VALUE_AT[j]
        qt, _ = QUERY_AT[j]
        ct, _ = CONTEXT_AT[j]
        query = q[g, rows, tile(qt)] * half_mask(kh, BF16)
        grad = dctx[g, rows, tile(ct)] * half_mask(vh, BF16)
        s = dot(kv[keys, tile(kt)], query, 1, 1) + bias[b]
        p = jnp.exp(s - lse[g, b, j : j + 1, :])
        dp = dot(kv[keys, tile(vt)], grad, 1, 1)
        ds = (p * (dp - delta[j : j + 1, rows])).astype(BF16)
        dkv[keys, tile(kt)] += dot(ds, query)
        dkv[keys, tile(vt)] += dot(p.astype(BF16), grad)
        back = dot(kv[keys, tile(kt)], ds, 0, 0)
        made.append(back[kh * HEAD : (kh + 1) * HEAD] * HEAD**-0.5)
    made.append(jnp.zeros((HEAD, sizes.block), F32))
    return jnp.concatenate(made, axis=0).T


def attend_back(sizes, me, kv, q, bias, lse, ctx, dctx, delta, dkv, dq):
    @pl.loop(0, sizes.groups)
    def _(g):
        delta[...] = delta_rows(dctx[g], ctx[g])
        dkv[g] = jnp.zeros_like(dkv[g])
        for b in range(sizes.blocks):
            rows = slice(b * sizes.block, (b + 1) * sizes.block)
            dq[g, rows, :] = attend_back_block(
                sizes, me, g, b, kv.at[g], q, bias, lse, dctx, delta, dkv.at[g]
            )


class Loads:
    def __init__(self, weights, w, sems):
        self.copies = [pltpu.make_async_copy(weights.at[s], w.at[s], sems.at[s]) for s in range(3)]

    def begin(self):
        for copy in self.copies:
            copy.start()

    def group(self, i):
        return i

    def near_heads(self):
        self.copies[0].wait()

    def far_heads(self):
        pass

    def ready(self, section):
        self.copies[section].wait()

    def tick(self, step):
        pass

    def end(self):
        pass


MESH = pl.DeviceIdType.MESH


class Route:
    def __init__(self, at, turn):
        flip, x_peer = 1 - turn, 2 * at.z + 1 - at.x
        near = at.mp + turn * (at.across - at.mp)
        far = at.mp + flip * (at.across - at.mp)
        self.first = (at.dp + flip * (x_peer - at.dp), near)
        self.second = (at.dp + turn * (x_peer - at.dp), far)
        self.first_column = (near, at.x + flip * (1 - 2 * at.x))
        self.second_columns = ((far, at.x + turn * (1 - 2 * at.x)), (at.across, 1 - at.x))


class Place:
    def __init__(self):
        self.dp, self.mp = lax.axis_index("dp"), lax.axis_index("mp")
        self.z, self.x, self.y, self.core = self.dp // 2, self.dp % 2, self.mp // 2, self.mp % 2
        flip = 1 - self.core
        self.across = 2 * (1 - self.y) + self.core
        self.sibling = (self.dp, 2 * self.y + flip)
        self.x_peer = (2 * self.z + 1 - self.x, self.mp)
        self.y_peer = (self.dp, self.across)
        self.diagonal = (self.dp, 2 * (1 - self.y) + flip)
        self.zs = [self.z, self.z + 1 - 2 * (self.z % 2), (self.z + 2) % 4, 3 - self.z]
        self.line = [(2 * z + self.x, self.mp) for z in self.zs]
        self.by_core = Route(self, self.core)
        self.x_first, self.y_first = Route(self, 0), Route(self, 1)
        self.own_column = (self.mp, self.x)
        self.peers = [*self.line[1:], self.x_peer, self.y_peer, self.sibling, self.diagonal]


def signal(peers):
    barrier = pltpu.get_barrier_semaphore()
    for peer in peers:
        pl.semaphore_signal(barrier, inc=1, device_id=peer, device_id_type=MESH)


def arrive(peers):
    pl.semaphore_wait(pltpu.get_barrier_semaphore(), len(peers))


GATHER_STEPS = {
    "begin": (("along", 0), ("out", 0), ("out", 1), ("out", 2)),
    "near": (("z", 0, 1, 2, 3), ("along", 1), ("first", 0, 0, 1, 2, 3)),
    0: (("z", 1, 1, 2, 3), ("along", 2)),
    1: (("second", 0, 0, 1, 2, 3),),
    2: (("first", 1, 0, 1), ("second", 0, 4, 5)),
    3: (("first", 1, 2, 3), ("second", 0, 6, 7)),
    4: (("z", 2, 1, 2, 3),),
    5: (("second", 1, 0, 1, 2, 3),),
    6: (("second", 1, 4, 5, 6, 7),),
    7: (("first", 2, 0, 1),),
    8: (("first", 2, 2, 3),),
    9: (("second", 2, 0, 1, 2, 3, 4, 5, 6, 7),),
}


class Gather:
    ROUTES = ("x_first", "by_core", "by_core")
    Z_LATER = (False, False, False)

    def __init__(self, place, packed, own_bias, w, biases, kept, send, recv, local, bias_sems):
        self.at, self.packed, self.w, self.kept = place, packed, w, kept
        self.own_bias, self.biases = own_bias, biases
        self.send_sems, self.recv_sems, self.local, self.bias_sems = send, recv, local, bias_sems
        self.rows = packed[1].shape[0]
        self.shards = w.shape[2] // self.rows
        self.routes = [getattr(place, name) for name in self.ROUTES]

    def shard(self, s, g, d):
        return self.w.at[s, g, pl.ds(pl.multiple_of(d * self.rows, 16), self.rows)]

    def copy(self, s, g, d, slot, peer, source=None):
        here = self.shard(s, g, d)
        return pltpu.make_async_remote_copy(
            src_ref=here if source is None else source,
            dst_ref=here,
            send_sem=self.send_sems.at[s, slot],
            recv_sem=self.recv_sems.at[s, g * self.shards + d],
            device_id=peer,
            device_id_type=MESH,
        )

    def arrived(self, s, g, d):
        self.copy(s, g, d, 0, self.at.sibling).wait_recv()

    def own_copy(self, s):
        return pltpu.make_async_copy(
            self.packed[s], self.shard(s, self.at.mp, self.at.dp), self.local.at[s]
        )

    def along_z(self, s):
        at = self.at
        for k in range(1, 4):
            self.copy(s, at.mp, at.dp, k - 1, at.line[k], self.packed[s]).start()

    def own_out(self, s):
        at = self.at
        self.own_copy(s).start()
        source = self.packed[s]
        self.copy(s, at.mp, at.dp, 3, self.routes[s].first, source).start()
        self.copy(s, at.mp, at.dp, 7, self.routes[s].second, source).start()
        self.copy(s, at.mp, at.dp, 15, at.sibling, source).start()

    def from_z(self, s, k):
        at, (g, x) = self.at, self.at.own_column
        d = 2 * at.zs[k] + x
        self.arrived(s, g, d)
        if not self.Z_LATER[s]:
            self.copy(s, g, d, 3 + k, self.routes[s].first).start()
        self.copy(s, g, d, 7 + k, self.routes[s].second).start()
        self.copy(s, g, d, 15 + k, at.sibling).start()

    def from_first(self, s, k):
        at, (g, x) = self.at, self.routes[s].first_column
        d = 2 * at.zs[k] + x
        self.arrived(s, g, d)
        if self.Z_LATER[s] and k == 0:
            for j in range(1, 4):
                self.copy(s, g, d, 3 + j, at.line[j]).start()
        self.copy(s, g, d, 11 + k, self.routes[s].second).start()
        self.copy(s, g, d, 19 + k, at.sibling).start()

    def from_second(self, s, k):
        at, (g, x) = self.at, self.routes[s].second_columns[k // 4]
        d = 2 * at.zs[k % 4] + x
        self.arrived(s, g, d)
        self.copy(s, g, d, 23 + k, at.sibling).start()

    def group(self, i):
        at = self.at
        return 2 * (at.y + (i // 2) * (1 - 2 * at.y)) + at.core + (i % 2) * (1 - 2 * at.core)

    def from_sibling(self, s, g):
        @pl.loop(0, self.shards)
        def _(d):
            self.arrived(s, g, d)

    def keep(self, s):
        return pltpu.make_async_copy(self.w.at[s], self.kept.at[s], self.local.at[3 + s])

    def bias_copy(self, k, peer):
        return pltpu.make_async_remote_copy(
            src_ref=self.own_bias,
            dst_ref=self.biases.at[self.at.mp],
            send_sem=self.bias_sems.at[0, k],
            recv_sem=self.bias_sems.at[1, k],
            device_id=peer,
            device_id_type=MESH,
        )

    def bias_copies(self):
        at = self.at
        across = (at.dp, at.across)
        return [self.bias_copy(k, peer) for k, peer in enumerate((at.sibling, across, at.diagonal))]

    def begin(self):
        signal(self.at.peers)
        self.fill()
        arrive(self.at.peers)
        self.steps("begin")
        for copy in self.bias_copies():
            copy.start()
        self.biases[self.at.mp] = self.own_bias[...]

    def near_heads(self):
        self.steps("near")
        for copy in self.bias_copies():
            copy.wait_recv()
        self.own_copy(0).wait()
        self.from_sibling(0, self.group(1))

    def far_heads(self):
        self.steps("far")
        self.from_sibling(0, self.group(3))
        self.keep(0).start()

    def ready(self, section):
        if section == 1:
            self.steps(8)
        else:
            self.steps(9)
        self.from_sibling(section, self.group(1))
        self.from_sibling(section, self.group(3))
        self.own_copy(section).wait()
        self.keep(section).start()

    def steps(self, step):
        actions = {
            "along": lambda s, k: self.along_z(s),
            "out": lambda s, k: self.own_out(s),
            "z": self.from_z,
            "first": self.from_first,
            "second": self.from_second,
        }
        for name, s, *ks in GATHER_STEPS.get(step, ()):
            for k in ks or (0,):
                actions[name](s, k)

    def tick(self, step):
        for k in range(8):
            pl.when(step == k)(functools.partial(self.steps, k))

    def end(self):
        for copy in self.bias_copies():
            copy.wait_send()
        for s in range(3):

            @pl.loop(0, 31)
            def _(slot):
                self.copy(s, 0, 0, slot, self.at.sibling).wait_send()

            self.keep(s).wait()


def forward_math(
    sizes,
    source,
    lens,
    tokens,
    biases,
    b_out,
    gain_1,
    shift_1,
    b_down,
    gain_2,
    shift_2,
    encoded,
    cls,
    n_1,
    r_1,
    n_2,
    r_2,
    z_out,
    slope_out,
    kv_out,
    q,
    lse,
    ctx,
    x,
    w,
    bias,
    hidden,
    kv,
    z,
    slope,
    sems,
):
    me = lax.axis_index("mp")
    first = pl.multiple_of(sizes.window_start(me), 16)
    load = pltpu.make_async_copy(tokens.at[pl.ds(first, sizes.window)], x, sems.at[0])
    load.start()
    source.begin()
    fill_mask(sizes, me, lens, bias)
    load.wait()
    save_kv = pltpu.make_async_copy(kv, kv_out, sems.at[1])
    half = sizes.groups // 2
    for span, ready in (((0, half), source.near_heads), ((half, sizes.groups), source.far_heads)):
        ready()
        project(sizes, me, source.group, span, x, w.at[0], biases, kv, q)
        if span[1] == sizes.groups:
            save_kv.start()
        attend(sizes, me, source.group, span, source.tick, kv, q, bias, lse, ctx)

    own = pl.ds(sizes.own_offset(me), sizes.own)
    hidden[...] = x[own, :].astype(F32) + as_row(b_out)
    for g in range(sizes.groups):
        hidden[...] += dot(ctx[g], w[0, g, :, tile(4, 2)], 1, 1)
    normed, factor = norm_stats(hidden[...])
    n_1[...] = normed
    r_1[...] = factor
    y_1 = normed * as_row(gain_1) + as_row(shift_1)
    hidden[...] = y_1 + as_row(b_down)
    encoded[...] = y_1.astype(BF16)
    source.ready(1)

    @pl.loop(0, sizes.groups)
    def _(g):
        a = dot(encoded[...], w[1, g]) + biases[g, :, 5 * LANES :]
        out, grad = gelu_and_slope(a)
        z[g] = out.astype(BF16)
        slope[g] = grad.astype(BF16)

    save_z = pltpu.make_async_copy(z, z_out, sems.at[2])
    save_slope = pltpu.make_async_copy(slope, slope_out, sems.at[3])
    save_z.start()
    save_slope.start()
    source.ready(2)

    @pl.loop(0, sizes.groups)
    def _(g):
        hidden[...] += dot(z[g], w[2, g], 1, 1)

    normed, factor = norm_stats(hidden[...])
    n_2[...] = normed
    r_2[...] = factor
    y_2 = (normed * as_row(gain_2) + as_row(shift_2)).astype(BF16)
    encoded[...] = y_2
    cls[...] = dot(start_rows(sizes, me, lens).astype(BF16), y_2)
    source.end()
    save_kv.wait()
    save_z.wait()
    save_slope.wait()


def forward_kernel(sizes, lens, tokens, weights, biases, *rest):
    *refs, w, bias, hidden, kv, z, slope, sems, loads = rest
    source = Loads(weights, w, loads)
    forward_math(sizes, source, lens, tokens, biases, *refs, w, bias, hidden, kv, z, slope, sems)


def pack(w_key, w_value, w_query, w_out, w_down, b_value, b_query, b_up, packed, own_bias):
    cols = w_key.shape[1]
    for k, weight in enumerate((w_key, w_value, w_query)):
        packed[0, :, k * cols : (k + 1) * cols] = weight[...]
    packed[0, :, 3 * cols :] = w_out[...].astype(F32).T.astype(BF16)
    packed[1] = w_down[...]
    own_bias[...] = jnp.zeros_like(own_bias)
    own_bias[:, cols : 2 * cols] = as_row(b_value)
    own_bias[:, 2 * cols : 3 * cols] = as_row(b_query)
    own_bias[:, 5 * LANES :] = as_row(b_up)


def gathering_kernel(sizes, lens, tokens, *rest):
    shards, rows, (kept, *outs) = rest[:9], rest[9:15], rest[15:]
    *refs, w, bias, hidden, kv, z, slope, sems, packed, own_bias, biases, send, recv, local, bias_sems = outs
    w_key, w_value, w_query, w_out, w_up, w_down, b_value, b_query, b_up = shards

    def fill():
        pack(w_key, w_value, w_query, w_out, w_down, b_value, b_query, b_up, packed, own_bias)

    source = Gather(
        Place(), (packed.at[0], w_up, packed.at[1]), own_bias, w, biases, kept, send, recv, local, bias_sems
    )
    source.fill = fill
    forward_math(
        sizes, source, lens, tokens, biases, *rows, *refs, w, bias, hidden, kv, z, slope, sems
    )


def backward_kernel(
    sizes,
    lens,
    cotangent,
    dcls,
    weights,
    gain_1,
    shift_1,
    gain_2,
    n_1,
    r_1,
    n_2,
    r_2,
    z,
    slope,
    kv,
    q,
    lse,
    ctx,
    dh_1,
    dkv,
    dq,
    grads,
    grads_out,
    small,
    w_attn,
    w_up,
    w_down,
    cot,
    dh,
    low,
    other,
    turned,
    stage,
    dctx,
    delta,
    bias,
    sems,
    out_sems,
):
    me = lax.axis_index("mp")
    load_cot = pltpu.make_async_copy(
        cotangent.at[pl.ds(pl.multiple_of(sizes.own * me, 16), sizes.own)], cot, sems.at[3]
    )
    load_cot.start()
    loads = []
    for s, buffer in ((2, w_down), (1, w_up), (0, w_attn)):
        loads.append(pltpu.make_async_copy(weights.at[s], buffer, sems.at[s]))
        loads[-1].start()
    fill_mask(sizes, me, lens, bias)
    picked = start_rows(sizes, me, lens).astype(BF16)
    high = dcls[...].astype(BF16)
    low_part = (dcls[...] - high.astype(F32)).astype(BF16)
    load_cot.wait()
    dy = cot[...].astype(F32) + dot(picked, high, 0, 0) + dot(picked, low_part, 0, 0)
    small[0:1, :] = jnp.sum(dy * n_2[...], axis=0, keepdims=True)
    small[1:2, :] = jnp.sum(dy, axis=0, keepdims=True)
    grad = norm_back(dy, n_2[...], r_2[...], as_row(gain_2))
    small[2:3, :] = jnp.sum(grad, axis=0, keepdims=True)
    dh[...] = grad
    low[...] = grad.astype(BF16)
    turned[0] = grad.T.astype(BF16)
    y_1 = n_1[...] * as_row(gain_1) + as_row(shift_1)
    other[...] = y_1.astype(BF16)
    turned[1] = y_1.T.astype(BF16)
    for load in loads:
        load.wait()

    def out_copy(section, g, slot):
        return pltpu.make_async_copy(
            stage.at[slot], grads.at[section, g], out_sems.at[slot]
        )

    @pl.loop(0, sizes.groups)
    def _(g):
        @pl.when(g > 0)
        def _():
            out_copy(1, 0, 0).wait()
            out_copy(1, 0, 1).wait()

        stage[1] = dot(turned[0], z[g]).astype(BF16)
        out_copy(1, g, 1).start()
        da = dot(low[...], w_down[g]) * slope[g].astype(F32)
        small[pl.ds(8 + g, 1), :] = jnp.sum(da, axis=0, keepdims=True)
        da_low = da.astype(BF16)
        stage[0] = dot(turned[1], da_low).astype(BF16)
        out_copy(0, g, 0).start()
        dh[...] += dot(da_low, w_up[g], 1, 1)

    dy = dh[...]
    small[3:4, :] = jnp.sum(dy * n_1[...], axis=0, keepdims=True)
    small[4:5, :] = jnp.sum(dy, axis=0, keepdims=True)
    grad = norm_back(dy, n_1[...], r_1[...], as_row(gain_1))
    small[5:6, :] = jnp.sum(grad, axis=0, keepdims=True)
    small[6:8, :] = jnp.zeros_like(small[6:8, :])
    small[12:16, :] = jnp.zeros_like(small[12:16, :])
    dh_1[...] = grad
    low[...] = grad.astype(BF16)
    turned[0] = grad.T.astype(BF16)

    @pl.loop(0, sizes.groups)
    def _(g):
        dctx[g] = dot(low[...], w_attn[g, :, tile(4, 2)]).astype(BF16)
        grads_out[g] = dot(turned[0], ctx[g])

    attend_back(sizes, me, kv, q, bias, lse, ctx, dctx, delta, dkv, dq)
    out_copy(1, 0, 0).wait()
    out_copy(1, 0, 1).wait()


def remote(source, target, send, recv, peer):
    return pltpu.make_async_remote_copy(
        src_ref=source,
        dst_ref=target,
        send_sem=send,
        recv_sem=recv,
        device_id=peer,
        device_id_type=MESH,
    )


def square(parts, index):
    side = parts.shape[1]
    return parts.at[pl.ds(pl.multiple_of(index * side, side), side)]


class Spread:
    def __init__(self, place, source, whole, send, recv, local):
        self.at, self.source, self.whole = place, source, whole
        self.send, self.recv, self.local = send, recv, local
        self.count = source.shape[0]

    def rows(self, mp):
        return self.whole.at[pl.ds(pl.multiple_of(mp * self.count, 16), self.count)]

    def copy(self, k):
        at = self.at
        target = self.rows(at.across if k == 2 else at.mp)
        source = target if k == 2 else self.source
        peer = (at.dp, at.across) if k == 1 else at.sibling
        return remote(source, target, self.send.at[k], self.recv.at[k], peer)

    def own(self):
        return pltpu.make_async_copy(self.source, self.rows(self.at.mp), self.local)

    def begin(self):
        self.copy(1).start()
        self.copy(0).start()
        self.own().start()

    def forward(self):
        self.copy(1).wait_recv()
        self.copy(2).start()

    def end(self):
        self.copy(0).wait()
        self.copy(1).wait_send()
        self.copy(2).wait()
        self.own().wait()


DURING = {
    0: (("encoded", 0),),
    1: (("second", 2),),
    5: (("first", 2),),
}
BEFORE_LAST = (("second", 1),)
AFTER_LAST = (
    ("begin", 0),
    ("chip", 0),
    ("line", 2),
    ("first", 1),
    ("tokens", 0),
    ("second", 0),
    ("small", 0),
    ("line", 1),
    ("small", 1),
    ("first", 0),
    ("small", 2),
    ("relay", 0),
    ("line", 0),
)


class Scatter:
    STAGE = (0, 2, 0)
    HELD = (8, 6, 4)
    ROUTES = ("by_core", "by_core", "by_core")
    Z_EARLY = ((1,), (1,), (1,))

    def __init__(self, place, parts, inbox, by_second, by_first, by_line, shards, sems):
        self.at, self.parts, self.inbox, self.shards = place, parts, inbox, shards
        self.by_second, self.by_first, self.by_line = by_second, by_first, by_line
        self.core_sems, self.second_sems, self.first_sems, self.line_sems = sems
        self.rows = shards.shape[1]
        self.routes = [getattr(place, name) for name in self.ROUTES]

    def shard(self, s, g, d):
        first = (self.HELD[s] + g // 2) * self.parts.shape[1] + d * self.rows
        return self.parts.at[pl.ds(pl.multiple_of(first, 16), self.rows)]

    def part(self, index):
        return square(self.parts, index)

    def to_sibling(self, s, k):
        at = self.STAGE[s] + k
        return remote(
            self.part(at),
            self.inbox.at[at],
            self.core_sems.at[0, s, k],
            self.core_sems.at[1, s, k],
            self.at.sibling,
        )

    def to_second(self, s, k):
        g, x = self.routes[s].second_columns[1 - k // 4]
        return remote(
            self.shard(s, g, 2 * (k % 4) + x),
            self.by_second.at[s, k],
            self.second_sems.at[0, s, k],
            self.second_sems.at[1, s, k],
            self.routes[s].second,
        )

    def to_first(self, s, k):
        g, x = self.routes[s].first_column
        return remote(
            self.shard(s, g, 2 * k + x),
            self.by_first.at[s, k],
            self.first_sems.at[0, s, k],
            self.first_sems.at[1, s, k],
            self.routes[s].first,
        )

    def to_line(self, s, j):
        at = self.at
        return remote(
            self.shard(s, at.mp, 2 * at.zs[j] + at.x),
            self.by_line.at[s, j - 1],
            self.line_sems.at[0, s, j - 1],
            self.line_sems.at[1, s, j - 1],
            at.line[j],
        )

    def chip_sum(self, s):
        for k in range(2):
            self.to_sibling(s, k).wait_recv()
            held, more = self.part(self.HELD[s] + k), self.inbox.at[self.STAGE[s] + k]

            @pl.loop(0, held.shape[0] // self.rows)
            def _(d):
                rows = pl.ds(pl.multiple_of(d * self.rows, 16), self.rows)
                held[rows, :] = (held[rows, :].astype(F32) + more[rows, :].astype(F32)).astype(BF16)

        for k in range(8):
            self.to_second(s, k).start()

    def other_line(self, s, j):
        g, x = self.routes[s].first_column
        return remote(
            self.shard(s, g, 2 * self.at.zs[j] + x),
            self.by_first.at[s, j],
            self.first_sems.at[0, s, j],
            self.first_sems.at[1, s, j],
            self.at.line[j],
        )

    def last_cross(self, s):
        g, x = self.routes[s].first_column
        return remote(
            self.shard(s, g, 2 * self.at.z + x),
            self.by_first.at[s, 0],
            self.first_sems.at[0, s, 0],
            self.first_sems.at[1, s, 0],
            self.routes[s].first,
        )

    def by_kind(self, s, early, late):
        cores = self.Z_EARLY[s]
        if len(cores) == 1:
            pl.when(self.at.core == cores[0])(functools.partial(early, s))
            pl.when(self.at.core != cores[0])(functools.partial(late, s))
        else:
            (early if cores else late)(s)

    def from_second(self, s):
        self.by_kind(s, self.from_second_early, self.from_second_late)

    def from_first(self, s):
        self.by_kind(s, self.from_first_early, self.from_first_late)

    def from_line(self, s):
        self.by_kind(s, self.from_line_early, self.from_line_late)

    def from_second_early(self, s):
        at, (g, x) = self.at, self.routes[s].first_column
        for k in range(8):
            self.to_second(s, k).wait_recv()
        for j in (3, 2, 1, 0):
            z = at.zs[j]
            mine = self.shard(s, g, 2 * z + x)
            mine[...] = (mine[...].astype(F32) + self.by_second[s, z].astype(F32)).astype(BF16)
            if j:
                self.other_line(s, j).start()
        for j in (3, 2, 1):
            z = at.zs[j]
            mine = self.shard(s, at.mp, 2 * z + at.x)
            mine[...] = (mine[...].astype(F32) + self.by_second[s, 4 + z].astype(F32)).astype(BF16)
            self.to_line(s, j).start()

    def from_first_early(self, s):
        g, x = self.routes[s].first_column
        mine = self.shard(s, g, 2 * self.at.z + x)
        total = mine[...].astype(F32)
        for j in (1, 2, 3):
            self.other_line(s, j).wait_recv()
            total = total + self.by_first[s, j].astype(F32)
        mine[...] = total.astype(BF16)
        self.last_cross(s).start()

    def from_line_early(self, s):
        at = self.at
        mine = self.shard(s, at.mp, 2 * at.z + at.x)
        total = mine[...].astype(F32) + self.by_second[s, 4 + at.z].astype(F32)
        for j in range(1, 4):
            self.to_line(s, j).wait_recv()
            total = total + self.by_line[s, j - 1].astype(F32)
        self.last_cross(s).wait_recv()
        self.shards[s] = total + self.by_first[s, 0].astype(F32)

    def from_second_late(self, s):
        g, x = self.routes[s].first_column
        for k in range(4):
            self.to_second(s, k).wait_recv()
            mine = self.shard(s, g, 2 * k + x)
            mine[...] = (mine[...].astype(F32) + self.by_second[s, k].astype(F32)).astype(BF16)
            self.to_first(s, k).start()

    def from_first_late(self, s):
        at = self.at
        for k in range(4):
            self.to_second(s, 4 + k).wait_recv()
            self.to_first(s, k).wait_recv()
        for j in (3, 2, 1, 0):
            z = at.zs[j]
            mine = self.shard(s, at.mp, 2 * z + at.x)
            total = (
                mine[...].astype(F32)
                + self.by_second[s, 4 + z].astype(F32)
                + self.by_first[s, z].astype(F32)
            )
            if j:
                mine[...] = total.astype(BF16)
                self.to_line(s, j).start()
            else:
                self.shards[s] = total

    def from_line_late(self, s):
        for j in range(1, 4):
            self.to_line(s, j).wait_recv()
            self.shards[s] += self.by_line[s, j - 1].astype(F32)

    def sent_to_sibling(self, s):
        for k in range(2):
            self.to_sibling(s, k).wait_send()

    def end(self):
        for s in range(3):
            for k in range(8):
                self.to_second(s, k).wait_send()
            for k in range(4):
                self.to_first(s, k).wait_send()
            for j in range(1, 4):
                self.to_line(s, j).wait_send()


class SmallSums:
    def __init__(self, place, sums, inbox, sems):
        self.at, self.sums, self.inbox, self.sems = place, sums, inbox, sems
        at = place
        self.peers = [at.sibling, at.x_peer, at.y_peer, *at.line[1:]]

    def copy(self, k):
        return remote(
            self.sums.at[min(k, 3)],
            self.inbox.at[k],
            self.sems.at[0, k],
            self.sems.at[1, k],
            self.peers[k],
        )

    def begin(self):
        self.copy(0).start()

    def step(self, k):
        self.copy(k).wait_recv()
        self.sums[k + 1] = self.sums[k] + self.inbox[k]
        for nxt in (k + 1,) if k < 2 else (3, 4, 5):
            self.copy(nxt).start()

    def end(self, out):
        for k in range(3, 6):
            self.copy(k).wait_recv()
        out[...] = (self.sums[3] + self.inbox[3]) + (self.inbox[4] + self.inbox[5])
        for k in range(6):
            self.copy(k).wait_send()


def fold(rows):
    half = rows.shape[1] // 2
    return jnp.concatenate([rows[:, :half], rows[:, half:]], axis=0).astype(BF16)


def unfold(packed):
    wide = packed.astype(F32)
    return jnp.concatenate([wide[:8], wide[8:]], axis=1)


class Scoring:
    def __init__(self, place, ways, cls, gold, passages, scores, lse, buffers, sems):
        self.at, self.ways, self.cls, self.gold = place, ways, cls, gold
        self.passages, self.scores, self.lse = passages, scores, lse
        self.part, self.parts, self.firsts, self.rows = buffers[:4]
        self.sent, self.got, self.stats, self.got_stats = buffers[4:]
        self.mp_sems, self.sems = sems
        at = place
        self.mates = (at.sibling, (at.dp, at.across), at.diagonal)
        self.others = [(lax.rem(at.dp + k, ways), at.mp) for k in range(1, ways)]

    def mate(self, k):
        return remote(
            self.part, self.parts.at[k], self.mp_sems.at[0, k], self.mp_sems.at[1, k], self.mates[k]
        )

    def first_copy(self, k):
        mine = self.firsts.at[self.at.dp]
        return remote(
            mine, mine, self.sems.at[0, 0, k - 1], self.sems.at[0, 1, k - 1], self.others[k - 1]
        )

    def back_copy(self, which, k):
        peer = self.others[k - 1]
        return remote(
            self.sent.at[which, peer[0]],
            self.got.at[which, self.at.dp],
            self.sems.at[1 + which, 0, k - 1],
            self.sems.at[1 + which, 1, k - 1],
            peer,
        )

    def stat_copy(self, k):
        peer = self.others[k - 1]
        return remote(
            self.stats.at[peer[0]],
            self.got_stats.at[self.at.dp],
            self.sems.at[3, 0, k - 1],
            self.sems.at[3, 1, k - 1],
            peer,
        )

    def start_cls(self):
        self.part[...] = fold(self.cls[...])
        for k in range(3):
            self.mate(k).start()

    def start_gold(self):
        places = self.at.dp * self.passages.shape[0] + lax.broadcasted_iota(
            jnp.int32, (self.passages.shape[0], self.gold.shape[0]), 0
        )
        target = jnp.where(as_row(self.gold) == places, 1.0, 0.0).astype(BF16)
        self.put(0, dot(target, self.passages[...], 0, 0))
        for k in range(1, self.ways):
            self.back_copy(0, k).start()

    def put(self, which, rows):
        for d in range(self.ways):
            self.sent[which, d] = fold(rows[8 * d : 8 * d + 8])
        self.got[which, self.at.dp] = self.sent[which, self.at.dp]

    def start_firsts(self):
        total = self.part[...].astype(F32)
        for k in range(3):
            self.mate(k).wait_recv()
            total = total + self.parts[k].astype(F32)
        self.firsts[self.at.dp] = total.astype(BF16)
        for k in range(1, self.ways):
            self.first_copy(k).start()

    def start_back(self):
        for k in range(1, self.ways):
            self.first_copy(k).wait_recv()
        for d in range(self.ways):
            self.rows[8 * d : 8 * d + 8, :] = unfold(self.firsts[d])
        table = dot(self.rows[...].astype(BF16), self.passages[...], 1, 1)
        self.scores[...] = table
        peak = jnp.max(table, axis=1, keepdims=True)
        e = jnp.exp(table - peak)
        total = jnp.sum(e, axis=1, keepdims=True)
        lane = lax.broadcasted_iota(jnp.int32, (8, LANES), 1)
        for d in range(self.ways):
            rows = slice(8 * d, 8 * d + 8)
            self.stats[d] = jnp.where(lane == 0, peak[rows], total[rows])
        self.got_stats[self.at.dp] = self.stats[self.at.dp]
        for k in range(1, self.ways):
            self.stat_copy(k).start()
        self.put(1, dot(e.astype(BF16), self.passages[...]))
        for k in range(1, self.ways):
            self.back_copy(1, k).start()

    def result(self):
        for k in range(1, self.ways):
            self.back_copy(0, k).wait_recv()
            self.stat_copy(k).wait_recv()
        peaks = [self.got_stats[d][:, 0:1] for d in range(self.ways)]
        top = functools.reduce(jnp.maximum, peaks)
        scales = [jnp.exp(peak - top) for peak in peaks]
        total = sum(scale * self.got_stats[d][:, 1:2] for d, scale in enumerate(scales))
        self.lse[...] = top + jnp.log(total)
        for k in range(1, self.ways):
            self.back_copy(1, k).wait_recv()
        grad = -sum(unfold(self.got[0, d]) for d in range(self.ways))
        for d in range(self.ways):
            grad = grad + (scales[d] / total) * unfold(self.got[1, d])
        return grad

    def end(self):
        for k in range(3):
            self.mate(k).wait_send()
        for k in range(1, self.ways):
            self.first_copy(k).wait_send()
            self.back_copy(0, k).wait_send()
            self.back_copy(1, k).wait_send()
            self.stat_copy(k).wait_send()


class Halo:
    def __init__(self, sizes, place, dkv, sent, got, sems):
        self.sizes, self.at, self.dkv, self.sent, self.got, self.sems = sizes, place, dkv, sent, got, sems
        self.has = (place.mp > 0, place.mp < sizes.groups - 1)
        offset = sizes.own_offset(place.mp)
        self.starts = (offset - LONGEST, offset + sizes.own)
        self.into = (sizes.own - LONGEST, 0)

    def copy(self, g, side):
        slot = g % 2
        return remote(
            self.sent.at[slot, side],
            self.got.at[g, side],
            self.sems.at[0, slot, side],
            self.sems.at[1, g, side],
            (self.at.dp, self.at.mp + 2 * side - 1),
        )

    def start(self, g):
        for side in range(2):

            @pl.when(self.has[side])
            def _():
                pl.when(g > 1)(self.copy(g, side).wait_send)
                rows = pl.ds(pl.multiple_of(self.starts[side], 16), LONGEST)
                self.sent[g % 2, side] = self.dkv[rows, :].astype(BF16)
                self.copy(g, side).start()

    def add(self, g, own):
        for side in range(2):

            @pl.when(self.has[1 - side])
            def _():
                self.copy(g, side).wait_recv()
                rows = pl.ds(self.into[side], LONGEST)
                own[rows, :] += self.got[g, side].astype(F32)

    def end(self):
        for side in range(2):

            @pl.when(self.has[side])
            def _():
                self.copy(2, side).wait_send()
                self.copy(3, side).wait_send()


def finish_kernel(
    sizes,
    lens,
    cls,
    gold,
    gain_1,
    shift_1,
    gain_2,
    r_1,
    r_2,
    lse,
    tokens,
    cotangent,
    passages,
    encoded,
    weights,
    n_1_in,
    n_2_in,
    z_in,
    slope_in,
    kv_in,
    q_in,
    ctx_in,
    scores,
    query_lse,
    small_out,
    shards,
    encoded_whole,
    token_whole,
    w,
    ffn,
    parts,
    inbox,
    by_second,
    by_first,
    by_line,
    kv,
    q,
    ctx,
    dctx,
    dkv,
    own_kv,
    halo_sent,
    halo_got,
    n_1,
    work,
    rows_low,
    row_in,
    turned,
    low,
    bias,
    delta,
    sums,
    sums_in,
    part,
    parts_in,
    firsts,
    first_rows,
    back_sent,
    back_got,
    stats,
    stats_got,
    load_sems,
    kv_sems,
    ffn_sems,
    spread_sems,
    core_sems,
    second_sems,
    first_sems,
    line_sems,
    halo_sems,
    small_sems,
    mp_sems,
    score_sems,
):
    at = Place()
    me = at.mp
    own_rows = pl.ds(pl.multiple_of(sizes.own * me, 16), sizes.own)
    ways = firsts.shape[0]
    table = parts.at[pl.ds(Scatter.HELD[0] * sizes.width, passages.shape[0])]
    scatter = Scatter(
        at, parts, inbox, by_second, by_first, by_line, shards,
        (core_sems, second_sems, first_sems, line_sems),
    )
    halo = Halo(sizes, at, dkv, halo_sent, halo_got, halo_sems)
    spread = Spread(at, encoded, encoded_whole, spread_sems.at[0, 0], spread_sems.at[0, 1], load_sems.at[8])
    token_spread = Spread(
        at, rows_low, token_whole, spread_sems.at[1, 0], spread_sems.at[1, 1], load_sems.at[9]
    )
    small = SmallSums(at, sums, sums_in, small_sems)

    def load(k, source, target):
        return pltpu.make_async_copy(source, target, load_sems.at[k])

    loads = [
        load(0, passages, table),
        load(1, cotangent.at[own_rows], row_in),
        load(2, n_2_in, work.at[1]),
        load(3, n_1_in, n_1),
        load(5, q_in, q),
        load(6, ctx_in, ctx),
    ]

    def kv_load(g):
        return pltpu.make_async_copy(kv_in.at[g], kv.at[g % 2], kv_sems.at[g % 2])

    for copy in loads:
        copy.start()
    kv_load(0).start()

    scoring = Scoring(
        at,
        ways,
        cls,
        gold,
        table,
        scores,
        query_lse,
        (part, parts_in, firsts, first_rows, back_sent, back_got, stats, stats_got),
        (mp_sems, score_sems),
    )
    signal([*scoring.mates, *scoring.others])

    def group_of(i):
        return jnp.where(i < 2, 1 - at.core + 2 * i, at.core + 2 * (i - 2))

    def z_load(i):
        return pltpu.make_async_copy(z_in.at[group_of(i)], ffn.at[0, i % 2], ffn_sems.at[i % 2, 0])

    def ffn_loads(i):
        slot, g = i % 2, group_of(i)
        return [
            pltpu.make_async_copy(weights.at[2, g], w.at[2 * slot], ffn_sems.at[slot, 1]),
            pltpu.make_async_copy(weights.at[1, g], w.at[2 * slot + 1], ffn_sems.at[slot, 2]),
            pltpu.make_async_copy(slope_in.at[g], ffn.at[1, slot], ffn_sems.at[slot, 3]),
        ]

    z_load(0).start()
    for copy in ffn_loads(0):
        copy.start()

    arrive([*scoring.mates, *scoring.others])
    scoring.start_cls()
    loads[0].wait()
    scoring.start_gold()
    scoring.start_firsts()
    spread.begin()
    fill_mask(sizes, me, lens, bias)
    picked = start_rows(sizes, me, lens).astype(BF16)
    loads[3].wait()
    turned[1] = (n_1[...] * as_row(gain_1) + as_row(shift_1)).T.astype(BF16)
    scoring.start_back()
    loads[1].wait()
    loads[2].wait()
    dcls = scoring.result()
    high = dcls.astype(BF16)
    rest = (dcls - high.astype(F32)).astype(BF16)
    dy = row_in[...].astype(F32) + dot(picked, high, 0, 0) + dot(picked, rest, 0, 0)
    mine = sums.at[0]
    mine[0:1, :] = jnp.sum(dy * work[1], axis=0, keepdims=True)
    mine[1:2, :] = jnp.sum(dy, axis=0, keepdims=True)
    grad = norm_back(dy, work[1], r_2[...], as_row(gain_2))
    mine[2:3, :] = jnp.sum(grad, axis=0, keepdims=True)
    work[0] = grad
    rows_low[...] = grad.astype(BF16)
    turned[0] = grad.T.astype(BF16)

    def into(s, i):
        return jnp.where(i < 2, Scatter.STAGE[s] + i, Scatter.HELD[s] + i - 2)

    @pl.loop(0, sizes.groups)
    def _(i):
        z_load(i).wait()

        @pl.when(i < 3)
        def _():
            z_load(i + 1).start()

        square(parts, into(2, i))[...] = dot(turned[0], ffn[0, i % 2]).astype(BF16)
        pl.when(i < 2)(lambda: scatter.to_sibling(2, i).start())

    scatter.chip_sum(2)

    @pl.loop(0, sizes.groups)
    def _(i):
        slot, g = i % 2, group_of(i)
        for copy in ffn_loads(i):
            copy.wait()

        @pl.when(i < 3)
        def _():
            for copy in ffn_loads(i + 1):
                copy.start()

        da = dot(rows_low[...], w[2 * slot]) * ffn[1, slot].astype(F32)
        mine[pl.ds(8 + g, 1), :] = jnp.sum(da, axis=0, keepdims=True)
        da_low = da.astype(BF16)
        square(parts, into(1, i))[...] = dot(turned[1], da_low).astype(BF16)
        pl.when(i < 2)(lambda: scatter.to_sibling(1, i).start())
        work[0] += dot(da_low, w[2 * slot + 1], 1, 1)

    load_w = pltpu.make_async_copy(weights.at[0], w, load_sems.at[7])
    load_w.start()
    load_x = load(1, tokens.at[own_rows], row_in)
    load_x.start()
    scatter.chip_sum(1)
    scatter.sent_to_sibling(2)

    dy = work[0]
    mine[3:4, :] = jnp.sum(dy * n_1[...], axis=0, keepdims=True)
    mine[4:5, :] = jnp.sum(dy, axis=0, keepdims=True)
    grad = norm_back(dy, n_1[...], r_1[...], as_row(gain_1))
    mine[5:6, :] = jnp.sum(grad, axis=0, keepdims=True)
    mine[6:8, :] = jnp.zeros((2, sizes.width), F32)
    mine[12:24, :] = jnp.zeros((12, sizes.width), F32)
    work[1] = grad
    rows_low[...] = grad.astype(BF16)
    turned[0] = grad.T.astype(BF16)
    load_x.wait()
    turned[1] = row_in[...].astype(F32).T.astype(BF16)
    load_w.wait()
    for copy in loads[4:]:
        copy.wait()

    @pl.loop(0, sizes.groups)
    def _(g):
        dctx[g] = dot(rows_low[...], w[g, :, tile(4, 2)]).astype(BF16)

    actions = {
        "second": scatter.from_second,
        "first": scatter.from_first,
        "line": scatter.from_line,
        "chip": scatter.chip_sum,
        "small": small.step,
        "begin": lambda s: small.begin(),
        "tokens": lambda s: token_spread.begin(),
        "relay": lambda s: token_spread.forward(),
        "encoded": lambda s: spread.forward(),
    }

    def run(names):
        for name, s in names:
            actions[name](s)

    def tick(now):
        for k, names in DURING.items():
            pl.when(now == k)(functools.partial(run, names))

    def finalize(g):
        slot = g % 2
        halo.add(g, own_kv.at[slot])
        dkv_own = own_kv[slot]
        mine[pl.ds(16 + g, 1), tile(0, 3)] = jnp.sum(dkv_own, axis=0, keepdims=True)
        low[slot, :, tile(0, 3)] = dkv_own.astype(BF16)
        work[1] += dot(low[slot], w[g, :, tile(0, 5)], 1, 1)
        into = jnp.where(g % 2 == at.core, Scatter.HELD[0], Scatter.STAGE[0]) + g // 2
        made = dot(turned[1], low[slot])
        more = dot(turned[0], ctx[g])
        target = square(parts, into)
        target[:, tile(0, 4)] = made[:, tile(0, 4)].astype(BF16)
        target[:, tile(4)] = (made[:, tile(4)] + more[:, tile(0)]).astype(BF16)
        target[:, tile(5)] = more[:, tile(1)].astype(BF16)

        @pl.when(g % 2 != at.core)
        def _():
            scatter.to_sibling(0, g // 2).start()

    own = pl.ds(sizes.own_offset(me), sizes.own)

    @pl.loop(0, sizes.groups)
    def _(g):
        slot = g % 2
        kv_load(g).wait()

        @pl.when(g < sizes.groups - 1)
        def _():
            kv_load(g + 1).start()

        delta[...] = delta_rows(dctx[g], ctx[g])
        dkv[...] = jnp.zeros_like(dkv)
        for b in range(sizes.blocks):
            tick(g * sizes.blocks + b)
            rows = slice(b * sizes.block, (b + 1) * sizes.block)
            dq = attend_back_block(
                sizes, me, g, b, kv.at[slot], q, bias, lse, dctx, delta, dkv
            )
            total = jnp.sum(dq, axis=0, keepdims=True)
            mine[pl.ds(16 + g, 1), tile(3, 2)] += total
            low[slot, rows, tile(3, 2)] = dq.astype(BF16)
        halo.start(g)
        own_kv[slot] = dkv[own, :]

        @pl.when(g > 0)
        def _():
            finalize(g - 1)

    run(BEFORE_LAST)
    finalize(sizes.groups - 1)
    rows_low[...] = work[1].astype(BF16)
    run(AFTER_LAST)
    small.end(small_out)
    scatter.sent_to_sibling(1)
    scatter.sent_to_sibling(0)
    scatter.end()
    halo.end()
    scoring.end()
    spread.end()
    token_spread.end()


def input_kernel(sizes, tokens, weights, dkv, dq, dh_1, grads_out, token_grad, grads, small, turned, low):
    turned[...] = tokens[...].astype(F32).T.astype(BF16)
    total = dh_1[...]
    for g in range(sizes.groups):
        small[g, :, tile(0, 3)] = jnp.sum(dkv[g], axis=0, keepdims=True)
        small[g, :, tile(3, 2)] = jnp.sum(dq[g], axis=0, keepdims=True)
        low[:, tile(0, 3)] = dkv[g].astype(BF16)
        low[:, tile(3, 2)] = dq[g].astype(BF16)
        total = total + dot(low[...], weights[g, :, tile(0, 5)], 1, 1)
        made = dot(turned[...], low[...])
        grads[g, :, tile(0, 4)] = made[:, tile(0, 4)].astype(BF16)
        grads[g, :, tile(4)] = (made[:, tile(4)] + grads_out[g, :, tile(0)]).astype(BF16)
        grads[g, :, tile(5)] = grads_out[g, :, tile(1)].astype(BF16)
    token_grad[...] = total.astype(BF16)


def specs(*spaces):
    return [pl.BlockSpec(memory_space=s) for s in spaces]


def params(**more):
    return pltpu.CompilerParams(vmem_limit_bytes=63 * 2**20, **more)


def run_forward(sizes, lengths, tokens, weights, rows, gathers):
    own, width, groups = sizes.own, sizes.width, sizes.groups
    docs = lengths.shape[1]
    shape = jax.ShapeDtypeStruct
    outs = [
        shape((own, width), BF16),
        shape((docs, width), F32),
        shape((own, width), F32),
        shape((own, 1), F32),
        shape((own, width), F32),
        shape((own, 1), F32),
        shape((groups, own, width), BF16),
        shape((groups, own, width), BF16),
        shape((groups, sizes.window, 3 * LANES), BF16),
        shape((groups, own, 2 * LANES), BF16),
        shape((groups, sizes.blocks, 8, sizes.block), F32),
        shape((groups, own, 2 * LANES), BF16),
    ]
    spaces = [*[VMEM] * 6, ANY, ANY, ANY, *[VMEM] * 3]
    scratch = [
        pltpu.VMEM((sizes.window, width), BF16),
        pltpu.VMEM((3, groups, width, width), BF16),
        pltpu.VMEM((sizes.blocks, sizes.keys, sizes.block), F32),
        pltpu.VMEM((own, width), F32),
        pltpu.VMEM((groups, sizes.window, 3 * LANES), BF16),
        pltpu.VMEM((groups, own, width), BF16),
        pltpu.VMEM((groups, own, width), BF16),
        pltpu.SemaphoreType.DMA((4,)),
    ]
    if gathers:
        outs.insert(0, shape((3, groups, width, width), BF16))
        spaces.insert(0, ANY)
        scratch += [
            pltpu.VMEM((2, weights[0].shape[0], width), BF16),
            pltpu.VMEM((1, 5 * LANES + weights[8].shape[0]), F32),
            pltpu.VMEM((groups, 1, 5 * LANES + weights[8].shape[0]), F32),
            pltpu.SemaphoreType.DMA((3, 31)),
            pltpu.SemaphoreType.DMA((3, 32)),
            pltpu.SemaphoreType.DMA((6,)),
            pltpu.SemaphoreType.DMA((2, 3)),
        ]
        kernel, more = gathering_kernel, {"collective_id": 0, "has_side_effects": True}
    else:
        scratch.append(pltpu.SemaphoreType.DMA((3,)))
        kernel, more = forward_kernel, {}
    return pl.pallas_call(
        functools.partial(kernel, sizes),
        out_shape=outs,
        in_specs=specs(SMEM, ANY, *([VMEM] * 15 if gathers else [ANY, *[VMEM] * 7])),
        out_specs=specs(*spaces),
        scratch_shapes=scratch,
        compiler_params=params(**more),
        name="forward",
    )(lengths, tokens, *weights, *rows)


def run_backward(sizes, lengths, cotangent, dcls, weights, gain_1, shift_1, gain_2, saved):
    own, width, groups = sizes.own, sizes.width, sizes.groups
    shape = jax.ShapeDtypeStruct
    outs = (
        shape((own, width), F32),
        shape((groups, sizes.window, 3 * LANES), F32),
        shape((groups, own, 2 * LANES), F32),
        shape((2, groups, width, width), BF16),
        shape((groups, width, 2 * LANES), F32),
        shape((16, width), F32),
    )
    return pl.pallas_call(
        functools.partial(backward_kernel, sizes),
        out_shape=outs,
        in_specs=specs(SMEM, ANY, VMEM, ANY, *[VMEM] * (3 + len(saved))),
        out_specs=specs(VMEM, VMEM, VMEM, ANY, VMEM, VMEM),
        scratch_shapes=[
            pltpu.VMEM((groups, width, width), BF16),
            pltpu.VMEM((groups, width, width), BF16),
            pltpu.VMEM((groups, width, width), BF16),
            pltpu.VMEM((own, width), BF16),
            pltpu.VMEM((own, width), F32),
            pltpu.VMEM((own, width), BF16),
            pltpu.VMEM((own, width), BF16),
            pltpu.VMEM((2, width, own), BF16),
            pltpu.VMEM((2, width, width), BF16),
            pltpu.VMEM((groups, own, 2 * LANES), BF16),
            pltpu.VMEM((8, own), F32),
            pltpu.VMEM((sizes.blocks, sizes.keys, sizes.block), F32),
            pltpu.SemaphoreType.DMA((4,)),
            pltpu.SemaphoreType.DMA((2,)),
        ],
        compiler_params=params(),
        name="backward",
    )(lengths, cotangent, dcls, weights, gain_1, shift_1, gain_2, *saved)


def run_input(sizes, own_tokens, w_attn, dkv, dq, dh_1, grads_out):
    own, width, groups = sizes.own, sizes.width, sizes.groups
    shape = jax.ShapeDtypeStruct
    outs = (
        shape((own, width), BF16),
        shape((groups, width, width), BF16),
        shape((groups, 1, 5 * LANES), F32),
    )
    return pl.pallas_call(
        functools.partial(input_kernel, sizes),
        out_shape=outs,
        in_specs=specs(*[VMEM] * 6),
        out_specs=specs(*[VMEM] * 3),
        scratch_shapes=[pltpu.VMEM((width, own), BF16), pltpu.VMEM((own, 5 * LANES), BF16)],
        compiler_params=params(),
        name="inputs",
    )(own_tokens, w_attn, dkv, dq, dh_1, grads_out)


def run_finish(sizes, small_in, large_in):
    own, width, groups = sizes.own, sizes.width, sizes.groups
    tokens, passages = large_in[0], large_in[2]
    queries = small_in[2].shape[0]
    ways = queries // 8
    shard = width // ways
    shape = jax.ShapeDtypeStruct
    outs = (
        shape((queries, passages.shape[0]), F32),
        shape((8, 1), F32),
        shape((24, width), F32),
        shape((3, shard, width), F32),
        shape(tokens.shape, BF16),
        shape(tokens.shape, BF16),
    )
    dma = pltpu.SemaphoreType.DMA
    scratch = [
        pltpu.VMEM((groups, width, width), BF16),
        pltpu.VMEM((2, 2, own, width), BF16),
        pltpu.VMEM((10 * width, width), BF16),
        pltpu.VMEM((4, width, width), BF16),
        pltpu.VMEM((3, 8, shard, width), BF16),
        pltpu.VMEM((3, 4, shard, width), BF16),
        pltpu.VMEM((3, 3, shard, width), BF16),
        pltpu.VMEM((2, sizes.window, 3 * LANES), BF16),
        pltpu.VMEM((groups, own, 2 * LANES), BF16),
        pltpu.VMEM((groups, own, 2 * LANES), BF16),
        pltpu.VMEM((groups, own, 2 * LANES), BF16),
        pltpu.VMEM((sizes.window, 3 * LANES), F32),
        pltpu.VMEM((2, own, 3 * LANES), F32),
        pltpu.VMEM((2, 2, LONGEST, 3 * LANES), BF16),
        pltpu.VMEM((groups, 2, LONGEST, 3 * LANES), BF16),
        pltpu.VMEM((own, width), F32),
        pltpu.VMEM((2, own, width), F32),
        pltpu.VMEM((own, width), BF16),
        pltpu.VMEM((own, width), BF16),
        pltpu.VMEM((2, width, own), BF16),
        pltpu.VMEM((2, own, 5 * LANES), BF16),
        pltpu.VMEM((sizes.blocks, sizes.keys, sizes.block), F32),
        pltpu.VMEM((8, own), F32),
        pltpu.VMEM((4, 24, width), F32),
        pltpu.VMEM((6, 24, width), F32),
        pltpu.VMEM((16, width // 2), BF16),
        pltpu.VMEM((3, 16, width // 2), BF16),
        pltpu.VMEM((ways, 16, width // 2), BF16),
        pltpu.VMEM((queries, width), F32),
        pltpu.VMEM((2, ways, 16, width // 2), BF16),
        pltpu.VMEM((2, ways, 16, width // 2), BF16),
        pltpu.VMEM((ways, 8, LANES), F32),
        pltpu.VMEM((ways, 8, LANES), F32),
        dma((10,)),
        dma((2,)),
        dma((2, 4)),
        dma((2, 2, 3)),
        dma((2, 3, 2)),
        dma((2, 3, 8)),
        dma((2, 3, 4)),
        dma((2, 3, 3)),
        dma((2, 4, 2)),
        dma((2, 6)),
        dma((2, 3)),
        dma((4, 2, ways - 1)),
    ]
    return pl.pallas_call(
        functools.partial(finish_kernel, sizes),
        out_shape=outs,
        in_specs=specs(SMEM, *[VMEM] * (len(small_in) - 1), *[ANY] * len(large_in)),
        out_specs=specs(*[VMEM] * 4, ANY, ANY),
        scratch_shapes=scratch,
        compiler_params=params(collective_id=1, has_side_effects=True),
        name="finish",
    )(*small_in, *large_in)


def cut_along(array, dim, devices):
    before, after = (array.shape[:dim], array.shape[dim + 1 :])
    return jnp.moveaxis(array.reshape(*before, devices, -1, *after), dim, 0)


def summed_on_arrival(array, axis, dim):
    pieces = cut_along(array, dim, lax.axis_size(axis))
    arrived = lax.all_to_all(pieces, axis, split_axis=0, concat_axis=0, tiled=True)
    return arrived.astype(F32).sum(axis=0)


def score(cls, passages, gold):
    all_first = lax.all_gather(cls, "dp", axis=0, tiled=True)
    table = dot(all_first, passages, 1, 1)
    peak = lax.pmax(jnp.max(table, axis=1), "dp")
    total = lax.psum(jnp.sum(jnp.exp(table - peak[:, None]), axis=1), "dp")
    own = cls.shape[0]
    lse = lax.dynamic_slice_in_dim(peak + jnp.log(total), lax.axis_index("dp") * own, own)
    soft = jnp.exp(table - peak[:, None]) / total[:, None]
    first = lax.axis_index("dp") * table.shape[1]
    columns = first + jnp.arange(table.shape[1], dtype=jnp.int32)
    target = (gold[:, None] == columns[None, :]).astype(F32)
    grad = dot((soft - target).astype(BF16), passages)
    return table, lse, summed_on_arrival(grad.astype(BF16), "dp", 0)


def plain_layer(sizes, tokens, cotangent, lengths, gold, passages, shards, rows):
    me, groups = lax.axis_index("mp"), sizes.groups
    w_key, w_value, w_query, w_out, w_up, w_down, b_value, b_query, b_up = shards
    packed = jnp.stack(
        [jnp.concatenate([w_key, w_value, w_query, w_out.T], axis=1), w_up, w_down]
    )
    c = w_key.shape[1]
    zeros = jnp.zeros((c,), F32)
    own_bias = jnp.concatenate([zeros, b_value, b_query, zeros[:HEAD], b_up])[None]
    whole = lax.all_gather(lax.all_gather(packed, "dp", axis=1, tiled=True), "mp", axis=1)
    biases = lax.all_gather(own_bias, "mp", axis=0)
    encoded, cls, *saved = run_forward(sizes, lengths, tokens, (whole, biases), rows, False)
    cls = lax.psum(cls, "mp").astype(BF16)
    table, lse, dcls = score(cls, passages, gold)
    n_1, r_1, n_2, r_2, z, slope, kv, q, logs, ctx = saved
    dh_1, dkv, dq, grads_ffn, grads_out, small = run_backward(
        sizes, lengths, cotangent, dcls, whole, rows[1], rows[2], rows[4], saved
    )
    halo, own = LONGEST, sizes.own
    offset = own * me - sizes.window_start(me)
    to_left = lax.dynamic_slice_in_dim(dkv, offset - halo, halo, axis=1).astype(BF16)
    to_right = lax.dynamic_slice_in_dim(dkv, offset + own, halo, axis=1).astype(BF16)
    from_right = lax.ppermute(to_left, "mp", [(i, i - 1) for i in range(1, groups)])
    from_left = lax.ppermute(to_right, "mp", [(i, i + 1) for i in range(groups - 1)])
    dkv = lax.dynamic_slice_in_dim(dkv, offset, own, axis=1)
    dkv = dkv.at[:, own - halo :].add(from_right.astype(F32))
    dkv = dkv.at[:, :halo].add(from_left.astype(F32))
    own_tokens = lax.dynamic_slice_in_dim(tokens, own * me, own, axis=0)
    token_part, grads_attn, small_attn = run_input(
        sizes, own_tokens, whole[0], dkv, dq, dh_1, grads_out
    )
    token_grad = lax.all_gather(token_part, "mp", axis=0, tiled=True).astype(F32)
    encoded = lax.all_gather(encoded, "mp", axis=0, tiled=True)
    grads = jnp.stack([grads_attn, grads_ffn[0], grads_ffn[1]])
    grads = summed_on_arrival(grads, "mp", 1)[:, 0].astype(BF16)
    grads = summed_on_arrival(grads, "dp", 1)
    small, small_attn = lax.psum((small, small_attn), ("dp", "mp"))
    mine = lax.dynamic_index_in_dim(small_attn[:, 0], me, 0, keepdims=False)
    up_bias = lax.dynamic_index_in_dim(small, 8 + me, 0, keepdims=False)
    return (
        table,
        lse,
        encoded,
        token_grad,
        grads[0, :, 2 * c : 3 * c],
        grads[0, :, :c],
        grads[0, :, c : 2 * c],
        mine[2 * c : 3 * c],
        mine[c : 2 * c],
        grads[0, :, 3 * c :].T,
        small[5],
        small[3],
        small[4],
        grads[1],
        up_bias,
        grads[2].T,
        small[2],
        small[0],
        small[1],
    )


def outputs_kernel(cols, table, lse, small, shards, encoded, tokens, *outs):
    *outs, got, wide, sems = outs
    (
        table_out,
        lse_out,
        encoded_out,
        tokens_out,
        g_query,
        g_key,
        g_value,
        gb_query,
        gb_value,
        g_out,
        gb_out,
        g_gain_1,
        g_shift_1,
        g_up,
        gb_up,
        g_down,
        gb_down,
        g_gain_2,
        g_shift_2,
    ) = outs
    steps = got.shape[0]
    rows = [pl.ds(k * got.shape[1], got.shape[1]) for k in range(steps)]
    copies = [pltpu.make_async_copy(tokens.at[rows[k]], got.at[k], sems.at[0, k]) for k in range(steps)]
    writes = [pltpu.make_async_copy(wide.at[k], tokens_out.at[rows[k]], sems.at[1, k]) for k in range(steps)]
    spare = pltpu.make_async_copy(encoded, encoded_out, sems.at[2, 0])
    for copy in copies:
        copy.start()
    spare.start()
    for k in range(steps):
        copies[k].wait()
        wide[k] = got[k].astype(F32)
        writes[k].start()
    me = lax.axis_index("mp")
    table_out[...] = table[...]
    lse_out[...] = lse[...].T.reshape(lse_out.shape)
    for k, target in enumerate((g_key, g_value, g_query)):
        target[...] = shards[0, :, k * cols : (k + 1) * cols]
    g_out[...] = shards[0, :, 3 * cols :].T
    g_up[...] = shards[1]
    g_down[...] = shards[2]
    heads = small[pl.ds(16 + me, 1), :]
    gb_value[...] = heads[:, cols : 2 * cols].reshape(gb_value.shape)
    gb_query[...] = heads[:, 2 * cols : 3 * cols].reshape(gb_query.shape)
    gb_up[...] = small[pl.ds(8 + me, 1), :].reshape(gb_up.shape)
    for k, target in enumerate((g_gain_2, g_shift_2, gb_down, g_gain_1, g_shift_1, gb_out)):
        target[...] = small[k : k + 1, :].reshape(target.shape)
    for write in writes:
        write.wait()
    spare.wait()


def run_outputs(made, cols):
    table, lse, small, shards, encoded, tokens = made
    rows, width = shards.shape[1:]
    shape = jax.ShapeDtypeStruct
    vector = shape((width,), F32)
    outs = (
        shape(table.shape, F32),
        shape((lse.shape[0],), F32),
        shape(encoded.shape, BF16),
        shape(tokens.shape, F32),
        *[shape((rows, cols), F32)] * 3,
        *[shape((cols,), F32)] * 2,
        shape((cols, rows), F32),
        *[vector] * 3,
        shape((rows, width), F32),
        vector,
        shape((rows, width), F32),
        *[vector] * 3,
    )
    steps = 8
    span = tokens.shape[0] // steps
    return pl.pallas_call(
        functools.partial(outputs_kernel, cols),
        out_shape=outs,
        in_specs=specs(*[VMEM] * 4, ANY, ANY),
        out_specs=specs(*[ANY if k in (2, 3) else VMEM for k in range(len(outs))]),
        scratch_shapes=[
            pltpu.VMEM((steps, span, width), BF16),
            pltpu.VMEM((steps, span, width), F32),
            pltpu.SemaphoreType.DMA((3, steps)),
        ],
        compiler_params=params(),
        name="outputs",
    )(*made)


def body(
    tokens,
    cotangent,
    lengths,
    gold,
    passages,
    w_query,
    w_key,
    w_value,
    b_query,
    b_value,
    w_out,
    b_out,
    gain_attn,
    shift_attn,
    w_up,
    b_up,
    w_down,
    b_down,
    gain_ffn,
    shift_ffn,
):
    groups = lax.axis_size("mp")
    sizes = Sizes(tokens.shape[0], tokens.shape[1], groups)
    rows = (b_out, gain_attn, shift_attn, b_down, gain_ffn, shift_ffn)
    shards = (w_key, w_value, w_query, w_out, w_up, w_down.T, b_value, b_query, b_up)
    if lax.axis_size("dp") == 8 and groups == 4:
        whole, encoded, cls, n_1, r_1, n_2, r_2, z, slope, kv, q, logs, ctx = run_forward(
            sizes, lengths, tokens, shards, rows, True
        )
        made = run_finish(
            sizes,
            (lengths, cls, gold, gain_attn, shift_attn, gain_ffn, r_1, r_2, logs),
            (tokens, cotangent, passages, encoded, whole, n_1, n_2, z, slope, kv, q, ctx),
        )
        outs = list(run_outputs(made, w_key.shape[1]))
        outs[15] = outs[15].T
        return tuple(outs)
    return plain_layer(sizes, tokens, cotangent, lengths, gold, passages, shards, rows)


def solution(mesh):
    by_dp, shared, cross = P("dp", None), P(), P("dp", "mp")
    return jax.shard_map(
        body,
        mesh=mesh,
        in_specs=(
            by_dp,
            by_dp,
            by_dp,
            shared,
            by_dp,
            cross,
            cross,
            cross,
            P("mp"),
            P("mp"),
            P("mp", "dp"),
            shared,
            shared,
            shared,
            cross,
            P("mp"),
            P("mp", "dp"),
            shared,
            shared,
            shared,
        ),
        out_specs=(
            P(None, "dp"),
            P("dp"),
            by_dp,
            by_dp,
            cross,
            cross,
            cross,
            P("mp"),
            P("mp"),
            P("mp", "dp"),
            shared,
            shared,
            shared,
            cross,
            P("mp"),
            P("mp", "dp"),
            shared,
            shared,
            shared,
        ),
        check_vma=False,
    )
```

```python
import functools

import jax
import jax.numpy as jnp
from jax import lax
from jax.experimental import pallas as pl
from jax.experimental.pallas import tpu as pltpu
from jax.sharding import PartitionSpec as P

HEAD = 64
LONGEST = 400
QUERY_BLOCK = 256
EPSILON = 1e-05
NEGATIVE = -1e30
LANES = 128
KEY_AT = ((0, 0), (0, 1), (1, 0))
VALUE_AT = ((1, 1), (2, 0), (2, 1))
QUERY_AT = ((0, 0), (0, 1), (1, 0))
CONTEXT_AT = ((0, 1), (1, 0), (1, 1))
F32, BF16 = jnp.float32, jnp.bfloat16
VMEM, ANY, SMEM = pltpu.VMEM, pl.ANY, pltpu.SMEM


def dot(left, right, left_dim=1, right_dim=0):
    return lax.dot_general(
        left, right, (((left_dim,), (right_dim,)), ((), ())), preferred_element_type=F32
    )


def tile(index, count=1):
    return slice(index * LANES, (index + count) * LANES)


def half_mask(half, dtype):
    lane = lax.broadcasted_iota(jnp.int32, (1, LANES), 1)
    return jnp.where((lane >= HEAD) == (half == 1), 1.0, 0.0).astype(dtype)


def norm_stats(hidden):
    centred = hidden - jnp.mean(hidden, axis=-1, keepdims=True)
    factor = lax.rsqrt(jnp.mean(centred * centred, axis=-1, keepdims=True) + EPSILON)
    return centred * factor, factor


def norm_back(grad_out, normed, factor, gain):
    scaled = grad_out * gain
    inner = jnp.mean(scaled * normed, axis=-1, keepdims=True)
    return factor * (scaled - jnp.mean(scaled, axis=-1, keepdims=True) - normed * inner)


def gelu_and_slope(a):
    size = jnp.abs(a)
    t = 1.0 / (1.0 + (0.3275911 * 0.7071067811865476) * size)
    bell = jnp.exp(-0.5 * a * a)
    poly = t * (
        0.127414796 + t * (-0.142248368 + t * (0.7107068705 + t * (-0.7265760135 + t * 0.5307027145)))
    )
    tail = poly * bell
    phi = jnp.where(a >= 0.0, 1.0 - tail, tail)
    return a * phi, phi + a * bell * 0.3989422804014327


def as_row(ref):
    return ref[...].reshape(1, ref.shape[0])


class Sizes:
    def __init__(self, length, width, groups):
        self.length, self.width, self.groups = length, width, groups
        self.own = length // groups
        self.window = min(length, self.own + 2 * LONGEST)
        self.block = min(QUERY_BLOCK, self.own)
        self.blocks = self.own // self.block
        self.keys = min(length, self.block + 2 * LONGEST)

    def window_start(self, me):
        return jnp.clip(self.own * me - LONGEST, 0, self.length - self.window)

    def own_offset(self, me):
        return pl.multiple_of(self.own * me - self.window_start(me), 16)

    def key_start(self, me, block):
        first = self.own * me + block * self.block
        return jnp.clip(first - LONGEST, 0, self.length - self.keys)

    def key_offset(self, me, block):
        return pl.multiple_of(self.key_start(me, block) - self.window_start(me), 16)


def document_bounds(lens, places):
    start = jnp.zeros_like(places)
    end = jnp.zeros_like(places)
    total = jnp.int32(0)
    for d in range(lens.shape[1]):
        count = lens[0, d]
        end = end + jnp.where(places >= total, count, 0)
        total = total + count
        start = start + jnp.where(places >= total, count, 0)
    return start, end


def fill_mask(sizes, me, lens, bias):
    for b in range(sizes.blocks):
        places = (
            sizes.own * me
            + b * sizes.block
            + lax.broadcasted_iota(jnp.int32, (1, sizes.block), 1)
        )
        start, end = document_bounds(lens, places)
        keys = sizes.key_start(me, b) + lax.broadcasted_iota(
            jnp.int32, (sizes.keys, sizes.block), 0
        )
        bias[b] = jnp.where((keys >= start) & (keys < end), 0.0, NEGATIVE)


def start_rows(sizes, me, lens):
    docs = lens.shape[1]
    row = lax.broadcasted_iota(jnp.int32, (docs, sizes.own), 0)
    place = sizes.own * me + lax.broadcasted_iota(jnp.int32, (docs, sizes.own), 1)
    picked = jnp.zeros((docs, sizes.own), F32)
    total = jnp.int32(0)
    for d in range(docs):
        picked = jnp.where((row == d) & (place == total), 1.0, picked)
        total = total + lens[0, d]
    return picked


def project(sizes, me, group, span, tokens, w_attn, biases, kv, q):
    cut = sizes.window // 2
    own = pl.ds(sizes.own_offset(me), sizes.own)

    @pl.loop(*span)
    def _(i):
        g = group(i)
        for part in range(2):
            rows = pl.ds(part * cut, cut)
            made = dot(tokens[rows, :], w_attn[g, :, tile(0, 3)]) + biases[g, :, tile(0, 3)]
            kv[g, rows, :] = made.astype(BF16)
        made = dot(tokens[own, :], w_attn[g, :, tile(3, 2)]) + biases[g, :, tile(3, 2)]
        q[g] = made.astype(BF16) * jnp.asarray(HEAD**-0.5, BF16)


def attend(sizes, me, group, span, tick, kv, q, bias, lse, ctx):
    @pl.loop(*span)
    def _(i):
        g = group(i)

        @pl.loop(0, sizes.blocks)
        def _(b):
            tick(i * sizes.blocks + b)
            keys = pl.ds(sizes.key_offset(me, b), sizes.keys)
            rows = pl.ds(pl.multiple_of(b * sizes.block, sizes.block), sizes.block)
            made = [jnp.zeros((HEAD, sizes.block), F32)]
            logs = []
            for j in range(3):
                kt, kh = KEY_AT[j]
                vt, vh = VALUE_AT[j]
                qt, _ = QUERY_AT[j]
                query = q[g, rows, tile(qt)] * half_mask(kh, BF16)
                s = dot(kv[g, keys, tile(kt)], query, 1, 1) + bias[b]
                peak = jnp.max(s, axis=0, keepdims=True)
                e = jnp.exp(s - peak)
                total = jnp.sum(e, axis=0, keepdims=True)
                mixed = dot(kv[g, keys, tile(vt)], e.astype(BF16), 0, 0)
                made.append(mixed[vh * HEAD : (vh + 1) * HEAD] / total)
                logs.append(peak + jnp.log(total))
            ctx[g, rows, :] = jnp.concatenate(made, axis=0).T.astype(BF16)
            for j in range(3):
                lse[g, b, j : j + 1, :] = logs[j]


def delta_rows(dctx, ctx):
    lane = lax.broadcasted_iota(jnp.int32, (8, 2 * LANES), 1)
    row = lax.broadcasted_iota(jnp.int32, (8, 2 * LANES), 0)
    pick = jnp.where(lane // HEAD == row + 1, 1.0, 0.0).astype(BF16)
    product = dctx.astype(F32) * ctx.astype(F32)
    high = product.astype(BF16)
    low = (product - high.astype(F32)).astype(BF16)
    return dot(pick, high, 1, 1) + dot(pick, low, 1, 1)


def attend_back_block(sizes, me, g, b, kv, q, bias, lse, dctx, delta, dkv):
    keys = pl.ds(sizes.key_offset(me, b), sizes.keys)
    rows = slice(b * sizes.block, (b + 1) * sizes.block)
    made = []
    for j in range(3):
        kt, kh = KEY_AT[j]
        vt, vh = VALUE_AT[j]
        qt, _ = QUERY_AT[j]
        ct, _ = CONTEXT_AT[j]
        query = q[g, rows, tile(qt)] * half_mask(kh, BF16)
        grad = dctx[g, rows, tile(ct)] * half_mask(vh, BF16)
        s = dot(kv[keys, tile(kt)], query, 1, 1) + bias[b]
        p = jnp.exp(s - lse[g, b, j : j + 1, :])
        dp = dot(kv[keys, tile(vt)], grad, 1, 1)
        ds = (p * (dp - delta[j : j + 1, rows])).astype(BF16)
        dkv[keys, tile(kt)] += dot(ds, query)
        dkv[keys, tile(vt)] += dot(p.astype(BF16), grad)
        back = dot(kv[keys, tile(kt)], ds, 0, 0)
        made.append(back[kh * HEAD : (kh + 1) * HEAD] * HEAD**-0.5)
    made.append(jnp.zeros((HEAD, sizes.block), F32))
    return jnp.concatenate(made, axis=0).T


def attend_back(sizes, me, kv, q, bias, lse, ctx, dctx, delta, dkv, dq):
    @pl.loop(0, sizes.groups)
    def _(g):
        delta[...] = delta_rows(dctx[g], ctx[g])
        dkv[g] = jnp.zeros_like(dkv[g])
        for b in range(sizes.blocks):
            rows = slice(b * sizes.block, (b + 1) * sizes.block)
            dq[g, rows, :] = attend_back_block(
                sizes, me, g, b, kv.at[g], q, bias, lse, dctx, delta, dkv.at[g]
            )


class Loads:
    def __init__(self, weights, w, sems):
        self.copies = [pltpu.make_async_copy(weights.at[s], w.at[s], sems.at[s]) for s in range(3)]

    def begin(self):
        for copy in self.copies:
            copy.start()

    def group(self, i):
        return i

    def near_heads(self):
        self.copies[0].wait()

    def far_heads(self):
        pass

    def ready(self, section):
        self.copies[section].wait()

    def tick(self, step):
        pass

    def end(self):
        pass


MESH = pl.DeviceIdType.MESH


class Route:
    def __init__(self, at, turn):
        flip, x_peer = 1 - turn, 2 * at.z + 1 - at.x
        near = at.mp + turn * (at.across - at.mp)
        far = at.mp + flip * (at.across - at.mp)
        self.first = (at.dp + flip * (x_peer - at.dp), near)
        self.second = (at.dp + turn * (x_peer - at.dp), far)
        self.first_column = (near, at.x + flip * (1 - 2 * at.x))
        self.second_columns = ((far, at.x + turn * (1 - 2 * at.x)), (at.across, 1 - at.x))


class Place:
    def __init__(self):
        self.dp, self.mp = lax.axis_index("dp"), lax.axis_index("mp")
        self.z, self.x, self.y, self.core = self.dp // 2, self.dp % 2, self.mp // 2, self.mp % 2
        flip = 1 - self.core
        self.across = 2 * (1 - self.y) + self.core
        self.sibling = (self.dp, 2 * self.y + flip)
        self.x_peer = (2 * self.z + 1 - self.x, self.mp)
        self.y_peer = (self.dp, self.across)
        self.diagonal = (self.dp, 2 * (1 - self.y) + flip)
        self.zs = [self.z, self.z + 1 - 2 * (self.z % 2), (self.z + 2) % 4, 3 - self.z]
        self.line = [(2 * z + self.x, self.mp) for z in self.zs]
        self.by_core = Route(self, self.core)
        self.x_first, self.y_first = Route(self, 0), Route(self, 1)
        self.own_column = (self.mp, self.x)
        self.peers = [*self.line[1:], self.x_peer, self.y_peer, self.sibling, self.diagonal]


def signal(peers):
    barrier = pltpu.get_barrier_semaphore()
    for peer in peers:
        pl.semaphore_signal(barrier, inc=1, device_id=peer, device_id_type=MESH)


def arrive(peers):
    pl.semaphore_wait(pltpu.get_barrier_semaphore(), len(peers))


GATHER_STEPS = {
    "begin": (("along", 0), ("out", 0), ("out", 1), ("out", 2)),
    "near": (("z", 0, 1, 2, 3), ("along", 1), ("first", 0, 0, 1, 2, 3)),
    0: (("z", 1, 1, 2, 3), ("along", 2)),
    1: (("second", 0, 0, 1, 2, 3),),
    2: (("first", 1, 0, 1), ("second", 0, 4, 5)),
    3: (("first", 1, 2, 3), ("second", 0, 6, 7)),
    4: (("z", 2, 1, 2, 3),),
    5: (("second", 1, 0, 1, 2, 3),),
    6: (("second", 1, 4, 5, 6, 7),),
    7: (("first", 2, 0, 1),),
    8: (("first", 2, 2, 3),),
    9: (("second", 2, 0, 1, 2, 3, 4, 5, 6, 7),),
}


class Gather:
    ROUTES = ("x_first", "by_core", "by_core")
    Z_LATER = (False, False, False)

    def __init__(self, place, packed, own_bias, w, biases, kept, send, recv, local, bias_sems):
        self.at, self.packed, self.w, self.kept = place, packed, w, kept
        self.own_bias, self.biases = own_bias, biases
        self.send_sems, self.recv_sems, self.local, self.bias_sems = send, recv, local, bias_sems
        self.rows = packed[1].shape[0]
        self.shards = w.shape[2] // self.rows
        self.routes = [getattr(place, name) for name in self.ROUTES]

    def shard(self, s, g, d):
        return self.w.at[s, g, pl.ds(pl.multiple_of(d * self.rows, 16), self.rows)]

    def copy(self, s, g, d, slot, peer, source=None):
        here = self.shard(s, g, d)
        return pltpu.make_async_remote_copy(
            src_ref=here if source is None else source,
            dst_ref=here,
            send_sem=self.send_sems.at[s, slot],
            recv_sem=self.recv_sems.at[s, g * self.shards + d],
            device_id=peer,
            device_id_type=MESH,
        )

    def arrived(self, s, g, d):
        self.copy(s, g, d, 0, self.at.sibling).wait_recv()

    def own_copy(self, s):
        return pltpu.make_async_copy(
            self.packed[s], self.shard(s, self.at.mp, self.at.dp), self.local.at[s]
        )

    def along_z(self, s):
        at = self.at
        for k in range(1, 4):
            self.copy(s, at.mp, at.dp, k - 1, at.line[k], self.packed[s]).start()

    def own_out(self, s):
        at = self.at
        self.own_copy(s).start()
        source = self.packed[s]
        self.copy(s, at.mp, at.dp, 3, self.routes[s].first, source).start()
        self.copy(s, at.mp, at.dp, 7, self.routes[s].second, source).start()
        self.copy(s, at.mp, at.dp, 15, at.sibling, source).start()

    def from_z(self, s, k):
        at, (g, x) = self.at, self.at.own_column
        d = 2 * at.zs[k] + x
        self.arrived(s, g, d)
        if not self.Z_LATER[s]:
            self.copy(s, g, d, 3 + k, self.routes[s].first).start()
        self.copy(s, g, d, 7 + k, self.routes[s].second).start()
        self.copy(s, g, d, 15 + k, at.sibling).start()

    def from_first(self, s, k):
        at, (g, x) = self.at, self.routes[s].first_column
        d = 2 * at.zs[k] + x
        self.arrived(s, g, d)
        if self.Z_LATER[s] and k == 0:
            for j in range(1, 4):
                self.copy(s, g, d, 3 + j, at.line[j]).start()
        self.copy(s, g, d, 11 + k, self.routes[s].second).start()
        self.copy(s, g, d, 19 + k, at.sibling).start()

    def from_second(self, s, k):
        at, (g, x) = self.at, self.routes[s].second_columns[k // 4]
        d = 2 * at.zs[k % 4] + x
        self.arrived(s, g, d)
        self.copy(s, g, d, 23 + k, at.sibling).start()

    def group(self, i):
        at = self.at
        return 2 * (at.y + (i // 2) * (1 - 2 * at.y)) + at.core + (i % 2) * (1 - 2 * at.core)

    def from_sibling(self, s, g):
        @pl.loop(0, self.shards)
        def _(d):
            self.arrived(s, g, d)

    def keep(self, s):
        return pltpu.make_async_copy(self.w.at[s], self.kept.at[s], self.local.at[3 + s])

    def bias_copy(self, k, peer):
        return pltpu.make_async_remote_copy(
            src_ref=self.own_bias,
            dst_ref=self.biases.at[self.at.mp],
            send_sem=self.bias_sems.at[0, k],
            recv_sem=self.bias_sems.at[1, k],
            device_id=peer,
            device_id_type=MESH,
        )

    def bias_copies(self):
        at = self.at
        across = (at.dp, at.across)
        return [self.bias_copy(k, peer) for k, peer in enumerate((at.sibling, across, at.diagonal))]

    def begin(self):
        signal(self.at.peers)
        self.fill()
        arrive(self.at.peers)
        self.steps("begin")
        for copy in self.bias_copies():
            copy.start()
        self.biases[self.at.mp] = self.own_bias[...]

    def near_heads(self):
        self.steps("near")
        for copy in self.bias_copies():
            copy.wait_recv()
        self.own_copy(0).wait()
        self.from_sibling(0, self.group(1))

    def far_heads(self):
        self.steps("far")
        self.from_sibling(0, self.group(3))
        self.keep(0).start()

    def ready(self, section):
        if section == 1:
            self.steps(8)
        else:
            self.steps(9)
        self.from_sibling(section, self.group(1))
        self.from_sibling(section, self.group(3))
        self.own_copy(section).wait()
        self.keep(section).start()

    def steps(self, step):
        actions = {
            "along": lambda s, k: self.along_z(s),
            "out": lambda s, k: self.own_out(s),
            "z": self.from_z,
            "first": self.from_first,
            "second": self.from_second,
        }
        for name, s, *ks in GATHER_STEPS.get(step, ()):
            for k in ks or (0,):
                actions[name](s, k)

    def tick(self, step):
        for k in range(8):
            pl.when(step == k)(functools.partial(self.steps, k))

    def end(self):
        for copy in self.bias_copies():
            copy.wait_send()
        for s in range(3):

            @pl.loop(0, 31)
            def _(slot):
                self.copy(s, 0, 0, slot, self.at.sibling).wait_send()

            self.keep(s).wait()


def forward_math(
    sizes,
    source,
    lens,
    tokens,
    biases,
    b_out,
    gain_1,
    shift_1,
    b_down,
    gain_2,
    shift_2,
    encoded,
    cls,
    n_1,
    r_1,
    n_2,
    r_2,
    z_out,
    slope_out,
    kv_out,
    q,
    lse,
    ctx,
    x,
    w,
    bias,
    hidden,
    kv,
    z,
    slope,
    sems,
):
    me = lax.axis_index("mp")
    first = pl.multiple_of(sizes.window_start(me), 16)
    load = pltpu.make_async_copy(tokens.at[pl.ds(first, sizes.window)], x, sems.at[0])
    load.start()
    source.begin()
    fill_mask(sizes, me, lens, bias)
    load.wait()
    save_kv = pltpu.make_async_copy(kv, kv_out, sems.at[1])
    half = sizes.groups // 2
    for span, ready in (((0, half), source.near_heads), ((half, sizes.groups), source.far_heads)):
        ready()
        project(sizes, me, source.group, span, x, w.at[0], biases, kv, q)
        if span[1] == sizes.groups:
            save_kv.start()
        attend(sizes, me, source.group, span, source.tick, kv, q, bias, lse, ctx)

    own = pl.ds(sizes.own_offset(me), sizes.own)
    hidden[...] = x[own, :].astype(F32) + as_row(b_out)
    for g in range(sizes.groups):
        hidden[...] += dot(ctx[g], w[0, g, :, tile(4, 2)], 1, 1)
    normed, factor = norm_stats(hidden[...])
    n_1[...] = normed
    r_1[...] = factor
    y_1 = normed * as_row(gain_1) + as_row(shift_1)
    hidden[...] = y_1 + as_row(b_down)
    encoded[...] = y_1.astype(BF16)
    source.ready(1)

    @pl.loop(0, sizes.groups)
    def _(g):
        a = dot(encoded[...], w[1, g]) + biases[g, :, 5 * LANES :]
        out, grad = gelu_and_slope(a)
        z[g] = out.astype(BF16)
        slope[g] = grad.astype(BF16)

    save_z = pltpu.make_async_copy(z, z_out, sems.at[2])
    save_slope = pltpu.make_async_copy(slope, slope_out, sems.at[3])
    save_z.start()
    save_slope.start()
    source.ready(2)

    @pl.loop(0, sizes.groups)
    def _(g):
        hidden[...] += dot(z[g], w[2, g], 1, 1)

    normed, factor = norm_stats(hidden[...])
    n_2[...] = normed
    r_2[...] = factor
    y_2 = (normed * as_row(gain_2) + as_row(shift_2)).astype(BF16)
    encoded[...] = y_2
    cls[...] = dot(start_rows(sizes, me, lens).astype(BF16), y_2)
    source.end()
    save_kv.wait()
    save_z.wait()
    save_slope.wait()


def forward_kernel(sizes, lens, tokens, weights, biases, *rest):
    *refs, w, bias, hidden, kv, z, slope, sems, loads = rest
    source = Loads(weights, w, loads)
    forward_math(sizes, source, lens, tokens, biases, *refs, w, bias, hidden, kv, z, slope, sems)


def pack(w_key, w_value, w_query, w_out, w_down, b_value, b_query, b_up, packed, own_bias):
    cols = w_key.shape[1]
    for k, weight in enumerate((w_key, w_value, w_query)):
        packed[0, :, k * cols : (k + 1) * cols] = weight[...]
    packed[0, :, 3 * cols :] = w_out[...].astype(F32).T.astype(BF16)
    packed[1] = w_down[...]
    own_bias[...] = jnp.zeros_like(own_bias)
    own_bias[:, cols : 2 * cols] = as_row(b_value)
    own_bias[:, 2 * cols : 3 * cols] = as_row(b_query)
    own_bias[:, 5 * LANES :] = as_row(b_up)


def gathering_kernel(sizes, lens, tokens, *rest):
    shards, rows, (kept, *outs) = rest[:9], rest[9:15], rest[15:]
    *refs, w, bias, hidden, kv, z, slope, sems, packed, own_bias, biases, send, recv, local, bias_sems = outs
    w_key, w_value, w_query, w_out, w_up, w_down, b_value, b_query, b_up = shards

    def fill():
        pack(w_key, w_value, w_query, w_out, w_down, b_value, b_query, b_up, packed, own_bias)

    source = Gather(
        Place(), (packed.at[0], w_up, packed.at[1]), own_bias, w, biases, kept, send, recv, local, bias_sems
    )
    source.fill = fill
    forward_math(
        sizes, source, lens, tokens, biases, *rows, *refs, w, bias, hidden, kv, z, slope, sems
    )


def backward_kernel(
    sizes,
    lens,
    cotangent,
    dcls,
    weights,
    gain_1,
    shift_1,
    gain_2,
    n_1,
    r_1,
    n_2,
    r_2,
    z,
    slope,
    kv,
    q,
    lse,
    ctx,
    dh_1,
    dkv,
    dq,
    grads,
    grads_out,
    small,
    w_attn,
    w_up,
    w_down,
    cot,
    dh,
    low,
    other,
    turned,
    stage,
    dctx,
    delta,
    bias,
    sems,
    out_sems,
):
    me = lax.axis_index("mp")
    load_cot = pltpu.make_async_copy(
        cotangent.at[pl.ds(pl.multiple_of(sizes.own * me, 16), sizes.own)], cot, sems.at[3]
    )
    load_cot.start()
    loads = []
    for s, buffer in ((2, w_down), (1, w_up), (0, w_attn)):
        loads.append(pltpu.make_async_copy(weights.at[s], buffer, sems.at[s]))
        loads[-1].start()
    fill_mask(sizes, me, lens, bias)
    picked = start_rows(sizes, me, lens).astype(BF16)
    high = dcls[...].astype(BF16)
    low_part = (dcls[...] - high.astype(F32)).astype(BF16)
    load_cot.wait()
    dy = cot[...].astype(F32) + dot(picked, high, 0, 0) + dot(picked, low_part, 0, 0)
    small[0:1, :] = jnp.sum(dy * n_2[...], axis=0, keepdims=True)
    small[1:2, :] = jnp.sum(dy, axis=0, keepdims=True)
    grad = norm_back(dy, n_2[...], r_2[...], as_row(gain_2))
    small[2:3, :] = jnp.sum(grad, axis=0, keepdims=True)
    dh[...] = grad
    low[...] = grad.astype(BF16)
    turned[0] = grad.T.astype(BF16)
    y_1 = n_1[...] * as_row(gain_1) + as_row(shift_1)
    other[...] = y_1.astype(BF16)
    turned[1] = y_1.T.astype(BF16)
    for load in loads:
        load.wait()

    def out_copy(section, g, slot):
        return pltpu.make_async_copy(
            stage.at[slot], grads.at[section, g], out_sems.at[slot]
        )

    @pl.loop(0, sizes.groups)
    def _(g):
        @pl.when(g > 0)
        def _():
            out_copy(1, 0, 0).wait()
            out_copy(1, 0, 1).wait()

        stage[1] = dot(turned[0], z[g]).astype(BF16)
        out_copy(1, g, 1).start()
        da = dot(low[...], w_down[g]) * slope[g].astype(F32)
        small[pl.ds(8 + g, 1), :] = jnp.sum(da, axis=0, keepdims=True)
        da_low = da.astype(BF16)
        stage[0] = dot(turned[1], da_low).astype(BF16)
        out_copy(0, g, 0).start()
        dh[...] += dot(da_low, w_up[g], 1, 1)

    dy = dh[...]
    small[3:4, :] = jnp.sum(dy * n_1[...], axis=0, keepdims=True)
    small[4:5, :] = jnp.sum(dy, axis=0, keepdims=True)
    grad = norm_back(dy, n_1[...], r_1[...], as_row(gain_1))
    small[5:6, :] = jnp.sum(grad, axis=0, keepdims=True)
    small[6:8, :] = jnp.zeros_like(small[6:8, :])
    small[12:16, :] = jnp.zeros_like(small[12:16, :])
    dh_1[...] = grad
    low[...] = grad.astype(BF16)
    turned[0] = grad.T.astype(BF16)

    @pl.loop(0, sizes.groups)
    def _(g):
        dctx[g] = dot(low[...], w_attn[g, :, tile(4, 2)]).astype(BF16)
        grads_out[g] = dot(turned[0], ctx[g])

    attend_back(sizes, me, kv, q, bias, lse, ctx, dctx, delta, dkv, dq)
    out_copy(1, 0, 0).wait()
    out_copy(1, 0, 1).wait()


def remote(source, target, send, recv, peer):
    return pltpu.make_async_remote_copy(
        src_ref=source,
        dst_ref=target,
        send_sem=send,
        recv_sem=recv,
        device_id=peer,
        device_id_type=MESH,
    )


def square(parts, index):
    side = parts.shape[1]
    return parts.at[pl.ds(pl.multiple_of(index * side, side), side)]


class Spread:
    def __init__(self, place, source, whole, send, recv, local):
        self.at, self.source, self.whole = place, source, whole
        self.send, self.recv, self.local = send, recv, local
        self.count = source.shape[0]

    def rows(self, mp):
        return self.whole.at[pl.ds(pl.multiple_of(mp * self.count, 16), self.count)]

    def copy(self, k):
        at = self.at
        target = self.rows(at.across if k == 2 else at.mp)
        source = target if k == 2 else self.source
        peer = (at.dp, at.across) if k == 1 else at.sibling
        return remote(source, target, self.send.at[k], self.recv.at[k], peer)

    def own(self):
        return pltpu.make_async_copy(self.source, self.rows(self.at.mp), self.local)

    def begin(self):
        self.copy(1).start()
        self.copy(0).start()
        self.own().start()

    def forward(self):
        self.copy(1).wait_recv()
        self.copy(2).start()

    def end(self):
        self.copy(0).wait()
        self.copy(1).wait_send()
        self.copy(2).wait()
        self.own().wait()


DURING = {
    0: (("encoded", 0),),
    1: (("second", 2),),
    5: (("first", 2),),
}
BEFORE_LAST = (("second", 1),)
AFTER_LAST = (
    ("begin", 0),
    ("chip", 0),
    ("line", 2),
    ("first", 1),
    ("tokens", 0),
    ("second", 0),
    ("small", 0),
    ("line", 1),
    ("small", 1),
    ("first", 0),
    ("small", 2),
    ("relay", 0),
    ("line", 0),
)


class Scatter:
    STAGE = (0, 2, 0)
    HELD = (8, 6, 4)
    ROUTES = ("by_core", "by_core", "by_core")
    Z_EARLY = ((1,), (1,), (1,))

    def __init__(self, place, parts, inbox, by_second, by_first, by_line, shards, sems):
        self.at, self.parts, self.inbox, self.shards = place, parts, inbox, shards
        self.by_second, self.by_first, self.by_line = by_second, by_first, by_line
        self.core_sems, self.second_sems, self.first_sems, self.line_sems = sems
        self.rows = shards.shape[1]
        self.routes = [getattr(place, name) for name in self.ROUTES]

    def shard(self, s, g, d):
        first = (self.HELD[s] + g // 2) * self.parts.shape[1] + d * self.rows
        return self.parts.at[pl.ds(pl.multiple_of(first, 16), self.rows)]

    def part(self, index):
        return square(self.parts, index)

    def to_sibling(self, s, k):
        at = self.STAGE[s] + k
        return remote(
            self.part(at),
            self.inbox.at[at],
            self.core_sems.at[0, s, k],
            self.core_sems.at[1, s, k],
            self.at.sibling,
        )

    def to_second(self, s, k):
        g, x = self.routes[s].second_columns[1 - k // 4]
        return remote(
            self.shard(s, g, 2 * (k % 4) + x),
            self.by_second.at[s, k],
            self.second_sems.at[0, s, k],
            self.second_sems.at[1, s, k],
            self.routes[s].second,
        )

    def to_first(self, s, k):
        g, x = self.routes[s].first_column
        return remote(
            self.shard(s, g, 2 * k + x),
            self.by_first.at[s, k],
            self.first_sems.at[0, s, k],
            self.first_sems.at[1, s, k],
            self.routes[s].first,
        )

    def to_line(self, s, j):
        at = self.at
        return remote(
            self.shard(s, at.mp, 2 * at.zs[j] + at.x),
            self.by_line.at[s, j - 1],
            self.line_sems.at[0, s, j - 1],
            self.line_sems.at[1, s, j - 1],
            at.line[j],
        )

    def chip_sum(self, s):
        for k in range(2):
            self.to_sibling(s, k).wait_recv()
            held, more = self.part(self.HELD[s] + k), self.inbox.at[self.STAGE[s] + k]

            @pl.loop(0, held.shape[0] // self.rows)
            def _(d):
                rows = pl.ds(pl.multiple_of(d * self.rows, 16), self.rows)
                held[rows, :] = (held[rows, :].astype(F32) + more[rows, :].astype(F32)).astype(BF16)

        for k in range(8):
            self.to_second(s, k).start()

    def other_line(self, s, j):
        g, x = self.routes[s].first_column
        return remote(
            self.shard(s, g, 2 * self.at.zs[j] + x),
            self.by_first.at[s, j],
            self.first_sems.at[0, s, j],
            self.first_sems.at[1, s, j],
            self.at.line[j],
        )

    def last_cross(self, s):
        g, x = self.routes[s].first_column
        return remote(
            self.shard(s, g, 2 * self.at.z + x),
            self.by_first.at[s, 0],
            self.first_sems.at[0, s, 0],
            self.first_sems.at[1, s, 0],
            self.routes[s].first,
        )

    def by_kind(self, s, early, late):
        cores = self.Z_EARLY[s]
        if len(cores) == 1:
            pl.when(self.at.core == cores[0])(functools.partial(early, s))
            pl.when(self.at.core != cores[0])(functools.partial(late, s))
        else:
            (early if cores else late)(s)

    def from_second(self, s):
        self.by_kind(s, self.from_second_early, self.from_second_late)

    def from_first(self, s):
        self.by_kind(s, self.from_first_early, self.from_first_late)

    def from_line(self, s):
        self.by_kind(s, self.from_line_early, self.from_line_late)

    def from_second_early(self, s):
        at, (g, x) = self.at, self.routes[s].first_column
        for k in range(8):
            self.to_second(s, k).wait_recv()
        for j in (3, 2, 1, 0):
            z = at.zs[j]
            mine = self.shard(s, g, 2 * z + x)
            mine[...] = (mine[...].astype(F32) + self.by_second[s, z].astype(F32)).astype(BF16)
            if j:
                self.other_line(s, j).start()
        for j in (3, 2, 1):
            z = at.zs[j]
            mine = self.shard(s, at.mp, 2 * z + at.x)
            mine[...] = (mine[...].astype(F32) + self.by_second[s, 4 + z].astype(F32)).astype(BF16)
            self.to_line(s, j).start()

    def from_first_early(self, s):
        g, x = self.routes[s].first_column
        mine = self.shard(s, g, 2 * self.at.z + x)
        total = mine[...].astype(F32)
        for j in (1, 2, 3):
            self.other_line(s, j).wait_recv()
            total = total + self.by_first[s, j].astype(F32)
        mine[...] = total.astype(BF16)
        self.last_cross(s).start()

    def from_line_early(self, s):
        at = self.at
        mine = self.shard(s, at.mp, 2 * at.z + at.x)
        total = mine[...].astype(F32) + self.by_second[s, 4 + at.z].astype(F32)
        for j in range(1, 4):
            self.to_line(s, j).wait_recv()
            total = total + self.by_line[s, j - 1].astype(F32)
        self.last_cross(s).wait_recv()
        self.shards[s] = total + self.by_first[s, 0].astype(F32)

    def from_second_late(self, s):
        g, x = self.routes[s].first_column
        for k in range(4):
            self.to_second(s, k).wait_recv()
            mine = self.shard(s, g, 2 * k + x)
            mine[...] = (mine[...].astype(F32) + self.by_second[s, k].astype(F32)).astype(BF16)
            self.to_first(s, k).start()

    def from_first_late(self, s):
        at = self.at
        for k in range(4):
            self.to_second(s, 4 + k).wait_recv()
            self.to_first(s, k).wait_recv()
        for j in (3, 2, 1, 0):
            z = at.zs[j]
            mine = self.shard(s, at.mp, 2 * z + at.x)
            total = (
                mine[...].astype(F32)
                + self.by_second[s, 4 + z].astype(F32)
                + self.by_first[s, z].astype(F32)
            )
            if j:
                mine[...] = total.astype(BF16)
                self.to_line(s, j).start()
            else:
                self.shards[s] = total

    def from_line_late(self, s):
        for j in range(1, 4):
            self.to_line(s, j).wait_recv()
            self.shards[s] += self.by_line[s, j - 1].astype(F32)

    def sent_to_sibling(self, s):
        for k in range(2):
            self.to_sibling(s, k).wait_send()

    def end(self):
        for s in range(3):
            for k in range(8):
                self.to_second(s, k).wait_send()
            for k in range(4):
                self.to_first(s, k).wait_send()
            for j in range(1, 4):
                self.to_line(s, j).wait_send()


class SmallSums:
    def __init__(self, place, sums, inbox, sems):
        self.at, self.sums, self.inbox, self.sems = place, sums, inbox, sems
        at = place
        self.peers = [at.sibling, at.x_peer, at.y_peer, *at.line[1:]]

    def copy(self, k):
        return remote(
            self.sums.at[min(k, 3)],
            self.inbox.at[k],
            self.sems.at[0, k],
            self.sems.at[1, k],
            self.peers[k],
        )

    def begin(self):
        self.copy(0).start()

    def step(self, k):
        self.copy(k).wait_recv()
        self.sums[k + 1] = self.sums[k] + self.inbox[k]
        for nxt in (k + 1,) if k < 2 else (3, 4, 5):
            self.copy(nxt).start()

    def end(self, out):
        for k in range(3, 6):
            self.copy(k).wait_recv()
        out[...] = (self.sums[3] + self.inbox[3]) + (self.inbox[4] + self.inbox[5])
        for k in range(6):
            self.copy(k).wait_send()


def fold(rows):
    half = rows.shape[1] // 2
    return jnp.concatenate([rows[:, :half], rows[:, half:]], axis=0).astype(BF16)


def unfold(packed):
    wide = packed.astype(F32)
    return jnp.concatenate([wide[:8], wide[8:]], axis=1)


class Scoring:
    def __init__(self, place, ways, cls, gold, passages, scores, lse, buffers, sems):
        self.at, self.ways, self.cls, self.gold = place, ways, cls, gold
        self.passages, self.scores, self.lse = passages, scores, lse
        self.part, self.parts, self.firsts, self.rows = buffers[:4]
        self.sent, self.got, self.stats, self.got_stats = buffers[4:]
        self.mp_sems, self.sems = sems
        at = place
        self.mates = (at.sibling, (at.dp, at.across), at.diagonal)
        self.others = [(lax.rem(at.dp + k, ways), at.mp) for k in range(1, ways)]

    def mate(self, k):
        return remote(
            self.part, self.parts.at[k], self.mp_sems.at[0, k], self.mp_sems.at[1, k], self.mates[k]
        )

    def first_copy(self, k):
        mine = self.firsts.at[self.at.dp]
        return remote(
            mine, mine, self.sems.at[0, 0, k - 1], self.sems.at[0, 1, k - 1], self.others[k - 1]
        )

    def back_copy(self, which, k):
        peer = self.others[k - 1]
        return remote(
            self.sent.at[which, peer[0]],
            self.got.at[which, self.at.dp],
            self.sems.at[1 + which, 0, k - 1],
            self.sems.at[1 + which, 1, k - 1],
            peer,
        )

    def stat_copy(self, k):
        peer = self.others[k - 1]
        return remote(
            self.stats.at[peer[0]],
            self.got_stats.at[self.at.dp],
            self.sems.at[3, 0, k - 1],
            self.sems.at[3, 1, k - 1],
            peer,
        )

    def start_cls(self):
        self.part[...] = fold(self.cls[...])
        for k in range(3):
            self.mate(k).start()

    def start_gold(self):
        places = self.at.dp * self.passages.shape[0] + lax.broadcasted_iota(
            jnp.int32, (self.passages.shape[0], self.gold.shape[0]), 0
        )
        target = jnp.where(as_row(self.gold) == places, 1.0, 0.0).astype(BF16)
        self.put(0, dot(target, self.passages[...], 0, 0))
        for k in range(1, self.ways):
            self.back_copy(0, k).start()

    def put(self, which, rows):
        for d in range(self.ways):
            self.sent[which, d] = fold(rows[8 * d : 8 * d + 8])
        self.got[which, self.at.dp] = self.sent[which, self.at.dp]

    def start_firsts(self):
        total = self.part[...].astype(F32)
        for k in range(3):
            self.mate(k).wait_recv()
            total = total + self.parts[k].astype(F32)
        self.firsts[self.at.dp] = total.astype(BF16)
        for k in range(1, self.ways):
            self.first_copy(k).start()

    def start_back(self):
        for k in range(1, self.ways):
            self.first_copy(k).wait_recv()
        for d in range(self.ways):
            self.rows[8 * d : 8 * d + 8, :] = unfold(self.firsts[d])
        table = dot(self.rows[...].astype(BF16), self.passages[...], 1, 1)
        self.scores[...] = table
        peak = jnp.max(table, axis=1, keepdims=True)
        e = jnp.exp(table - peak)
        total = jnp.sum(e, axis=1, keepdims=True)
        lane = lax.broadcasted_iota(jnp.int32, (8, LANES), 1)
        for d in range(self.ways):
            rows = slice(8 * d, 8 * d + 8)
            self.stats[d] = jnp.where(lane == 0, peak[rows], total[rows])
        self.got_stats[self.at.dp] = self.stats[self.at.dp]
        for k in range(1, self.ways):
            self.stat_copy(k).start()
        self.put(1, dot(e.astype(BF16), self.passages[...]))
        for k in range(1, self.ways):
            self.back_copy(1, k).start()

    def result(self):
        for k in range(1, self.ways):
            self.back_copy(0, k).wait_recv()
            self.stat_copy(k).wait_recv()
        peaks = [self.got_stats[d][:, 0:1] for d in range(self.ways)]
        top = functools.reduce(jnp.maximum, peaks)
        scales = [jnp.exp(peak - top) for peak in peaks]
        total = sum(scale * self.got_stats[d][:, 1:2] for d, scale in enumerate(scales))
        self.lse[...] = top + jnp.log(total)
        for k in range(1, self.ways):
            self.back_copy(1, k).wait_recv()
        grad = -sum(unfold(self.got[0, d]) for d in range(self.ways))
        for d in range(self.ways):
            grad = grad + (scales[d] / total) * unfold(self.got[1, d])
        return grad

    def end(self):
        for k in range(3):
            self.mate(k).wait_send()
        for k in range(1, self.ways):
            self.first_copy(k).wait_send()
            self.back_copy(0, k).wait_send()
            self.back_copy(1, k).wait_send()
            self.stat_copy(k).wait_send()


class Halo:
    def __init__(self, sizes, place, dkv, sent, got, sems):
        self.sizes, self.at, self.dkv, self.sent, self.got, self.sems = sizes, place, dkv, sent, got, sems
        self.has = (place.mp > 0, place.mp < sizes.groups - 1)
        offset = sizes.own_offset(place.mp)
        self.starts = (offset - LONGEST, offset + sizes.own)
        self.into = (sizes.own - LONGEST, 0)

    def copy(self, g, side):
        slot = g % 2
        return remote(
            self.sent.at[slot, side],
            self.got.at[g, side],
            self.sems.at[0, slot, side],
            self.sems.at[1, g, side],
            (self.at.dp, self.at.mp + 2 * side - 1),
        )

    def start(self, g):
        for side in range(2):

            @pl.when(self.has[side])
            def _():
                pl.when(g > 1)(self.copy(g, side).wait_send)
                rows = pl.ds(pl.multiple_of(self.starts[side], 16), LONGEST)
                self.sent[g % 2, side] = self.dkv[rows, :].astype(BF16)
                self.copy(g, side).start()

    def add(self, g, own):
        for side in range(2):

            @pl.when(self.has[1 - side])
            def _():
                self.copy(g, side).wait_recv()
                rows = pl.ds(self.into[side], LONGEST)
                own[rows, :] += self.got[g, side].astype(F32)

    def end(self):
        for side in range(2):

            @pl.when(self.has[side])
            def _():
                self.copy(2, side).wait_send()
                self.copy(3, side).wait_send()


def finish_kernel(
    sizes,
    lens,
    cls,
    gold,
    gain_1,
    shift_1,
    gain_2,
    r_1,
    r_2,
    lse,
    tokens,
    cotangent,
    passages,
    encoded,
    weights,
    n_1_in,
    n_2_in,
    z_in,
    slope_in,
    kv_in,
    q_in,
    ctx_in,
    scores,
    query_lse,
    small_out,
    shards,
    encoded_whole,
    token_whole,
    w,
    ffn,
    parts,
    inbox,
    by_second,
    by_first,
    by_line,
    kv,
    q,
    ctx,
    dctx,
    dkv,
    own_kv,
    halo_sent,
    halo_got,
    n_1,
    work,
    rows_low,
    row_in,
    turned,
    low,
    bias,
    delta,
    sums,
    sums_in,
    part,
    parts_in,
    firsts,
    first_rows,
    back_sent,
    back_got,
    stats,
    stats_got,
    load_sems,
    kv_sems,
    ffn_sems,
    spread_sems,
    core_sems,
    second_sems,
    first_sems,
    line_sems,
    halo_sems,
    small_sems,
    mp_sems,
    score_sems,
):
    at = Place()
    me = at.mp
    own_rows = pl.ds(pl.multiple_of(sizes.own * me, 16), sizes.own)
    ways = firsts.shape[0]
    table = parts.at[pl.ds(Scatter.HELD[0] * sizes.width, passages.shape[0])]
    scatter = Scatter(
        at, parts, inbox, by_second, by_first, by_line, shards,
        (core_sems, second_sems, first_sems, line_sems),
    )
    halo = Halo(sizes, at, dkv, halo_sent, halo_got, halo_sems)
    spread = Spread(at, encoded, encoded_whole, spread_sems.at[0, 0], spread_sems.at[0, 1], load_sems.at[8])
    token_spread = Spread(
        at, rows_low, token_whole, spread_sems.at[1, 0], spread_sems.at[1, 1], load_sems.at[9]
    )
    small = SmallSums(at, sums, sums_in, small_sems)

    def load(k, source, target):
        return pltpu.make_async_copy(source, target, load_sems.at[k])

    loads = [
        load(0, passages, table),
        load(1, cotangent.at[own_rows], row_in),
        load(2, n_2_in, work.at[1]),
        load(3, n_1_in, n_1),
        load(5, q_in, q),
        load(6, ctx_in, ctx),
    ]

    def kv_load(g):
        return pltpu.make_async_copy(kv_in.at[g], kv.at[g % 2], kv_sems.at[g % 2])

    for copy in loads:
        copy.start()
    kv_load(0).start()

    scoring = Scoring(
        at,
        ways,
        cls,
        gold,
        table,
        scores,
        query_lse,
        (part, parts_in, firsts, first_rows, back_sent, back_got, stats, stats_got),
        (mp_sems, score_sems),
    )
    signal([*scoring.mates, *scoring.others])

    def group_of(i):
        return jnp.where(i < 2, 1 - at.core + 2 * i, at.core + 2 * (i - 2))

    def z_load(i):
        return pltpu.make_async_copy(z_in.at[group_of(i)], ffn.at[0, i % 2], ffn_sems.at[i % 2, 0])

    def ffn_loads(i):
        slot, g = i % 2, group_of(i)
        return [
            pltpu.make_async_copy(weights.at[2, g], w.at[2 * slot], ffn_sems.at[slot, 1]),
            pltpu.make_async_copy(weights.at[1, g], w.at[2 * slot + 1], ffn_sems.at[slot, 2]),
            pltpu.make_async_copy(slope_in.at[g], ffn.at[1, slot], ffn_sems.at[slot, 3]),
        ]

    z_load(0).start()
    for copy in ffn_loads(0):
        copy.start()

    arrive([*scoring.mates, *scoring.others])
    scoring.start_cls()
    loads[0].wait()
    scoring.start_gold()
    scoring.start_firsts()
    spread.begin()
    fill_mask(sizes, me, lens, bias)
    picked = start_rows(sizes, me, lens).astype(BF16)
    loads[3].wait()
    turned[1] = (n_1[...] * as_row(gain_1) + as_row(shift_1)).T.astype(BF16)
    scoring.start_back()
    loads[1].wait()
    loads[2].wait()
    dcls = scoring.result()
    high = dcls.astype(BF16)
    rest = (dcls - high.astype(F32)).astype(BF16)
    dy = row_in[...].astype(F32) + dot(picked, high, 0, 0) + dot(picked, rest, 0, 0)
    mine = sums.at[0]
    mine[0:1, :] = jnp.sum(dy * work[1], axis=0, keepdims=True)
    mine[1:2, :] = jnp.sum(dy, axis=0, keepdims=True)
    grad = norm_back(dy, work[1], r_2[...], as_row(gain_2))
    mine[2:3, :] = jnp.sum(grad, axis=0, keepdims=True)
    work[0] = grad
    rows_low[...] = grad.astype(BF16)
    turned[0] = grad.T.astype(BF16)

    def into(s, i):
        return jnp.where(i < 2, Scatter.STAGE[s] + i, Scatter.HELD[s] + i - 2)

    @pl.loop(0, sizes.groups)
    def _(i):
        z_load(i).wait()

        @pl.when(i < 3)
        def _():
            z_load(i + 1).start()

        square(parts, into(2, i))[...] = dot(turned[0], ffn[0, i % 2]).astype(BF16)
        pl.when(i < 2)(lambda: scatter.to_sibling(2, i).start())

    scatter.chip_sum(2)

    @pl.loop(0, sizes.groups)
    def _(i):
        slot, g = i % 2, group_of(i)
        for copy in ffn_loads(i):
            copy.wait()

        @pl.when(i < 3)
        def _():
            for copy in ffn_loads(i + 1):
                copy.start()

        da = dot(rows_low[...], w[2 * slot]) * ffn[1, slot].astype(F32)
        mine[pl.ds(8 + g, 1), :] = jnp.sum(da, axis=0, keepdims=True)
        da_low = da.astype(BF16)
        square(parts, into(1, i))[...] = dot(turned[1], da_low).astype(BF16)
        pl.when(i < 2)(lambda: scatter.to_sibling(1, i).start())
        work[0] += dot(da_low, w[2 * slot + 1], 1, 1)

    load_w = pltpu.make_async_copy(weights.at[0], w, load_sems.at[7])
    load_w.start()
    load_x = load(1, tokens.at[own_rows], row_in)
    load_x.start()
    scatter.chip_sum(1)
    scatter.sent_to_sibling(2)

    dy = work[0]
    mine[3:4, :] = jnp.sum(dy * n_1[...], axis=0, keepdims=True)
    mine[4:5, :] = jnp.sum(dy, axis=0, keepdims=True)
    grad = norm_back(dy, n_1[...], r_1[...], as_row(gain_1))
    mine[5:6, :] = jnp.sum(grad, axis=0, keepdims=True)
    mine[6:8, :] = jnp.zeros((2, sizes.width), F32)
    mine[12:24, :] = jnp.zeros((12, sizes.width), F32)
    work[1] = grad
    rows_low[...] = grad.astype(BF16)
    turned[0] = grad.T.astype(BF16)
    load_x.wait()
    turned[1] = row_in[...].astype(F32).T.astype(BF16)
    load_w.wait()
    for copy in loads[4:]:
        copy.wait()

    @pl.loop(0, sizes.groups)
    def _(g):
        dctx[g] = dot(rows_low[...], w[g, :, tile(4, 2)]).astype(BF16)

    actions = {
        "second": scatter.from_second,
        "first": scatter.from_first,
        "line": scatter.from_line,
        "chip": scatter.chip_sum,
        "small": small.step,
        "begin": lambda s: small.begin(),
        "tokens": lambda s: token_spread.begin(),
        "relay": lambda s: token_spread.forward(),
        "encoded": lambda s: spread.forward(),
    }

    def run(names):
        for name, s in names:
            actions[name](s)

    def tick(now):
        for k, names in DURING.items():
            pl.when(now == k)(functools.partial(run, names))

    def finalize(g):
        slot = g % 2
        halo.add(g, own_kv.at[slot])
        dkv_own = own_kv[slot]
        mine[pl.ds(16 + g, 1), tile(0, 3)] = jnp.sum(dkv_own, axis=0, keepdims=True)
        low[slot, :, tile(0, 3)] = dkv_own.astype(BF16)
        work[1] += dot(low[slot], w[g, :, tile(0, 5)], 1, 1)
        into = jnp.where(g % 2 == at.core, Scatter.HELD[0], Scatter.STAGE[0]) + g // 2
        made = dot(turned[1], low[slot])
        more = dot(turned[0], ctx[g])
        target = square(parts, into)
        target[:, tile(0, 4)] = made[:, tile(0, 4)].astype(BF16)
        target[:, tile(4)] = (made[:, tile(4)] + more[:, tile(0)]).astype(BF16)
        target[:, tile(5)] = more[:, tile(1)].astype(BF16)

        @pl.when(g % 2 != at.core)
        def _():
            scatter.to_sibling(0, g // 2).start()

    own = pl.ds(sizes.own_offset(me), sizes.own)

    @pl.loop(0, sizes.groups)
    def _(g):
        slot = g % 2
        kv_load(g).wait()

        @pl.when(g < sizes.groups - 1)
        def _():
            kv_load(g + 1).start()

        delta[...] = delta_rows(dctx[g], ctx[g])
        dkv[...] = jnp.zeros_like(dkv)
        for b in range(sizes.blocks):
            tick(g * sizes.blocks + b)
            rows = slice(b * sizes.block, (b + 1) * sizes.block)
            dq = attend_back_block(
                sizes, me, g, b, kv.at[slot], q, bias, lse, dctx, delta, dkv
            )
            total = jnp.sum(dq, axis=0, keepdims=True)
            mine[pl.ds(16 + g, 1), tile(3, 2)] += total
            low[slot, rows, tile(3, 2)] = dq.astype(BF16)
        halo.start(g)
        own_kv[slot] = dkv[own, :]

        @pl.when(g > 0)
        def _():
            finalize(g - 1)

    run(BEFORE_LAST)
    finalize(sizes.groups - 1)
    rows_low[...] = work[1].astype(BF16)
    run(AFTER_LAST)
    small.end(small_out)
    scatter.sent_to_sibling(1)
    scatter.sent_to_sibling(0)
    scatter.end()
    halo.end()
    scoring.end()
    spread.end()
    token_spread.end()


def input_kernel(sizes, tokens, weights, dkv, dq, dh_1, grads_out, token_grad, grads, small, turned, low):
    turned[...] = tokens[...].astype(F32).T.astype(BF16)
    total = dh_1[...]
    for g in range(sizes.groups):
        small[g, :, tile(0, 3)] = jnp.sum(dkv[g], axis=0, keepdims=True)
        small[g, :, tile(3, 2)] = jnp.sum(dq[g], axis=0, keepdims=True)
        low[:, tile(0, 3)] = dkv[g].astype(BF16)
        low[:, tile(3, 2)] = dq[g].astype(BF16)
        total = total + dot(low[...], weights[g, :, tile(0, 5)], 1, 1)
        made = dot(turned[...], low[...])
        grads[g, :, tile(0, 4)] = made[:, tile(0, 4)].astype(BF16)
        grads[g, :, tile(4)] = (made[:, tile(4)] + grads_out[g, :, tile(0)]).astype(BF16)
        grads[g, :, tile(5)] = grads_out[g, :, tile(1)].astype(BF16)
    token_grad[...] = total.astype(BF16)


def specs(*spaces):
    return [pl.BlockSpec(memory_space=s) for s in spaces]


def params(**more):
    return pltpu.CompilerParams(vmem_limit_bytes=63 * 2**20, **more)


def run_forward(sizes, lengths, tokens, weights, rows, gathers):
    own, width, groups = sizes.own, sizes.width, sizes.groups
    docs = lengths.shape[1]
    shape = jax.ShapeDtypeStruct
    outs = [
        shape((own, width), BF16),
        shape((docs, width), F32),
        shape((own, width), F32),
        shape((own, 1), F32),
        shape((own, width), F32),
        shape((own, 1), F32),
        shape((groups, own, width), BF16),
        shape((groups, own, width), BF16),
        shape((groups, sizes.window, 3 * LANES), BF16),
        shape((groups, own, 2 * LANES), BF16),
        shape((groups, sizes.blocks, 8, sizes.block), F32),
        shape((groups, own, 2 * LANES), BF16),
    ]
    spaces = [*[VMEM] * 6, ANY, ANY, ANY, *[VMEM] * 3]
    scratch = [
        pltpu.VMEM((sizes.window, width), BF16),
        pltpu.VMEM((3, groups, width, width), BF16),
        pltpu.VMEM((sizes.blocks, sizes.keys, sizes.block), F32),
        pltpu.VMEM((own, width), F32),
        pltpu.VMEM((groups, sizes.window, 3 * LANES), BF16),
        pltpu.VMEM((groups, own, width), BF16),
        pltpu.VMEM((groups, own, width), BF16),
        pltpu.SemaphoreType.DMA((4,)),
    ]
    if gathers:
        outs.insert(0, shape((3, groups, width, width), BF16))
        spaces.insert(0, ANY)
        scratch += [
            pltpu.VMEM((2, weights[0].shape[0], width), BF16),
            pltpu.VMEM((1, 5 * LANES + weights[8].shape[0]), F32),
            pltpu.VMEM((groups, 1, 5 * LANES + weights[8].shape[0]), F32),
            pltpu.SemaphoreType.DMA((3, 31)),
            pltpu.SemaphoreType.DMA((3, 32)),
            pltpu.SemaphoreType.DMA((6,)),
            pltpu.SemaphoreType.DMA((2, 3)),
        ]
        kernel, more = gathering_kernel, {"collective_id": 0, "has_side_effects": True}
    else:
        scratch.append(pltpu.SemaphoreType.DMA((3,)))
        kernel, more = forward_kernel, {}
    return pl.pallas_call(
        functools.partial(kernel, sizes),
        out_shape=outs,
        in_specs=specs(SMEM, ANY, *([VMEM] * 15 if gathers else [ANY, *[VMEM] * 7])),
        out_specs=specs(*spaces),
        scratch_shapes=scratch,
        compiler_params=params(**more),
        name="forward",
    )(lengths, tokens, *weights, *rows)


def run_backward(sizes, lengths, cotangent, dcls, weights, gain_1, shift_1, gain_2, saved):
    own, width, groups = sizes.own, sizes.width, sizes.groups
    shape = jax.ShapeDtypeStruct
    outs = (
        shape((own, width), F32),
        shape((groups, sizes.window, 3 * LANES), F32),
        shape((groups, own, 2 * LANES), F32),
        shape((2, groups, width, width), BF16),
        shape((groups, width, 2 * LANES), F32),
        shape((16, width), F32),
    )
    return pl.pallas_call(
        functools.partial(backward_kernel, sizes),
        out_shape=outs,
        in_specs=specs(SMEM, ANY, VMEM, ANY, *[VMEM] * (3 + len(saved))),
        out_specs=specs(VMEM, VMEM, VMEM, ANY, VMEM, VMEM),
        scratch_shapes=[
            pltpu.VMEM((groups, width, width), BF16),
            pltpu.VMEM((groups, width, width), BF16),
            pltpu.VMEM((groups, width, width), BF16),
            pltpu.VMEM((own, width), BF16),
            pltpu.VMEM((own, width), F32),
            pltpu.VMEM((own, width), BF16),
            pltpu.VMEM((own, width), BF16),
            pltpu.VMEM((2, width, own), BF16),
            pltpu.VMEM((2, width, width), BF16),
            pltpu.VMEM((groups, own, 2 * LANES), BF16),
            pltpu.VMEM((8, own), F32),
            pltpu.VMEM((sizes.blocks, sizes.keys, sizes.block), F32),
            pltpu.SemaphoreType.DMA((4,)),
            pltpu.SemaphoreType.DMA((2,)),
        ],
        compiler_params=params(),
        name="backward",
    )(lengths, cotangent, dcls, weights, gain_1, shift_1, gain_2, *saved)


def run_input(sizes, own_tokens, w_attn, dkv, dq, dh_1, grads_out):
    own, width, groups = sizes.own, sizes.width, sizes.groups
    shape = jax.ShapeDtypeStruct
    outs = (
        shape((own, width), BF16),
        shape((groups, width, width), BF16),
        shape((groups, 1, 5 * LANES), F32),
    )
    return pl.pallas_call(
        functools.partial(input_kernel, sizes),
        out_shape=outs,
        in_specs=specs(*[VMEM] * 6),
        out_specs=specs(*[VMEM] * 3),
        scratch_shapes=[pltpu.VMEM((width, own), BF16), pltpu.VMEM((own, 5 * LANES), BF16)],
        compiler_params=params(),
        name="inputs",
    )(own_tokens, w_attn, dkv, dq, dh_1, grads_out)


def run_finish(sizes, small_in, large_in):
    own, width, groups = sizes.own, sizes.width, sizes.groups
    tokens, passages = large_in[0], large_in[2]
    queries = small_in[2].shape[0]
    ways = queries // 8
    shard = width // ways
    shape = jax.ShapeDtypeStruct
    outs = (
        shape((queries, passages.shape[0]), F32),
        shape((8, 1), F32),
        shape((24, width), F32),
        shape((3, shard, width), F32),
        shape(tokens.shape, BF16),
        shape(tokens.shape, BF16),
    )
    dma = pltpu.SemaphoreType.DMA
    scratch = [
        pltpu.VMEM((groups, width, width), BF16),
        pltpu.VMEM((2, 2, own, width), BF16),
        pltpu.VMEM((10 * width, width), BF16),
        pltpu.VMEM((4, width, width), BF16),
        pltpu.VMEM((3, 8, shard, width), BF16),
        pltpu.VMEM((3, 4, shard, width), BF16),
        pltpu.VMEM((3, 3, shard, width), BF16),
        pltpu.VMEM((2, sizes.window, 3 * LANES), BF16),
        pltpu.VMEM((groups, own, 2 * LANES), BF16),
        pltpu.VMEM((groups, own, 2 * LANES), BF16),
        pltpu.VMEM((groups, own, 2 * LANES), BF16),
        pltpu.VMEM((sizes.window, 3 * LANES), F32),
        pltpu.VMEM((2, own, 3 * LANES), F32),
        pltpu.VMEM((2, 2, LONGEST, 3 * LANES), BF16),
        pltpu.VMEM((groups, 2, LONGEST, 3 * LANES), BF16),
        pltpu.VMEM((own, width), F32),
        pltpu.VMEM((2, own, width), F32),
        pltpu.VMEM((own, width), BF16),
        pltpu.VMEM((own, width), BF16),
        pltpu.VMEM((2, width, own), BF16),
        pltpu.VMEM((2, own, 5 * LANES), BF16),
        pltpu.VMEM((sizes.blocks, sizes.keys, sizes.block), F32),
        pltpu.VMEM((8, own), F32),
        pltpu.VMEM((4, 24, width), F32),
        pltpu.VMEM((6, 24, width), F32),
        pltpu.VMEM((16, width // 2), BF16),
        pltpu.VMEM((3, 16, width // 2), BF16),
        pltpu.VMEM((ways, 16, width // 2), BF16),
        pltpu.VMEM((queries, width), F32),
        pltpu.VMEM((2, ways, 16, width // 2), BF16),
        pltpu.VMEM((2, ways, 16, width // 2), BF16),
        pltpu.VMEM((ways, 8, LANES), F32),
        pltpu.VMEM((ways, 8, LANES), F32),
        dma((10,)),
        dma((2,)),
        dma((2, 4)),
        dma((2, 2, 3)),
        dma((2, 3, 2)),
        dma((2, 3, 8)),
        dma((2, 3, 4)),
        dma((2, 3, 3)),
        dma((2, 4, 2)),
        dma((2, 6)),
        dma((2, 3)),
        dma((4, 2, ways - 1)),
    ]
    return pl.pallas_call(
        functools.partial(finish_kernel, sizes),
        out_shape=outs,
        in_specs=specs(SMEM, *[VMEM] * (len(small_in) - 1), *[ANY] * len(large_in)),
        out_specs=specs(*[VMEM] * 4, ANY, ANY),
        scratch_shapes=scratch,
        compiler_params=params(collective_id=1, has_side_effects=True),
        name="finish",
    )(*small_in, *large_in)


def cut_along(array, dim, devices):
    before, after = (array.shape[:dim], array.shape[dim + 1 :])
    return jnp.moveaxis(array.reshape(*before, devices, -1, *after), dim, 0)


def summed_on_arrival(array, axis, dim):
    pieces = cut_along(array, dim, lax.axis_size(axis))
    arrived = lax.all_to_all(pieces, axis, split_axis=0, concat_axis=0, tiled=True)
    return arrived.astype(F32).sum(axis=0)


def score(cls, passages, gold):
    all_first = lax.all_gather(cls, "dp", axis=0, tiled=True)
    table = dot(all_first, passages, 1, 1)
    peak = lax.pmax(jnp.max(table, axis=1), "dp")
    total = lax.psum(jnp.sum(jnp.exp(table - peak[:, None]), axis=1), "dp")
    own = cls.shape[0]
    lse = lax.dynamic_slice_in_dim(peak + jnp.log(total), lax.axis_index("dp") * own, own)
    soft = jnp.exp(table - peak[:, None]) / total[:, None]
    first = lax.axis_index("dp") * table.shape[1]
    columns = first + jnp.arange(table.shape[1], dtype=jnp.int32)
    target = (gold[:, None] == columns[None, :]).astype(F32)
    grad = dot((soft - target).astype(BF16), passages)
    return table, lse, summed_on_arrival(grad.astype(BF16), "dp", 0)


def plain_layer(sizes, tokens, cotangent, lengths, gold, passages, shards, rows):
    me, groups = lax.axis_index("mp"), sizes.groups
    w_key, w_value, w_query, w_out, w_up, w_down, b_value, b_query, b_up = shards
    packed = jnp.stack(
        [jnp.concatenate([w_key, w_value, w_query, w_out.T], axis=1), w_up, w_down]
    )
    c = w_key.shape[1]
    zeros = jnp.zeros((c,), F32)
    own_bias = jnp.concatenate([zeros, b_value, b_query, zeros[:HEAD], b_up])[None]
    whole = lax.all_gather(lax.all_gather(packed, "dp", axis=1, tiled=True), "mp", axis=1)
    biases = lax.all_gather(own_bias, "mp", axis=0)
    encoded, cls, *saved = run_forward(sizes, lengths, tokens, (whole, biases), rows, False)
    cls = lax.psum(cls, "mp").astype(BF16)
    table, lse, dcls = score(cls, passages, gold)
    n_1, r_1, n_2, r_2, z, slope, kv, q, logs, ctx = saved
    dh_1, dkv, dq, grads_ffn, grads_out, small = run_backward(
        sizes, lengths, cotangent, dcls, whole, rows[1], rows[2], rows[4], saved
    )
    halo, own = LONGEST, sizes.own
    offset = own * me - sizes.window_start(me)
    to_left = lax.dynamic_slice_in_dim(dkv, offset - halo, halo, axis=1).astype(BF16)
    to_right = lax.dynamic_slice_in_dim(dkv, offset + own, halo, axis=1).astype(BF16)
    from_right = lax.ppermute(to_left, "mp", [(i, i - 1) for i in range(1, groups)])
    from_left = lax.ppermute(to_right, "mp", [(i, i + 1) for i in range(groups - 1)])
    dkv = lax.dynamic_slice_in_dim(dkv, offset, own, axis=1)
    dkv = dkv.at[:, own - halo :].add(from_right.astype(F32))
    dkv = dkv.at[:, :halo].add(from_left.astype(F32))
    own_tokens = lax.dynamic_slice_in_dim(tokens, own * me, own, axis=0)
    token_part, grads_attn, small_attn = run_input(
        sizes, own_tokens, whole[0], dkv, dq, dh_1, grads_out
    )
    token_grad = lax.all_gather(token_part, "mp", axis=0, tiled=True).astype(F32)
    encoded = lax.all_gather(encoded, "mp", axis=0, tiled=True)
    grads = jnp.stack([grads_attn, grads_ffn[0], grads_ffn[1]])
    grads = summed_on_arrival(grads, "mp", 1)[:, 0].astype(BF16)
    grads = summed_on_arrival(grads, "dp", 1)
    small, small_attn = lax.psum((small, small_attn), ("dp", "mp"))
    mine = lax.dynamic_index_in_dim(small_attn[:, 0], me, 0, keepdims=False)
    up_bias = lax.dynamic_index_in_dim(small, 8 + me, 0, keepdims=False)
    return (
        table,
        lse,
        encoded,
        token_grad,
        grads[0, :, 2 * c : 3 * c],
        grads[0, :, :c],
        grads[0, :, c : 2 * c],
        mine[2 * c : 3 * c],
        mine[c : 2 * c],
        grads[0, :, 3 * c :].T,
        small[5],
        small[3],
        small[4],
        grads[1],
        up_bias,
        grads[2].T,
        small[2],
        small[0],
        small[1],
    )


def outputs_kernel(cols, table, lse, small, shards, encoded, tokens, *outs):
    *outs, got, wide, passed, sems = outs
    (
        table_out,
        lse_out,
        encoded_out,
        tokens_out,
        g_query,
        g_key,
        g_value,
        gb_query,
        gb_value,
        g_out,
        gb_out,
        g_gain_1,
        g_shift_1,
        g_up,
        gb_up,
        g_down,
        gb_down,
        g_gain_2,
        g_shift_2,
    ) = outs
    steps = got.shape[0]
    rows = [pl.ds(k * got.shape[1], got.shape[1]) for k in range(steps)]
    copies = [pltpu.make_async_copy(tokens.at[rows[k]], got.at[k], sems.at[0, k]) for k in range(steps)]
    writes = [pltpu.make_async_copy(wide.at[k], tokens_out.at[rows[k]], sems.at[1, k]) for k in range(steps)]
    takes = [pltpu.make_async_copy(encoded.at[rows[k]], passed.at[k], sems.at[2, k]) for k in range(steps)]
    gives = [pltpu.make_async_copy(passed.at[k], encoded_out.at[rows[k]], sems.at[3, k]) for k in range(steps)]
    for k in range(steps):
        copies[k].start()
        takes[k].start()
    for k in range(steps):
        copies[k].wait()
        wide[k] = got[k].astype(F32)
        writes[k].start()
        takes[k].wait()
        gives[k].start()
    me = lax.axis_index("mp")
    table_out[...] = table[...]
    lse_out[...] = lse[...].T.reshape(lse_out.shape)
    for k, target in enumerate((g_key, g_value, g_query)):
        target[...] = shards[0, :, k * cols : (k + 1) * cols]
    g_out[...] = shards[0, :, 3 * cols :].T
    g_up[...] = shards[1]
    g_down[...] = shards[2]
    heads = small[pl.ds(16 + me, 1), :]
    gb_value[...] = heads[:, cols : 2 * cols].reshape(gb_value.shape)
    gb_query[...] = heads[:, 2 * cols : 3 * cols].reshape(gb_query.shape)
    gb_up[...] = small[pl.ds(8 + me, 1), :].reshape(gb_up.shape)
    for k, target in enumerate((g_gain_2, g_shift_2, gb_down, g_gain_1, g_shift_1, gb_out)):
        target[...] = small[k : k + 1, :].reshape(target.shape)
    for k in range(steps):
        writes[k].wait()
        gives[k].wait()


def run_outputs(made, cols):
    table, lse, small, shards, encoded, tokens = made
    rows, width = shards.shape[1:]
    shape = jax.ShapeDtypeStruct
    vector = shape((width,), F32)
    outs = (
        shape(table.shape, F32),
        shape((lse.shape[0],), F32),
        shape(encoded.shape, BF16),
        shape(tokens.shape, F32),
        *[shape((rows, cols), F32)] * 3,
        *[shape((cols,), F32)] * 2,
        shape((cols, rows), F32),
        *[vector] * 3,
        shape((rows, width), F32),
        vector,
        shape((rows, width), F32),
        *[vector] * 3,
    )
    steps = 8
    span = tokens.shape[0] // steps
    return pl.pallas_call(
        functools.partial(outputs_kernel, cols),
        out_shape=outs,
        in_specs=specs(*[VMEM] * 4, ANY, ANY),
        out_specs=specs(*[ANY if k in (2, 3) else VMEM for k in range(len(outs))]),
        scratch_shapes=[
            pltpu.VMEM((steps, span, width), BF16),
            pltpu.VMEM((steps, span, width), F32),
            pltpu.VMEM((steps, span, width), BF16),
            pltpu.SemaphoreType.DMA((4, steps)),
        ],
        compiler_params=params(),
        name="outputs",
    )(*made)


def body(
    tokens,
    cotangent,
    lengths,
    gold,
    passages,
    w_query,
    w_key,
    w_value,
    b_query,
    b_value,
    w_out,
    b_out,
    gain_attn,
    shift_attn,
    w_up,
    b_up,
    w_down,
    b_down,
    gain_ffn,
    shift_ffn,
):
    groups = lax.axis_size("mp")
    sizes = Sizes(tokens.shape[0], tokens.shape[1], groups)
    rows = (b_out, gain_attn, shift_attn, b_down, gain_ffn, shift_ffn)
    shards = (w_key, w_value, w_query, w_out, w_up, w_down.T, b_value, b_query, b_up)
    if lax.axis_size("dp") == 8 and groups == 4:
        whole, encoded, cls, n_1, r_1, n_2, r_2, z, slope, kv, q, logs, ctx = run_forward(
            sizes, lengths, tokens, shards, rows, True
        )
        made = run_finish(
            sizes,
            (lengths, cls, gold, gain_attn, shift_attn, gain_ffn, r_1, r_2, logs),
            (tokens, cotangent, passages, encoded, whole, n_1, n_2, z, slope, kv, q, ctx),
        )
        outs = list(run_outputs(made, w_key.shape[1]))
        outs[15] = outs[15].T
        return tuple(outs)
    return plain_layer(sizes, tokens, cotangent, lengths, gold, passages, shards, rows)


def solution(mesh):
    by_dp, shared, cross = P("dp", None), P(), P("dp", "mp")
    return jax.shard_map(
        body,
        mesh=mesh,
        in_specs=(
            by_dp,
            by_dp,
            by_dp,
            shared,
            by_dp,
            cross,
            cross,
            cross,
            P("mp"),
            P("mp"),
            P("mp", "dp"),
            shared,
            shared,
            shared,
            cross,
            P("mp"),
            P("mp", "dp"),
            shared,
            shared,
            shared,
        ),
        out_specs=(
            P(None, "dp"),
            P("dp"),
            by_dp,
            by_dp,
            cross,
            cross,
            cross,
            P("mp"),
            P("mp"),
            P("mp", "dp"),
            shared,
            shared,
            shared,
            cross,
            P("mp"),
            P("mp", "dp"),
            shared,
            shared,
            shared,
        ),
        check_vma=False,
    )
```

```python
import functools

import jax
import jax.numpy as jnp
from jax import lax
from jax.experimental import pallas as pl
from jax.experimental.pallas import tpu as pltpu
from jax.sharding import PartitionSpec as P

HEAD = 64
LONGEST = 400
QUERY_BLOCK = 256
EPSILON = 1e-05
NEGATIVE = -1e30
LANES = 128
KEY_AT = ((0, 0), (0, 1), (1, 0))
VALUE_AT = ((1, 1), (2, 0), (2, 1))
QUERY_AT = ((0, 0), (0, 1), (1, 0))
CONTEXT_AT = ((0, 1), (1, 0), (1, 1))
F32, BF16 = jnp.float32, jnp.bfloat16
VMEM, ANY, SMEM = pltpu.VMEM, pl.ANY, pltpu.SMEM


def dot(left, right, left_dim=1, right_dim=0):
    return lax.dot_general(
        left, right, (((left_dim,), (right_dim,)), ((), ())), preferred_element_type=F32
    )


def tile(index, count=1):
    return slice(index * LANES, (index + count) * LANES)


def half_mask(half, dtype):
    lane = lax.broadcasted_iota(jnp.int32, (1, LANES), 1)
    return jnp.where((lane >= HEAD) == (half == 1), 1.0, 0.0).astype(dtype)


def norm_stats(hidden):
    centred = hidden - jnp.mean(hidden, axis=-1, keepdims=True)
    factor = lax.rsqrt(jnp.mean(centred * centred, axis=-1, keepdims=True) + EPSILON)
    return centred * factor, factor


def norm_back(grad_out, normed, factor, gain):
    scaled = grad_out * gain
    inner = jnp.mean(scaled * normed, axis=-1, keepdims=True)
    return factor * (scaled - jnp.mean(scaled, axis=-1, keepdims=True) - normed * inner)


def gelu_and_slope(a):
    size = jnp.abs(a)
    t = 1.0 / (1.0 + (0.3275911 * 0.7071067811865476) * size)
    bell = jnp.exp(-0.5 * a * a)
    poly = t * (
        0.127414796 + t * (-0.142248368 + t * (0.7107068705 + t * (-0.7265760135 + t * 0.5307027145)))
    )
    tail = poly * bell
    phi = jnp.where(a >= 0.0, 1.0 - tail, tail)
    return a * phi, phi + a * bell * 0.3989422804014327


def as_row(ref):
    return ref[...].reshape(1, ref.shape[0])


class Sizes:
    def __init__(self, length, width, groups):
        self.length, self.width, self.groups = length, width, groups
        self.own = length // groups
        self.window = min(length, self.own + 2 * LONGEST)
        self.block = min(QUERY_BLOCK, self.own)
        self.blocks = self.own // self.block
        self.keys = min(length, self.block + 2 * LONGEST)

    def window_start(self, me):
        return jnp.clip(self.own * me - LONGEST, 0, self.length - self.window)

    def own_offset(self, me):
        return pl.multiple_of(self.own * me - self.window_start(me), 16)

    def key_start(self, me, block):
        first = self.own * me + block * self.block
        return jnp.clip(first - LONGEST, 0, self.length - self.keys)

    def key_offset(self, me, block):
        return pl.multiple_of(self.key_start(me, block) - self.window_start(me), 16)


def document_bounds(lens, places):
    start = jnp.zeros_like(places)
    end = jnp.zeros_like(places)
    total = jnp.int32(0)
    for d in range(lens.shape[1]):
        count = lens[0, d]
        end = end + jnp.where(places >= total, count, 0)
        total = total + count
        start = start + jnp.where(places >= total, count, 0)
    return start, end


def fill_mask(sizes, me, lens, bias):
    for b in range(sizes.blocks):
        places = (
            sizes.own * me
            + b * sizes.block
            + lax.broadcasted_iota(jnp.int32, (1, sizes.block), 1)
        )
        start, end = document_bounds(lens, places)
        keys = sizes.key_start(me, b) + lax.broadcasted_iota(
            jnp.int32, (sizes.keys, sizes.block), 0
        )
        bias[b] = jnp.where((keys >= start) & (keys < end), 0.0, NEGATIVE)


def start_rows(sizes, me, lens):
    docs = lens.shape[1]
    row = lax.broadcasted_iota(jnp.int32, (docs, sizes.own), 0)
    place = sizes.own * me + lax.broadcasted_iota(jnp.int32, (docs, sizes.own), 1)
    picked = jnp.zeros((docs, sizes.own), F32)
    total = jnp.int32(0)
    for d in range(docs):
        picked = jnp.where((row == d) & (place == total), 1.0, picked)
        total = total + lens[0, d]
    return picked


def project(sizes, me, group, span, tokens, w_attn, biases, kv, q):
    cut = sizes.window // 2
    own = pl.ds(sizes.own_offset(me), sizes.own)

    @pl.loop(*span)
    def _(i):
        g = group(i)
        for part in range(2):
            rows = pl.ds(part * cut, cut)
            made = dot(tokens[rows, :], w_attn[g, :, tile(0, 3)]) + biases[g, :, tile(0, 3)]
            kv[g, rows, :] = made.astype(BF16)
        made = dot(tokens[own, :], w_attn[g, :, tile(3, 2)]) + biases[g, :, tile(3, 2)]
        q[g] = made.astype(BF16) * jnp.asarray(HEAD**-0.5, BF16)


def attend(sizes, me, group, span, tick, kv, q, bias, lse, ctx):
    @pl.loop(*span)
    def _(i):
        g = group(i)

        @pl.loop(0, sizes.blocks)
        def _(b):
            tick(i * sizes.blocks + b)
            keys = pl.ds(sizes.key_offset(me, b), sizes.keys)
            rows = pl.ds(pl.multiple_of(b * sizes.block, sizes.block), sizes.block)
            made = [jnp.zeros((HEAD, sizes.block), F32)]
            logs = []
            for j in range(3):
                kt, kh = KEY_AT[j]
                vt, vh = VALUE_AT[j]
                qt, _ = QUERY_AT[j]
                query = q[g, rows, tile(qt)] * half_mask(kh, BF16)
                s = dot(kv[g, keys, tile(kt)], query, 1, 1) + bias[b]
                peak = jnp.max(s, axis=0, keepdims=True)
                e = jnp.exp(s - peak)
                total = jnp.sum(e, axis=0, keepdims=True)
                mixed = dot(kv[g, keys, tile(vt)], e.astype(BF16), 0, 0)
                made.append(mixed[vh * HEAD : (vh + 1) * HEAD] / total)
                logs.append(peak + jnp.log(total))
            ctx[g, rows, :] = jnp.concatenate(made, axis=0).T.astype(BF16)
            for j in range(3):
                lse[g, b, j : j + 1, :] = logs[j]


def delta_rows(dctx, ctx):
    lane = lax.broadcasted_iota(jnp.int32, (8, 2 * LANES), 1)
    row = lax.broadcasted_iota(jnp.int32, (8, 2 * LANES), 0)
    pick = jnp.where(lane // HEAD == row + 1, 1.0, 0.0).astype(BF16)
    product = dctx.astype(F32) * ctx.astype(F32)
    high = product.astype(BF16)
    low = (product - high.astype(F32)).astype(BF16)
    return dot(pick, high, 1, 1) + dot(pick, low, 1, 1)


def attend_back_block(sizes, me, g, b, kv, q, bias, lse, dctx, delta, dkv):
    keys = pl.ds(sizes.key_offset(me, b), sizes.keys)
    rows = slice(b * sizes.block, (b + 1) * sizes.block)
    made = []
    for j in range(3):
        kt, kh = KEY_AT[j]
        vt, vh = VALUE_AT[j]
        qt, _ = QUERY_AT[j]
        ct, _ = CONTEXT_AT[j]
        query = q[g, rows, tile(qt)] * half_mask(kh, BF16)
        grad = dctx[g, rows, tile(ct)] * half_mask(vh, BF16)
        s = dot(kv[keys, tile(kt)], query, 1, 1) + bias[b]
        p = jnp.exp(s - lse[g, b, j : j + 1, :])
        dp = dot(kv[keys, tile(vt)], grad, 1, 1)
        ds = (p * (dp - delta[j : j + 1, rows])).astype(BF16)
        dkv[keys, tile(kt)] += dot(ds, query)
        dkv[keys, tile(vt)] += dot(p.astype(BF16), grad)
        back = dot(kv[keys, tile(kt)], ds, 0, 0)
        made.append(back[kh * HEAD : (kh + 1) * HEAD] * HEAD**-0.5)
    made.append(jnp.zeros((HEAD, sizes.block), F32))
    return jnp.concatenate(made, axis=0).T


def attend_back(sizes, me, kv, q, bias, lse, ctx, dctx, delta, dkv, dq):
    @pl.loop(0, sizes.groups)
    def _(g):
        delta[...] = delta_rows(dctx[g], ctx[g])
        dkv[g] = jnp.zeros_like(dkv[g])
        for b in range(sizes.blocks):
            rows = slice(b * sizes.block, (b + 1) * sizes.block)
            dq[g, rows, :] = attend_back_block(
                sizes, me, g, b, kv.at[g], q, bias, lse, dctx, delta, dkv.at[g]
            )


class Loads:
    def __init__(self, weights, w, sems):
        self.copies = [pltpu.make_async_copy(weights.at[s], w.at[s], sems.at[s]) for s in range(3)]

    def begin(self):
        for copy in self.copies:
            copy.start()

    def group(self, i):
        return i

    def near_heads(self):
        self.copies[0].wait()

    def far_heads(self):
        pass

    def ready(self, section):
        self.copies[section].wait()

    def group_ready(self, section, i):
        pass

    def done(self, section):
        pass

    def tick(self, step):
        pass

    def end(self):
        pass


MESH = pl.DeviceIdType.MESH


class Route:
    def __init__(self, at, turn):
        flip, x_peer = 1 - turn, 2 * at.z + 1 - at.x
        near = at.mp + turn * (at.across - at.mp)
        far = at.mp + flip * (at.across - at.mp)
        self.first = (at.dp + flip * (x_peer - at.dp), near)
        self.second = (at.dp + turn * (x_peer - at.dp), far)
        self.first_column = (near, at.x + flip * (1 - 2 * at.x))
        self.second_columns = ((far, at.x + turn * (1 - 2 * at.x)), (at.across, 1 - at.x))


class Place:
    def __init__(self):
        self.dp, self.mp = lax.axis_index("dp"), lax.axis_index("mp")
        self.z, self.x, self.y, self.core = self.dp // 2, self.dp % 2, self.mp // 2, self.mp % 2
        flip = 1 - self.core
        self.across = 2 * (1 - self.y) + self.core
        self.sibling = (self.dp, 2 * self.y + flip)
        self.x_peer = (2 * self.z + 1 - self.x, self.mp)
        self.y_peer = (self.dp, self.across)
        self.diagonal = (self.dp, 2 * (1 - self.y) + flip)
        self.zs = [self.z, self.z + 1 - 2 * (self.z % 2), (self.z + 2) % 4, 3 - self.z]
        self.line = [(2 * z + self.x, self.mp) for z in self.zs]
        self.by_core = Route(self, self.core)
        self.x_first, self.y_first = Route(self, 0), Route(self, 1)
        self.own_column = (self.mp, self.x)
        self.peers = [*self.line[1:], self.x_peer, self.y_peer, self.sibling, self.diagonal]


def signal(peers):
    barrier = pltpu.get_barrier_semaphore()
    for peer in peers:
        pl.semaphore_signal(barrier, inc=1, device_id=peer, device_id_type=MESH)


def arrive(peers):
    pl.semaphore_wait(pltpu.get_barrier_semaphore(), len(peers))


GATHER_STEPS = {
    "begin": (("along", 0), ("out", 0), ("out", 1), ("out", 2)),
    "near": (("z", 0, 1, 2, 3), ("along", 1), ("first", 0, 0, 1, 2, 3)),
    0: (("z", 1, 1, 2, 3), ("along", 2)),
    1: (("second", 0, 0, 1, 2, 3),),
    2: (("first", 1, 0, 1), ("second", 0, 4, 5)),
    3: (("first", 1, 2, 3), ("second", 0, 6, 7)),
    4: (("z", 2, 1, 2, 3),),
    5: (("second", 1, 0, 1, 2, 3),),
    6: (("second", 1, 4, 5, 6, 7),),
    7: (("first", 2, 0, 1),),
    8: (("first", 2, 2, 3),),
    9: (("second", 2, 0, 1, 2, 3, 4, 5, 6, 7),),
}


class Gather:
    ROUTES = ("x_first", "by_core", "by_core")
    Z_LATER = (False, False, False)

    def __init__(self, place, packed, own_bias, w, biases, kept, send, recv, local, bias_sems):
        self.at, self.packed, self.w, self.kept = place, packed, w, kept
        self.own_bias, self.biases = own_bias, biases
        self.send_sems, self.recv_sems, self.local, self.bias_sems = send, recv, local, bias_sems
        self.rows = packed[1].shape[0]
        self.shards = w.shape[2] // self.rows
        self.routes = [getattr(place, name) for name in self.ROUTES]

    def shard(self, s, g, d):
        return self.w.at[s, g, pl.ds(pl.multiple_of(d * self.rows, 16), self.rows)]

    def copy(self, s, g, d, slot, peer, source=None):
        here = self.shard(s, g, d)
        return pltpu.make_async_remote_copy(
            src_ref=here if source is None else source,
            dst_ref=here,
            send_sem=self.send_sems.at[s, slot],
            recv_sem=self.recv_sems.at[s, g * self.shards + d],
            device_id=peer,
            device_id_type=MESH,
        )

    def arrived(self, s, g, d):
        self.copy(s, g, d, 0, self.at.sibling).wait_recv()

    def own_copy(self, s):
        return pltpu.make_async_copy(
            self.packed[s], self.shard(s, self.at.mp, self.at.dp), self.local.at[s]
        )

    def along_z(self, s):
        at = self.at
        for k in range(1, 4):
            self.copy(s, at.mp, at.dp, k - 1, at.line[k], self.packed[s]).start()

    def own_out(self, s):
        at = self.at
        self.own_copy(s).start()
        source = self.packed[s]
        self.copy(s, at.mp, at.dp, 3, self.routes[s].first, source).start()
        self.copy(s, at.mp, at.dp, 7, self.routes[s].second, source).start()
        self.copy(s, at.mp, at.dp, 15, at.sibling, source).start()

    def from_z(self, s, k):
        at, (g, x) = self.at, self.at.own_column
        d = 2 * at.zs[k] + x
        self.arrived(s, g, d)
        if not self.Z_LATER[s]:
            self.copy(s, g, d, 3 + k, self.routes[s].first).start()
        self.copy(s, g, d, 7 + k, self.routes[s].second).start()
        self.copy(s, g, d, 15 + k, at.sibling).start()

    def from_first(self, s, k):
        at, (g, x) = self.at, self.routes[s].first_column
        d = 2 * at.zs[k] + x
        self.arrived(s, g, d)
        if self.Z_LATER[s] and k == 0:
            for j in range(1, 4):
                self.copy(s, g, d, 3 + j, at.line[j]).start()
        self.copy(s, g, d, 11 + k, self.routes[s].second).start()
        self.copy(s, g, d, 19 + k, at.sibling).start()

    def from_second(self, s, k):
        at, (g, x) = self.at, self.routes[s].second_columns[k // 4]
        d = 2 * at.zs[k % 4] + x
        self.arrived(s, g, d)
        self.copy(s, g, d, 23 + k, at.sibling).start()

    def group(self, i):
        at = self.at
        return 2 * (at.y + (i // 2) * (1 - 2 * at.y)) + at.core + (i % 2) * (1 - 2 * at.core)

    def from_sibling(self, s, g):
        @pl.loop(0, self.shards)
        def _(d):
            self.arrived(s, g, d)

    def keep(self, s):
        return pltpu.make_async_copy(self.w.at[s], self.kept.at[s], self.local.at[3 + s])

    def bias_copy(self, k, peer):
        return pltpu.make_async_remote_copy(
            src_ref=self.own_bias,
            dst_ref=self.biases.at[self.at.mp],
            send_sem=self.bias_sems.at[0, k],
            recv_sem=self.bias_sems.at[1, k],
            device_id=peer,
            device_id_type=MESH,
        )

    def bias_copies(self):
        at = self.at
        across = (at.dp, at.across)
        return [self.bias_copy(k, peer) for k, peer in enumerate((at.sibling, across, at.diagonal))]

    def begin(self):
        signal(self.at.peers)
        self.fill()
        arrive(self.at.peers)
        self.steps("begin")
        for copy in self.bias_copies():
            copy.start()
        self.biases[self.at.mp] = self.own_bias[...]

    def near_heads(self):
        self.steps("near")
        for copy in self.bias_copies():
            copy.wait_recv()
        self.own_copy(0).wait()
        self.from_sibling(0, self.group(1))

    def far_heads(self):
        self.steps("far")
        self.from_sibling(0, self.group(3))
        self.keep(0).start()

    def ready(self, section):
        self.steps(7 + section)
        self.own_copy(section).wait()
        if section == 1:
            for i in (1, 3):
                self.group_ready(1, i)
            self.done(1)

    def group_ready(self, section, i):
        if isinstance(i, int):
            self.from_sibling(section, self.group(i))
        else:
            pl.when(i % 2 == 1)(lambda: self.from_sibling(section, self.group(i)))

    def done(self, section):
        self.keep(section).start()

    def steps(self, step):
        actions = {
            "along": lambda s, k: self.along_z(s),
            "out": lambda s, k: self.own_out(s),
            "z": self.from_z,
            "first": self.from_first,
            "second": self.from_second,
        }
        for name, s, *ks in GATHER_STEPS.get(step, ()):
            for k in ks or (0,):
                actions[name](s, k)

    def tick(self, step):
        for k in range(8):
            pl.when(step == k)(functools.partial(self.steps, k))

    def end(self):
        for copy in self.bias_copies():
            copy.wait_send()
        for s in range(3):

            @pl.loop(0, 31)
            def _(slot):
                self.copy(s, 0, 0, slot, self.at.sibling).wait_send()

            self.keep(s).wait()


def forward_math(
    sizes,
    source,
    lens,
    tokens,
    biases,
    b_out,
    gain_1,
    shift_1,
    b_down,
    gain_2,
    shift_2,
    encoded,
    cls,
    n_1,
    r_1,
    n_2,
    r_2,
    z_out,
    slope_out,
    kv_out,
    q,
    lse,
    ctx,
    x,
    w,
    bias,
    hidden,
    kv,
    z,
    slope,
    sems,
):
    me = lax.axis_index("mp")
    first = pl.multiple_of(sizes.window_start(me), 16)
    load = pltpu.make_async_copy(tokens.at[pl.ds(first, sizes.window)], x, sems.at[0])
    load.start()
    source.begin()
    fill_mask(sizes, me, lens, bias)
    load.wait()
    save_kv = pltpu.make_async_copy(kv, kv_out, sems.at[1])
    half = sizes.groups // 2
    for span, ready in (((0, half), source.near_heads), ((half, sizes.groups), source.far_heads)):
        ready()
        project(sizes, me, source.group, span, x, w.at[0], biases, kv, q)
        if span[1] == sizes.groups:
            save_kv.start()
        attend(sizes, me, source.group, span, source.tick, kv, q, bias, lse, ctx)

    own = pl.ds(sizes.own_offset(me), sizes.own)
    hidden[...] = x[own, :].astype(F32) + as_row(b_out)
    for g in range(sizes.groups):
        hidden[...] += dot(ctx[g], w[0, g, :, tile(4, 2)], 1, 1)
    normed, factor = norm_stats(hidden[...])
    n_1[...] = normed
    r_1[...] = factor
    y_1 = normed * as_row(gain_1) + as_row(shift_1)
    hidden[...] = y_1 + as_row(b_down)
    encoded[...] = y_1.astype(BF16)
    source.ready(1)

    @pl.loop(0, sizes.groups)
    def _(g):
        a = dot(encoded[...], w[1, g]) + biases[g, :, 5 * LANES :]
        out, grad = gelu_and_slope(a)
        z[g] = out.astype(BF16)
        slope[g] = grad.astype(BF16)

    save_z = pltpu.make_async_copy(z, z_out, sems.at[2])
    save_slope = pltpu.make_async_copy(slope, slope_out, sems.at[3])
    save_z.start()
    save_slope.start()
    source.ready(2)

    @pl.loop(0, sizes.groups)
    def _(i):
        g = source.group(i)
        source.group_ready(2, i)
        hidden[...] += dot(z[g], w[2, g], 1, 1)

    source.done(2)

    normed, factor = norm_stats(hidden[...])
    n_2[...] = normed
    r_2[...] = factor
    y_2 = (normed * as_row(gain_2) + as_row(shift_2)).astype(BF16)
    encoded[...] = y_2
    cls[...] = dot(start_rows(sizes, me, lens).astype(BF16), y_2)
    source.end()
    save_kv.wait()
    save_z.wait()
    save_slope.wait()


def forward_kernel(sizes, lens, tokens, weights, biases, *rest):
    *refs, w, bias, hidden, kv, z, slope, sems, loads = rest
    source = Loads(weights, w, loads)
    forward_math(sizes, source, lens, tokens, biases, *refs, w, bias, hidden, kv, z, slope, sems)


def pack(w_key, w_value, w_query, w_out, w_down, b_value, b_query, b_up, packed, own_bias):
    cols = w_key.shape[1]
    for k, weight in enumerate((w_key, w_value, w_query)):
        packed[0, :, k * cols : (k + 1) * cols] = weight[...]
    packed[0, :, 3 * cols :] = w_out[...].astype(F32).T.astype(BF16)
    packed[1] = w_down[...]
    own_bias[...] = jnp.zeros_like(own_bias)
    own_bias[:, cols : 2 * cols] = as_row(b_value)
    own_bias[:, 2 * cols : 3 * cols] = as_row(b_query)
    own_bias[:, 5 * LANES :] = as_row(b_up)


def gathering_kernel(sizes, lens, tokens, *rest):
    shards, rows, (kept, *outs) = rest[:9], rest[9:15], rest[15:]
    *refs, w, bias, hidden, kv, z, slope, sems, packed, own_bias, biases, send, recv, local, bias_sems = outs
    w_key, w_value, w_query, w_out, w_up, w_down, b_value, b_query, b_up = shards

    def fill():
        pack(w_key, w_value, w_query, w_out, w_down, b_value, b_query, b_up, packed, own_bias)

    source = Gather(
        Place(), (packed.at[0], w_up, packed.at[1]), own_bias, w, biases, kept, send, recv, local, bias_sems
    )
    source.fill = fill
    forward_math(
        sizes, source, lens, tokens, biases, *rows, *refs, w, bias, hidden, kv, z, slope, sems
    )


def backward_kernel(
    sizes,
    lens,
    cotangent,
    dcls,
    weights,
    gain_1,
    shift_1,
    gain_2,
    n_1,
    r_1,
    n_2,
    r_2,
    z,
    slope,
    kv,
    q,
    lse,
    ctx,
    dh_1,
    dkv,
    dq,
    grads,
    grads_out,
    small,
    w_attn,
    w_up,
    w_down,
    cot,
    dh,
    low,
    other,
    turned,
    stage,
    dctx,
    delta,
    bias,
    sems,
    out_sems,
):
    me = lax.axis_index("mp")
    load_cot = pltpu.make_async_copy(
        cotangent.at[pl.ds(pl.multiple_of(sizes.own * me, 16), sizes.own)], cot, sems.at[3]
    )
    load_cot.start()
    loads = []
    for s, buffer in ((2, w_down), (1, w_up), (0, w_attn)):
        loads.append(pltpu.make_async_copy(weights.at[s], buffer, sems.at[s]))
        loads[-1].start()
    fill_mask(sizes, me, lens, bias)
    picked = start_rows(sizes, me, lens).astype(BF16)
    high = dcls[...].astype(BF16)
    low_part = (dcls[...] - high.astype(F32)).astype(BF16)
    load_cot.wait()
    dy = cot[...].astype(F32) + dot(picked, high, 0, 0) + dot(picked, low_part, 0, 0)
    small[0:1, :] = jnp.sum(dy * n_2[...], axis=0, keepdims=True)
    small[1:2, :] = jnp.sum(dy, axis=0, keepdims=True)
    grad = norm_back(dy, n_2[...], r_2[...], as_row(gain_2))
    small[2:3, :] = jnp.sum(grad, axis=0, keepdims=True)
    dh[...] = grad
    low[...] = grad.astype(BF16)
    turned[0] = grad.T.astype(BF16)
    y_1 = n_1[...] * as_row(gain_1) + as_row(shift_1)
    other[...] = y_1.astype(BF16)
    turned[1] = y_1.T.astype(BF16)
    for load in loads:
        load.wait()

    def out_copy(section, g, slot):
        return pltpu.make_async_copy(
            stage.at[slot], grads.at[section, g], out_sems.at[slot]
        )

    @pl.loop(0, sizes.groups)
    def _(g):
        @pl.when(g > 0)
        def _():
            out_copy(1, 0, 0).wait()
            out_copy(1, 0, 1).wait()

        stage[1] = dot(turned[0], z[g]).astype(BF16)
        out_copy(1, g, 1).start()
        da = dot(low[...], w_down[g]) * slope[g].astype(F32)
        small[pl.ds(8 + g, 1), :] = jnp.sum(da, axis=0, keepdims=True)
        da_low = da.astype(BF16)
        stage[0] = dot(turned[1], da_low).astype(BF16)
        out_copy(0, g, 0).start()
        dh[...] += dot(da_low, w_up[g], 1, 1)

    dy = dh[...]
    small[3:4, :] = jnp.sum(dy * n_1[...], axis=0, keepdims=True)
    small[4:5, :] = jnp.sum(dy, axis=0, keepdims=True)
    grad = norm_back(dy, n_1[...], r_1[...], as_row(gain_1))
    small[5:6, :] = jnp.sum(grad, axis=0, keepdims=True)
    small[6:8, :] = jnp.zeros_like(small[6:8, :])
    small[12:16, :] = jnp.zeros_like(small[12:16, :])
    dh_1[...] = grad
    low[...] = grad.astype(BF16)
    turned[0] = grad.T.astype(BF16)

    @pl.loop(0, sizes.groups)
    def _(g):
        dctx[g] = dot(low[...], w_attn[g, :, tile(4, 2)]).astype(BF16)
        grads_out[g] = dot(turned[0], ctx[g])

    attend_back(sizes, me, kv, q, bias, lse, ctx, dctx, delta, dkv, dq)
    out_copy(1, 0, 0).wait()
    out_copy(1, 0, 1).wait()


def remote(source, target, send, recv, peer):
    return pltpu.make_async_remote_copy(
        src_ref=source,
        dst_ref=target,
        send_sem=send,
        recv_sem=recv,
        device_id=peer,
        device_id_type=MESH,
    )


def square(parts, index):
    side = parts.shape[1]
    return parts.at[pl.ds(pl.multiple_of(index * side, side), side)]


class Spread:
    def __init__(self, place, source, whole, send, recv, local):
        self.at, self.source, self.whole = place, source, whole
        self.send, self.recv, self.local = send, recv, local
        self.count = source.shape[0]

    def rows(self, mp):
        return self.whole.at[pl.ds(pl.multiple_of(mp * self.count, 16), self.count)]

    def copy(self, k):
        at = self.at
        target = self.rows(at.across if k == 2 else at.mp)
        source = target if k == 2 else self.source
        peer = (at.dp, at.across) if k == 1 else at.sibling
        return remote(source, target, self.send.at[k], self.recv.at[k], peer)

    def own(self):
        return pltpu.make_async_copy(self.source, self.rows(self.at.mp), self.local)

    def begin(self):
        self.copy(1).start()
        self.copy(0).start()
        self.own().start()

    def forward(self):
        self.copy(1).wait_recv()
        self.copy(2).start()

    def end(self):
        self.copy(0).wait()
        self.copy(1).wait_send()
        self.copy(2).wait()
        self.own().wait()


DURING = {
    0: (("encoded", 0),),
    2: (("second", 2),),
    5: (("first", 2),),
    7: (("second", 1),),
}
BEFORE_LAST = (("line", 2),)
AFTER_LAST = (
    ("begin", 0),
    ("chip", 0),
    ("small", 0),
    ("first", 1),
    ("small", 1),
    ("tokens", 0),
    ("second", 0),
    ("small", 2),
    ("line", 1),
    ("first", 0),
    ("relay", 0),
    ("line", 0),
)


class Scatter:
    STAGE = (0, 2, 0)
    HELD = (8, 6, 4)
    ROUTES = ("by_core", "by_core", "by_core")
    Z_EARLY = ((1,), (1,), (1,))

    def __init__(self, place, parts, inbox, by_second, by_first, by_line, shards, sems):
        self.at, self.parts, self.inbox, self.shards = place, parts, inbox, shards
        self.by_second, self.by_first, self.by_line = by_second, by_first, by_line
        self.core_sems, self.second_sems, self.first_sems, self.line_sems = sems
        self.rows = shards.shape[1]
        self.routes = [getattr(place, name) for name in self.ROUTES]

    def shard(self, s, g, d):
        first = (self.HELD[s] + g // 2) * self.parts.shape[1] + d * self.rows
        return self.parts.at[pl.ds(pl.multiple_of(first, 16), self.rows)]

    def part(self, index):
        return square(self.parts, index)

    def to_sibling(self, s, k):
        at = self.STAGE[s] + k
        return remote(
            self.part(at),
            self.inbox.at[at],
            self.core_sems.at[0, s, k],
            self.core_sems.at[1, s, k],
            self.at.sibling,
        )

    def to_second(self, s, k):
        g, x = self.routes[s].second_columns[1 - k // 4]
        return remote(
            self.shard(s, g, 2 * self.at.zs[3 - k % 4] + x),
            self.by_second.at[s, k],
            self.second_sems.at[0, s, k],
            self.second_sems.at[1, s, k],
            self.routes[s].second,
        )

    def to_first(self, s, k):
        g, x = self.routes[s].first_column
        return remote(
            self.shard(s, g, 2 * self.at.zs[3 - k] + x),
            self.by_first.at[s, k],
            self.first_sems.at[0, s, k],
            self.first_sems.at[1, s, k],
            self.routes[s].first,
        )

    def to_line(self, s, j):
        at = self.at
        return remote(
            self.shard(s, at.mp, 2 * at.zs[j] + at.x),
            self.by_line.at[s, j - 1],
            self.line_sems.at[0, s, j - 1],
            self.line_sems.at[1, s, j - 1],
            at.line[j],
        )

    def chip_shard(self, s, g, z, x):
        d = 2 * z + x
        rows = pl.ds(pl.multiple_of(d * self.rows, 16), self.rows)
        self.shard(s, g, d)[...] += self.inbox[self.STAGE[s] + g // 2, rows]

    def chip_sum(self, s):
        for k in range(2):
            self.to_sibling(s, k).wait_recv()
        for k in range(8):
            g, x = self.routes[s].second_columns[1 - k // 4]
            self.chip_shard(s, g, self.at.zs[3 - k % 4], x)
            self.to_second(s, k).start()
        for g, x in (self.routes[s].first_column, self.at.own_column):

            @pl.loop(0, 4)
            def _(z):
                self.chip_shard(s, g, z, x)

    def other_line(self, s, j):
        g, x = self.routes[s].first_column
        return remote(
            self.shard(s, g, 2 * self.at.zs[j] + x),
            self.by_first.at[s, j],
            self.first_sems.at[0, s, j],
            self.first_sems.at[1, s, j],
            self.at.line[j],
        )

    def last_cross(self, s):
        g, x = self.routes[s].first_column
        return remote(
            self.shard(s, g, 2 * self.at.z + x),
            self.by_first.at[s, 0],
            self.first_sems.at[0, s, 0],
            self.first_sems.at[1, s, 0],
            self.routes[s].first,
        )

    def by_kind(self, s, early, late):
        cores = self.Z_EARLY[s]
        if len(cores) == 1:
            pl.when(self.at.core == cores[0])(functools.partial(early, s))
            pl.when(self.at.core != cores[0])(functools.partial(late, s))
        else:
            (early if cores else late)(s)

    def from_second(self, s):
        self.by_kind(s, self.from_second_early, self.from_second_late)

    def from_first(self, s):
        self.by_kind(s, self.from_first_early, self.from_first_late)

    def from_line(self, s):
        self.by_kind(s, self.from_line_early, self.from_line_late)

    def from_second_early(self, s):
        at, (g, x) = self.at, self.routes[s].first_column
        for k in range(8):
            self.to_second(s, k).wait_recv()
            j = 3 - k % 4
            mine = self.shard(s, g, 2 * at.zs[j] + x) if k < 4 else self.shard(s, at.mp, 2 * at.zs[j] + at.x)
            if k < 7:
                mine[...] += self.by_second[s, k]
            if j:
                (self.other_line if k < 4 else self.to_line)(s, j).start()

    def from_first_early(self, s):
        g, x = self.routes[s].first_column
        mine = self.shard(s, g, 2 * self.at.z + x)
        total = mine[...].astype(F32)
        for j in (1, 2, 3):
            self.other_line(s, j).wait_recv()
            total = total + self.by_first[s, j].astype(F32)
        mine[...] = total.astype(BF16)
        self.last_cross(s).start()

    def from_line_early(self, s):
        at = self.at
        mine = self.shard(s, at.mp, 2 * at.z + at.x)
        total = mine[...].astype(F32) + self.by_second[s, 7].astype(F32)
        for j in range(1, 4):
            self.to_line(s, j).wait_recv()
            total = total + self.by_line[s, j - 1].astype(F32)
        self.last_cross(s).wait_recv()
        self.shards[s] = total + self.by_first[s, 0].astype(F32)

    def from_second_late(self, s):
        g, x = self.routes[s].first_column
        for k in range(4):
            self.to_second(s, k).wait_recv()
            self.shard(s, g, 2 * self.at.zs[3 - k] + x)[...] += self.by_second[s, k]
            self.to_first(s, k).start()

    def from_first_late(self, s):
        at = self.at
        for k in range(4):
            self.to_second(s, 4 + k).wait_recv()
            self.to_first(s, k).wait_recv()
            mine = self.shard(s, at.mp, 2 * at.zs[3 - k] + at.x)
            total = (
                mine[...].astype(F32)
                + self.by_second[s, 4 + k].astype(F32)
                + self.by_first[s, k].astype(F32)
            )
            if k < 3:
                mine[...] = total.astype(BF16)
                self.to_line(s, 3 - k).start()
            else:
                self.shards[s] = total

    def from_line_late(self, s):
        for j in range(1, 4):
            self.to_line(s, j).wait_recv()
            self.shards[s] += self.by_line[s, j - 1].astype(F32)

    def sent_to_sibling(self, s):
        for k in range(2):
            self.to_sibling(s, k).wait_send()

    def end(self):
        for s in range(3):
            for k in range(8):
                self.to_second(s, k).wait_send()
            for k in range(4):
                self.to_first(s, k).wait_send()
            for j in range(1, 4):
                self.to_line(s, j).wait_send()


class SmallSums:
    def __init__(self, place, sums, inbox, sems):
        self.at, self.sums, self.inbox, self.sems = place, sums, inbox, sems
        at = place
        self.peers = [at.sibling, at.x_peer, at.y_peer, *at.line[1:]]

    def copy(self, k):
        return remote(
            self.sums.at[min(k, 3)],
            self.inbox.at[k],
            self.sems.at[0, k],
            self.sems.at[1, k],
            self.peers[k],
        )

    def begin(self):
        self.copy(0).start()

    def step(self, k):
        self.copy(k).wait_recv()
        self.sums[k + 1] = self.sums[k] + self.inbox[k]
        for nxt in (k + 1,) if k < 2 else (3, 4, 5):
            self.copy(nxt).start()

    def end(self, out):
        for k in range(3, 6):
            self.copy(k).wait_recv()
        out[...] = (self.sums[3] + self.inbox[3]) + (self.inbox[4] + self.inbox[5])
        for k in range(6):
            self.copy(k).wait_send()


def fold(rows):
    half = rows.shape[1] // 2
    return jnp.concatenate([rows[:, :half], rows[:, half:]], axis=0).astype(BF16)


def unfold(packed):
    wide = packed.astype(F32)
    return jnp.concatenate([wide[:8], wide[8:]], axis=1)


class Scoring:
    def __init__(self, place, ways, cls, gold, passages, scores, lse, buffers, sems):
        self.at, self.ways, self.cls, self.gold = place, ways, cls, gold
        self.passages, self.scores, self.lse = passages, scores, lse
        self.part, self.parts, self.firsts, self.rows = buffers[:4]
        self.sent, self.got, self.stats, self.got_stats = buffers[4:]
        self.mp_sems, self.sems = sems
        at = place
        self.mates = (at.sibling, (at.dp, at.across), at.diagonal)
        self.others = [(lax.rem(at.dp + k, ways), at.mp) for k in range(1, ways)]

    def mate(self, k):
        return remote(
            self.part, self.parts.at[k], self.mp_sems.at[0, k], self.mp_sems.at[1, k], self.mates[k]
        )

    def first_copy(self, k):
        mine = self.firsts.at[self.at.dp]
        return remote(
            mine, mine, self.sems.at[0, 0, k - 1], self.sems.at[0, 1, k - 1], self.others[k - 1]
        )

    def back_copy(self, which, k):
        peer = self.others[k - 1]
        return remote(
            self.sent.at[which, peer[0]],
            self.got.at[which, self.at.dp],
            self.sems.at[1 + which, 0, k - 1],
            self.sems.at[1 + which, 1, k - 1],
            peer,
        )

    def stat_copy(self, k):
        peer = self.others[k - 1]
        return remote(
            self.stats.at[peer[0]],
            self.got_stats.at[self.at.dp],
            self.sems.at[3, 0, k - 1],
            self.sems.at[3, 1, k - 1],
            peer,
        )

    def start_cls(self):
        self.part[...] = fold(self.cls[...])
        for k in range(3):
            self.mate(k).start()

    def start_gold(self):
        places = self.at.dp * self.passages.shape[0] + lax.broadcasted_iota(
            jnp.int32, (self.passages.shape[0], self.gold.shape[0]), 0
        )
        target = jnp.where(as_row(self.gold) == places, 1.0, 0.0).astype(BF16)
        self.put(0, dot(target, self.passages[...], 0, 0))
        for k in range(1, self.ways):
            self.back_copy(0, k).start()

    def put(self, which, rows):
        for d in range(self.ways):
            self.sent[which, d] = fold(rows[8 * d : 8 * d + 8])
        self.got[which, self.at.dp] = self.sent[which, self.at.dp]

    def start_firsts(self):
        total = self.part[...].astype(F32)
        for k in range(3):
            self.mate(k).wait_recv()
            total = total + self.parts[k].astype(F32)
        self.firsts[self.at.dp] = total.astype(BF16)
        for k in range(1, self.ways):
            self.first_copy(k).start()

    def start_back(self):
        for k in range(1, self.ways):
            self.first_copy(k).wait_recv()
        for d in range(self.ways):
            self.rows[8 * d : 8 * d + 8, :] = unfold(self.firsts[d])
        table = dot(self.rows[...].astype(BF16), self.passages[...], 1, 1)
        self.scores[...] = table
        peak = jnp.max(table, axis=1, keepdims=True)
        e = jnp.exp(table - peak)
        total = jnp.sum(e, axis=1, keepdims=True)
        lane = lax.broadcasted_iota(jnp.int32, (8, LANES), 1)
        for d in range(self.ways):
            rows = slice(8 * d, 8 * d + 8)
            self.stats[d] = jnp.where(lane == 0, peak[rows], total[rows])
        self.got_stats[self.at.dp] = self.stats[self.at.dp]
        for k in range(1, self.ways):
            self.stat_copy(k).start()
        self.put(1, dot(e.astype(BF16), self.passages[...]))
        for k in range(1, self.ways):
            self.back_copy(1, k).start()

    def result(self):
        for k in range(1, self.ways):
            self.back_copy(0, k).wait_recv()
            self.stat_copy(k).wait_recv()
        peaks = [self.got_stats[d][:, 0:1] for d in range(self.ways)]
        top = functools.reduce(jnp.maximum, peaks)
        scales = [jnp.exp(peak - top) for peak in peaks]
        total = sum(scale * self.got_stats[d][:, 1:2] for d, scale in enumerate(scales))
        self.lse[...] = top + jnp.log(total)
        for k in range(1, self.ways):
            self.back_copy(1, k).wait_recv()
        grad = -sum(unfold(self.got[0, d]) for d in range(self.ways))
        for d in range(self.ways):
            grad = grad + (scales[d] / total) * unfold(self.got[1, d])
        return grad

    def end(self):
        for k in range(3):
            self.mate(k).wait_send()
        for k in range(1, self.ways):
            self.first_copy(k).wait_send()
            self.back_copy(0, k).wait_send()
            self.back_copy(1, k).wait_send()
            self.stat_copy(k).wait_send()


class Halo:
    def __init__(self, sizes, place, dkv, sent, got, sems):
        self.sizes, self.at, self.dkv, self.sent, self.got, self.sems = sizes, place, dkv, sent, got, sems
        self.has = (place.mp > 0, place.mp < sizes.groups - 1)
        offset = sizes.own_offset(place.mp)
        self.starts = (offset - LONGEST, offset + sizes.own)
        self.into = (sizes.own - LONGEST, 0)

    def copy(self, g, side):
        slot = g % 2
        return remote(
            self.sent.at[slot, side],
            self.got.at[g, side],
            self.sems.at[0, slot, side],
            self.sems.at[1, g, side],
            (self.at.dp, self.at.mp + 2 * side - 1),
        )

    def start(self, g):
        for side in range(2):

            @pl.when(self.has[side])
            def _():
                pl.when(g > 1)(self.copy(g, side).wait_send)
                rows = pl.ds(pl.multiple_of(self.starts[side], 16), LONGEST)
                self.sent[g % 2, side] = self.dkv[rows, :].astype(BF16)
                self.copy(g, side).start()

    def add(self, g, own):
        for side in range(2):

            @pl.when(self.has[1 - side])
            def _():
                self.copy(g, side).wait_recv()
                rows = pl.ds(self.into[side], LONGEST)
                own[rows, :] += self.got[g, side].astype(F32)

    def end(self):
        for side in range(2):

            @pl.when(self.has[side])
            def _():
                self.copy(2, side).wait_send()
                self.copy(3, side).wait_send()


def finish_kernel(
    sizes,
    lens,
    cls,
    gold,
    gain_1,
    shift_1,
    gain_2,
    r_1,
    r_2,
    lse,
    tokens,
    cotangent,
    passages,
    encoded,
    weights,
    n_1_in,
    n_2_in,
    z_in,
    slope_in,
    kv_in,
    q_in,
    ctx_in,
    scores,
    query_lse,
    small_out,
    shards,
    encoded_whole,
    token_whole,
    w,
    ffn,
    parts,
    inbox,
    by_second,
    by_first,
    by_line,
    kv,
    q,
    ctx,
    dctx,
    dkv,
    own_kv,
    halo_sent,
    halo_got,
    n_1,
    work,
    rows_low,
    row_in,
    turned,
    low,
    bias,
    delta,
    sums,
    sums_in,
    part,
    parts_in,
    firsts,
    first_rows,
    back_sent,
    back_got,
    stats,
    stats_got,
    load_sems,
    kv_sems,
    ffn_sems,
    spread_sems,
    core_sems,
    second_sems,
    first_sems,
    line_sems,
    halo_sems,
    small_sems,
    mp_sems,
    score_sems,
):
    at = Place()
    me = at.mp
    own_rows = pl.ds(pl.multiple_of(sizes.own * me, 16), sizes.own)
    ways = firsts.shape[0]
    table = parts.at[pl.ds(Scatter.HELD[0] * sizes.width, passages.shape[0])]
    scatter = Scatter(
        at, parts, inbox, by_second, by_first, by_line, shards,
        (core_sems, second_sems, first_sems, line_sems),
    )
    halo = Halo(sizes, at, dkv, halo_sent, halo_got, halo_sems)
    spread = Spread(at, encoded, encoded_whole, spread_sems.at[0, 0], spread_sems.at[0, 1], load_sems.at[8])
    token_spread = Spread(
        at, rows_low, token_whole, spread_sems.at[1, 0], spread_sems.at[1, 1], load_sems.at[9]
    )
    small = SmallSums(at, sums, sums_in, small_sems)

    def load(k, source, target):
        return pltpu.make_async_copy(source, target, load_sems.at[k])

    loads = [
        load(0, passages, table),
        load(1, cotangent.at[own_rows], row_in),
        load(2, n_2_in, work.at[1]),
        load(3, n_1_in, n_1),
        load(5, q_in, q),
        load(6, ctx_in, ctx),
    ]

    def kv_load(g):
        return pltpu.make_async_copy(kv_in.at[g], kv.at[g % 2], kv_sems.at[g % 2])

    for copy in loads:
        copy.start()
    kv_load(0).start()

    scoring = Scoring(
        at,
        ways,
        cls,
        gold,
        table,
        scores,
        query_lse,
        (part, parts_in, firsts, first_rows, back_sent, back_got, stats, stats_got),
        (mp_sems, score_sems),
    )
    signal([*scoring.mates, *scoring.others])

    def group_of(i):
        return jnp.where(i < 2, 1 - at.core + 2 * i, at.core + 2 * (i - 2))

    def z_load(i):
        return pltpu.make_async_copy(z_in.at[group_of(i)], ffn.at[0, i % 2], ffn_sems.at[i % 2, 0])

    def ffn_loads(i):
        slot, g = i % 2, group_of(i)
        return [
            pltpu.make_async_copy(weights.at[2, g], w.at[2 * slot], ffn_sems.at[slot, 1]),
            pltpu.make_async_copy(weights.at[1, g], w.at[2 * slot + 1], ffn_sems.at[slot, 2]),
            pltpu.make_async_copy(slope_in.at[g], ffn.at[1, slot], ffn_sems.at[slot, 3]),
        ]

    z_load(0).start()
    for copy in ffn_loads(0):
        copy.start()

    arrive([*scoring.mates, *scoring.others])
    scoring.start_cls()
    loads[0].wait()
    scoring.start_gold()
    scoring.start_firsts()
    spread.begin()
    fill_mask(sizes, me, lens, bias)
    picked = start_rows(sizes, me, lens).astype(BF16)
    loads[3].wait()
    turned[1] = (n_1[...] * as_row(gain_1) + as_row(shift_1)).T.astype(BF16)
    scoring.start_back()
    loads[1].wait()
    loads[2].wait()
    dcls = scoring.result()
    high = dcls.astype(BF16)
    rest = (dcls - high.astype(F32)).astype(BF16)
    dy = row_in[...].astype(F32) + dot(picked, high, 0, 0) + dot(picked, rest, 0, 0)
    mine = sums.at[0]
    mine[0:1, :] = jnp.sum(dy * work[1], axis=0, keepdims=True)
    mine[1:2, :] = jnp.sum(dy, axis=0, keepdims=True)
    grad = norm_back(dy, work[1], r_2[...], as_row(gain_2))
    mine[2:3, :] = jnp.sum(grad, axis=0, keepdims=True)
    work[0] = grad
    rows_low[...] = grad.astype(BF16)
    turned[0] = grad.T.astype(BF16)

    def into(s, i):
        return jnp.where(i < 2, Scatter.STAGE[s] + i, Scatter.HELD[s] + i - 2)

    @pl.loop(0, sizes.groups)
    def _(i):
        z_load(i).wait()

        @pl.when(i < 3)
        def _():
            z_load(i + 1).start()

        square(parts, into(2, i))[...] = dot(turned[0], ffn[0, i % 2]).astype(BF16)
        pl.when(i < 2)(lambda: scatter.to_sibling(2, i).start())

    scatter.chip_sum(2)

    @pl.loop(0, sizes.groups)
    def _(i):
        slot, g = i % 2, group_of(i)
        for copy in ffn_loads(i):
            copy.wait()

        @pl.when(i < 3)
        def _():
            for copy in ffn_loads(i + 1):
                copy.start()

        da = dot(rows_low[...], w[2 * slot]) * ffn[1, slot].astype(F32)
        mine[pl.ds(8 + g, 1), :] = jnp.sum(da, axis=0, keepdims=True)
        da_low = da.astype(BF16)
        square(parts, into(1, i))[...] = dot(turned[1], da_low).astype(BF16)
        pl.when(i < 2)(lambda: scatter.to_sibling(1, i).start())
        work[0] += dot(da_low, w[2 * slot + 1], 1, 1)

    load_w = pltpu.make_async_copy(weights.at[0], w, load_sems.at[7])
    load_w.start()
    load_x = load(1, tokens.at[own_rows], row_in)
    load_x.start()
    scatter.chip_sum(1)
    scatter.sent_to_sibling(2)

    dy = work[0]
    mine[3:4, :] = jnp.sum(dy * n_1[...], axis=0, keepdims=True)
    mine[4:5, :] = jnp.sum(dy, axis=0, keepdims=True)
    grad = norm_back(dy, n_1[...], r_1[...], as_row(gain_1))
    mine[5:6, :] = jnp.sum(grad, axis=0, keepdims=True)
    mine[6:8, :] = jnp.zeros((2, sizes.width), F32)
    mine[12:24, :] = jnp.zeros((12, sizes.width), F32)
    work[1] = grad
    rows_low[...] = grad.astype(BF16)
    turned[0] = grad.T.astype(BF16)
    load_x.wait()
    turned[1] = row_in[...].astype(F32).T.astype(BF16)
    load_w.wait()
    for copy in loads[4:]:
        copy.wait()

    @pl.loop(0, sizes.groups)
    def _(g):
        dctx[g] = dot(rows_low[...], w[g, :, tile(4, 2)]).astype(BF16)

    actions = {
        "second": scatter.from_second,
        "first": scatter.from_first,
        "line": scatter.from_line,
        "chip": scatter.chip_sum,
        "small": small.step,
        "begin": lambda s: small.begin(),
        "tokens": lambda s: token_spread.begin(),
        "relay": lambda s: token_spread.forward(),
        "encoded": lambda s: spread.forward(),
    }

    def run(names):
        for name, s in names:
            actions[name](s)

    def tick(now):
        for k, names in DURING.items():
            pl.when(now == k)(functools.partial(run, names))

    def finalize(g):
        slot = g % 2
        halo.add(g, own_kv.at[slot])
        dkv_own = own_kv[slot]
        mine[pl.ds(16 + g, 1), tile(0, 3)] = jnp.sum(dkv_own, axis=0, keepdims=True)
        low[slot, :, tile(0, 3)] = dkv_own.astype(BF16)
        work[1] += dot(low[slot], w[g, :, tile(0, 5)], 1, 1)
        into = jnp.where(g % 2 == at.core, Scatter.HELD[0], Scatter.STAGE[0]) + g // 2
        made = dot(turned[1], low[slot])
        more = dot(turned[0], ctx[g])
        target = square(parts, into)
        target[:, tile(0, 4)] = made[:, tile(0, 4)].astype(BF16)
        target[:, tile(4)] = (made[:, tile(4)] + more[:, tile(0)]).astype(BF16)
        target[:, tile(5)] = more[:, tile(1)].astype(BF16)

        @pl.when(g % 2 != at.core)
        def _():
            scatter.to_sibling(0, g // 2).start()

    own = pl.ds(sizes.own_offset(me), sizes.own)

    @pl.loop(0, sizes.groups)
    def _(g):
        slot = g % 2
        kv_load(g).wait()

        @pl.when(g < sizes.groups - 1)
        def _():
            kv_load(g + 1).start()

        delta[...] = delta_rows(dctx[g], ctx[g])
        dkv[...] = jnp.zeros_like(dkv)
        for b in range(sizes.blocks):
            tick(g * sizes.blocks + b)
            rows = slice(b * sizes.block, (b + 1) * sizes.block)
            dq = attend_back_block(
                sizes, me, g, b, kv.at[slot], q, bias, lse, dctx, delta, dkv
            )
            total = jnp.sum(dq, axis=0, keepdims=True)
            mine[pl.ds(16 + g, 1), tile(3, 2)] += total
            low[slot, rows, tile(3, 2)] = dq.astype(BF16)
        halo.start(g)
        own_kv[slot] = dkv[own, :]

        @pl.when(g > 0)
        def _():
            finalize(g - 1)

    run(BEFORE_LAST)
    finalize(sizes.groups - 1)
    rows_low[...] = work[1].astype(BF16)
    run(AFTER_LAST)
    small.end(small_out)
    scatter.sent_to_sibling(1)
    scatter.sent_to_sibling(0)
    scatter.end()
    halo.end()
    scoring.end()
    spread.end()
    token_spread.end()


def input_kernel(sizes, tokens, weights, dkv, dq, dh_1, grads_out, token_grad, grads, small, turned, low):
    turned[...] = tokens[...].astype(F32).T.astype(BF16)
    total = dh_1[...]
    for g in range(sizes.groups):
        small[g, :, tile(0, 3)] = jnp.sum(dkv[g], axis=0, keepdims=True)
        small[g, :, tile(3, 2)] = jnp.sum(dq[g], axis=0, keepdims=True)
        low[:, tile(0, 3)] = dkv[g].astype(BF16)
        low[:, tile(3, 2)] = dq[g].astype(BF16)
        total = total + dot(low[...], weights[g, :, tile(0, 5)], 1, 1)
        made = dot(turned[...], low[...])
        grads[g, :, tile(0, 4)] = made[:, tile(0, 4)].astype(BF16)
        grads[g, :, tile(4)] = (made[:, tile(4)] + grads_out[g, :, tile(0)]).astype(BF16)
        grads[g, :, tile(5)] = grads_out[g, :, tile(1)].astype(BF16)
    token_grad[...] = total.astype(BF16)


def specs(*spaces):
    return [pl.BlockSpec(memory_space=s) for s in spaces]


def params(**more):
    return pltpu.CompilerParams(vmem_limit_bytes=63 * 2**20, **more)


def run_forward(sizes, lengths, tokens, weights, rows, gathers):
    own, width, groups = sizes.own, sizes.width, sizes.groups
    docs = lengths.shape[1]
    shape = jax.ShapeDtypeStruct
    outs = [
        shape((own, width), BF16),
        shape((docs, width), F32),
        shape((own, width), F32),
        shape((own, 1), F32),
        shape((own, width), F32),
        shape((own, 1), F32),
        shape((groups, own, width), BF16),
        shape((groups, own, width), BF16),
        shape((groups, sizes.window, 3 * LANES), BF16),
        shape((groups, own, 2 * LANES), BF16),
        shape((groups, sizes.blocks, 8, sizes.block), F32),
        shape((groups, own, 2 * LANES), BF16),
    ]
    spaces = [*[VMEM] * 6, ANY, ANY, ANY, *[VMEM] * 3]
    scratch = [
        pltpu.VMEM((sizes.window, width), BF16),
        pltpu.VMEM((3, groups, width, width), BF16),
        pltpu.VMEM((sizes.blocks, sizes.keys, sizes.block), F32),
        pltpu.VMEM((own, width), F32),
        pltpu.VMEM((groups, sizes.window, 3 * LANES), BF16),
        pltpu.VMEM((groups, own, width), BF16),
        pltpu.VMEM((groups, own, width), BF16),
        pltpu.SemaphoreType.DMA((4,)),
    ]
    if gathers:
        outs.insert(0, shape((3, groups, width, width), BF16))
        spaces.insert(0, ANY)
        scratch += [
            pltpu.VMEM((2, weights[0].shape[0], width), BF16),
            pltpu.VMEM((1, 5 * LANES + weights[8].shape[0]), F32),
            pltpu.VMEM((groups, 1, 5 * LANES + weights[8].shape[0]), F32),
            pltpu.SemaphoreType.DMA((3, 31)),
            pltpu.SemaphoreType.DMA((3, 32)),
            pltpu.SemaphoreType.DMA((6,)),
            pltpu.SemaphoreType.DMA((2, 3)),
        ]
        kernel, more = gathering_kernel, {"collective_id": 0, "has_side_effects": True}
    else:
        scratch.append(pltpu.SemaphoreType.DMA((3,)))
        kernel, more = forward_kernel, {}
    return pl.pallas_call(
        functools.partial(kernel, sizes),
        out_shape=outs,
        in_specs=specs(SMEM, ANY, *([VMEM] * 15 if gathers else [ANY, *[VMEM] * 7])),
        out_specs=specs(*spaces),
        scratch_shapes=scratch,
        compiler_params=params(**more),
        name="forward",
    )(lengths, tokens, *weights, *rows)


def run_backward(sizes, lengths, cotangent, dcls, weights, gain_1, shift_1, gain_2, saved):
    own, width, groups = sizes.own, sizes.width, sizes.groups
    shape = jax.ShapeDtypeStruct
    outs = (
        shape((own, width), F32),
        shape((groups, sizes.window, 3 * LANES), F32),
        shape((groups, own, 2 * LANES), F32),
        shape((2, groups, width, width), BF16),
        shape((groups, width, 2 * LANES), F32),
        shape((16, width), F32),
    )
    return pl.pallas_call(
        functools.partial(backward_kernel, sizes),
        out_shape=outs,
        in_specs=specs(SMEM, ANY, VMEM, ANY, *[VMEM] * (3 + len(saved))),
        out_specs=specs(VMEM, VMEM, VMEM, ANY, VMEM, VMEM),
        scratch_shapes=[
            pltpu.VMEM((groups, width, width), BF16),
            pltpu.VMEM((groups, width, width), BF16),
            pltpu.VMEM((groups, width, width), BF16),
            pltpu.VMEM((own, width), BF16),
            pltpu.VMEM((own, width), F32),
            pltpu.VMEM((own, width), BF16),
            pltpu.VMEM((own, width), BF16),
            pltpu.VMEM((2, width, own), BF16),
            pltpu.VMEM((2, width, width), BF16),
            pltpu.VMEM((groups, own, 2 * LANES), BF16),
            pltpu.VMEM((8, own), F32),
            pltpu.VMEM((sizes.blocks, sizes.keys, sizes.block), F32),
            pltpu.SemaphoreType.DMA((4,)),
            pltpu.SemaphoreType.DMA((2,)),
        ],
        compiler_params=params(),
        name="backward",
    )(lengths, cotangent, dcls, weights, gain_1, shift_1, gain_2, *saved)


def run_input(sizes, own_tokens, w_attn, dkv, dq, dh_1, grads_out):
    own, width, groups = sizes.own, sizes.width, sizes.groups
    shape = jax.ShapeDtypeStruct
    outs = (
        shape((own, width), BF16),
        shape((groups, width, width), BF16),
        shape((groups, 1, 5 * LANES), F32),
    )
    return pl.pallas_call(
        functools.partial(input_kernel, sizes),
        out_shape=outs,
        in_specs=specs(*[VMEM] * 6),
        out_specs=specs(*[VMEM] * 3),
        scratch_shapes=[pltpu.VMEM((width, own), BF16), pltpu.VMEM((own, 5 * LANES), BF16)],
        compiler_params=params(),
        name="inputs",
    )(own_tokens, w_attn, dkv, dq, dh_1, grads_out)


def run_finish(sizes, small_in, large_in):
    own, width, groups = sizes.own, sizes.width, sizes.groups
    tokens, passages = large_in[0], large_in[2]
    queries = small_in[2].shape[0]
    ways = queries // 8
    shard = width // ways
    shape = jax.ShapeDtypeStruct
    outs = (
        shape((queries, passages.shape[0]), F32),
        shape((8, 1), F32),
        shape((24, width), F32),
        shape((3, shard, width), F32),
        shape(tokens.shape, BF16),
        shape(tokens.shape, BF16),
    )
    dma = pltpu.SemaphoreType.DMA
    scratch = [
        pltpu.VMEM((groups, width, width), BF16),
        pltpu.VMEM((2, 2, own, width), BF16),
        pltpu.VMEM((10 * width, width), BF16),
        pltpu.VMEM((4, width, width), BF16),
        pltpu.VMEM((3, 8, shard, width), BF16),
        pltpu.VMEM((3, 4, shard, width), BF16),
        pltpu.VMEM((3, 3, shard, width), BF16),
        pltpu.VMEM((2, sizes.window, 3 * LANES), BF16),
        pltpu.VMEM((groups, own, 2 * LANES), BF16),
        pltpu.VMEM((groups, own, 2 * LANES), BF16),
        pltpu.VMEM((groups, own, 2 * LANES), BF16),
        pltpu.VMEM((sizes.window, 3 * LANES), F32),
        pltpu.VMEM((2, own, 3 * LANES), F32),
        pltpu.VMEM((2, 2, LONGEST, 3 * LANES), BF16),
        pltpu.VMEM((groups, 2, LONGEST, 3 * LANES), BF16),
        pltpu.VMEM((own, width), F32),
        pltpu.VMEM((2, own, width), F32),
        pltpu.VMEM((own, width), BF16),
        pltpu.VMEM((own, width), BF16),
        pltpu.VMEM((2, width, own), BF16),
        pltpu.VMEM((2, own, 5 * LANES), BF16),
        pltpu.VMEM((sizes.blocks, sizes.keys, sizes.block), F32),
        pltpu.VMEM((8, own), F32),
        pltpu.VMEM((4, 24, width), F32),
        pltpu.VMEM((6, 24, width), F32),
        pltpu.VMEM((16, width // 2), BF16),
        pltpu.VMEM((3, 16, width // 2), BF16),
        pltpu.VMEM((ways, 16, width // 2), BF16),
        pltpu.VMEM((queries, width), F32),
        pltpu.VMEM((2, ways, 16, width // 2), BF16),
        pltpu.VMEM((2, ways, 16, width // 2), BF16),
        pltpu.VMEM((ways, 8, LANES), F32),
        pltpu.VMEM((ways, 8, LANES), F32),
        dma((10,)),
        dma((2,)),
        dma((2, 4)),
        dma((2, 2, 3)),
        dma((2, 3, 2)),
        dma((2, 3, 8)),
        dma((2, 3, 4)),
        dma((2, 3, 3)),
        dma((2, 4, 2)),
        dma((2, 6)),
        dma((2, 3)),
        dma((4, 2, ways - 1)),
    ]
    return pl.pallas_call(
        functools.partial(finish_kernel, sizes),
        out_shape=outs,
        in_specs=specs(SMEM, *[VMEM] * (len(small_in) - 1), *[ANY] * len(large_in)),
        out_specs=specs(*[VMEM] * 4, ANY, ANY),
        scratch_shapes=scratch,
        compiler_params=params(collective_id=1, has_side_effects=True),
        name="finish",
    )(*small_in, *large_in)


def cut_along(array, dim, devices):
    before, after = (array.shape[:dim], array.shape[dim + 1 :])
    return jnp.moveaxis(array.reshape(*before, devices, -1, *after), dim, 0)


def summed_on_arrival(array, axis, dim):
    pieces = cut_along(array, dim, lax.axis_size(axis))
    arrived = lax.all_to_all(pieces, axis, split_axis=0, concat_axis=0, tiled=True)
    return arrived.astype(F32).sum(axis=0)


def score(cls, passages, gold):
    all_first = lax.all_gather(cls, "dp", axis=0, tiled=True)
    table = dot(all_first, passages, 1, 1)
    peak = lax.pmax(jnp.max(table, axis=1), "dp")
    total = lax.psum(jnp.sum(jnp.exp(table - peak[:, None]), axis=1), "dp")
    own = cls.shape[0]
    lse = lax.dynamic_slice_in_dim(peak + jnp.log(total), lax.axis_index("dp") * own, own)
    soft = jnp.exp(table - peak[:, None]) / total[:, None]
    first = lax.axis_index("dp") * table.shape[1]
    columns = first + jnp.arange(table.shape[1], dtype=jnp.int32)
    target = (gold[:, None] == columns[None, :]).astype(F32)
    grad = dot((soft - target).astype(BF16), passages)
    return table, lse, summed_on_arrival(grad.astype(BF16), "dp", 0)


def plain_layer(sizes, tokens, cotangent, lengths, gold, passages, shards, rows):
    me, groups = lax.axis_index("mp"), sizes.groups
    w_key, w_value, w_query, w_out, w_up, w_down, b_value, b_query, b_up = shards
    packed = jnp.stack(
        [jnp.concatenate([w_key, w_value, w_query, w_out.T], axis=1), w_up, w_down]
    )
    c = w_key.shape[1]
    zeros = jnp.zeros((c,), F32)
    own_bias = jnp.concatenate([zeros, b_value, b_query, zeros[:HEAD], b_up])[None]
    whole = lax.all_gather(lax.all_gather(packed, "dp", axis=1, tiled=True), "mp", axis=1)
    biases = lax.all_gather(own_bias, "mp", axis=0)
    encoded, cls, *saved = run_forward(sizes, lengths, tokens, (whole, biases), rows, False)
    cls = lax.psum(cls, "mp").astype(BF16)
    table, lse, dcls = score(cls, passages, gold)
    n_1, r_1, n_2, r_2, z, slope, kv, q, logs, ctx = saved
    dh_1, dkv, dq, grads_ffn, grads_out, small = run_backward(
        sizes, lengths, cotangent, dcls, whole, rows[1], rows[2], rows[4], saved
    )
    halo, own = LONGEST, sizes.own
    offset = own * me - sizes.window_start(me)
    to_left = lax.dynamic_slice_in_dim(dkv, offset - halo, halo, axis=1).astype(BF16)
    to_right = lax.dynamic_slice_in_dim(dkv, offset + own, halo, axis=1).astype(BF16)
    from_right = lax.ppermute(to_left, "mp", [(i, i - 1) for i in range(1, groups)])
    from_left = lax.ppermute(to_right, "mp", [(i, i + 1) for i in range(groups - 1)])
    dkv = lax.dynamic_slice_in_dim(dkv, offset, own, axis=1)
    dkv = dkv.at[:, own - halo :].add(from_right.astype(F32))
    dkv = dkv.at[:, :halo].add(from_left.astype(F32))
    own_tokens = lax.dynamic_slice_in_dim(tokens, own * me, own, axis=0)
    token_part, grads_attn, small_attn = run_input(
        sizes, own_tokens, whole[0], dkv, dq, dh_1, grads_out
    )
    token_grad = lax.all_gather(token_part, "mp", axis=0, tiled=True).astype(F32)
    encoded = lax.all_gather(encoded, "mp", axis=0, tiled=True)
    grads = jnp.stack([grads_attn, grads_ffn[0], grads_ffn[1]])
    grads = summed_on_arrival(grads, "mp", 1)[:, 0].astype(BF16)
    grads = summed_on_arrival(grads, "dp", 1)
    small, small_attn = lax.psum((small, small_attn), ("dp", "mp"))
    mine = lax.dynamic_index_in_dim(small_attn[:, 0], me, 0, keepdims=False)
    up_bias = lax.dynamic_index_in_dim(small, 8 + me, 0, keepdims=False)
    return (
        table,
        lse,
        encoded,
        token_grad,
        grads[0, :, 2 * c : 3 * c],
        grads[0, :, :c],
        grads[0, :, c : 2 * c],
        mine[2 * c : 3 * c],
        mine[c : 2 * c],
        grads[0, :, 3 * c :].T,
        small[5],
        small[3],
        small[4],
        grads[1],
        up_bias,
        grads[2].T,
        small[2],
        small[0],
        small[1],
    )


def outputs_kernel(cols, table, lse, small, shards, encoded, tokens, *outs):
    *outs, got, wide, passed, sems = outs
    (
        table_out,
        lse_out,
        encoded_out,
        tokens_out,
        g_query,
        g_key,
        g_value,
        gb_query,
        gb_value,
        g_out,
        gb_out,
        g_gain_1,
        g_shift_1,
        g_up,
        gb_up,
        g_down,
        gb_down,
        g_gain_2,
        g_shift_2,
    ) = outs
    steps = got.shape[0]
    rows = [pl.ds(k * got.shape[1], got.shape[1]) for k in range(steps)]
    copies = [pltpu.make_async_copy(tokens.at[rows[k]], got.at[k], sems.at[0, k]) for k in range(steps)]
    writes = [pltpu.make_async_copy(wide.at[k], tokens_out.at[rows[k]], sems.at[1, k]) for k in range(steps)]
    takes = [pltpu.make_async_copy(encoded.at[rows[k]], passed.at[k], sems.at[2, k]) for k in range(steps)]
    gives = [pltpu.make_async_copy(passed.at[k], encoded_out.at[rows[k]], sems.at[3, k]) for k in range(steps)]
    for k in range(steps):
        copies[k].start()
        takes[k].start()
    for k in range(steps):
        copies[k].wait()
        wide[k] = got[k].astype(F32)
        writes[k].start()
        takes[k].wait()
        gives[k].start()
    me = lax.axis_index("mp")
    table_out[...] = table[...]
    lse_out[...] = lse[...].T.reshape(lse_out.shape)
    for k, target in enumerate((g_key, g_value, g_query)):
        target[...] = shards[0, :, k * cols : (k + 1) * cols]
    g_out[...] = shards[0, :, 3 * cols :].T
    g_up[...] = shards[1]
    g_down[...] = shards[2]
    heads = small[pl.ds(16 + me, 1), :]
    gb_value[...] = heads[:, cols : 2 * cols].reshape(gb_value.shape)
    gb_query[...] = heads[:, 2 * cols : 3 * cols].reshape(gb_query.shape)
    gb_up[...] = small[pl.ds(8 + me, 1), :].reshape(gb_up.shape)
    for k, target in enumerate((g_gain_2, g_shift_2, gb_down, g_gain_1, g_shift_1, gb_out)):
        target[...] = small[k : k + 1, :].reshape(target.shape)
    for k in range(steps):
        writes[k].wait()
        gives[k].wait()


def run_outputs(made, cols):
    table, lse, small, shards, encoded, tokens = made
    rows, width = shards.shape[1:]
    shape = jax.ShapeDtypeStruct
    vector = shape((width,), F32)
    outs = (
        shape(table.shape, F32),
        shape((lse.shape[0],), F32),
        shape(encoded.shape, BF16),
        shape(tokens.shape, F32),
        *[shape((rows, cols), F32)] * 3,
        *[shape((cols,), F32)] * 2,
        shape((cols, rows), F32),
        *[vector] * 3,
        shape((rows, width), F32),
        vector,
        shape((rows, width), F32),
        *[vector] * 3,
    )
    steps = 8
    span = tokens.shape[0] // steps
    return pl.pallas_call(
        functools.partial(outputs_kernel, cols),
        out_shape=outs,
        in_specs=specs(*[VMEM] * 4, ANY, ANY),
        out_specs=specs(*[ANY if k in (2, 3) else VMEM for k in range(len(outs))]),
        scratch_shapes=[
            pltpu.VMEM((steps, span, width), BF16),
            pltpu.VMEM((steps, span, width), F32),
            pltpu.VMEM((steps, span, width), BF16),
            pltpu.SemaphoreType.DMA((4, steps)),
        ],
        compiler_params=params(),
        name="outputs",
    )(*made)


def body(
    tokens,
    cotangent,
    lengths,
    gold,
    passages,
    w_query,
    w_key,
    w_value,
    b_query,
    b_value,
    w_out,
    b_out,
    gain_attn,
    shift_attn,
    w_up,
    b_up,
    w_down,
    b_down,
    gain_ffn,
    shift_ffn,
):
    groups = lax.axis_size("mp")
    sizes = Sizes(tokens.shape[0], tokens.shape[1], groups)
    rows = (b_out, gain_attn, shift_attn, b_down, gain_ffn, shift_ffn)
    shards = (w_key, w_value, w_query, w_out, w_up, w_down.T, b_value, b_query, b_up)
    if lax.axis_size("dp") == 8 and groups == 4:
        whole, encoded, cls, n_1, r_1, n_2, r_2, z, slope, kv, q, logs, ctx = run_forward(
            sizes, lengths, tokens, shards, rows, True
        )
        made = run_finish(
            sizes,
            (lengths, cls, gold, gain_attn, shift_attn, gain_ffn, r_1, r_2, logs),
            (tokens, cotangent, passages, encoded, whole, n_1, n_2, z, slope, kv, q, ctx),
        )
        outs = list(run_outputs(made, w_key.shape[1]))
        outs[15] = outs[15].T
        return tuple(outs)
    return plain_layer(sizes, tokens, cotangent, lengths, gold, passages, shards, rows)


def solution(mesh):
    by_dp, shared, cross = P("dp", None), P(), P("dp", "mp")
    return jax.shard_map(
        body,
        mesh=mesh,
        in_specs=(
            by_dp,
            by_dp,
            by_dp,
            shared,
            by_dp,
            cross,
            cross,
            cross,
            P("mp"),
            P("mp"),
            P("mp", "dp"),
            shared,
            shared,
            shared,
            cross,
            P("mp"),
            P("mp", "dp"),
            shared,
            shared,
            shared,
        ),
        out_specs=(
            P(None, "dp"),
            P("dp"),
            by_dp,
            by_dp,
            cross,
            cross,
            cross,
            P("mp"),
            P("mp"),
            P("mp", "dp"),
            shared,
            shared,
            shared,
            cross,
            P("mp"),
            P("mp", "dp"),
            shared,
            shared,
            shared,
        ),
        check_vma=False,
    )
```

```python
import functools

import jax
import jax.numpy as jnp
from jax import lax
from jax.experimental import pallas as pl
from jax.experimental.pallas import tpu as pltpu
from jax.sharding import PartitionSpec as P

HEAD = 64
LONGEST = 400
QUERY_BLOCK = 256
EPSILON = 1e-05
NEGATIVE = -1e30
LANES = 128
KEY_AT = ((0, 0), (0, 1), (1, 0))
VALUE_AT = ((1, 1), (2, 0), (2, 1))
QUERY_AT = ((0, 0), (0, 1), (1, 0))
CONTEXT_AT = ((0, 1), (1, 0), (1, 1))
F32, BF16 = jnp.float32, jnp.bfloat16
VMEM, ANY, SMEM = pltpu.VMEM, pl.ANY, pltpu.SMEM


def dot(left, right, left_dim=1, right_dim=0):
    return lax.dot_general(
        left, right, (((left_dim,), (right_dim,)), ((), ())), preferred_element_type=F32
    )


def tile(index, count=1):
    return slice(index * LANES, (index + count) * LANES)


def half_mask(half, dtype):
    lane = lax.broadcasted_iota(jnp.int32, (1, LANES), 1)
    return jnp.where((lane >= HEAD) == (half == 1), 1.0, 0.0).astype(dtype)


def norm_stats(hidden):
    centred = hidden - jnp.mean(hidden, axis=-1, keepdims=True)
    factor = lax.rsqrt(jnp.mean(centred * centred, axis=-1, keepdims=True) + EPSILON)
    return centred * factor, factor


def norm_back(grad_out, normed, factor, gain):
    scaled = grad_out * gain
    inner = jnp.mean(scaled * normed, axis=-1, keepdims=True)
    return factor * (scaled - jnp.mean(scaled, axis=-1, keepdims=True) - normed * inner)


def gelu_and_slope(a):
    size = jnp.abs(a)
    t = 1.0 / (1.0 + (0.3275911 * 0.7071067811865476) * size)
    bell = jnp.exp(-0.5 * a * a)
    poly = t * (
        0.127414796 + t * (-0.142248368 + t * (0.7107068705 + t * (-0.7265760135 + t * 0.5307027145)))
    )
    tail = poly * bell
    phi = jnp.where(a >= 0.0, 1.0 - tail, tail)
    return a * phi, phi + a * bell * 0.3989422804014327


def as_row(ref):
    return ref[...].reshape(1, ref.shape[0])


class Sizes:
    def __init__(self, length, width, groups):
        self.length, self.width, self.groups = length, width, groups
        self.own = length // groups
        self.window = min(length, self.own + 2 * LONGEST)
        self.block = min(QUERY_BLOCK, self.own)
        self.blocks = self.own // self.block
        self.keys = min(length, self.block + 2 * LONGEST)

    def window_start(self, me):
        return jnp.clip(self.own * me - LONGEST, 0, self.length - self.window)

    def own_offset(self, me):
        return pl.multiple_of(self.own * me - self.window_start(me), 16)

    def key_start(self, me, block):
        first = self.own * me + block * self.block
        return jnp.clip(first - LONGEST, 0, self.length - self.keys)

    def key_offset(self, me, block):
        return pl.multiple_of(self.key_start(me, block) - self.window_start(me), 16)


def square(parts, index):
    side = parts.shape[1]
    return parts.at[pl.ds(pl.multiple_of(index * side, side), side)]


def document_bounds(lens, places):
    start = jnp.zeros_like(places)
    end = jnp.zeros_like(places)
    total = jnp.int32(0)
    for d in range(lens.shape[1]):
        count = lens[0, d]
        end = end + jnp.where(places >= total, count, 0)
        total = total + count
        start = start + jnp.where(places >= total, count, 0)
    return start, end


def fill_mask(sizes, me, lens, bias):
    for b in range(sizes.blocks):
        places = (
            sizes.own * me
            + b * sizes.block
            + lax.broadcasted_iota(jnp.int32, (1, sizes.block), 1)
        )
        start, end = document_bounds(lens, places)
        keys = sizes.key_start(me, b) + lax.broadcasted_iota(
            jnp.int32, (sizes.keys, sizes.block), 0
        )
        bias[b] = jnp.where((keys >= start) & (keys < end), 0.0, NEGATIVE)


def start_rows(sizes, me, lens):
    docs = lens.shape[1]
    row = lax.broadcasted_iota(jnp.int32, (docs, sizes.own), 0)
    place = sizes.own * me + lax.broadcasted_iota(jnp.int32, (docs, sizes.own), 1)
    picked = jnp.zeros((docs, sizes.own), F32)
    total = jnp.int32(0)
    for d in range(docs):
        picked = jnp.where((row == d) & (place == total), 1.0, picked)
        total = total + lens[0, d]
    return picked


def project(sizes, me, group, slot, span, tokens, weight, biases, kv, q):
    cut = sizes.window // 2
    own = pl.ds(sizes.own_offset(me), sizes.own)

    @pl.loop(*span)
    def _(i):
        g = group(i)
        for part in range(2):
            rows = pl.ds(part * cut, cut)
            made = dot(tokens[rows, :], weight(0, g)[:, tile(0, 3)]) + biases[g, :, tile(0, 3)]
            kv[slot(i), rows, :] = made.astype(BF16)
        made = dot(tokens[own, :], weight(0, g)[:, tile(3, 2)]) + biases[g, :, tile(3, 2)]
        q[g] = made.astype(BF16) * jnp.asarray(HEAD**-0.5, BF16)


def attend(sizes, me, group, slot, span, tick, kv, q, bias, lse, ctx):
    @pl.loop(*span)
    def _(i):
        g = group(i)

        @pl.loop(0, sizes.blocks)
        def _(b):
            tick(i * sizes.blocks + b)
            keys = pl.ds(sizes.key_offset(me, b), sizes.keys)
            rows = pl.ds(pl.multiple_of(b * sizes.block, sizes.block), sizes.block)
            made = [jnp.zeros((HEAD, sizes.block), F32)]
            logs = []
            for j in range(3):
                kt, kh = KEY_AT[j]
                vt, vh = VALUE_AT[j]
                qt, _ = QUERY_AT[j]
                query = q[g, rows, tile(qt)] * half_mask(kh, BF16)
                s = dot(kv[slot(i), keys, tile(kt)], query, 1, 1) + bias[b]
                peak = jnp.max(s, axis=0, keepdims=True)
                e = jnp.exp(s - peak)
                total = jnp.sum(e, axis=0, keepdims=True)
                mixed = dot(kv[slot(i), keys, tile(vt)], e.astype(BF16), 0, 0)
                made.append(mixed[vh * HEAD : (vh + 1) * HEAD] / total)
                logs.append(peak + jnp.log(total))
            ctx[g, rows, :] = jnp.concatenate(made, axis=0).T.astype(BF16)
            for j in range(3):
                lse[g, b, j : j + 1, :] = logs[j]


def delta_rows(dctx, ctx):
    lane = lax.broadcasted_iota(jnp.int32, (8, 2 * LANES), 1)
    row = lax.broadcasted_iota(jnp.int32, (8, 2 * LANES), 0)
    pick = jnp.where(lane // HEAD == row + 1, 1.0, 0.0).astype(BF16)
    product = dctx.astype(F32) * ctx.astype(F32)
    high = product.astype(BF16)
    low = (product - high.astype(F32)).astype(BF16)
    return dot(pick, high, 1, 1) + dot(pick, low, 1, 1)


def attend_back_block(sizes, me, g, b, kv, q, bias, lse, dctx, delta, dkv):
    keys = pl.ds(sizes.key_offset(me, b), sizes.keys)
    rows = slice(b * sizes.block, (b + 1) * sizes.block)
    made = []
    for j in range(3):
        kt, kh = KEY_AT[j]
        vt, vh = VALUE_AT[j]
        qt, _ = QUERY_AT[j]
        ct, _ = CONTEXT_AT[j]
        query = q[g, rows, tile(qt)] * half_mask(kh, BF16)
        grad = dctx[g, rows, tile(ct)] * half_mask(vh, BF16)
        s = dot(kv[keys, tile(kt)], query, 1, 1) + bias[b]
        p = jnp.exp(s - lse[g, b, j : j + 1, :])
        dp = dot(kv[keys, tile(vt)], grad, 1, 1)
        ds = (p * (dp - delta[j : j + 1, rows])).astype(BF16)
        dkv[keys, tile(kt)] += dot(ds, query)
        dkv[keys, tile(vt)] += dot(p.astype(BF16), grad)
        back = dot(kv[keys, tile(kt)], ds, 0, 0)
        made.append(back[kh * HEAD : (kh + 1) * HEAD] * HEAD**-0.5)
    made.append(jnp.zeros((HEAD, sizes.block), F32))
    return jnp.concatenate(made, axis=0).T


def attend_back(sizes, me, kv, q, bias, lse, ctx, dctx, delta, dkv, dq):
    @pl.loop(0, sizes.groups)
    def _(g):
        delta[...] = delta_rows(dctx[g], ctx[g])
        dkv[g] = jnp.zeros_like(dkv[g])
        for b in range(sizes.blocks):
            rows = slice(b * sizes.block, (b + 1) * sizes.block)
            dq[g, rows, :] = attend_back_block(
                sizes, me, g, b, kv.at[g], q, bias, lse, dctx, delta, dkv.at[g]
            )


class Loads:
    def __init__(self, weights, w, sems):
        self.copies = [pltpu.make_async_copy(weights.at[s], w.at[s], sems.at[s]) for s in range(3)]

    def begin(self):
        for copy in self.copies:
            copy.start()

    def group(self, i):
        return i

    def slot(self, i):
        return i

    def near_heads(self):
        self.copies[0].wait()

    def far_heads(self):
        pass

    def ready(self, section):
        self.copies[section].wait()

    def group_ready(self, section, i):
        pass

    def tick(self, step):
        pass

    def end(self):
        pass


MESH = pl.DeviceIdType.MESH


class Route:
    def __init__(self, at, turn):
        flip, x_peer = 1 - turn, 2 * at.z + 1 - at.x
        near = at.mp + turn * (at.across - at.mp)
        far = at.mp + flip * (at.across - at.mp)
        self.first = (at.dp + flip * (x_peer - at.dp), near)
        self.second = (at.dp + turn * (x_peer - at.dp), far)
        self.first_column = (near, at.x + flip * (1 - 2 * at.x))
        self.second_columns = ((far, at.x + turn * (1 - 2 * at.x)), (at.across, 1 - at.x))


class Place:
    def __init__(self):
        self.dp, self.mp = lax.axis_index("dp"), lax.axis_index("mp")
        self.z, self.x, self.y, self.core = self.dp // 2, self.dp % 2, self.mp // 2, self.mp % 2
        flip = 1 - self.core
        self.across = 2 * (1 - self.y) + self.core
        self.sibling = (self.dp, 2 * self.y + flip)
        self.x_peer = (2 * self.z + 1 - self.x, self.mp)
        self.y_peer = (self.dp, self.across)
        self.diagonal = (self.dp, 2 * (1 - self.y) + flip)
        self.zs = [self.z, self.z + 1 - 2 * (self.z % 2), (self.z + 2) % 4, 3 - self.z]
        self.line = [(2 * z + self.x, self.mp) for z in self.zs]
        self.by_core = Route(self, self.core)
        self.x_first, self.y_first = Route(self, 0), Route(self, 1)
        self.own_column = (self.mp, self.x)
        self.mates = (self.sibling, self.y_peer, self.diagonal)
        self.others = [(lax.rem(self.dp + k, 8), self.mp) for k in range(1, 8)]
        self.peers = [*self.mates, *self.others]


def signal(peers):
    barrier = pltpu.get_barrier_semaphore()
    for peer in peers:
        pl.semaphore_signal(barrier, inc=1, device_id=peer, device_id_type=MESH)


def arrive(peers):
    pl.semaphore_wait(pltpu.get_barrier_semaphore(), len(peers))


GATHER_STEPS = {
    "begin": (("along", 0), ("out", 0), ("out", 1), ("out", 2)),
    "near": (("z", 0, 1, 2, 3), ("along", 1), ("first", 0, 0, 1, 2, 3)),
    0: (("z", 1, 1, 2, 3), ("along", 2)),
    1: (("second", 0, 0, 1, 2, 3),),
    2: (("first", 1, 0, 1), ("second", 0, 4, 5)),
    3: (("first", 1, 2, 3), ("second", 0, 6, 7)),
    4: (("z", 2, 1, 2, 3),),
    5: (("second", 1, 0, 1, 2, 3),),
    6: (("second", 1, 4, 5, 6, 7),),
    7: (("first", 2, 0, 1),),
    8: (("first", 2, 2, 3),),
    9: (("second", 2, 0, 1, 2, 3, 4, 5, 6, 7),),
}


class Gather:
    ROUTES = ("x_first", "by_core", "by_core")
    Z_LATER = (False, False, False)

    def __init__(self, place, packed, own_bias, w, biases, kept, send, recv, local, bias_sems):
        self.at, self.packed, self.w, self.kept = place, packed, w, kept
        self.own_bias, self.biases = own_bias, biases
        self.send_sems, self.recv_sems, self.local, self.bias_sems = send, recv, local, bias_sems
        self.rows = packed[1].shape[0]
        self.shards = w.shape[1] // self.rows
        self.routes = [getattr(place, name) for name in self.ROUTES]

    def shard(self, s, g, d):
        first = (4 * s + g) * self.w.shape[1] + d * self.rows
        return self.w.at[pl.ds(pl.multiple_of(first, 16), self.rows)]

    def copy(self, s, g, d, slot, peer, source=None):
        here = self.shard(s, g, d)
        return pltpu.make_async_remote_copy(
            src_ref=here if source is None else source,
            dst_ref=here,
            send_sem=self.send_sems.at[s, slot],
            recv_sem=self.recv_sems.at[s, g * self.shards + d],
            device_id=peer,
            device_id_type=MESH,
        )

    def arrived(self, s, g, d):
        self.copy(s, g, d, 0, self.at.sibling).wait_recv()

    def own_copy(self, s):
        return pltpu.make_async_copy(
            self.packed[s], self.shard(s, self.at.mp, self.at.dp), self.local.at[s]
        )

    def along_z(self, s):
        at = self.at
        for k in range(1, 4):
            self.copy(s, at.mp, at.dp, k - 1, at.line[k], self.packed[s]).start()

    def own_out(self, s):
        at = self.at
        self.own_copy(s).start()
        source = self.packed[s]
        self.copy(s, at.mp, at.dp, 3, self.routes[s].first, source).start()
        self.copy(s, at.mp, at.dp, 7, self.routes[s].second, source).start()
        self.copy(s, at.mp, at.dp, 15, at.sibling, source).start()

    def from_z(self, s, k):
        at, (g, x) = self.at, self.at.own_column
        d = 2 * at.zs[k] + x
        self.arrived(s, g, d)
        if not self.Z_LATER[s]:
            self.copy(s, g, d, 3 + k, self.routes[s].first).start()
        self.copy(s, g, d, 7 + k, self.routes[s].second).start()
        self.copy(s, g, d, 15 + k, at.sibling).start()

    def from_first(self, s, k):
        at, (g, x) = self.at, self.routes[s].first_column
        d = 2 * at.zs[k] + x
        self.arrived(s, g, d)
        if self.Z_LATER[s] and k == 0:
            for j in range(1, 4):
                self.copy(s, g, d, 3 + j, at.line[j]).start()
        self.copy(s, g, d, 11 + k, self.routes[s].second).start()
        self.copy(s, g, d, 19 + k, at.sibling).start()

    def from_second(self, s, k):
        at, (g, x) = self.at, self.routes[s].second_columns[k // 4]
        d = 2 * at.zs[k % 4] + x
        self.arrived(s, g, d)
        self.copy(s, g, d, 23 + k, at.sibling).start()

    def group(self, i):
        at = self.at
        return 2 * (at.y + (i // 2) * (1 - 2 * at.y)) + at.core + (i % 2) * (1 - 2 * at.core)

    def slot(self, i):
        return i % 2

    def from_sibling(self, s, g):
        @pl.loop(0, self.shards)
        def _(d):
            self.arrived(s, g, d)

    def keep(self, s, i):
        index = 4 * s + self.group(i)
        return pltpu.make_async_copy(
            square(self.w, index), square(self.kept, index), self.local.at[3 + 4 * s + i]
        )

    def bias_copy(self, k, peer):
        return pltpu.make_async_remote_copy(
            src_ref=self.own_bias,
            dst_ref=self.biases.at[self.at.mp],
            send_sem=self.bias_sems.at[0, k],
            recv_sem=self.bias_sems.at[1, k],
            device_id=peer,
            device_id_type=MESH,
        )

    def bias_copies(self):
        at = self.at
        across = (at.dp, at.across)
        return [self.bias_copy(k, peer) for k, peer in enumerate((at.sibling, across, at.diagonal))]

    def begin(self):
        signal(self.at.peers)
        self.fill()
        arrive(self.at.peers)
        self.steps("begin")
        for copy in self.bias_copies():
            copy.start()
        self.biases[self.at.mp] = self.own_bias[...]

    def near_heads(self):
        self.steps("near")
        for copy in self.bias_copies():
            copy.wait_recv()
        self.own_copy(0).wait()
        self.from_sibling(0, self.group(1))
        self.keep(0, 0).start()
        self.keep(0, 1).start()

    def far_heads(self):
        self.steps("far")
        self.from_sibling(0, self.group(3))
        self.keep(0, 2).start()
        self.keep(0, 3).start()

    def ready(self, section):
        self.steps(7 + section)
        self.own_copy(section).wait()
        for i in (0, 2):
            self.keep(section, i).start()
        if section == 1:
            for i in (1, 3):
                self.group_ready(1, i)

    def group_ready(self, section, i):
        def take():
            self.from_sibling(section, self.group(i))
            self.keep(section, i).start()

        if isinstance(i, int):
            take()
        else:
            pl.when(i % 2 == 1)(take)

    def steps(self, step):
        actions = {
            "along": lambda s, k: self.along_z(s),
            "out": lambda s, k: self.own_out(s),
            "z": self.from_z,
            "first": self.from_first,
            "second": self.from_second,
        }
        for name, s, *ks in GATHER_STEPS.get(step, ()):
            for k in ks or (0,):
                actions[name](s, k)

    def tick(self, step):
        for k in range(8):
            pl.when(step == k)(functools.partial(self.steps, k))

    def end(self):
        for copy in self.bias_copies():
            copy.wait_send()
        for s in range(3):

            @pl.loop(0, 31)
            def _(slot):
                self.copy(s, 0, 0, slot, self.at.sibling).wait_send()

            for i in range(4):
                self.keep(s, i).wait()


def forward_math(
    sizes,
    source,
    lens,
    tokens,
    biases,
    b_out,
    gain_1,
    shift_1,
    b_down,
    gain_2,
    shift_2,
    encoded,
    cls,
    n_1,
    r_1,
    n_2,
    r_2,
    z_out,
    slope_out,
    kv_out,
    q,
    lse,
    ctx,
    x,
    weight,
    bias,
    hidden,
    kv,
    z,
    slope,
    sems,
):
    me = lax.axis_index("mp")
    first = pl.multiple_of(sizes.window_start(me), 16)
    load = pltpu.make_async_copy(tokens.at[pl.ds(first, sizes.window)], x, sems.at[0])
    load.start()
    source.begin()
    fill_mask(sizes, me, lens, bias)
    load.wait()
    half = sizes.groups // 2

    def save_kv(i):
        return pltpu.make_async_copy(
            kv.at[source.slot(i)], kv_out.at[source.group(i)], sems.at[4 + i]
        )

    for span, ready in (((0, half), source.near_heads), ((half, sizes.groups), source.far_heads)):
        ready()
        project(sizes, me, source.group, source.slot, span, x, weight, biases, kv, q)
        for i in range(*span):
            save_kv(i).start()
        attend(sizes, me, source.group, source.slot, span, source.tick, kv, q, bias, lse, ctx)
        for i in range(*span):
            save_kv(i).wait()

    own = pl.ds(sizes.own_offset(me), sizes.own)
    hidden[...] = x[own, :].astype(F32) + as_row(b_out)
    for g in range(sizes.groups):
        hidden[...] += dot(ctx[g], weight(0, g)[:, tile(4, 2)], 1, 1)
    normed, factor = norm_stats(hidden[...])
    n_1[...] = normed
    r_1[...] = factor
    y_1 = normed * as_row(gain_1) + as_row(shift_1)
    hidden[...] = y_1 + as_row(b_down)
    encoded[...] = y_1.astype(BF16)
    source.ready(1)

    @pl.loop(0, sizes.groups)
    def _(g):
        a = dot(encoded[...], weight(1, g)[...]) + biases[g, :, 5 * LANES :]
        out, grad = gelu_and_slope(a)
        z[g] = out.astype(BF16)
        slope[g] = grad.astype(BF16)

    save_z = pltpu.make_async_copy(z, z_out, sems.at[2])
    save_slope = pltpu.make_async_copy(slope, slope_out, sems.at[3])
    save_z.start()
    save_slope.start()
    source.ready(2)

    @pl.loop(0, sizes.groups)
    def _(i):
        g = source.group(i)
        source.group_ready(2, i)
        hidden[...] += dot(z[g], weight(2, g)[...], 1, 1)

    normed, factor = norm_stats(hidden[...])
    n_2[...] = normed
    r_2[...] = factor
    y_2 = (normed * as_row(gain_2) + as_row(shift_2)).astype(BF16)
    encoded[...] = y_2
    cls[...] = dot(start_rows(sizes, me, lens).astype(BF16), y_2)
    source.end()
    save_z.wait()
    save_slope.wait()


def forward_kernel(sizes, lens, tokens, weights, biases, *rest):
    *refs, w, bias, hidden, kv, z, slope, sems, loads = rest
    source = Loads(weights, w, loads)

    def weight(section, g):
        return w.at[section, g]

    forward_math(
        sizes, source, lens, tokens, biases, *refs, weight, bias, hidden, kv, z, slope, sems
    )


def pack(w_key, w_value, w_query, w_out, w_down, b_value, b_query, b_up, packed, own_bias):
    cols = w_key.shape[1]
    for k, weight in enumerate((w_key, w_value, w_query)):
        packed[0, :, k * cols : (k + 1) * cols] = weight[...]
    packed[0, :, 3 * cols :] = w_out[...].astype(F32).T.astype(BF16)
    packed[1] = w_down[...]
    own_bias[...] = jnp.zeros_like(own_bias)
    own_bias[:, cols : 2 * cols] = as_row(b_value)
    own_bias[:, 2 * cols : 3 * cols] = as_row(b_query)
    own_bias[:, 5 * LANES :] = as_row(b_up)


def backward_kernel(
    sizes,
    lens,
    cotangent,
    dcls,
    weights,
    gain_1,
    shift_1,
    gain_2,
    n_1,
    r_1,
    n_2,
    r_2,
    z,
    slope,
    kv,
    q,
    lse,
    ctx,
    dh_1,
    dkv,
    dq,
    grads,
    grads_out,
    small,
    w_attn,
    w_up,
    w_down,
    cot,
    dh,
    low,
    other,
    turned,
    stage,
    dctx,
    delta,
    bias,
    sems,
    out_sems,
):
    me = lax.axis_index("mp")
    load_cot = pltpu.make_async_copy(
        cotangent.at[pl.ds(pl.multiple_of(sizes.own * me, 16), sizes.own)], cot, sems.at[3]
    )
    load_cot.start()
    loads = []
    for s, buffer in ((2, w_down), (1, w_up), (0, w_attn)):
        loads.append(pltpu.make_async_copy(weights.at[s], buffer, sems.at[s]))
        loads[-1].start()
    fill_mask(sizes, me, lens, bias)
    picked = start_rows(sizes, me, lens).astype(BF16)
    high = dcls[...].astype(BF16)
    low_part = (dcls[...] - high.astype(F32)).astype(BF16)
    load_cot.wait()
    dy = cot[...].astype(F32) + dot(picked, high, 0, 0) + dot(picked, low_part, 0, 0)
    small[0:1, :] = jnp.sum(dy * n_2[...], axis=0, keepdims=True)
    small[1:2, :] = jnp.sum(dy, axis=0, keepdims=True)
    grad = norm_back(dy, n_2[...], r_2[...], as_row(gain_2))
    small[2:3, :] = jnp.sum(grad, axis=0, keepdims=True)
    dh[...] = grad
    low[...] = grad.astype(BF16)
    turned[0] = grad.T.astype(BF16)
    y_1 = n_1[...] * as_row(gain_1) + as_row(shift_1)
    other[...] = y_1.astype(BF16)
    turned[1] = y_1.T.astype(BF16)
    for load in loads:
        load.wait()

    def out_copy(section, g, slot):
        return pltpu.make_async_copy(
            stage.at[slot], grads.at[section, g], out_sems.at[slot]
        )

    @pl.loop(0, sizes.groups)
    def _(g):
        @pl.when(g > 0)
        def _():
            out_copy(1, 0, 0).wait()
            out_copy(1, 0, 1).wait()

        stage[1] = dot(turned[0], z[g]).astype(BF16)
        out_copy(1, g, 1).start()
        da = dot(low[...], w_down[g]) * slope[g].astype(F32)
        small[pl.ds(8 + g, 1), :] = jnp.sum(da, axis=0, keepdims=True)
        da_low = da.astype(BF16)
        stage[0] = dot(turned[1], da_low).astype(BF16)
        out_copy(0, g, 0).start()
        dh[...] += dot(da_low, w_up[g], 1, 1)

    dy = dh[...]
    small[3:4, :] = jnp.sum(dy * n_1[...], axis=0, keepdims=True)
    small[4:5, :] = jnp.sum(dy, axis=0, keepdims=True)
    grad = norm_back(dy, n_1[...], r_1[...], as_row(gain_1))
    small[5:6, :] = jnp.sum(grad, axis=0, keepdims=True)
    small[6:8, :] = jnp.zeros_like(small[6:8, :])
    small[12:16, :] = jnp.zeros_like(small[12:16, :])
    dh_1[...] = grad
    low[...] = grad.astype(BF16)
    turned[0] = grad.T.astype(BF16)

    @pl.loop(0, sizes.groups)
    def _(g):
        dctx[g] = dot(low[...], w_attn[g, :, tile(4, 2)]).astype(BF16)
        grads_out[g] = dot(turned[0], ctx[g])

    attend_back(sizes, me, kv, q, bias, lse, ctx, dctx, delta, dkv, dq)
    out_copy(1, 0, 0).wait()
    out_copy(1, 0, 1).wait()


def remote(source, target, send, recv, peer):
    return pltpu.make_async_remote_copy(
        src_ref=source,
        dst_ref=target,
        send_sem=send,
        recv_sem=recv,
        device_id=peer,
        device_id_type=MESH,
    )


class Spread:
    def __init__(self, place, source, whole, send, recv, local):
        self.at, self.source, self.whole = place, source, whole
        self.send, self.recv, self.local = send, recv, local
        self.count = source.shape[0]

    def rows(self, mp):
        return self.whole.at[pl.ds(pl.multiple_of(mp * self.count, 16), self.count)]

    def copy(self, k):
        at = self.at
        target = self.rows(at.across if k == 2 else at.mp)
        source = target if k == 2 else self.source
        peer = (at.dp, at.across) if k == 1 else at.sibling
        return remote(source, target, self.send.at[k], self.recv.at[k], peer)

    def own(self):
        return pltpu.make_async_copy(self.source, self.rows(self.at.mp), self.local)

    def begin(self):
        self.copy(1).start()
        self.copy(0).start()
        self.own().start()

    def forward(self):
        self.copy(1).wait_recv()
        self.copy(2).start()

    def end(self):
        self.copy(0).wait()
        self.copy(1).wait_send()
        self.copy(2).wait()
        self.own().wait()


DURING = {
    0: (("encoded", 0),),
    1: (("second", 2),),
    5: (("first", 2),),
    6: (("second", 1),),
}
BEFORE_LAST = (("line", 2),)
AFTER_LAST = (
    ("begin", 0),
    ("first", 1),
    ("chip", 0),
    ("small", 0),
    ("small", 1),
    ("tokens", 0),
    ("second", 0),
    ("small", 2),
    ("line", 1),
    ("first", 0),
    ("relay", 0),
    ("line", 0),
)


class Scatter:
    STAGE = (0, 2, 0)
    HELD = (8, 6, 4)
    ROUTES = ("by_core", "by_core", "by_core")
    Z_EARLY = ((1,), (1,), (1,))

    def __init__(self, place, parts, inbox, by_second, by_first, by_line, shards, sems):
        self.at, self.parts, self.inbox, self.shards = place, parts, inbox, shards
        self.by_second, self.by_first, self.by_line = by_second, by_first, by_line
        self.core_sems, self.second_sems, self.first_sems, self.line_sems = sems
        self.rows = shards.shape[1]
        self.routes = [getattr(place, name) for name in self.ROUTES]

    def shard(self, s, g, d):
        first = (self.HELD[s] + g // 2) * self.parts.shape[1] + d * self.rows
        return self.parts.at[pl.ds(pl.multiple_of(first, 16), self.rows)]

    def part(self, index):
        return square(self.parts, index)

    def to_sibling(self, s, k):
        at = self.STAGE[s] + k
        return remote(
            self.part(at),
            self.inbox.at[at],
            self.core_sems.at[0, s, k],
            self.core_sems.at[1, s, k],
            self.at.sibling,
        )

    def to_second(self, s, k):
        g, x = self.routes[s].second_columns[1 - k // 4]
        return remote(
            self.shard(s, g, 2 * self.at.zs[3 - k % 4] + x),
            self.by_second.at[s, k],
            self.second_sems.at[0, s, k],
            self.second_sems.at[1, s, k],
            self.routes[s].second,
        )

    def to_first(self, s, k):
        g, x = self.routes[s].first_column
        return remote(
            self.shard(s, g, 2 * self.at.zs[3 - k] + x),
            self.by_first.at[s, k],
            self.first_sems.at[0, s, k],
            self.first_sems.at[1, s, k],
            self.routes[s].first,
        )

    def to_line(self, s, j):
        at = self.at
        return remote(
            self.shard(s, at.mp, 2 * at.zs[j] + at.x),
            self.by_line.at[s, j - 1],
            self.line_sems.at[0, s, j - 1],
            self.line_sems.at[1, s, j - 1],
            at.line[j],
        )

    def chip_shard(self, s, g, z, x):
        d = 2 * z + x
        rows = pl.ds(pl.multiple_of(d * self.rows, 16), self.rows)
        self.shard(s, g, d)[...] += self.inbox[self.STAGE[s] + g // 2, rows]

    def chip_sum(self, s):
        for k in range(2):
            self.to_sibling(s, k).wait_recv()
        for k in range(8):
            g, x = self.routes[s].second_columns[1 - k // 4]
            self.chip_shard(s, g, self.at.zs[3 - k % 4], x)
            self.to_second(s, k).start()
        for g, x in (self.routes[s].first_column, self.at.own_column):

            @pl.loop(0, 4)
            def _(z):
                self.chip_shard(s, g, z, x)

    def other_line(self, s, j):
        g, x = self.routes[s].first_column
        return remote(
            self.shard(s, g, 2 * self.at.zs[j] + x),
            self.by_first.at[s, j],
            self.first_sems.at[0, s, j],
            self.first_sems.at[1, s, j],
            self.at.line[j],
        )

    def last_cross(self, s):
        g, x = self.routes[s].first_column
        return remote(
            self.shard(s, g, 2 * self.at.z + x),
            self.by_first.at[s, 0],
            self.first_sems.at[0, s, 0],
            self.first_sems.at[1, s, 0],
            self.routes[s].first,
        )

    def by_kind(self, s, early, late):
        cores = self.Z_EARLY[s]
        if len(cores) == 1:
            pl.when(self.at.core == cores[0])(functools.partial(early, s))
            pl.when(self.at.core != cores[0])(functools.partial(late, s))
        else:
            (early if cores else late)(s)

    def from_second(self, s):
        self.by_kind(s, self.from_second_early, self.from_second_late)

    def from_first(self, s):
        self.by_kind(s, self.from_first_early, self.from_first_late)

    def from_line(self, s):
        self.by_kind(s, self.from_line_early, self.from_line_late)

    def from_second_early(self, s):
        at, (g, x) = self.at, self.routes[s].first_column
        for k in range(8):
            self.to_second(s, k).wait_recv()
            j = 3 - k % 4
            mine = self.shard(s, g, 2 * at.zs[j] + x) if k < 4 else self.shard(s, at.mp, 2 * at.zs[j] + at.x)
            if k < 7:
                mine[...] += self.by_second[s, k]
            if j:
                (self.other_line if k < 4 else self.to_line)(s, j).start()

    def from_first_early(self, s):
        g, x = self.routes[s].first_column
        mine = self.shard(s, g, 2 * self.at.z + x)
        total = mine[...].astype(F32)
        for j in (1, 2, 3):
            self.other_line(s, j).wait_recv()
            total = total + self.by_first[s, j].astype(F32)
        mine[...] = total.astype(BF16)
        self.last_cross(s).start()

    def from_line_early(self, s):
        at = self.at
        mine = self.shard(s, at.mp, 2 * at.z + at.x)
        total = mine[...].astype(F32) + self.by_second[s, 7].astype(F32)
        for j in range(1, 4):
            self.to_line(s, j).wait_recv()
            total = total + self.by_line[s, j - 1].astype(F32)
        self.last_cross(s).wait_recv()
        self.shards[s] = total + self.by_first[s, 0].astype(F32)

    def from_second_late(self, s):
        g, x = self.routes[s].first_column
        for k in range(4):
            self.to_second(s, k).wait_recv()
            self.shard(s, g, 2 * self.at.zs[3 - k] + x)[...] += self.by_second[s, k]
            self.to_first(s, k).start()

    def from_first_late(self, s):
        at = self.at
        for k in range(4):
            self.to_second(s, 4 + k).wait_recv()
            self.to_first(s, k).wait_recv()
            mine = self.shard(s, at.mp, 2 * at.zs[3 - k] + at.x)
            total = (
                mine[...].astype(F32)
                + self.by_second[s, 4 + k].astype(F32)
                + self.by_first[s, k].astype(F32)
            )
            if k < 3:
                mine[...] = total.astype(BF16)
                self.to_line(s, 3 - k).start()
            else:
                self.shards[s] = total

    def from_line_late(self, s):
        for j in range(1, 4):
            self.to_line(s, j).wait_recv()
            self.shards[s] += self.by_line[s, j - 1].astype(F32)

    def sent_to_sibling(self, s):
        for k in range(2):
            self.to_sibling(s, k).wait_send()

    def end(self):
        for s in range(3):
            for k in range(8):
                self.to_second(s, k).wait_send()
            for k in range(4):
                self.to_first(s, k).wait_send()
            for j in range(1, 4):
                self.to_line(s, j).wait_send()


class SmallSums:
    def __init__(self, place, sums, inbox, sems):
        self.at, self.sums, self.inbox, self.sems = place, sums, inbox, sems
        at = place
        self.peers = [at.sibling, at.x_peer, at.y_peer, *at.line[1:]]

    def copy(self, k):
        return remote(
            self.sums.at[min(k, 3)],
            self.inbox.at[k],
            self.sems.at[0, k],
            self.sems.at[1, k],
            self.peers[k],
        )

    def begin(self):
        self.copy(0).start()

    def step(self, k):
        self.copy(k).wait_recv()
        self.sums[k + 1] = self.sums[k] + self.inbox[k]
        for nxt in (k + 1,) if k < 2 else (3, 4, 5):
            self.copy(nxt).start()

    def end(self, out):
        for k in range(3, 6):
            self.copy(k).wait_recv()
        out[...] = (self.sums[3] + self.inbox[3]) + (self.inbox[4] + self.inbox[5])
        for k in range(6):
            self.copy(k).wait_send()


def fold(rows):
    half = rows.shape[1] // 2
    return jnp.concatenate([rows[:, :half], rows[:, half:]], axis=0).astype(BF16)


def unfold(packed):
    wide = packed.astype(F32)
    return jnp.concatenate([wide[:8], wide[8:]], axis=1)


class Scoring:
    def __init__(self, place, ways, cls, gold, passages, scores, lse, buffers, sems):
        self.at, self.ways, self.cls, self.gold = place, ways, cls, gold
        self.passages, self.scores, self.lse = passages, scores, lse
        self.part, self.parts, self.firsts, self.rows = buffers[:4]
        self.sent, self.got, self.stats, self.got_stats = buffers[4:]
        self.mp_sems, self.sems = sems
        at = place
        self.mates = (at.sibling, (at.dp, at.across), at.diagonal)
        self.others = [(lax.rem(at.dp + k, ways), at.mp) for k in range(1, ways)]

    def mate(self, k):
        return remote(
            self.part, self.parts.at[k], self.mp_sems.at[0, k], self.mp_sems.at[1, k], self.mates[k]
        )

    def first_copy(self, k):
        mine = self.firsts.at[self.at.dp]
        return remote(
            mine, mine, self.sems.at[0, 0, k - 1], self.sems.at[0, 1, k - 1], self.others[k - 1]
        )

    def back_copy(self, which, k):
        peer = self.others[k - 1]
        return remote(
            self.sent.at[which, peer[0]],
            self.got.at[which, self.at.dp],
            self.sems.at[1 + which, 0, k - 1],
            self.sems.at[1 + which, 1, k - 1],
            peer,
        )

    def stat_copy(self, k):
        peer = self.others[k - 1]
        return remote(
            self.stats.at[peer[0]],
            self.got_stats.at[self.at.dp],
            self.sems.at[3, 0, k - 1],
            self.sems.at[3, 1, k - 1],
            peer,
        )

    def start_cls(self):
        self.part[...] = fold(self.cls[...])
        for k in range(3):
            self.mate(k).start()

    def start_gold(self):
        places = self.at.dp * self.passages.shape[0] + lax.broadcasted_iota(
            jnp.int32, (self.passages.shape[0], self.gold.shape[0]), 0
        )
        target = jnp.where(as_row(self.gold) == places, 1.0, 0.0).astype(BF16)
        self.put(0, dot(target, self.passages[...], 0, 0))
        for k in range(1, self.ways):
            self.back_copy(0, k).start()

    def put(self, which, rows):
        for d in range(self.ways):
            self.sent[which, d] = fold(rows[8 * d : 8 * d + 8])
        self.got[which, self.at.dp] = self.sent[which, self.at.dp]

    def start_firsts(self):
        total = self.part[...].astype(F32)
        for k in range(3):
            self.mate(k).wait_recv()
            total = total + self.parts[k].astype(F32)
        self.firsts[self.at.dp] = total.astype(BF16)
        for k in range(1, self.ways):
            self.first_copy(k).start()

    def start_back(self):
        for k in range(1, self.ways):
            self.first_copy(k).wait_recv()
        for d in range(self.ways):
            self.rows[8 * d : 8 * d + 8, :] = unfold(self.firsts[d])
        table = dot(self.rows[...].astype(BF16), self.passages[...], 1, 1)
        self.scores[...] = table
        peak = jnp.max(table, axis=1, keepdims=True)
        e = jnp.exp(table - peak)
        total = jnp.sum(e, axis=1, keepdims=True)
        lane = lax.broadcasted_iota(jnp.int32, (8, LANES), 1)
        for d in range(self.ways):
            rows = slice(8 * d, 8 * d + 8)
            self.stats[d] = jnp.where(lane == 0, peak[rows], total[rows])
        self.got_stats[self.at.dp] = self.stats[self.at.dp]
        for k in range(1, self.ways):
            self.stat_copy(k).start()
        self.put(1, dot(e.astype(BF16), self.passages[...]))
        for k in range(1, self.ways):
            self.back_copy(1, k).start()

    def result(self):
        for k in range(1, self.ways):
            self.back_copy(0, k).wait_recv()
            self.stat_copy(k).wait_recv()
        peaks = [self.got_stats[d][:, 0:1] for d in range(self.ways)]
        top = functools.reduce(jnp.maximum, peaks)
        scales = [jnp.exp(peak - top) for peak in peaks]
        total = sum(scale * self.got_stats[d][:, 1:2] for d, scale in enumerate(scales))
        self.lse[...] = top + jnp.log(total)
        for k in range(1, self.ways):
            self.back_copy(1, k).wait_recv()
        grad = -sum(unfold(self.got[0, d]) for d in range(self.ways))
        for d in range(self.ways):
            grad = grad + (scales[d] / total) * unfold(self.got[1, d])
        return grad

    def end(self):
        for k in range(3):
            self.mate(k).wait_send()
        for k in range(1, self.ways):
            self.first_copy(k).wait_send()
            self.back_copy(0, k).wait_send()
            self.back_copy(1, k).wait_send()
            self.stat_copy(k).wait_send()


class Halo:
    def __init__(self, sizes, place, dkv, sent, got, sems):
        self.sizes, self.at, self.dkv, self.sent, self.got, self.sems = sizes, place, dkv, sent, got, sems
        self.has = (place.mp > 0, place.mp < sizes.groups - 1)
        offset = sizes.own_offset(place.mp)
        self.starts = (offset - LONGEST, offset + sizes.own)
        self.into = (sizes.own - LONGEST, 0)

    def copy(self, g, side):
        slot = g % 2
        return remote(
            self.sent.at[slot, side],
            self.got.at[g, side],
            self.sems.at[0, slot, side],
            self.sems.at[1, g, side],
            (self.at.dp, self.at.mp + 2 * side - 1),
        )

    def start(self, g):
        for side in range(2):

            @pl.when(self.has[side])
            def _():
                pl.when(g > 1)(self.copy(g, side).wait_send)
                rows = pl.ds(pl.multiple_of(self.starts[side], 16), LONGEST)
                self.sent[g % 2, side] = self.dkv[rows, :].astype(BF16)
                self.copy(g, side).start()

    def add(self, g, own, total):
        for side in range(2):

            @pl.when(self.has[1 - side])
            def _():
                self.copy(g, side).wait_recv()
                rows = pl.ds(self.into[side], LONGEST)
                more = self.got[g, side].astype(F32)
                total[:, tile(0, 3)] += jnp.sum(more, axis=0, keepdims=True)
                own[rows, tile(0, 3)] = (own[rows, tile(0, 3)].astype(F32) + more).astype(BF16)

    def end(self):
        for side in range(2):

            @pl.when(self.has[side])
            def _():
                self.copy(2, side).wait_send()
                self.copy(3, side).wait_send()


def finish_math(
    sizes,
    at,
    lens,
    cotangent,
    tokens,
    passages,
    gold,
    gain_1,
    shift_1,
    gain_2,
    held,
    kept,
    outs,
    landing,
    sems,
    ffn,
    kv,
    dctx,
    dkv,
    halo_sent,
    rows_low,
    turned,
    low,
    delta,
):
    parts, cls, r_1, r_2, lse, q, ctx, encoded, n_1, work, bias = held
    weights, z_in, slope_in, kv_in = kept
    scores, query_lse, small_out, shards, encoded_whole, token_whole = outs
    inbox, by_second, by_first, by_line, halo_got, sums, sums_in, *scored = landing
    part, parts_in, firsts, first_rows, back_sent, back_got, stats, stats_got = scored
    (
        load_sems,
        kv_sems,
        ffn_sems,
        spread_sems,
        core_sems,
        second_sems,
        first_sems,
        line_sems,
        halo_sems,
        small_sems,
        mp_sems,
        score_sems,
    ) = sems
    me = at.mp
    own_rows = pl.ds(pl.multiple_of(sizes.own * me, 16), sizes.own)
    ways = firsts.shape[0]
    table = parts.at[pl.ds(Scatter.HELD[0] * sizes.width, passages.shape[0])]
    scatter = Scatter(
        at, parts, inbox, by_second, by_first, by_line, shards,
        (core_sems, second_sems, first_sems, line_sems),
    )
    halo = Halo(sizes, at, dkv, halo_sent, halo_got, halo_sems)
    spread = Spread(at, encoded, encoded_whole, spread_sems.at[0, 0], spread_sems.at[0, 1], load_sems.at[8])
    token_spread = Spread(
        at, rows_low, token_whole, spread_sems.at[1, 0], spread_sems.at[1, 1], load_sems.at[9]
    )
    small = SmallSums(at, sums, sums_in, small_sems)

    def load(k, source, target):
        return pltpu.make_async_copy(source, target, load_sems.at[k])

    loads = [
        load(0, passages, table),
        load(1, cotangent.at[own_rows], ffn.at[1]),
    ]
    weight_slots = 10

    def kv_load(g):
        return pltpu.make_async_copy(kv_in.at[g], kv, kv_sems.at[0])

    for copy in loads:
        copy.start()

    scoring = Scoring(
        at,
        ways,
        cls,
        gold,
        table,
        scores,
        query_lse,
        (part, parts_in, firsts, first_rows, back_sent, back_got, stats, stats_got),
        (mp_sems, score_sems),
    )
    scoring.start_cls()
    kv_load(0).start()

    def group_of(i):
        return jnp.where(i < 2, 1 - at.core + 2 * i, at.core + 2 * (i - 2))

    def wide(k):
        return square(parts, weight_slots + k)

    def z_load(i):
        return pltpu.make_async_copy(z_in.at[group_of(i)], ffn.at[i % 2], ffn_sems.at[i % 2, 0])

    def ffn_loads(i):
        slot, g = i % 2, group_of(i)
        return [
            pltpu.make_async_copy(square(weights, 8 + g), wide(2 * slot), ffn_sems.at[slot, 1]),
            pltpu.make_async_copy(square(weights, 4 + g), wide(2 * slot + 1), ffn_sems.at[slot, 2]),
            pltpu.make_async_copy(slope_in.at[g], ffn.at[2 - 2 * slot], ffn_sems.at[slot, 3]),
        ]

    z_load(0).start()
    for copy in ffn_loads(0):
        copy.start()

    loads[0].wait()
    scoring.start_gold()
    scoring.start_firsts()
    spread.begin()
    picked = start_rows(sizes, me, lens).astype(BF16)
    turned[1] = (n_1[...] * as_row(gain_1) + as_row(shift_1)).T.astype(BF16)
    scoring.start_back()
    loads[1].wait()
    dcls = scoring.result()
    high = dcls.astype(BF16)
    rest = (dcls - high.astype(F32)).astype(BF16)
    dy = ffn[1].astype(F32) + dot(picked, high, 0, 0) + dot(picked, rest, 0, 0)
    mine = sums.at[0]
    mine[0:1, :] = jnp.sum(dy * work[1], axis=0, keepdims=True)
    mine[1:2, :] = jnp.sum(dy, axis=0, keepdims=True)
    grad = norm_back(dy, work[1], r_2[...], as_row(gain_2))
    mine[2:3, :] = jnp.sum(grad, axis=0, keepdims=True)
    work[0] = grad
    rows_low[...] = grad.astype(BF16)
    turned[0] = grad.T.astype(BF16)

    def into(s, i):
        return jnp.where(i < 2, Scatter.STAGE[s] + i, Scatter.HELD[s] + i - 2)

    @pl.loop(0, sizes.groups)
    def _(i):
        z_load(i).wait()

        @pl.when(i < 3)
        def _():
            z_load(i + 1).start()

        square(parts, into(2, i))[...] = dot(turned[0], ffn[i % 2]).astype(BF16)
        pl.when(i < 2)(lambda: scatter.to_sibling(2, i).start())

    scatter.chip_sum(2)

    @pl.loop(0, sizes.groups)
    def _(i):
        slot, g = i % 2, group_of(i)
        for copy in ffn_loads(i):
            copy.wait()

        @pl.when(i < 3)
        def _():
            for copy in ffn_loads(i + 1):
                copy.start()

        da = dot(rows_low[...], wide(2 * slot)[...]) * ffn[2 - 2 * slot].astype(F32)
        mine[pl.ds(8 + g, 1), :] = jnp.sum(da, axis=0, keepdims=True)
        da_low = da.astype(BF16)
        square(parts, into(1, i))[...] = dot(turned[1], da_low).astype(BF16)
        pl.when(i < 2)(lambda: scatter.to_sibling(1, i).start())
        work[0] += dot(da_low, wide(2 * slot + 1)[...], 1, 1)

    load_w = pltpu.make_async_copy(
        weights.at[pl.ds(0, 4 * sizes.width)],
        parts.at[pl.ds(weight_slots * sizes.width, 4 * sizes.width)],
        load_sems.at[7],
    )
    load_w.start()
    load_x = load(1, tokens.at[own_rows], ffn.at[0])
    load_x.start()
    scatter.chip_sum(1)
    scatter.sent_to_sibling(2)

    dy = work[0]
    mine[3:4, :] = jnp.sum(dy * n_1[...], axis=0, keepdims=True)
    mine[4:5, :] = jnp.sum(dy, axis=0, keepdims=True)
    grad = norm_back(dy, n_1[...], r_1[...], as_row(gain_1))
    mine[5:6, :] = jnp.sum(grad, axis=0, keepdims=True)
    mine[6:8, :] = jnp.zeros((2, sizes.width), F32)
    mine[12:24, :] = jnp.zeros((12, sizes.width), F32)
    work[1] = grad
    rows_low[...] = grad.astype(BF16)
    turned[0] = grad.T.astype(BF16)
    load_x.wait()
    turned[1] = ffn[0].astype(F32).T.astype(BF16)
    load_w.wait()

    @pl.loop(0, sizes.groups)
    def _(g):
        dctx[g] = dot(rows_low[...], wide(g)[:, tile(4, 2)]).astype(BF16)

    actions = {
        "second": scatter.from_second,
        "first": scatter.from_first,
        "line": scatter.from_line,
        "chip": scatter.chip_sum,
        "small": small.step,
        "begin": lambda s: small.begin(),
        "tokens": lambda s: token_spread.begin(),
        "relay": lambda s: token_spread.forward(),
        "encoded": lambda s: spread.forward(),
    }

    def run(names):
        for name, s in names:
            actions[name](s)

    def tick(now):
        for k, names in DURING.items():
            pl.when(now == k)(functools.partial(run, names))

    def finalize(g):
        slot = g % 2
        halo.add(g, low.at[slot], mine.at[pl.ds(16 + g, 1)])
        work[1] += dot(low[slot], wide(g)[:, tile(0, 5)], 1, 1)
        into = jnp.where(g % 2 == at.core, Scatter.HELD[0], Scatter.STAGE[0]) + g // 2
        made = dot(turned[1], low[slot])
        more = dot(turned[0], ctx[g])
        target = square(parts, into)
        target[:, tile(0, 4)] = made[:, tile(0, 4)].astype(BF16)
        target[:, tile(4)] = (made[:, tile(4)] + more[:, tile(0)]).astype(BF16)
        target[:, tile(5)] = more[:, tile(1)].astype(BF16)

        @pl.when(g % 2 != at.core)
        def _():
            scatter.to_sibling(0, g // 2).start()

    own = pl.ds(sizes.own_offset(me), sizes.own)

    @pl.loop(0, sizes.groups)
    def _(g):
        slot = g % 2
        kv_load(g).wait()
        delta[...] = delta_rows(dctx[g], ctx[g])
        dkv[...] = jnp.zeros_like(dkv)
        for b in range(sizes.blocks):
            tick(g * sizes.blocks + b)
            rows = slice(b * sizes.block, (b + 1) * sizes.block)
            dq = attend_back_block(
                sizes, me, g, b, kv, q, bias, lse, dctx, delta, dkv
            )
            total = jnp.sum(dq, axis=0, keepdims=True)
            mine[pl.ds(16 + g, 1), tile(3, 2)] += total
            low[slot, rows, tile(3, 2)] = dq.astype(BF16)

        @pl.when(g < sizes.groups - 1)
        def _():
            kv_load(g + 1).start()

        halo.start(g)
        mine[pl.ds(16 + g, 1), tile(0, 3)] = jnp.sum(dkv[own, :], axis=0, keepdims=True)
        low[slot, :, tile(0, 3)] = dkv[own, :].astype(BF16)

        @pl.when(g > 0)
        def _():
            finalize(g - 1)

    run(BEFORE_LAST)
    finalize(sizes.groups - 1)
    rows_low[...] = work[1].astype(BF16)
    run(AFTER_LAST)
    small.end(small_out)
    scatter.sent_to_sibling(1)
    scatter.sent_to_sibling(0)
    scatter.end()
    halo.end()
    scoring.end()
    spread.end()
    token_spread.end()


def layer_kernel(sizes, lens, tokens, cotangent, passages, gold, *rest):
    weights, rows, outs, kept = rest[:9], rest[9:15], rest[15:21], rest[21:25]
    w, cls, r_1, r_2, lse, q, ctx, encoded, n_1, work, bias, packed, own_bias, biases = rest[25:39]
    landing, sems = rest[39:54], rest[54:]
    w_key, w_value, w_query, w_out, w_up, w_down, b_value, b_query, b_up = weights
    own, width, groups = sizes.own, sizes.width, sizes.groups
    at = Place()
    source = Gather(at, (packed.at[0], w_up, packed.at[1]), own_bias, w, biases, kept[0], *sems[:4])

    def fill():
        pack(w_key, w_value, w_query, w_out, w_down, b_value, b_query, b_up, packed, own_bias)

    source.fill = fill

    def weight(section, g):
        return square(w, 4 * section + g)

    def forward(x, kv, z, slope):
        forward_math(
            sizes, source, lens, tokens, biases, *rows, encoded, cls, n_1, r_1, work.at[1], r_2,
            *kept[1:], q, lse, ctx, x, weight, bias, work.at[0], kv, z, slope, sems[4],
        )

    pl.run_scoped(
        forward,
        pltpu.VMEM((sizes.window, width), BF16),
        pltpu.VMEM((2, sizes.window, 3 * LANES), BF16),
        pltpu.VMEM((groups, own, width), BF16),
        pltpu.VMEM((groups, own, width), BF16),
    )
    held = (w, cls, r_1, r_2, lse, q, ctx, encoded, n_1, work, bias)
    z_kept, slope_kept, kv_kept = kept[1:]
    finish = functools.partial(
        finish_math, sizes, at, lens, cotangent, tokens, passages, gold, rows[1], rows[2], rows[4],
        held, (kept[0], z_kept, slope_kept, kv_kept), outs, landing, sems[5:],
    )
    pl.run_scoped(
        finish,
        pltpu.VMEM((3, own, width), BF16),
        pltpu.VMEM((sizes.window, 3 * LANES), BF16),
        pltpu.VMEM((groups, own, 2 * LANES), BF16),
        pltpu.VMEM((sizes.window, 3 * LANES), F32),
        pltpu.VMEM((2, 2, LONGEST, 3 * LANES), BF16),
        pltpu.VMEM((own, width), BF16),
        pltpu.VMEM((2, width, own), BF16),
        pltpu.VMEM((2, own, 5 * LANES), BF16),
        pltpu.VMEM((8, own), F32),
    )


def input_kernel(sizes, tokens, weights, dkv, dq, dh_1, grads_out, token_grad, grads, small, turned, low):
    turned[...] = tokens[...].astype(F32).T.astype(BF16)
    total = dh_1[...]
    for g in range(sizes.groups):
        small[g, :, tile(0, 3)] = jnp.sum(dkv[g], axis=0, keepdims=True)
        small[g, :, tile(3, 2)] = jnp.sum(dq[g], axis=0, keepdims=True)
        low[:, tile(0, 3)] = dkv[g].astype(BF16)
        low[:, tile(3, 2)] = dq[g].astype(BF16)
        total = total + dot(low[...], weights[g, :, tile(0, 5)], 1, 1)
        made = dot(turned[...], low[...])
        grads[g, :, tile(0, 4)] = made[:, tile(0, 4)].astype(BF16)
        grads[g, :, tile(4)] = (made[:, tile(4)] + grads_out[g, :, tile(0)]).astype(BF16)
        grads[g, :, tile(5)] = grads_out[g, :, tile(1)].astype(BF16)
    token_grad[...] = total.astype(BF16)


def specs(*spaces):
    return [pl.BlockSpec(memory_space=s) for s in spaces]


def params(**more):
    return pltpu.CompilerParams(vmem_limit_bytes=64 * 2**20, **more)


def run_forward(sizes, lengths, tokens, weights, rows):
    own, width, groups = sizes.own, sizes.width, sizes.groups
    docs = lengths.shape[1]
    shape = jax.ShapeDtypeStruct
    outs = [
        shape((own, width), BF16),
        shape((docs, width), F32),
        shape((own, width), F32),
        shape((own, 1), F32),
        shape((own, width), F32),
        shape((own, 1), F32),
        shape((groups, own, width), BF16),
        shape((groups, own, width), BF16),
        shape((groups, sizes.window, 3 * LANES), BF16),
        shape((groups, own, 2 * LANES), BF16),
        shape((groups, sizes.blocks, 8, sizes.block), F32),
        shape((groups, own, 2 * LANES), BF16),
    ]
    spaces = [*[VMEM] * 6, ANY, ANY, ANY, *[VMEM] * 3]
    scratch = [
        pltpu.VMEM((sizes.window, width), BF16),
        pltpu.VMEM((3, groups, width, width), BF16),
        pltpu.VMEM((sizes.blocks, sizes.keys, sizes.block), F32),
        pltpu.VMEM((own, width), F32),
        pltpu.VMEM((groups, sizes.window, 3 * LANES), BF16),
        pltpu.VMEM((groups, own, width), BF16),
        pltpu.VMEM((groups, own, width), BF16),
        pltpu.SemaphoreType.DMA((4 + groups,)),
    ]
    scratch.append(pltpu.SemaphoreType.DMA((3,)))
    return pl.pallas_call(
        functools.partial(forward_kernel, sizes),
        out_shape=outs,
        in_specs=specs(SMEM, ANY, ANY, *[VMEM] * 7),
        out_specs=specs(*spaces),
        scratch_shapes=scratch,
        compiler_params=params(),
        name="forward",
    )(lengths, tokens, *weights, *rows)


def run_backward(sizes, lengths, cotangent, dcls, weights, gain_1, shift_1, gain_2, saved):
    own, width, groups = sizes.own, sizes.width, sizes.groups
    shape = jax.ShapeDtypeStruct
    outs = (
        shape((own, width), F32),
        shape((groups, sizes.window, 3 * LANES), F32),
        shape((groups, own, 2 * LANES), F32),
        shape((2, groups, width, width), BF16),
        shape((groups, width, 2 * LANES), F32),
        shape((16, width), F32),
    )
    return pl.pallas_call(
        functools.partial(backward_kernel, sizes),
        out_shape=outs,
        in_specs=specs(SMEM, ANY, VMEM, ANY, *[VMEM] * (3 + len(saved))),
        out_specs=specs(VMEM, VMEM, VMEM, ANY, VMEM, VMEM),
        scratch_shapes=[
            pltpu.VMEM((groups, width, width), BF16),
            pltpu.VMEM((groups, width, width), BF16),
            pltpu.VMEM((groups, width, width), BF16),
            pltpu.VMEM((own, width), BF16),
            pltpu.VMEM((own, width), F32),
            pltpu.VMEM((own, width), BF16),
            pltpu.VMEM((own, width), BF16),
            pltpu.VMEM((2, width, own), BF16),
            pltpu.VMEM((2, width, width), BF16),
            pltpu.VMEM((groups, own, 2 * LANES), BF16),
            pltpu.VMEM((8, own), F32),
            pltpu.VMEM((sizes.blocks, sizes.keys, sizes.block), F32),
            pltpu.SemaphoreType.DMA((4,)),
            pltpu.SemaphoreType.DMA((2,)),
        ],
        compiler_params=params(),
        name="backward",
    )(lengths, cotangent, dcls, weights, gain_1, shift_1, gain_2, *saved)


def run_input(sizes, own_tokens, w_attn, dkv, dq, dh_1, grads_out):
    own, width, groups = sizes.own, sizes.width, sizes.groups
    shape = jax.ShapeDtypeStruct
    outs = (
        shape((own, width), BF16),
        shape((groups, width, width), BF16),
        shape((groups, 1, 5 * LANES), F32),
    )
    return pl.pallas_call(
        functools.partial(input_kernel, sizes),
        out_shape=outs,
        in_specs=specs(*[VMEM] * 6),
        out_specs=specs(*[VMEM] * 3),
        scratch_shapes=[pltpu.VMEM((width, own), BF16), pltpu.VMEM((own, 5 * LANES), BF16)],
        compiler_params=params(),
        name="inputs",
    )(own_tokens, w_attn, dkv, dq, dh_1, grads_out)


def run_layer(sizes, lengths, tokens, cotangent, passages, gold, weights, rows):
    own, width, groups = sizes.own, sizes.width, sizes.groups
    queries, docs = gold.shape[0], lengths.shape[1]
    ways = queries // docs
    shard, half = width // ways, width // 2
    shape, vmem, dma = jax.ShapeDtypeStruct, pltpu.VMEM, pltpu.SemaphoreType.DMA
    outs = (
        shape((queries, passages.shape[0]), F32),
        shape((docs, 1), F32),
        shape((24, width), F32),
        shape((3, shard, width), F32),
        shape(tokens.shape, BF16),
        shape(tokens.shape, BF16),
        shape((12 * width, width), BF16),
        shape((groups, own, width), BF16),
        shape((groups, own, width), BF16),
        shape((groups, sizes.window, 3 * LANES), BF16),
    )
    bias_width = 5 * LANES + weights[8].shape[0]
    scratch = [
        vmem((14 * width, width), BF16),
        vmem((docs, width), F32),
        vmem((own, 1), F32),
        vmem((own, 1), F32),
        vmem((groups, sizes.blocks, 8, sizes.block), F32),
        vmem((groups, own, 2 * LANES), BF16),
        vmem((groups, own, 2 * LANES), BF16),
        vmem((own, width), BF16),
        vmem((own, width), F32),
        vmem((2, own, width), F32),
        vmem((sizes.blocks, sizes.keys, sizes.block), F32),
        vmem((2, shard, width), BF16),
        vmem((1, bias_width), F32),
        vmem((groups, 1, bias_width), F32),
        vmem((4, width, width), BF16),
        vmem((3, 8, shard, width), BF16),
        vmem((3, 4, shard, width), BF16),
        vmem((3, 3, shard, width), BF16),
        vmem((groups, 2, LONGEST, 3 * LANES), BF16),
        vmem((4, 24, width), F32),
        vmem((6, 24, width), F32),
        vmem((16, half), BF16),
        vmem((3, 16, half), BF16),
        vmem((ways, 16, half), BF16),
        vmem((queries, width), F32),
        vmem((2, ways, 16, half), BF16),
        vmem((2, ways, 16, half), BF16),
        vmem((ways, 8, LANES), F32),
        vmem((ways, 8, LANES), F32),
        dma((3, 31)),
        dma((3, 32)),
        dma((15,)),
        dma((2, 3)),
        dma((4 + groups,)),
        dma((10,)),
        dma((1,)),
        dma((2, 4)),
        dma((2, 2, 3)),
        dma((2, 3, 2)),
        dma((2, 3, 8)),
        dma((2, 3, 4)),
        dma((2, 3, 3)),
        dma((2, 4, 2)),
        dma((2, 6)),
        dma((2, 3)),
        dma((4, 2, ways - 1)),
    ]
    return pl.pallas_call(
        functools.partial(layer_kernel, sizes),
        out_shape=outs,
        in_specs=specs(SMEM, ANY, ANY, ANY, *[VMEM] * (1 + len(weights) + len(rows))),
        out_specs=specs(*[VMEM] * 4, *[ANY] * 6),
        scratch_shapes=scratch,
        compiler_params=params(collective_id=0, has_side_effects=True),
        name="layer",
    )(lengths, tokens, cotangent, passages, gold, *weights, *rows)[:6]


def cut_along(array, dim, devices):
    before, after = (array.shape[:dim], array.shape[dim + 1 :])
    return jnp.moveaxis(array.reshape(*before, devices, -1, *after), dim, 0)


def summed_on_arrival(array, axis, dim):
    pieces = cut_along(array, dim, lax.axis_size(axis))
    arrived = lax.all_to_all(pieces, axis, split_axis=0, concat_axis=0, tiled=True)
    return arrived.astype(F32).sum(axis=0)


def score(cls, passages, gold):
    all_first = lax.all_gather(cls, "dp", axis=0, tiled=True)
    table = dot(all_first, passages, 1, 1)
    peak = lax.pmax(jnp.max(table, axis=1), "dp")
    total = lax.psum(jnp.sum(jnp.exp(table - peak[:, None]), axis=1), "dp")
    own = cls.shape[0]
    lse = lax.dynamic_slice_in_dim(peak + jnp.log(total), lax.axis_index("dp") * own, own)
    soft = jnp.exp(table - peak[:, None]) / total[:, None]
    first = lax.axis_index("dp") * table.shape[1]
    columns = first + jnp.arange(table.shape[1], dtype=jnp.int32)
    target = (gold[:, None] == columns[None, :]).astype(F32)
    grad = dot((soft - target).astype(BF16), passages)
    return table, lse, summed_on_arrival(grad.astype(BF16), "dp", 0)


def plain_layer(sizes, tokens, cotangent, lengths, gold, passages, shards, rows):
    me, groups = lax.axis_index("mp"), sizes.groups
    w_key, w_value, w_query, w_out, w_up, w_down, b_value, b_query, b_up = shards
    packed = jnp.stack(
        [jnp.concatenate([w_key, w_value, w_query, w_out.T], axis=1), w_up, w_down]
    )
    c = w_key.shape[1]
    zeros = jnp.zeros((c,), F32)
    own_bias = jnp.concatenate([zeros, b_value, b_query, zeros[:HEAD], b_up])[None]
    whole = lax.all_gather(lax.all_gather(packed, "dp", axis=1, tiled=True), "mp", axis=1)
    biases = lax.all_gather(own_bias, "mp", axis=0)
    encoded, cls, *saved = run_forward(sizes, lengths, tokens, (whole, biases), rows)
    cls = lax.psum(cls, "mp").astype(BF16)
    table, lse, dcls = score(cls, passages, gold)
    n_1, r_1, n_2, r_2, z, slope, kv, q, logs, ctx = saved
    dh_1, dkv, dq, grads_ffn, grads_out, small = run_backward(
        sizes, lengths, cotangent, dcls, whole, rows[1], rows[2], rows[4], saved
    )
    halo, own = LONGEST, sizes.own
    offset = own * me - sizes.window_start(me)
    to_left = lax.dynamic_slice_in_dim(dkv, offset - halo, halo, axis=1).astype(BF16)
    to_right = lax.dynamic_slice_in_dim(dkv, offset + own, halo, axis=1).astype(BF16)
    from_right = lax.ppermute(to_left, "mp", [(i, i - 1) for i in range(1, groups)])
    from_left = lax.ppermute(to_right, "mp", [(i, i + 1) for i in range(groups - 1)])
    dkv = lax.dynamic_slice_in_dim(dkv, offset, own, axis=1)
    dkv = dkv.at[:, own - halo :].add(from_right.astype(F32))
    dkv = dkv.at[:, :halo].add(from_left.astype(F32))
    own_tokens = lax.dynamic_slice_in_dim(tokens, own * me, own, axis=0)
    token_part, grads_attn, small_attn = run_input(
        sizes, own_tokens, whole[0], dkv, dq, dh_1, grads_out
    )
    token_grad = lax.all_gather(token_part, "mp", axis=0, tiled=True).astype(F32)
    encoded = lax.all_gather(encoded, "mp", axis=0, tiled=True)
    grads = jnp.stack([grads_attn, grads_ffn[0], grads_ffn[1]])
    grads = summed_on_arrival(grads, "mp", 1)[:, 0].astype(BF16)
    grads = summed_on_arrival(grads, "dp", 1)
    small, small_attn = lax.psum((small, small_attn), ("dp", "mp"))
    mine = lax.dynamic_index_in_dim(small_attn[:, 0], me, 0, keepdims=False)
    up_bias = lax.dynamic_index_in_dim(small, 8 + me, 0, keepdims=False)
    return (
        table,
        lse,
        encoded,
        token_grad,
        grads[0, :, 2 * c : 3 * c],
        grads[0, :, :c],
        grads[0, :, c : 2 * c],
        mine[2 * c : 3 * c],
        mine[c : 2 * c],
        grads[0, :, 3 * c :].T,
        small[5],
        small[3],
        small[4],
        grads[1],
        up_bias,
        grads[2].T,
        small[2],
        small[0],
        small[1],
    )


def outputs_kernel(cols, table, lse, small, shards, encoded, tokens, *outs):
    *outs, got, wide, passed, sems = outs
    (
        table_out,
        lse_out,
        encoded_out,
        tokens_out,
        g_query,
        g_key,
        g_value,
        gb_query,
        gb_value,
        g_out,
        gb_out,
        g_gain_1,
        g_shift_1,
        g_up,
        gb_up,
        g_down,
        gb_down,
        g_gain_2,
        g_shift_2,
    ) = outs
    steps = got.shape[0]
    rows = [pl.ds(k * got.shape[1], got.shape[1]) for k in range(steps)]
    copies = [pltpu.make_async_copy(tokens.at[rows[k]], got.at[k], sems.at[0, k]) for k in range(steps)]
    writes = [pltpu.make_async_copy(wide.at[k], tokens_out.at[rows[k]], sems.at[1, k]) for k in range(steps)]
    takes = [pltpu.make_async_copy(encoded.at[rows[k]], passed.at[k], sems.at[2, k]) for k in range(steps)]
    gives = [pltpu.make_async_copy(passed.at[k], encoded_out.at[rows[k]], sems.at[3, k]) for k in range(steps)]
    for k in range(steps):
        copies[k].start()
        takes[k].start()
    for k in range(steps):
        copies[k].wait()
        wide[k] = got[k].astype(F32)
        writes[k].start()
        takes[k].wait()
        gives[k].start()
    me = lax.axis_index("mp")
    table_out[...] = table[...]
    lse_out[...] = lse[...].T.reshape(lse_out.shape)
    for k, target in enumerate((g_key, g_value, g_query)):
        target[...] = shards[0, :, k * cols : (k + 1) * cols]
    g_out[...] = shards[0, :, 3 * cols :].T
    g_up[...] = shards[1]
    g_down[...] = shards[2]
    heads = small[pl.ds(16 + me, 1), :]
    gb_value[...] = heads[:, cols : 2 * cols].reshape(gb_value.shape)
    gb_query[...] = heads[:, 2 * cols : 3 * cols].reshape(gb_query.shape)
    gb_up[...] = small[pl.ds(8 + me, 1), :].reshape(gb_up.shape)
    for k, target in enumerate((g_gain_2, g_shift_2, gb_down, g_gain_1, g_shift_1, gb_out)):
        target[...] = small[k : k + 1, :].reshape(target.shape)
    for k in range(steps):
        writes[k].wait()
        gives[k].wait()


def run_outputs(made, cols):
    table, lse, small, shards, encoded, tokens = made
    rows, width = shards.shape[1:]
    shape = jax.ShapeDtypeStruct
    vector = shape((width,), F32)
    outs = (
        shape(table.shape, F32),
        shape((lse.shape[0],), F32),
        shape(encoded.shape, BF16),
        shape(tokens.shape, F32),
        *[shape((rows, cols), F32)] * 3,
        *[shape((cols,), F32)] * 2,
        shape((cols, rows), F32),
        *[vector] * 3,
        shape((rows, width), F32),
        vector,
        shape((rows, width), F32),
        *[vector] * 3,
    )
    steps = 8
    span = tokens.shape[0] // steps
    return pl.pallas_call(
        functools.partial(outputs_kernel, cols),
        out_shape=outs,
        in_specs=specs(*[VMEM] * 4, ANY, ANY),
        out_specs=specs(*[ANY if k in (2, 3) else VMEM for k in range(len(outs))]),
        scratch_shapes=[
            pltpu.VMEM((steps, span, width), BF16),
            pltpu.VMEM((steps, span, width), F32),
            pltpu.VMEM((steps, span, width), BF16),
            pltpu.SemaphoreType.DMA((4, steps)),
        ],
        compiler_params=params(),
        name="outputs",
    )(*made)


def body(
    tokens,
    cotangent,
    lengths,
    gold,
    passages,
    w_query,
    w_key,
    w_value,
    b_query,
    b_value,
    w_out,
    b_out,
    gain_attn,
    shift_attn,
    w_up,
    b_up,
    w_down,
    b_down,
    gain_ffn,
    shift_ffn,
):
    groups = lax.axis_size("mp")
    sizes = Sizes(tokens.shape[0], tokens.shape[1], groups)
    rows = (b_out, gain_attn, shift_attn, b_down, gain_ffn, shift_ffn)
    shards = (w_key, w_value, w_query, w_out, w_up, w_down.T, b_value, b_query, b_up)
    if lax.axis_size("dp") == 8 and groups == 4:
        made = run_layer(sizes, lengths, tokens, cotangent, passages, gold, shards, rows)
        outs = list(run_outputs(made, w_key.shape[1]))
        outs[15] = outs[15].T
        return tuple(outs)
    return plain_layer(sizes, tokens, cotangent, lengths, gold, passages, shards, rows)


def solution(mesh):
    by_dp, shared, cross = P("dp", None), P(), P("dp", "mp")
    return jax.shard_map(
        body,
        mesh=mesh,
        in_specs=(
            by_dp,
            by_dp,
            by_dp,
            shared,
            by_dp,
            cross,
            cross,
            cross,
            P("mp"),
            P("mp"),
            P("mp", "dp"),
            shared,
            shared,
            shared,
            cross,
            P("mp"),
            P("mp", "dp"),
            shared,
            shared,
            shared,
        ),
        out_specs=(
            P(None, "dp"),
            P("dp"),
            by_dp,
            by_dp,
            cross,
            cross,
            cross,
            P("mp"),
            P("mp"),
            P("mp", "dp"),
            shared,
            shared,
            shared,
            cross,
            P("mp"),
            P("mp", "dp"),
            shared,
            shared,
            shared,
        ),
        check_vma=False,
    )
```

```python
import functools

import jax
import jax.numpy as jnp
from jax import lax
from jax.experimental import pallas as pl
from jax.experimental.pallas import tpu as pltpu
from jax.sharding import PartitionSpec as P

HEAD = 64
LONGEST = 400
QUERY_BLOCK = 256
EPSILON = 1e-05
NEGATIVE = -1e30
LANES = 128
KEY_AT = ((0, 0), (0, 1), (1, 0))
VALUE_AT = ((1, 1), (2, 0), (2, 1))
QUERY_AT = ((0, 0), (0, 1), (1, 0))
CONTEXT_AT = ((0, 1), (1, 0), (1, 1))
F32, BF16 = jnp.float32, jnp.bfloat16
VMEM, ANY, SMEM = pltpu.VMEM, pl.ANY, pltpu.SMEM


def dot(left, right, left_dim=1, right_dim=0):
    return lax.dot_general(
        left, right, (((left_dim,), (right_dim,)), ((), ())), preferred_element_type=F32
    )


def tile(index, count=1):
    return slice(index * LANES, (index + count) * LANES)


def half_mask(half, dtype):
    lane = lax.broadcasted_iota(jnp.int32, (1, LANES), 1)
    return jnp.where((lane >= HEAD) == (half == 1), 1.0, 0.0).astype(dtype)


def norm_stats(hidden):
    centred = hidden - jnp.mean(hidden, axis=-1, keepdims=True)
    factor = lax.rsqrt(jnp.mean(centred * centred, axis=-1, keepdims=True) + EPSILON)
    return centred * factor, factor


def norm_back(grad_out, normed, factor, gain):
    scaled = grad_out * gain
    inner = jnp.mean(scaled * normed, axis=-1, keepdims=True)
    return factor * (scaled - jnp.mean(scaled, axis=-1, keepdims=True) - normed * inner)


def gelu_and_slope(a):
    size = jnp.abs(a)
    t = 1.0 / (1.0 + (0.3275911 * 0.7071067811865476) * size)
    bell = jnp.exp(-0.5 * a * a)
    poly = t * (
        0.127414796 + t * (-0.142248368 + t * (0.7107068705 + t * (-0.7265760135 + t * 0.5307027145)))
    )
    tail = poly * bell
    phi = jnp.where(a >= 0.0, 1.0 - tail, tail)
    return a * phi, phi + a * bell * 0.3989422804014327


def as_row(ref):
    return ref[...].reshape(1, ref.shape[0])


class Sizes:
    def __init__(self, length, width, groups):
        self.length, self.width, self.groups = length, width, groups
        self.own = length // groups
        self.window = min(length, self.own + 2 * LONGEST)
        self.block = min(QUERY_BLOCK, self.own)
        self.blocks = self.own // self.block
        self.keys = min(length, self.block + 2 * LONGEST)

    def window_start(self, me):
        return jnp.clip(self.own * me - LONGEST, 0, self.length - self.window)

    def own_offset(self, me):
        return pl.multiple_of(self.own * me - self.window_start(me), 16)

    def key_start(self, me, block):
        first = self.own * me + block * self.block
        return jnp.clip(first - LONGEST, 0, self.length - self.keys)

    def key_offset(self, me, block):
        return pl.multiple_of(self.key_start(me, block) - self.window_start(me), 16)


def square(parts, index):
    side = parts.shape[1]
    return parts.at[pl.ds(pl.multiple_of(index * side, side), side)]


def document_bounds(lens, places):
    start = jnp.zeros_like(places)
    end = jnp.zeros_like(places)
    total = jnp.int32(0)
    for d in range(lens.shape[1]):
        count = lens[0, d]
        end = end + jnp.where(places >= total, count, 0)
        total = total + count
        start = start + jnp.where(places >= total, count, 0)
    return start, end


def fill_mask(sizes, me, lens, bias):
    for b in range(sizes.blocks):
        places = (
            sizes.own * me
            + b * sizes.block
            + lax.broadcasted_iota(jnp.int32, (1, sizes.block), 1)
        )
        start, end = document_bounds(lens, places)
        keys = sizes.key_start(me, b) + lax.broadcasted_iota(
            jnp.int32, (sizes.keys, sizes.block), 0
        )
        bias[b] = jnp.where((keys >= start) & (keys < end), 0.0, NEGATIVE)


def start_rows(sizes, me, lens):
    docs = lens.shape[1]
    row = lax.broadcasted_iota(jnp.int32, (docs, sizes.own), 0)
    place = sizes.own * me + lax.broadcasted_iota(jnp.int32, (docs, sizes.own), 1)
    picked = jnp.zeros((docs, sizes.own), F32)
    total = jnp.int32(0)
    for d in range(docs):
        picked = jnp.where((row == d) & (place == total), 1.0, picked)
        total = total + lens[0, d]
    return picked


def project(sizes, me, group, slot, span, tokens, weight, biases, kv, q):
    cut = sizes.window // 2
    own = pl.ds(sizes.own_offset(me), sizes.own)

    @pl.loop(*span)
    def _(i):
        g = group(i)
        for part in range(2):
            rows = pl.ds(part * cut, cut)
            made = dot(tokens[rows, :], weight(0, g)[:, tile(0, 3)]) + biases[g, :, tile(0, 3)]
            kv[slot(i), rows, :] = made.astype(BF16)
        made = dot(tokens[own, :], weight(0, g)[:, tile(3, 2)]) + biases[g, :, tile(3, 2)]
        q[g] = made.astype(BF16) * jnp.asarray(HEAD**-0.5, BF16)


def attend(sizes, me, group, slot, span, tick, kv, q, bias, lse, ctx):
    @pl.loop(*span)
    def _(i):
        g = group(i)

        @pl.loop(0, sizes.blocks)
        def _(b):
            tick(i * sizes.blocks + b)
            keys = pl.ds(sizes.key_offset(me, b), sizes.keys)
            rows = pl.ds(pl.multiple_of(b * sizes.block, sizes.block), sizes.block)
            made = [jnp.zeros((HEAD, sizes.block), F32)]
            logs = []
            for j in range(3):
                kt, kh = KEY_AT[j]
                vt, vh = VALUE_AT[j]
                qt, _ = QUERY_AT[j]
                query = q[g, rows, tile(qt)] * half_mask(kh, BF16)
                s = dot(kv[slot(i), keys, tile(kt)], query, 1, 1) + bias[b]
                peak = jnp.max(s, axis=0, keepdims=True)
                e = jnp.exp(s - peak)
                total = jnp.sum(e, axis=0, keepdims=True)
                mixed = dot(kv[slot(i), keys, tile(vt)], e.astype(BF16), 0, 0)
                made.append(mixed[vh * HEAD : (vh + 1) * HEAD] / total)
                logs.append(peak + jnp.log(total))
            ctx[g, rows, :] = jnp.concatenate(made, axis=0).T.astype(BF16)
            for j in range(3):
                lse[g, b, j : j + 1, :] = logs[j]


def delta_rows(dctx, ctx):
    lane = lax.broadcasted_iota(jnp.int32, (8, 2 * LANES), 1)
    row = lax.broadcasted_iota(jnp.int32, (8, 2 * LANES), 0)
    pick = jnp.where(lane // HEAD == row + 1, 1.0, 0.0).astype(BF16)
    product = dctx.astype(F32) * ctx.astype(F32)
    high = product.astype(BF16)
    low = (product - high.astype(F32)).astype(BF16)
    return dot(pick, high, 1, 1) + dot(pick, low, 1, 1)


def attend_back_block(sizes, me, g, b, kv, q, bias, lse, dctx, delta, dkv):
    keys = pl.ds(sizes.key_offset(me, b), sizes.keys)
    rows = slice(b * sizes.block, (b + 1) * sizes.block)
    made = []
    for j in range(3):
        kt, kh = KEY_AT[j]
        vt, vh = VALUE_AT[j]
        qt, _ = QUERY_AT[j]
        ct, _ = CONTEXT_AT[j]
        query = q[g, rows, tile(qt)] * half_mask(kh, BF16)
        grad = dctx[g, rows, tile(ct)] * half_mask(vh, BF16)
        s = dot(kv[keys, tile(kt)], query, 1, 1) + bias[b]
        p = jnp.exp(s - lse[g, b, j : j + 1, :])
        dp = dot(kv[keys, tile(vt)], grad, 1, 1)
        ds = (p * (dp - delta[j : j + 1, rows])).astype(BF16)
        dkv[keys, tile(kt)] += dot(ds, query)
        dkv[keys, tile(vt)] += dot(p.astype(BF16), grad)
        back = dot(kv[keys, tile(kt)], ds, 0, 0)
        made.append(back[kh * HEAD : (kh + 1) * HEAD] * HEAD**-0.5)
    made.append(jnp.zeros((HEAD, sizes.block), F32))
    return jnp.concatenate(made, axis=0).T


def attend_back(sizes, me, kv, q, bias, lse, ctx, dctx, delta, dkv, dq):
    @pl.loop(0, sizes.groups)
    def _(g):
        delta[...] = delta_rows(dctx[g], ctx[g])
        dkv[g] = jnp.zeros_like(dkv[g])
        for b in range(sizes.blocks):
            rows = slice(b * sizes.block, (b + 1) * sizes.block)
            dq[g, rows, :] = attend_back_block(
                sizes, me, g, b, kv.at[g], q, bias, lse, dctx, delta, dkv.at[g]
            )


class Loads:
    def __init__(self, weights, w, sems):
        self.copies = [pltpu.make_async_copy(weights.at[s], w.at[s], sems.at[s]) for s in range(3)]

    def begin(self):
        for copy in self.copies:
            copy.start()

    def group(self, i):
        return i

    def slot(self, i):
        return i

    def near_heads(self):
        self.copies[0].wait()

    def far_heads(self):
        pass

    def ready(self, section):
        self.copies[section].wait()

    def group_ready(self, section, i):
        pass

    def tick(self, step):
        pass

    def end(self):
        pass


MESH = pl.DeviceIdType.MESH


class Route:
    def __init__(self, at, turn):
        flip, x_peer = 1 - turn, 2 * at.z + 1 - at.x
        near = at.mp + turn * (at.across - at.mp)
        far = at.mp + flip * (at.across - at.mp)
        self.first = (at.dp + flip * (x_peer - at.dp), near)
        self.second = (at.dp + turn * (x_peer - at.dp), far)
        self.first_column = (near, at.x + flip * (1 - 2 * at.x))
        self.second_columns = ((far, at.x + turn * (1 - 2 * at.x)), (at.across, 1 - at.x))


class Place:
    def __init__(self):
        self.dp, self.mp = lax.axis_index("dp"), lax.axis_index("mp")
        self.z, self.x, self.y, self.core = self.dp // 2, self.dp % 2, self.mp // 2, self.mp % 2
        flip = 1 - self.core
        self.across = 2 * (1 - self.y) + self.core
        self.sibling = (self.dp, 2 * self.y + flip)
        self.x_peer = (2 * self.z + 1 - self.x, self.mp)
        self.y_peer = (self.dp, self.across)
        self.diagonal = (self.dp, 2 * (1 - self.y) + flip)
        self.zs = [self.z, self.z + 1 - 2 * (self.z % 2), (self.z + 2) % 4, 3 - self.z]
        self.line = [(2 * z + self.x, self.mp) for z in self.zs]
        self.by_core = Route(self, self.core)
        self.x_first, self.y_first = Route(self, 0), Route(self, 1)
        self.own_column = (self.mp, self.x)
        self.mates = (self.sibling, self.y_peer, self.diagonal)
        self.others = [(lax.rem(self.dp + k, 8), self.mp) for k in range(1, 8)]
        self.peers = [*self.mates, *self.others]


def signal(peers):
    barrier = pltpu.get_barrier_semaphore()
    for peer in peers:
        pl.semaphore_signal(barrier, inc=1, device_id=peer, device_id_type=MESH)


def arrive(peers):
    pl.semaphore_wait(pltpu.get_barrier_semaphore(), len(peers))


GATHER_STEPS = {
    "begin": (("along", 0), ("out", 0), ("out", 1), ("out", 2)),
    "near": (("z", 0, 1, 2, 3), ("along", 1), ("first", 0, 0, 1, 2, 3)),
    0: (("z", 1, 1, 2, 3), ("along", 2), ("second", 0, 0, 1, 2, 3)),
    1: (("second", 0, 4, 5, 6, 7),),
    2: (("first", 1, 0, 1),),
    3: (("first", 1, 2, 3),),
    4: (("z", 2, 1, 2, 3), ("second", 1, 0, 1)),
    5: (("second", 1, 2, 3, 4, 5),),
    6: (("second", 1, 6, 7), ("first", 2, 0)),
    7: (("first", 2, 1, 2),),
    8: (("first", 2, 3), ("second", 2, 0, 1, 2, 3)),
    9: (("second", 2, 4, 5, 6, 7),),
}


class Gather:
    ROUTES = ("x_first", "by_core", "by_core")
    Z_LATER = (False, False, False)

    def __init__(self, place, packed, own_bias, w, biases, kept, send, recv, local, bias_sems):
        self.at, self.packed, self.w, self.kept = place, packed, w, kept
        self.own_bias, self.biases = own_bias, biases
        self.send_sems, self.recv_sems, self.local, self.bias_sems = send, recv, local, bias_sems
        self.rows = packed[1].shape[0]
        self.shards = w.shape[1] // self.rows
        self.routes = [getattr(place, name) for name in self.ROUTES]

    def shard(self, s, g, d):
        first = (4 * s + g) * self.w.shape[1] + d * self.rows
        return self.w.at[pl.ds(pl.multiple_of(first, 16), self.rows)]

    def copy(self, s, g, d, slot, peer, source=None):
        here = self.shard(s, g, d)
        return pltpu.make_async_remote_copy(
            src_ref=here if source is None else source,
            dst_ref=here,
            send_sem=self.send_sems.at[s, slot],
            recv_sem=self.recv_sems.at[s, g * self.shards + d],
            device_id=peer,
            device_id_type=MESH,
        )

    def arrived(self, s, g, d):
        self.copy(s, g, d, 0, self.at.sibling).wait_recv()

    def own_copy(self, s):
        return pltpu.make_async_copy(
            self.packed[s], self.shard(s, self.at.mp, self.at.dp), self.local.at[s]
        )

    def along_z(self, s):
        at = self.at
        for k in range(1, 4):
            self.copy(s, at.mp, at.dp, k - 1, at.line[k], self.packed[s]).start()

    def own_out(self, s):
        at = self.at
        self.own_copy(s).start()
        source = self.packed[s]
        self.copy(s, at.mp, at.dp, 3, self.routes[s].first, source).start()
        self.copy(s, at.mp, at.dp, 7, self.routes[s].second, source).start()
        self.copy(s, at.mp, at.dp, 15, at.sibling, source).start()

    def from_z(self, s, k):
        at, (g, x) = self.at, self.at.own_column
        d = 2 * at.zs[k] + x
        self.arrived(s, g, d)
        if not self.Z_LATER[s]:
            self.copy(s, g, d, 3 + k, self.routes[s].first).start()
        self.copy(s, g, d, 7 + k, self.routes[s].second).start()
        self.copy(s, g, d, 15 + k, at.sibling).start()

    def from_first(self, s, k):
        at, (g, x) = self.at, self.routes[s].first_column
        d = 2 * at.zs[k] + x
        self.arrived(s, g, d)
        if self.Z_LATER[s] and k == 0:
            for j in range(1, 4):
                self.copy(s, g, d, 3 + j, at.line[j]).start()
        self.copy(s, g, d, 11 + k, self.routes[s].second).start()
        self.copy(s, g, d, 19 + k, at.sibling).start()

    def from_second(self, s, k):
        at, (g, x) = self.at, self.routes[s].second_columns[k // 4]
        d = 2 * at.zs[k % 4] + x
        self.arrived(s, g, d)
        self.copy(s, g, d, 23 + k, at.sibling).start()

    def group(self, i):
        at = self.at
        return 2 * (at.y + (i // 2) * (1 - 2 * at.y)) + at.core + (i % 2) * (1 - 2 * at.core)

    def slot(self, i):
        return i % 2

    def from_sibling(self, s, g):
        @pl.loop(0, self.shards)
        def _(d):
            self.arrived(s, g, d)

    def keep(self, s, i):
        index = 4 * s + self.group(i)
        return pltpu.make_async_copy(
            square(self.w, index), square(self.kept, index), self.local.at[3 + 4 * s + i]
        )

    def bias_copy(self, k, peer):
        return pltpu.make_async_remote_copy(
            src_ref=self.own_bias,
            dst_ref=self.biases.at[self.at.mp],
            send_sem=self.bias_sems.at[0, k],
            recv_sem=self.bias_sems.at[1, k],
            device_id=peer,
            device_id_type=MESH,
        )

    def bias_copies(self):
        at = self.at
        across = (at.dp, at.across)
        return [self.bias_copy(k, peer) for k, peer in enumerate((at.sibling, across, at.diagonal))]

    def begin(self):
        signal(self.at.peers)
        self.fill()
        arrive(self.at.peers)
        self.steps("begin")
        for copy in self.bias_copies():
            copy.start()
        self.biases[self.at.mp] = self.own_bias[...]

    def near_heads(self):
        self.steps("near")
        for copy in self.bias_copies():
            copy.wait_recv()
        self.own_copy(0).wait()
        self.from_sibling(0, self.group(1))
        self.keep(0, 0).start()
        self.keep(0, 1).start()

    def far_heads(self):
        self.steps("far")
        self.from_sibling(0, self.group(3))
        self.keep(0, 2).start()
        self.keep(0, 3).start()

    def ready(self, section):
        self.steps(7 + section)
        self.own_copy(section).wait()
        for i in (0, 2):
            self.keep(section, i).start()
        if section == 1:
            for i in (1, 3):
                self.group_ready(1, i)

    def group_ready(self, section, i):
        def take():
            self.from_sibling(section, self.group(i))
            self.keep(section, i).start()

        if isinstance(i, int):
            take()
        else:
            pl.when(i % 2 == 1)(take)

    def steps(self, step):
        actions = {
            "along": lambda s, k: self.along_z(s),
            "out": lambda s, k: self.own_out(s),
            "z": self.from_z,
            "first": self.from_first,
            "second": self.from_second,
        }
        for name, s, *ks in GATHER_STEPS.get(step, ()):
            for k in ks or (0,):
                actions[name](s, k)

    def tick(self, step):
        for k in range(8):
            pl.when(step == k)(functools.partial(self.steps, k))

    def end(self):
        for copy in self.bias_copies():
            copy.wait_send()
        for s in range(3):

            @pl.loop(0, 31)
            def _(slot):
                self.copy(s, 0, 0, slot, self.at.sibling).wait_send()

            for i in range(4):
                self.keep(s, i).wait()


def forward_math(
    sizes,
    source,
    lens,
    tokens,
    biases,
    b_out,
    gain_1,
    shift_1,
    b_down,
    gain_2,
    shift_2,
    encoded,
    cls,
    n_1,
    r_1,
    n_2,
    r_2,
    z_out,
    slope_out,
    kv_out,
    q,
    lse,
    ctx,
    x,
    weight,
    bias,
    hidden,
    kv,
    z,
    slope,
    sems,
):
    me = lax.axis_index("mp")
    first = pl.multiple_of(sizes.window_start(me), 16)
    load = pltpu.make_async_copy(tokens.at[pl.ds(first, sizes.window)], x, sems.at[0])
    load.start()
    source.begin()
    fill_mask(sizes, me, lens, bias)
    load.wait()
    half = sizes.groups // 2

    def save_kv(i):
        return pltpu.make_async_copy(
            kv.at[source.slot(i)], kv_out.at[source.group(i)], sems.at[4 + i]
        )

    for span, ready in (((0, half), source.near_heads), ((half, sizes.groups), source.far_heads)):
        ready()
        project(sizes, me, source.group, source.slot, span, x, weight, biases, kv, q)
        for i in range(*span):
            save_kv(i).start()
        attend(sizes, me, source.group, source.slot, span, source.tick, kv, q, bias, lse, ctx)
        for i in range(*span):
            save_kv(i).wait()

    own = pl.ds(sizes.own_offset(me), sizes.own)
    hidden[...] = x[own, :].astype(F32) + as_row(b_out)
    for g in range(sizes.groups):
        hidden[...] += dot(ctx[g], weight(0, g)[:, tile(4, 2)], 1, 1)
    normed, factor = norm_stats(hidden[...])
    n_1[...] = normed
    r_1[...] = factor
    y_1 = normed * as_row(gain_1) + as_row(shift_1)
    hidden[...] = y_1 + as_row(b_down)
    encoded[...] = y_1.astype(BF16)
    source.ready(1)

    @pl.loop(0, sizes.groups)
    def _(g):
        a = dot(encoded[...], weight(1, g)[...]) + biases[g, :, 5 * LANES :]
        out, grad = gelu_and_slope(a)
        z[g] = out.astype(BF16)
        slope[g] = grad.astype(BF16)

    save_z = pltpu.make_async_copy(z, z_out, sems.at[2])
    save_slope = pltpu.make_async_copy(slope, slope_out, sems.at[3])
    save_z.start()
    save_slope.start()
    source.ready(2)

    @pl.loop(0, sizes.groups)
    def _(i):
        g = source.group(i)
        source.group_ready(2, i)
        hidden[...] += dot(z[g], weight(2, g)[...], 1, 1)

    normed, factor = norm_stats(hidden[...])
    n_2[...] = normed
    r_2[...] = factor
    y_2 = (normed * as_row(gain_2) + as_row(shift_2)).astype(BF16)
    encoded[...] = y_2
    cls[...] = dot(start_rows(sizes, me, lens).astype(BF16), y_2)
    source.end()
    save_z.wait()
    save_slope.wait()


def forward_kernel(sizes, lens, tokens, weights, biases, *rest):
    *refs, w, bias, hidden, kv, z, slope, sems, loads = rest
    source = Loads(weights, w, loads)

    def weight(section, g):
        return w.at[section, g]

    forward_math(
        sizes, source, lens, tokens, biases, *refs, weight, bias, hidden, kv, z, slope, sems
    )


def pack(w_key, w_value, w_query, w_out, w_down, b_value, b_query, b_up, packed, own_bias):
    cols = w_key.shape[1]
    for k, weight in enumerate((w_key, w_value, w_query)):
        packed[0, :, k * cols : (k + 1) * cols] = weight[...]
    packed[0, :, 3 * cols :] = w_out[...].astype(F32).T.astype(BF16)
    packed[1] = w_down[...]
    own_bias[...] = jnp.zeros_like(own_bias)
    own_bias[:, cols : 2 * cols] = as_row(b_value)
    own_bias[:, 2 * cols : 3 * cols] = as_row(b_query)
    own_bias[:, 5 * LANES :] = as_row(b_up)


def backward_kernel(
    sizes,
    lens,
    cotangent,
    dcls,
    weights,
    gain_1,
    shift_1,
    gain_2,
    n_1,
    r_1,
    n_2,
    r_2,
    z,
    slope,
    kv,
    q,
    lse,
    ctx,
    dh_1,
    dkv,
    dq,
    grads,
    grads_out,
    small,
    w_attn,
    w_up,
    w_down,
    cot,
    dh,
    low,
    other,
    turned,
    stage,
    dctx,
    delta,
    bias,
    sems,
    out_sems,
):
    me = lax.axis_index("mp")
    load_cot = pltpu.make_async_copy(
        cotangent.at[pl.ds(pl.multiple_of(sizes.own * me, 16), sizes.own)], cot, sems.at[3]
    )
    load_cot.start()
    loads = []
    for s, buffer in ((2, w_down), (1, w_up), (0, w_attn)):
        loads.append(pltpu.make_async_copy(weights.at[s], buffer, sems.at[s]))
        loads[-1].start()
    fill_mask(sizes, me, lens, bias)
    picked = start_rows(sizes, me, lens).astype(BF16)
    high = dcls[...].astype(BF16)
    low_part = (dcls[...] - high.astype(F32)).astype(BF16)
    load_cot.wait()
    dy = cot[...].astype(F32) + dot(picked, high, 0, 0) + dot(picked, low_part, 0, 0)
    small[0:1, :] = jnp.sum(dy * n_2[...], axis=0, keepdims=True)
    small[1:2, :] = jnp.sum(dy, axis=0, keepdims=True)
    grad = norm_back(dy, n_2[...], r_2[...], as_row(gain_2))
    small[2:3, :] = jnp.sum(grad, axis=0, keepdims=True)
    dh[...] = grad
    low[...] = grad.astype(BF16)
    turned[0] = grad.T.astype(BF16)
    y_1 = n_1[...] * as_row(gain_1) + as_row(shift_1)
    other[...] = y_1.astype(BF16)
    turned[1] = y_1.T.astype(BF16)
    for load in loads:
        load.wait()

    def out_copy(section, g, slot):
        return pltpu.make_async_copy(
            stage.at[slot], grads.at[section, g], out_sems.at[slot]
        )

    @pl.loop(0, sizes.groups)
    def _(g):
        @pl.when(g > 0)
        def _():
            out_copy(1, 0, 0).wait()
            out_copy(1, 0, 1).wait()

        stage[1] = dot(turned[0], z[g]).astype(BF16)
        out_copy(1, g, 1).start()
        da = dot(low[...], w_down[g]) * slope[g].astype(F32)
        small[pl.ds(8 + g, 1), :] = jnp.sum(da, axis=0, keepdims=True)
        da_low = da.astype(BF16)
        stage[0] = dot(turned[1], da_low).astype(BF16)
        out_copy(0, g, 0).start()
        dh[...] += dot(da_low, w_up[g], 1, 1)

    dy = dh[...]
    small[3:4, :] = jnp.sum(dy * n_1[...], axis=0, keepdims=True)
    small[4:5, :] = jnp.sum(dy, axis=0, keepdims=True)
    grad = norm_back(dy, n_1[...], r_1[...], as_row(gain_1))
    small[5:6, :] = jnp.sum(grad, axis=0, keepdims=True)
    small[6:8, :] = jnp.zeros_like(small[6:8, :])
    small[12:16, :] = jnp.zeros_like(small[12:16, :])
    dh_1[...] = grad
    low[...] = grad.astype(BF16)
    turned[0] = grad.T.astype(BF16)

    @pl.loop(0, sizes.groups)
    def _(g):
        dctx[g] = dot(low[...], w_attn[g, :, tile(4, 2)]).astype(BF16)
        grads_out[g] = dot(turned[0], ctx[g])

    attend_back(sizes, me, kv, q, bias, lse, ctx, dctx, delta, dkv, dq)
    out_copy(1, 0, 0).wait()
    out_copy(1, 0, 1).wait()


def remote(source, target, send, recv, peer):
    return pltpu.make_async_remote_copy(
        src_ref=source,
        dst_ref=target,
        send_sem=send,
        recv_sem=recv,
        device_id=peer,
        device_id_type=MESH,
    )


class Spread:
    def __init__(self, place, source, whole, send, recv, local):
        self.at, self.source, self.whole = place, source, whole
        self.send, self.recv, self.local = send, recv, local
        self.count = source.shape[0]

    def rows(self, mp):
        return self.whole.at[pl.ds(pl.multiple_of(mp * self.count, 16), self.count)]

    def copy(self, k):
        at = self.at
        target = self.rows(at.across if k == 2 else at.mp)
        source = target if k == 2 else self.source
        peer = (at.dp, at.across) if k == 1 else at.sibling
        return remote(source, target, self.send.at[k], self.recv.at[k], peer)

    def own(self):
        return pltpu.make_async_copy(self.source, self.rows(self.at.mp), self.local)

    def begin(self):
        self.copy(1).start()
        self.copy(0).start()
        self.own().start()

    def forward(self):
        self.copy(1).wait_recv()
        self.copy(2).start()

    def end(self):
        self.copy(0).wait()
        self.copy(1).wait_send()
        self.copy(2).wait()
        self.own().wait()


DURING = {
    0: (("encoded", 0),),
    1: (("second", 2),),
    5: (("first", 2),),
    6: (("second", 1),),
}
BEFORE_LAST = (("line", 2),)
AFTER_LAST = (
    ("begin", 0),
    ("first", 1),
    ("chip", 0),
    ("small", 0),
    ("small", 1),
    ("tokens", 0),
    ("second", 0),
    ("small", 2),
    ("line", 1),
    ("first", 0),
    ("relay", 0),
    ("line", 0),
)


class Scatter:
    STAGE = (0, 2, 0)
    HELD = (8, 6, 4)
    ROUTES = ("by_core", "by_core", "by_core")
    Z_EARLY = ((1,), (1,), (1,))

    def __init__(self, place, parts, inbox, by_second, by_first, by_line, shards, sems):
        self.at, self.parts, self.inbox, self.shards = place, parts, inbox, shards
        self.by_second, self.by_first, self.by_line = by_second, by_first, by_line
        self.core_sems, self.second_sems, self.first_sems, self.line_sems = sems
        self.rows = shards.shape[1]
        self.routes = [getattr(place, name) for name in self.ROUTES]

    def shard(self, s, g, d):
        first = (self.HELD[s] + g // 2) * self.parts.shape[1] + d * self.rows
        return self.parts.at[pl.ds(pl.multiple_of(first, 16), self.rows)]

    def part(self, index):
        return square(self.parts, index)

    def to_sibling(self, s, k):
        at = self.STAGE[s] + k
        return remote(
            self.part(at),
            self.inbox.at[at],
            self.core_sems.at[0, s, k],
            self.core_sems.at[1, s, k],
            self.at.sibling,
        )

    def to_second(self, s, k):
        g, x = self.routes[s].second_columns[1 - k // 4]
        return remote(
            self.shard(s, g, 2 * self.at.zs[3 - k % 4] + x),
            self.by_second.at[s, k],
            self.second_sems.at[0, s, k],
            self.second_sems.at[1, s, k],
            self.routes[s].second,
        )

    def to_first(self, s, k):
        g, x = self.routes[s].first_column
        return remote(
            self.shard(s, g, 2 * self.at.zs[3 - k] + x),
            self.by_first.at[s, k],
            self.first_sems.at[0, s, k],
            self.first_sems.at[1, s, k],
            self.routes[s].first,
        )

    def to_line(self, s, j):
        at = self.at
        return remote(
            self.shard(s, at.mp, 2 * at.zs[j] + at.x),
            self.by_line.at[s, j - 1],
            self.line_sems.at[0, s, j - 1],
            self.line_sems.at[1, s, j - 1],
            at.line[j],
        )

    def chip_shard(self, s, g, z, x):
        d = 2 * z + x
        rows = pl.ds(pl.multiple_of(d * self.rows, 16), self.rows)
        self.shard(s, g, d)[...] += self.inbox[self.STAGE[s] + g // 2, rows]

    def chip_sum(self, s):
        for k in range(2):
            self.to_sibling(s, k).wait_recv()
        for k in range(8):
            g, x = self.routes[s].second_columns[1 - k // 4]
            self.chip_shard(s, g, self.at.zs[3 - k % 4], x)
            self.to_second(s, k).start()
        for g, x in (self.routes[s].first_column, self.at.own_column):

            @pl.loop(0, 4)
            def _(z):
                self.chip_shard(s, g, z, x)

    def other_line(self, s, j):
        g, x = self.routes[s].first_column
        return remote(
            self.shard(s, g, 2 * self.at.zs[j] + x),
            self.by_first.at[s, j],
            self.first_sems.at[0, s, j],
            self.first_sems.at[1, s, j],
            self.at.line[j],
        )

    def last_cross(self, s):
        g, x = self.routes[s].first_column
        return remote(
            self.shard(s, g, 2 * self.at.z + x),
            self.by_first.at[s, 0],
            self.first_sems.at[0, s, 0],
            self.first_sems.at[1, s, 0],
            self.routes[s].first,
        )

    def by_kind(self, s, early, late):
        cores = self.Z_EARLY[s]
        if len(cores) == 1:
            pl.when(self.at.core == cores[0])(functools.partial(early, s))
            pl.when(self.at.core != cores[0])(functools.partial(late, s))
        else:
            (early if cores else late)(s)

    def from_second(self, s):
        self.by_kind(s, self.from_second_early, self.from_second_late)

    def from_first(self, s):
        self.by_kind(s, self.from_first_early, self.from_first_late)

    def from_line(self, s):
        self.by_kind(s, self.from_line_early, self.from_line_late)

    def from_second_early(self, s):
        at, (g, x) = self.at, self.routes[s].first_column
        for k in range(8):
            self.to_second(s, k).wait_recv()
            j = 3 - k % 4
            mine = self.shard(s, g, 2 * at.zs[j] + x) if k < 4 else self.shard(s, at.mp, 2 * at.zs[j] + at.x)
            if k < 7:
                mine[...] += self.by_second[s, k]
            if j:
                (self.other_line if k < 4 else self.to_line)(s, j).start()

    def from_first_early(self, s):
        g, x = self.routes[s].first_column
        mine = self.shard(s, g, 2 * self.at.z + x)
        total = mine[...].astype(F32)
        for j in (1, 2, 3):
            self.other_line(s, j).wait_recv()
            total = total + self.by_first[s, j].astype(F32)
        mine[...] = total.astype(BF16)
        self.last_cross(s).start()

    def from_line_early(self, s):
        at = self.at
        mine = self.shard(s, at.mp, 2 * at.z + at.x)
        total = mine[...].astype(F32) + self.by_second[s, 7].astype(F32)
        for j in range(1, 4):
            self.to_line(s, j).wait_recv()
            total = total + self.by_line[s, j - 1].astype(F32)
        self.last_cross(s).wait_recv()
        self.shards[s] = total + self.by_first[s, 0].astype(F32)

    def from_second_late(self, s):
        g, x = self.routes[s].first_column
        for k in range(4):
            self.to_second(s, k).wait_recv()
            self.shard(s, g, 2 * self.at.zs[3 - k] + x)[...] += self.by_second[s, k]
            self.to_first(s, k).start()

    def from_first_late(self, s):
        at = self.at
        for k in range(4):
            self.to_second(s, 4 + k).wait_recv()
            self.to_first(s, k).wait_recv()
            mine = self.shard(s, at.mp, 2 * at.zs[3 - k] + at.x)
            total = (
                mine[...].astype(F32)
                + self.by_second[s, 4 + k].astype(F32)
                + self.by_first[s, k].astype(F32)
            )
            if k < 3:
                mine[...] = total.astype(BF16)
                self.to_line(s, 3 - k).start()
            else:
                self.shards[s] = total

    def from_line_late(self, s):
        for j in range(1, 4):
            self.to_line(s, j).wait_recv()
            self.shards[s] += self.by_line[s, j - 1].astype(F32)

    def sent_to_sibling(self, s):
        for k in range(2):
            self.to_sibling(s, k).wait_send()

    def end(self):
        for s in range(3):
            for k in range(8):
                self.to_second(s, k).wait_send()
            for k in range(4):
                self.to_first(s, k).wait_send()
            for j in range(1, 4):
                self.to_line(s, j).wait_send()


class SmallSums:
    def __init__(self, place, sums, inbox, sems):
        self.at, self.sums, self.inbox, self.sems = place, sums, inbox, sems
        at = place
        self.peers = [at.sibling, at.x_peer, at.y_peer, *at.line[1:]]

    def copy(self, k):
        return remote(
            self.sums.at[min(k, 3)],
            self.inbox.at[k],
            self.sems.at[0, k],
            self.sems.at[1, k],
            self.peers[k],
        )

    def begin(self):
        self.copy(0).start()

    def step(self, k):
        self.copy(k).wait_recv()
        self.sums[k + 1] = self.sums[k] + self.inbox[k]
        for nxt in (k + 1,) if k < 2 else (3, 4, 5):
            self.copy(nxt).start()

    def end(self, out):
        for k in range(3, 6):
            self.copy(k).wait_recv()
        out[...] = (self.sums[3] + self.inbox[3]) + (self.inbox[4] + self.inbox[5])
        for k in range(6):
            self.copy(k).wait_send()


def fold(rows):
    half = rows.shape[1] // 2
    return jnp.concatenate([rows[:, :half], rows[:, half:]], axis=0).astype(BF16)


def unfold(packed):
    wide = packed.astype(F32)
    return jnp.concatenate([wide[:8], wide[8:]], axis=1)


class Scoring:
    def __init__(self, place, ways, cls, gold, passages, scores, lse, buffers, sems):
        self.at, self.ways, self.cls, self.gold = place, ways, cls, gold
        self.passages, self.scores, self.lse = passages, scores, lse
        self.part, self.parts, self.firsts, self.rows = buffers[:4]
        self.sent, self.got, self.stats, self.got_stats = buffers[4:]
        self.mp_sems, self.sems = sems
        at = place
        self.mates = (at.sibling, (at.dp, at.across), at.diagonal)
        self.others = [(lax.rem(at.dp + k, ways), at.mp) for k in range(1, ways)]

    def mate(self, k):
        return remote(
            self.part, self.parts.at[k], self.mp_sems.at[0, k], self.mp_sems.at[1, k], self.mates[k]
        )

    def first_copy(self, k):
        mine = self.firsts.at[self.at.dp]
        return remote(
            mine, mine, self.sems.at[0, 0, k - 1], self.sems.at[0, 1, k - 1], self.others[k - 1]
        )

    def back_copy(self, which, k):
        peer = self.others[k - 1]
        return remote(
            self.sent.at[which, peer[0]],
            self.got.at[which, self.at.dp],
            self.sems.at[1 + which, 0, k - 1],
            self.sems.at[1 + which, 1, k - 1],
            peer,
        )

    def stat_copy(self, k):
        peer = self.others[k - 1]
        return remote(
            self.stats.at[peer[0]],
            self.got_stats.at[self.at.dp],
            self.sems.at[3, 0, k - 1],
            self.sems.at[3, 1, k - 1],
            peer,
        )

    def start_cls(self):
        self.part[...] = fold(self.cls[...])
        for k in range(3):
            self.mate(k).start()

    def start_gold(self):
        places = self.at.dp * self.passages.shape[0] + lax.broadcasted_iota(
            jnp.int32, (self.passages.shape[0], self.gold.shape[0]), 0
        )
        target = jnp.where(as_row(self.gold) == places, 1.0, 0.0).astype(BF16)
        self.put(0, dot(target, self.passages[...], 0, 0))
        for k in range(1, self.ways):
            self.back_copy(0, k).start()

    def put(self, which, rows):
        for d in range(self.ways):
            self.sent[which, d] = fold(rows[8 * d : 8 * d + 8])
        self.got[which, self.at.dp] = self.sent[which, self.at.dp]

    def start_firsts(self):
        total = self.part[...].astype(F32)
        for k in range(3):
            self.mate(k).wait_recv()
            total = total + self.parts[k].astype(F32)
        self.firsts[self.at.dp] = total.astype(BF16)
        for k in range(1, self.ways):
            self.first_copy(k).start()

    def start_back(self):
        for k in range(1, self.ways):
            self.first_copy(k).wait_recv()
        for d in range(self.ways):
            self.rows[8 * d : 8 * d + 8, :] = unfold(self.firsts[d])
        table = dot(self.rows[...].astype(BF16), self.passages[...], 1, 1)
        self.scores[...] = table
        peak = jnp.max(table, axis=1, keepdims=True)
        e = jnp.exp(table - peak)
        total = jnp.sum(e, axis=1, keepdims=True)
        lane = lax.broadcasted_iota(jnp.int32, (8, LANES), 1)
        for d in range(self.ways):
            rows = slice(8 * d, 8 * d + 8)
            self.stats[d] = jnp.where(lane == 0, peak[rows], total[rows])
        self.got_stats[self.at.dp] = self.stats[self.at.dp]
        for k in range(1, self.ways):
            self.stat_copy(k).start()
        self.put(1, dot(e.astype(BF16), self.passages[...]))
        for k in range(1, self.ways):
            self.back_copy(1, k).start()

    def result(self):
        for k in range(1, self.ways):
            self.back_copy(0, k).wait_recv()
            self.stat_copy(k).wait_recv()
        peaks = [self.got_stats[d][:, 0:1] for d in range(self.ways)]
        top = functools.reduce(jnp.maximum, peaks)
        scales = [jnp.exp(peak - top) for peak in peaks]
        total = sum(scale * self.got_stats[d][:, 1:2] for d, scale in enumerate(scales))
        self.lse[...] = top + jnp.log(total)
        for k in range(1, self.ways):
            self.back_copy(1, k).wait_recv()
        grad = -sum(unfold(self.got[0, d]) for d in range(self.ways))
        for d in range(self.ways):
            grad = grad + (scales[d] / total) * unfold(self.got[1, d])
        return grad

    def end(self):
        for k in range(3):
            self.mate(k).wait_send()
        for k in range(1, self.ways):
            self.first_copy(k).wait_send()
            self.back_copy(0, k).wait_send()
            self.back_copy(1, k).wait_send()
            self.stat_copy(k).wait_send()


class Halo:
    def __init__(self, sizes, place, dkv, sent, got, sems):
        self.sizes, self.at, self.dkv, self.sent, self.got, self.sems = sizes, place, dkv, sent, got, sems
        self.has = (place.mp > 0, place.mp < sizes.groups - 1)
        offset = sizes.own_offset(place.mp)
        self.starts = (offset - LONGEST, offset + sizes.own)
        self.into = (sizes.own - LONGEST, 0)

    def copy(self, g, side):
        slot = g % 2
        return remote(
            self.sent.at[slot, side],
            self.got.at[g, side],
            self.sems.at[0, slot, side],
            self.sems.at[1, g, side],
            (self.at.dp, self.at.mp + 2 * side - 1),
        )

    def start(self, g):
        for side in range(2):

            @pl.when(self.has[side])
            def _():
                pl.when(g > 1)(self.copy(g, side).wait_send)
                rows = pl.ds(pl.multiple_of(self.starts[side], 16), LONGEST)
                self.sent[g % 2, side] = self.dkv[rows, :].astype(BF16)
                self.copy(g, side).start()

    def add(self, g, own, total):
        for side in range(2):

            @pl.when(self.has[1 - side])
            def _():
                self.copy(g, side).wait_recv()
                rows = pl.ds(self.into[side], LONGEST)
                more = self.got[g, side].astype(F32)
                total[:, tile(0, 3)] += jnp.sum(more, axis=0, keepdims=True)
                own[rows, tile(0, 3)] = (own[rows, tile(0, 3)].astype(F32) + more).astype(BF16)

    def end(self):
        for side in range(2):

            @pl.when(self.has[side])
            def _():
                self.copy(2, side).wait_send()
                self.copy(3, side).wait_send()


def finish_math(
    sizes,
    at,
    lens,
    cotangent,
    tokens,
    passages,
    gold,
    gain_1,
    shift_1,
    gain_2,
    held,
    kept,
    outs,
    landing,
    sems,
    ffn,
    kv,
    dctx,
    dkv,
    halo_sent,
    rows_low,
    turned,
    low,
    delta,
):
    parts, cls, r_1, r_2, lse, q, ctx, encoded, n_1, work, bias = held
    weights, z_in, slope_in, kv_in = kept
    scores, query_lse, small_out, shards, encoded_whole, token_whole = outs
    inbox, by_second, by_first, by_line, halo_got, sums, sums_in, *scored = landing
    part, parts_in, firsts, first_rows, back_sent, back_got, stats, stats_got = scored
    (
        load_sems,
        kv_sems,
        ffn_sems,
        spread_sems,
        core_sems,
        second_sems,
        first_sems,
        line_sems,
        halo_sems,
        small_sems,
        mp_sems,
        score_sems,
    ) = sems
    me = at.mp
    own_rows = pl.ds(pl.multiple_of(sizes.own * me, 16), sizes.own)
    ways = firsts.shape[0]
    table = parts.at[pl.ds(Scatter.HELD[0] * sizes.width, passages.shape[0])]
    scatter = Scatter(
        at, parts, inbox, by_second, by_first, by_line, shards,
        (core_sems, second_sems, first_sems, line_sems),
    )
    halo = Halo(sizes, at, dkv, halo_sent, halo_got, halo_sems)
    spread = Spread(at, encoded, encoded_whole, spread_sems.at[0, 0], spread_sems.at[0, 1], load_sems.at[8])
    token_spread = Spread(
        at, rows_low, token_whole, spread_sems.at[1, 0], spread_sems.at[1, 1], load_sems.at[9]
    )
    small = SmallSums(at, sums, sums_in, small_sems)

    def load(k, source, target):
        return pltpu.make_async_copy(source, target, load_sems.at[k])

    loads = [
        load(0, passages, table),
        load(1, cotangent.at[own_rows], ffn.at[1]),
    ]
    weight_slots = 10

    def kv_load(g):
        return pltpu.make_async_copy(kv_in.at[g], kv, kv_sems.at[0])

    for copy in loads:
        copy.start()

    scoring = Scoring(
        at,
        ways,
        cls,
        gold,
        table,
        scores,
        query_lse,
        (part, parts_in, firsts, first_rows, back_sent, back_got, stats, stats_got),
        (mp_sems, score_sems),
    )
    scoring.start_cls()
    kv_load(0).start()

    def group_of(i):
        return jnp.where(i < 2, 1 - at.core + 2 * i, at.core + 2 * (i - 2))

    def wide(k):
        return square(parts, weight_slots + k)

    def z_load(i):
        return pltpu.make_async_copy(z_in.at[group_of(i)], ffn.at[i % 2], ffn_sems.at[i % 2, 0])

    def ffn_loads(i):
        slot, g = i % 2, group_of(i)
        return [
            pltpu.make_async_copy(square(weights, 8 + g), wide(2 * slot), ffn_sems.at[slot, 1]),
            pltpu.make_async_copy(square(weights, 4 + g), wide(2 * slot + 1), ffn_sems.at[slot, 2]),
            pltpu.make_async_copy(slope_in.at[g], ffn.at[2 - 2 * slot], ffn_sems.at[slot, 3]),
        ]

    z_load(0).start()
    for copy in ffn_loads(0):
        copy.start()

    loads[0].wait()
    scoring.start_gold()
    scoring.start_firsts()
    spread.begin()
    picked = start_rows(sizes, me, lens).astype(BF16)
    turned[1] = (n_1[...] * as_row(gain_1) + as_row(shift_1)).T.astype(BF16)
    scoring.start_back()
    loads[1].wait()
    dcls = scoring.result()
    high = dcls.astype(BF16)
    rest = (dcls - high.astype(F32)).astype(BF16)
    dy = ffn[1].astype(F32) + dot(picked, high, 0, 0) + dot(picked, rest, 0, 0)
    mine = sums.at[0]
    mine[0:1, :] = jnp.sum(dy * work[1], axis=0, keepdims=True)
    mine[1:2, :] = jnp.sum(dy, axis=0, keepdims=True)
    grad = norm_back(dy, work[1], r_2[...], as_row(gain_2))
    mine[2:3, :] = jnp.sum(grad, axis=0, keepdims=True)
    work[0] = grad
    rows_low[...] = grad.astype(BF16)
    turned[0] = grad.T.astype(BF16)

    def into(s, i):
        return jnp.where(i < 2, Scatter.STAGE[s] + i, Scatter.HELD[s] + i - 2)

    @pl.loop(0, sizes.groups)
    def _(i):
        z_load(i).wait()

        @pl.when(i < 3)
        def _():
            z_load(i + 1).start()

        square(parts, into(2, i))[...] = dot(turned[0], ffn[i % 2]).astype(BF16)
        pl.when(i < 2)(lambda: scatter.to_sibling(2, i).start())

    scatter.chip_sum(2)

    @pl.loop(0, sizes.groups)
    def _(i):
        slot, g = i % 2, group_of(i)
        for copy in ffn_loads(i):
            copy.wait()

        @pl.when(i < 3)
        def _():
            for copy in ffn_loads(i + 1):
                copy.start()

        da = dot(rows_low[...], wide(2 * slot)[...]) * ffn[2 - 2 * slot].astype(F32)
        mine[pl.ds(8 + g, 1), :] = jnp.sum(da, axis=0, keepdims=True)
        da_low = da.astype(BF16)
        square(parts, into(1, i))[...] = dot(turned[1], da_low).astype(BF16)
        pl.when(i < 2)(lambda: scatter.to_sibling(1, i).start())
        work[0] += dot(da_low, wide(2 * slot + 1)[...], 1, 1)

    load_w = pltpu.make_async_copy(
        weights.at[pl.ds(0, 4 * sizes.width)],
        parts.at[pl.ds(weight_slots * sizes.width, 4 * sizes.width)],
        load_sems.at[7],
    )
    load_w.start()
    load_x = load(1, tokens.at[own_rows], ffn.at[0])
    load_x.start()
    scatter.chip_sum(1)
    scatter.sent_to_sibling(2)

    dy = work[0]
    mine[3:4, :] = jnp.sum(dy * n_1[...], axis=0, keepdims=True)
    mine[4:5, :] = jnp.sum(dy, axis=0, keepdims=True)
    grad = norm_back(dy, n_1[...], r_1[...], as_row(gain_1))
    mine[5:6, :] = jnp.sum(grad, axis=0, keepdims=True)
    mine[6:8, :] = jnp.zeros((2, sizes.width), F32)
    mine[12:24, :] = jnp.zeros((12, sizes.width), F32)
    work[1] = grad
    rows_low[...] = grad.astype(BF16)
    turned[0] = grad.T.astype(BF16)
    load_x.wait()
    turned[1] = ffn[0].astype(F32).T.astype(BF16)
    load_w.wait()

    @pl.loop(0, sizes.groups)
    def _(g):
        dctx[g] = dot(rows_low[...], wide(g)[:, tile(4, 2)]).astype(BF16)

    actions = {
        "second": scatter.from_second,
        "first": scatter.from_first,
        "line": scatter.from_line,
        "chip": scatter.chip_sum,
        "small": small.step,
        "begin": lambda s: small.begin(),
        "tokens": lambda s: token_spread.begin(),
        "relay": lambda s: token_spread.forward(),
        "encoded": lambda s: spread.forward(),
    }

    def run(names):
        for name, s in names:
            actions[name](s)

    def tick(now):
        for k, names in DURING.items():
            pl.when(now == k)(functools.partial(run, names))

    def finalize(g):
        slot = g % 2
        halo.add(g, low.at[slot], mine.at[pl.ds(16 + g, 1)])
        work[1] += dot(low[slot], wide(g)[:, tile(0, 5)], 1, 1)
        into = jnp.where(g % 2 == at.core, Scatter.HELD[0], Scatter.STAGE[0]) + g // 2
        made = dot(turned[1], low[slot])
        more = dot(turned[0], ctx[g])
        target = square(parts, into)
        target[:, tile(0, 4)] = made[:, tile(0, 4)].astype(BF16)
        target[:, tile(4)] = (made[:, tile(4)] + more[:, tile(0)]).astype(BF16)
        target[:, tile(5)] = more[:, tile(1)].astype(BF16)

        @pl.when(g % 2 != at.core)
        def _():
            scatter.to_sibling(0, g // 2).start()

    own = pl.ds(sizes.own_offset(me), sizes.own)

    @pl.loop(0, sizes.groups)
    def _(g):
        slot = g % 2
        kv_load(g).wait()
        delta[...] = delta_rows(dctx[g], ctx[g])
        dkv[...] = jnp.zeros_like(dkv)
        for b in range(sizes.blocks):
            tick(g * sizes.blocks + b)
            rows = slice(b * sizes.block, (b + 1) * sizes.block)
            dq = attend_back_block(
                sizes, me, g, b, kv, q, bias, lse, dctx, delta, dkv
            )
            total = jnp.sum(dq, axis=0, keepdims=True)
            mine[pl.ds(16 + g, 1), tile(3, 2)] += total
            low[slot, rows, tile(3, 2)] = dq.astype(BF16)

        @pl.when(g < sizes.groups - 1)
        def _():
            kv_load(g + 1).start()

        halo.start(g)
        mine[pl.ds(16 + g, 1), tile(0, 3)] = jnp.sum(dkv[own, :], axis=0, keepdims=True)
        low[slot, :, tile(0, 3)] = dkv[own, :].astype(BF16)

        @pl.when(g > 0)
        def _():
            finalize(g - 1)

    run(BEFORE_LAST)
    finalize(sizes.groups - 1)
    rows_low[...] = work[1].astype(BF16)
    run(AFTER_LAST)
    small.end(small_out)
    scatter.sent_to_sibling(1)
    scatter.sent_to_sibling(0)
    scatter.end()
    halo.end()
    scoring.end()
    spread.end()
    token_spread.end()


def layer_kernel(sizes, lens, tokens, cotangent, passages, gold, *rest):
    weights, rows, outs, kept = rest[:9], rest[9:15], rest[15:21], rest[21:25]
    w, cls, r_1, r_2, lse, q, ctx, encoded, n_1, work, bias, packed, own_bias, biases = rest[25:39]
    landing, sems = rest[39:54], rest[54:]
    w_key, w_value, w_query, w_out, w_up, w_down, b_value, b_query, b_up = weights
    own, width, groups = sizes.own, sizes.width, sizes.groups
    at = Place()
    source = Gather(at, (packed.at[0], w_up, packed.at[1]), own_bias, w, biases, kept[0], *sems[:4])

    def fill():
        pack(w_key, w_value, w_query, w_out, w_down, b_value, b_query, b_up, packed, own_bias)

    source.fill = fill

    def weight(section, g):
        return square(w, 4 * section + g)

    def forward(x, kv, z, slope):
        forward_math(
            sizes, source, lens, tokens, biases, *rows, encoded, cls, n_1, r_1, work.at[1], r_2,
            *kept[1:], q, lse, ctx, x, weight, bias, work.at[0], kv, z, slope, sems[4],
        )

    pl.run_scoped(
        forward,
        pltpu.VMEM((sizes.window, width), BF16),
        pltpu.VMEM((2, sizes.window, 3 * LANES), BF16),
        pltpu.VMEM((groups, own, width), BF16),
        pltpu.VMEM((groups, own, width), BF16),
    )
    held = (w, cls, r_1, r_2, lse, q, ctx, encoded, n_1, work, bias)
    z_kept, slope_kept, kv_kept = kept[1:]
    finish = functools.partial(
        finish_math, sizes, at, lens, cotangent, tokens, passages, gold, rows[1], rows[2], rows[4],
        held, (kept[0], z_kept, slope_kept, kv_kept), outs, landing, sems[5:],
    )
    pl.run_scoped(
        finish,
        pltpu.VMEM((3, own, width), BF16),
        pltpu.VMEM((sizes.window, 3 * LANES), BF16),
        pltpu.VMEM((groups, own, 2 * LANES), BF16),
        pltpu.VMEM((sizes.window, 3 * LANES), F32),
        pltpu.VMEM((2, 2, LONGEST, 3 * LANES), BF16),
        pltpu.VMEM((own, width), BF16),
        pltpu.VMEM((2, width, own), BF16),
        pltpu.VMEM((2, own, 5 * LANES), BF16),
        pltpu.VMEM((8, own), F32),
    )


def input_kernel(sizes, tokens, weights, dkv, dq, dh_1, grads_out, token_grad, grads, small, turned, low):
    turned[...] = tokens[...].astype(F32).T.astype(BF16)
    total = dh_1[...]
    for g in range(sizes.groups):
        small[g, :, tile(0, 3)] = jnp.sum(dkv[g], axis=0, keepdims=True)
        small[g, :, tile(3, 2)] = jnp.sum(dq[g], axis=0, keepdims=True)
        low[:, tile(0, 3)] = dkv[g].astype(BF16)
        low[:, tile(3, 2)] = dq[g].astype(BF16)
        total = total + dot(low[...], weights[g, :, tile(0, 5)], 1, 1)
        made = dot(turned[...], low[...])
        grads[g, :, tile(0, 4)] = made[:, tile(0, 4)].astype(BF16)
        grads[g, :, tile(4)] = (made[:, tile(4)] + grads_out[g, :, tile(0)]).astype(BF16)
        grads[g, :, tile(5)] = grads_out[g, :, tile(1)].astype(BF16)
    token_grad[...] = total.astype(BF16)


def specs(*spaces):
    return [pl.BlockSpec(memory_space=s) for s in spaces]


def params(**more):
    return pltpu.CompilerParams(vmem_limit_bytes=64 * 2**20, **more)


def run_forward(sizes, lengths, tokens, weights, rows):
    own, width, groups = sizes.own, sizes.width, sizes.groups
    docs = lengths.shape[1]
    shape = jax.ShapeDtypeStruct
    outs = [
        shape((own, width), BF16),
        shape((docs, width), F32),
        shape((own, width), F32),
        shape((own, 1), F32),
        shape((own, width), F32),
        shape((own, 1), F32),
        shape((groups, own, width), BF16),
        shape((groups, own, width), BF16),
        shape((groups, sizes.window, 3 * LANES), BF16),
        shape((groups, own, 2 * LANES), BF16),
        shape((groups, sizes.blocks, 8, sizes.block), F32),
        shape((groups, own, 2 * LANES), BF16),
    ]
    spaces = [*[VMEM] * 6, ANY, ANY, ANY, *[VMEM] * 3]
    scratch = [
        pltpu.VMEM((sizes.window, width), BF16),
        pltpu.VMEM((3, groups, width, width), BF16),
        pltpu.VMEM((sizes.blocks, sizes.keys, sizes.block), F32),
        pltpu.VMEM((own, width), F32),
        pltpu.VMEM((groups, sizes.window, 3 * LANES), BF16),
        pltpu.VMEM((groups, own, width), BF16),
        pltpu.VMEM((groups, own, width), BF16),
        pltpu.SemaphoreType.DMA((4 + groups,)),
    ]
    scratch.append(pltpu.SemaphoreType.DMA((3,)))
    return pl.pallas_call(
        functools.partial(forward_kernel, sizes),
        out_shape=outs,
        in_specs=specs(SMEM, ANY, ANY, *[VMEM] * 7),
        out_specs=specs(*spaces),
        scratch_shapes=scratch,
        compiler_params=params(),
        name="forward",
    )(lengths, tokens, *weights, *rows)


def run_backward(sizes, lengths, cotangent, dcls, weights, gain_1, shift_1, gain_2, saved):
    own, width, groups = sizes.own, sizes.width, sizes.groups
    shape = jax.ShapeDtypeStruct
    outs = (
        shape((own, width), F32),
        shape((groups, sizes.window, 3 * LANES), F32),
        shape((groups, own, 2 * LANES), F32),
        shape((2, groups, width, width), BF16),
        shape((groups, width, 2 * LANES), F32),
        shape((16, width), F32),
    )
    return pl.pallas_call(
        functools.partial(backward_kernel, sizes),
        out_shape=outs,
        in_specs=specs(SMEM, ANY, VMEM, ANY, *[VMEM] * (3 + len(saved))),
        out_specs=specs(VMEM, VMEM, VMEM, ANY, VMEM, VMEM),
        scratch_shapes=[
            pltpu.VMEM((groups, width, width), BF16),
            pltpu.VMEM((groups, width, width), BF16),
            pltpu.VMEM((groups, width, width), BF16),
            pltpu.VMEM((own, width), BF16),
            pltpu.VMEM((own, width), F32),
            pltpu.VMEM((own, width), BF16),
            pltpu.VMEM((own, width), BF16),
            pltpu.VMEM((2, width, own), BF16),
            pltpu.VMEM((2, width, width), BF16),
            pltpu.VMEM((groups, own, 2 * LANES), BF16),
            pltpu.VMEM((8, own), F32),
            pltpu.VMEM((sizes.blocks, sizes.keys, sizes.block), F32),
            pltpu.SemaphoreType.DMA((4,)),
            pltpu.SemaphoreType.DMA((2,)),
        ],
        compiler_params=params(),
        name="backward",
    )(lengths, cotangent, dcls, weights, gain_1, shift_1, gain_2, *saved)


def run_input(sizes, own_tokens, w_attn, dkv, dq, dh_1, grads_out):
    own, width, groups = sizes.own, sizes.width, sizes.groups
    shape = jax.ShapeDtypeStruct
    outs = (
        shape((own, width), BF16),
        shape((groups, width, width), BF16),
        shape((groups, 1, 5 * LANES), F32),
    )
    return pl.pallas_call(
        functools.partial(input_kernel, sizes),
        out_shape=outs,
        in_specs=specs(*[VMEM] * 6),
        out_specs=specs(*[VMEM] * 3),
        scratch_shapes=[pltpu.VMEM((width, own), BF16), pltpu.VMEM((own, 5 * LANES), BF16)],
        compiler_params=params(),
        name="inputs",
    )(own_tokens, w_attn, dkv, dq, dh_1, grads_out)


def run_layer(sizes, lengths, tokens, cotangent, passages, gold, weights, rows):
    own, width, groups = sizes.own, sizes.width, sizes.groups
    queries, docs = gold.shape[0], lengths.shape[1]
    ways = queries // docs
    shard, half = width // ways, width // 2
    shape, vmem, dma = jax.ShapeDtypeStruct, pltpu.VMEM, pltpu.SemaphoreType.DMA
    outs = (
        shape((queries, passages.shape[0]), F32),
        shape((docs, 1), F32),
        shape((24, width), F32),
        shape((3, shard, width), F32),
        shape(tokens.shape, BF16),
        shape(tokens.shape, BF16),
        shape((12 * width, width), BF16),
        shape((groups, own, width), BF16),
        shape((groups, own, width), BF16),
        shape((groups, sizes.window, 3 * LANES), BF16),
    )
    bias_width = 5 * LANES + weights[8].shape[0]
    scratch = [
        vmem((14 * width, width), BF16),
        vmem((docs, width), F32),
        vmem((own, 1), F32),
        vmem((own, 1), F32),
        vmem((groups, sizes.blocks, 8, sizes.block), F32),
        vmem((groups, own, 2 * LANES), BF16),
        vmem((groups, own, 2 * LANES), BF16),
        vmem((own, width), BF16),
        vmem((own, width), F32),
        vmem((2, own, width), F32),
        vmem((sizes.blocks, sizes.keys, sizes.block), F32),
        vmem((2, shard, width), BF16),
        vmem((1, bias_width), F32),
        vmem((groups, 1, bias_width), F32),
        vmem((4, width, width), BF16),
        vmem((3, 8, shard, width), BF16),
        vmem((3, 4, shard, width), BF16),
        vmem((3, 3, shard, width), BF16),
        vmem((groups, 2, LONGEST, 3 * LANES), BF16),
        vmem((4, 24, width), F32),
        vmem((6, 24, width), F32),
        vmem((16, half), BF16),
        vmem((3, 16, half), BF16),
        vmem((ways, 16, half), BF16),
        vmem((queries, width), F32),
        vmem((2, ways, 16, half), BF16),
        vmem((2, ways, 16, half), BF16),
        vmem((ways, 8, LANES), F32),
        vmem((ways, 8, LANES), F32),
        dma((3, 31)),
        dma((3, 32)),
        dma((15,)),
        dma((2, 3)),
        dma((4 + groups,)),
        dma((10,)),
        dma((1,)),
        dma((2, 4)),
        dma((2, 2, 3)),
        dma((2, 3, 2)),
        dma((2, 3, 8)),
        dma((2, 3, 4)),
        dma((2, 3, 3)),
        dma((2, 4, 2)),
        dma((2, 6)),
        dma((2, 3)),
        dma((4, 2, ways - 1)),
    ]
    return pl.pallas_call(
        functools.partial(layer_kernel, sizes),
        out_shape=outs,
        in_specs=specs(SMEM, ANY, ANY, ANY, *[VMEM] * (1 + len(weights) + len(rows))),
        out_specs=specs(*[VMEM] * 4, *[ANY] * 6),
        scratch_shapes=scratch,
        compiler_params=params(collective_id=0, has_side_effects=True),
        name="layer",
    )(lengths, tokens, cotangent, passages, gold, *weights, *rows)[:6]


def cut_along(array, dim, devices):
    before, after = (array.shape[:dim], array.shape[dim + 1 :])
    return jnp.moveaxis(array.reshape(*before, devices, -1, *after), dim, 0)


def summed_on_arrival(array, axis, dim):
    pieces = cut_along(array, dim, lax.axis_size(axis))
    arrived = lax.all_to_all(pieces, axis, split_axis=0, concat_axis=0, tiled=True)
    return arrived.astype(F32).sum(axis=0)


def score(cls, passages, gold):
    all_first = lax.all_gather(cls, "dp", axis=0, tiled=True)
    table = dot(all_first, passages, 1, 1)
    peak = lax.pmax(jnp.max(table, axis=1), "dp")
    total = lax.psum(jnp.sum(jnp.exp(table - peak[:, None]), axis=1), "dp")
    own = cls.shape[0]
    lse = lax.dynamic_slice_in_dim(peak + jnp.log(total), lax.axis_index("dp") * own, own)
    soft = jnp.exp(table - peak[:, None]) / total[:, None]
    first = lax.axis_index("dp") * table.shape[1]
    columns = first + jnp.arange(table.shape[1], dtype=jnp.int32)
    target = (gold[:, None] == columns[None, :]).astype(F32)
    grad = dot((soft - target).astype(BF16), passages)
    return table, lse, summed_on_arrival(grad.astype(BF16), "dp", 0)


def plain_layer(sizes, tokens, cotangent, lengths, gold, passages, shards, rows):
    me, groups = lax.axis_index("mp"), sizes.groups
    w_key, w_value, w_query, w_out, w_up, w_down, b_value, b_query, b_up = shards
    packed = jnp.stack(
        [jnp.concatenate([w_key, w_value, w_query, w_out.T], axis=1), w_up, w_down]
    )
    c = w_key.shape[1]
    zeros = jnp.zeros((c,), F32)
    own_bias = jnp.concatenate([zeros, b_value, b_query, zeros[:HEAD], b_up])[None]
    whole = lax.all_gather(lax.all_gather(packed, "dp", axis=1, tiled=True), "mp", axis=1)
    biases = lax.all_gather(own_bias, "mp", axis=0)
    encoded, cls, *saved = run_forward(sizes, lengths, tokens, (whole, biases), rows)
    cls = lax.psum(cls, "mp").astype(BF16)
    table, lse, dcls = score(cls, passages, gold)
    n_1, r_1, n_2, r_2, z, slope, kv, q, logs, ctx = saved
    dh_1, dkv, dq, grads_ffn, grads_out, small = run_backward(
        sizes, lengths, cotangent, dcls, whole, rows[1], rows[2], rows[4], saved
    )
    halo, own = LONGEST, sizes.own
    offset = own * me - sizes.window_start(me)
    to_left = lax.dynamic_slice_in_dim(dkv, offset - halo, halo, axis=1).astype(BF16)
    to_right = lax.dynamic_slice_in_dim(dkv, offset + own, halo, axis=1).astype(BF16)
    from_right = lax.ppermute(to_left, "mp", [(i, i - 1) for i in range(1, groups)])
    from_left = lax.ppermute(to_right, "mp", [(i, i + 1) for i in range(groups - 1)])
    dkv = lax.dynamic_slice_in_dim(dkv, offset, own, axis=1)
    dkv = dkv.at[:, own - halo :].add(from_right.astype(F32))
    dkv = dkv.at[:, :halo].add(from_left.astype(F32))
    own_tokens = lax.dynamic_slice_in_dim(tokens, own * me, own, axis=0)
    token_part, grads_attn, small_attn = run_input(
        sizes, own_tokens, whole[0], dkv, dq, dh_1, grads_out
    )
    token_grad = lax.all_gather(token_part, "mp", axis=0, tiled=True).astype(F32)
    encoded = lax.all_gather(encoded, "mp", axis=0, tiled=True)
    grads = jnp.stack([grads_attn, grads_ffn[0], grads_ffn[1]])
    grads = summed_on_arrival(grads, "mp", 1)[:, 0].astype(BF16)
    grads = summed_on_arrival(grads, "dp", 1)
    small, small_attn = lax.psum((small, small_attn), ("dp", "mp"))
    mine = lax.dynamic_index_in_dim(small_attn[:, 0], me, 0, keepdims=False)
    up_bias = lax.dynamic_index_in_dim(small, 8 + me, 0, keepdims=False)
    return (
        table,
        lse,
        encoded,
        token_grad,
        grads[0, :, 2 * c : 3 * c],
        grads[0, :, :c],
        grads[0, :, c : 2 * c],
        mine[2 * c : 3 * c],
        mine[c : 2 * c],
        grads[0, :, 3 * c :].T,
        small[5],
        small[3],
        small[4],
        grads[1],
        up_bias,
        grads[2].T,
        small[2],
        small[0],
        small[1],
    )


def outputs_kernel(cols, table, lse, small, shards, encoded, tokens, *outs):
    *outs, got, wide, passed, sems = outs
    (
        table_out,
        lse_out,
        encoded_out,
        tokens_out,
        g_query,
        g_key,
        g_value,
        gb_query,
        gb_value,
        g_out,
        gb_out,
        g_gain_1,
        g_shift_1,
        g_up,
        gb_up,
        g_down,
        gb_down,
        g_gain_2,
        g_shift_2,
    ) = outs
    steps = got.shape[0]
    rows = [pl.ds(k * got.shape[1], got.shape[1]) for k in range(steps)]
    copies = [pltpu.make_async_copy(tokens.at[rows[k]], got.at[k], sems.at[0, k]) for k in range(steps)]
    writes = [pltpu.make_async_copy(wide.at[k], tokens_out.at[rows[k]], sems.at[1, k]) for k in range(steps)]
    takes = [pltpu.make_async_copy(encoded.at[rows[k]], passed.at[k], sems.at[2, k]) for k in range(steps)]
    gives = [pltpu.make_async_copy(passed.at[k], encoded_out.at[rows[k]], sems.at[3, k]) for k in range(steps)]
    for k in range(steps):
        copies[k].start()
        takes[k].start()
    for k in range(steps):
        copies[k].wait()
        wide[k] = got[k].astype(F32)
        writes[k].start()
        takes[k].wait()
        gives[k].start()
    me = lax.axis_index("mp")
    table_out[...] = table[...]
    lse_out[...] = lse[...].T.reshape(lse_out.shape)
    for k, target in enumerate((g_key, g_value, g_query)):
        target[...] = shards[0, :, k * cols : (k + 1) * cols]
    g_out[...] = shards[0, :, 3 * cols :].T
    g_up[...] = shards[1]
    g_down[...] = shards[2]
    heads = small[pl.ds(16 + me, 1), :]
    gb_value[...] = heads[:, cols : 2 * cols].reshape(gb_value.shape)
    gb_query[...] = heads[:, 2 * cols : 3 * cols].reshape(gb_query.shape)
    gb_up[...] = small[pl.ds(8 + me, 1), :].reshape(gb_up.shape)
    for k, target in enumerate((g_gain_2, g_shift_2, gb_down, g_gain_1, g_shift_1, gb_out)):
        target[...] = small[k : k + 1, :].reshape(target.shape)
    for k in range(steps):
        writes[k].wait()
        gives[k].wait()


def run_outputs(made, cols):
    table, lse, small, shards, encoded, tokens = made
    rows, width = shards.shape[1:]
    shape = jax.ShapeDtypeStruct
    vector = shape((width,), F32)
    outs = (
        shape(table.shape, F32),
        shape((lse.shape[0],), F32),
        shape(encoded.shape, BF16),
        shape(tokens.shape, F32),
        *[shape((rows, cols), F32)] * 3,
        *[shape((cols,), F32)] * 2,
        shape((cols, rows), F32),
        *[vector] * 3,
        shape((rows, width), F32),
        vector,
        shape((rows, width), F32),
        *[vector] * 3,
    )
    steps = 4
    span = tokens.shape[0] // steps
    return pl.pallas_call(
        functools.partial(outputs_kernel, cols),
        out_shape=outs,
        in_specs=specs(*[VMEM] * 4, ANY, ANY),
        out_specs=specs(*[ANY if k in (2, 3) else VMEM for k in range(len(outs))]),
        scratch_shapes=[
            pltpu.VMEM((steps, span, width), BF16),
            pltpu.VMEM((steps, span, width), F32),
            pltpu.VMEM((steps, span, width), BF16),
            pltpu.SemaphoreType.DMA((4, steps)),
        ],
        compiler_params=params(),
        name="outputs",
    )(*made)


def body(
    tokens,
    cotangent,
    lengths,
    gold,
    passages,
    w_query,
    w_key,
    w_value,
    b_query,
    b_value,
    w_out,
    b_out,
    gain_attn,
    shift_attn,
    w_up,
    b_up,
    w_down,
    b_down,
    gain_ffn,
    shift_ffn,
):
    groups = lax.axis_size("mp")
    sizes = Sizes(tokens.shape[0], tokens.shape[1], groups)
    rows = (b_out, gain_attn, shift_attn, b_down, gain_ffn, shift_ffn)
    shards = (w_key, w_value, w_query, w_out, w_up, w_down.T, b_value, b_query, b_up)
    if lax.axis_size("dp") == 8 and groups == 4:
        made = run_layer(sizes, lengths, tokens, cotangent, passages, gold, shards, rows)
        outs = list(run_outputs(made, w_key.shape[1]))
        outs[15] = outs[15].T
        return tuple(outs)
    return plain_layer(sizes, tokens, cotangent, lengths, gold, passages, shards, rows)


def solution(mesh):
    by_dp, shared, cross = P("dp", None), P(), P("dp", "mp")
    return jax.shard_map(
        body,
        mesh=mesh,
        in_specs=(
            by_dp,
            by_dp,
            by_dp,
            shared,
            by_dp,
            cross,
            cross,
            cross,
            P("mp"),
            P("mp"),
            P("mp", "dp"),
            shared,
            shared,
            shared,
            cross,
            P("mp"),
            P("mp", "dp"),
            shared,
            shared,
            shared,
        ),
        out_specs=(
            P(None, "dp"),
            P("dp"),
            by_dp,
            by_dp,
            cross,
            cross,
            cross,
            P("mp"),
            P("mp"),
            P("mp", "dp"),
            shared,
            shared,
            shared,
            cross,
            P("mp"),
            P("mp", "dp"),
            shared,
            shared,
            shared,
        ),
        check_vma=False,
    )
```
